32 devices in a mesh: dp: 8 (over y, x, core), tensor: 4 (over z).
Axes of the slice: x: 2, y: 2, z: 4, core: 2. Of those that a mesh axis runs over, the one named last changes fastest.
Arguments:
- hidden_in: bfloat16 [1024, 2048], P('dp'), may hold values from -6 to 6
- seq_lengths: int32 [16, 4], P('dp'), may hold values from 1 to 32, 64 in all within a row
- norm_gains: float32 [4, 2048], replicated, may hold values from 0.25 to 1.75
- mixer_in: bfloat16 [2, 2048, 4096], P(None, 'dp', 'tensor'), may hold values from -0.125 to 0.125
- mixer_rows: bfloat16 [2336, 4096], P('dp', 'tensor'), may hold values from -0.375 to 0.375
- conv_weight: float32 [4096, 4], P('tensor'), may hold values from -3 to 3
- conv_bias: float32 [4096], P('tensor'), may hold values from -3 to 3
- step_bias: float32 [4096], P('tensor'), may hold values from -5 to -2
- decay_log: float32 [4096, 16], P('tensor'), may hold values from 0 to 2.8
- skip_gain: float32 [4096], P('tensor'), may hold values from 0.5 to 1.5
- early_gate_up: bfloat16 [2, 2048, 8192], P(None, 'dp', 'tensor'), may hold values from -0.125 to 0.125
- early_down: bfloat16 [2048, 8192], P('dp', 'tensor'), may hold values from -0.0625 to 0.0625
- attention_in: bfloat16 [3, 2048, 2048], P(None, 'dp', 'tensor'), may hold values from -0.1875 to 0.1875
- attention_out: bfloat16 [2048, 2048], P('dp', 'tensor'), may hold values from -0.5 to 0.5
- late_gate_up: bfloat16 [2, 2048, 8192], P(None, 'dp', 'tensor'), may hold values from -0.125 to 0.125
- late_down: bfloat16 [2048, 8192], P('dp', 'tensor'), may hold values from -0.0625 to 0.0625
- output_grad: bfloat16 [1024, 2048], P('dp'), may hold values from -6 to 6
Outputs:
- output: float32 [1024, 2048], P('dp')
- input_grad: float32 [1024, 2048], P('dp')
- norm_gains_grad: float32 [4, 2048], replicated
- mixer_in_grad: float32 [2, 2048, 4096], P(None, 'dp', 'tensor')
- mixer_rows_grad: float32 [2336, 4096], P('dp', 'tensor')
- conv_weight_grad: float32 [4096, 4], P('tensor')
- conv_bias_grad: float32 [4096], P('tensor')
- step_bias_grad: float32 [4096], P('tensor')
- decay_log_grad: float32 [4096, 16], P('tensor')
- skip_gain_grad: float32 [4096], P('tensor')
- early_gate_up_grad: float32 [2, 2048, 8192], P(None, 'dp', 'tensor')
- early_down_grad: float32 [2048, 8192], P('dp', 'tensor')
- attention_in_grad: float32 [3, 2048, 2048], P(None, 'dp', 'tensor')
- attention_out_grad: float32 [2048, 2048], P('dp', 'tensor')
- late_gate_up_grad: float32 [2, 2048, 8192], P(None, 'dp', 'tensor')
- late_down_grad: float32 [2048, 8192], P('dp', 'tensor')
The draws below stay inside these ranges and needn't reach their ends.
Inputs may be any that keep to these rules, and one draw needn't show every extreme that they name: `seq_lengths`: each row lists the lengths of the 4 sequences packed one after another into one micro-batch; every row sums to 64 and its longest sequence has exactly 32 tokens.
All inputs are finite; a program needn't handle non-finite values.
Results may differ from the reference program's by a relative error of at most 0.025.
The reference program's roundings to bfloat16 on the way (of `first`, `channel`, `mixer_out`, `hidden`, `third`, `query` and `attended`) count: a program that leaves them out, or rounds other values in their place, can miss the bound.
Values may be sent and summed in bfloat16 or wider, within the bound.
A program may use at most 320 MiB of HBM per device.

```python
import math
from functools import partial
import jax
import jax.numpy as jnp
import numpy as np
from jax import lax

D = 2048
INNER = 4096
STATE = 16
CONV = 4
DT_RANK = 128
FF = 8192
HEADS = 16
HEAD_DIM = 128
WINDOW = 2048
MICRO = 2
SEQS = 4
TOK_MB = 64
TOK_DEV = 128
TOKENS = 1024
HD = 2048
PROJ_OUT = 160
N_DP = 8


def strengthened(array, own_key, source, target, blocks, factor):
    owner, partner = [(jnp.arange(array.shape[position]) // (array.shape[position] // blocks)).reshape([-1 if axis == position else 1 for axis in range(array.ndim)]) for position in (source, target)]
    chosen = jax.random.permutation(own_key, blocks)[partner]
    strong = (owner == chosen) | (owner == (partner + blocks // 2) % blocks)
    return jnp.where(strong, factor * array, array)


def level_of(key, shape, split, smallest, top_value):
    gain = 1.0
    for axis_at, blocks in split:
        steps = jax.random.uniform(jax.random.fold_in(jax.random.fold_in(key, 6), axis_at), (blocks,), jnp.float32, smallest / len(split), top_value / len(split))
        gain = gain * jnp.repeat(jnp.exp(steps), shape[axis_at] // blocks).reshape((-1,) + (1,) * (len(shape) - 1 - axis_at))
    return gain


def profile(count, total, reach, lean):
    weights = [(1 << 20) // math.isqrt(rank ** lean) + 1 for rank in range(2, count + 1)]
    surplus, holding = total - reach - (count - 1), [1] * (count - 1)
    while surplus > 0:
        candidates = [i for i in range(count - 1) if holding[i] < reach]
        pool, left = sum([weights[i] for i in candidates]), surplus
        for i in candidates:
            more = min(reach - holding[i], max(1, left * weights[i] // pool), surplus)
            holding[i] = holding[i] + more
            surplus = surplus - more
    return np.array([reach] + holding)


def ragged(key, amount, total, most, lean):
    if amount == 2:
        one = jax.random.randint(key, (), max(1, total - most), min(most, total - 1) + 1)
        return jnp.stack([one, total - one])
    sizes = jnp.asarray(profile(amount, total, most, lean), jnp.int32)
    twos = (amount - 1) // 2
    source_of, receiver = sizes[1:1 + 2 * twos:2], sizes[2:2 + 2 * twos:2]
    slack = jnp.minimum(source_of - 1, most - receiver)
    moved = jax.random.randint(jax.random.fold_in(key, 1), (twos,), 0, 1 << 20) % (slack + 1)
    sizes = sizes.at[1:1 + 2 * twos:2].set(source_of - moved).at[2:2 + 2 * twos:2].set(receiver + moved)
    return sizes[jax.random.permutation(jax.random.fold_in(key, 2), amount)]


def noise(rng, dims, scale, limit, split=(), held_as=jnp.bfloat16):
    factor_of = level_of(rng, dims, split, -0.22, 0.18) if split else 1.0
    values = jax.random.normal(rng, dims, jnp.float32) * scale * factor_of
    return jnp.minimum(jnp.maximum(values, -limit), limit).astype(held_as)


def gaussian_with(key, dims, scale, most, shards, heavy, kind=jnp.bfloat16):
    entries = scale * jax.random.normal(key, dims, jnp.float32)
    if shards:
        entries = entries * level_of(key, dims, shards, -0.22, 0.18)
    return jnp.clip(strengthened(entries, jax.random.fold_in(key, 3), *heavy), -most, most).astype(kind)


def setup_inputs(seed: int = 0) -> dict:
    seeds = jax.random.split(jax.random.key(seed), 18)
    return {
        "hidden_in": noise(seeds[0], (TOKENS, D), 1.0, 6.0, ((0, 8),)),
        "seq_lengths": jax.vmap(lambda own: ragged(own, SEQS, TOK_MB, TOK_MB // 2, 2))(jax.random.split(seeds[1], (N_DP * MICRO))).reshape((N_DP * MICRO, SEQS)).astype(jnp.int32),
        "norm_gains": jnp.clip(1.0 + 0.15 * jax.random.normal(seeds[2], (4, D), jnp.float32), 0.25, 1.75),
        "mixer_in": noise(seeds[3], (2, D, INNER), D ** -0.5, 0.125, ((1, 8), (2, 4))),
        "mixer_rows": noise(seeds[4], (D + PROJ_OUT + DT_RANK, INNER), (INNER // 16) ** -0.5, 0.375, ((0, 8), (1, 4))),
        "conv_weight": noise(seeds[5], (INNER, CONV), CONV ** -0.5, 3.0, ((0, 4),), jnp.float32),
        "conv_bias": noise(seeds[6], (INNER,), 0.5, 3.0, ((0, 4),), jnp.float32),
        "step_bias": jnp.clip(-5.0 + 3.0 * jax.random.uniform(seeds[7], (INNER,), jnp.float32) ** level_of(seeds[7], (INNER,), ((0, 4),), -0.2, 0.2), -5.0, -2.0),
        "decay_log": jnp.clip(2.8 * jax.random.uniform(seeds[8], (INNER, STATE), jnp.float32) ** level_of(seeds[8], (INNER, STATE), ((0, 4),), -0.2, 0.2), 0.0, 2.8),
        "skip_gain": jnp.clip(0.5 + 1.0 * jax.random.uniform(seeds[9], (INNER,), jnp.float32) ** level_of(seeds[9], (INNER,), ((0, 4),), -0.2, 0.2), 0.5, 1.5),
        "early_gate_up": noise(seeds[10], (2, D, FF), D ** -0.5, 0.125, ((1, 8), (2, 4))),
        "early_down": noise(seeds[11], (D, FF), FF ** -0.5, 0.0625, ((0, 8), (1, 4))),
        "attention_in": noise(seeds[12], (3, D, HD), (D // 2) ** -0.5, 0.1875, ((1, 8), (2, 4))),
        "attention_out": noise(seeds[13], (D, HD), (HD // 16) ** -0.5, 0.5, ((0, 8), (1, 4))),
        "late_gate_up": noise(seeds[14], (2, D, FF), D ** -0.5, 0.125, ((1, 8), (2, 4))),
        "late_down": noise(seeds[15], (D, FF), FF ** -0.5, 0.0625, ((0, 8), (1, 4))),
        "output_grad": gaussian_with(seeds[16], (TOKENS, D), 1.0, 6.0, ((0, 8),), (0, 1, 8, 2.0)),
    }


EPS = 1e-05
SCAN_BLOCK = 32
NEG_FILL = -1e+30

@jax.custom_vjp
def low(v):
    return lax.optimization_barrier(v.astype(jnp.bfloat16)).astype(jnp.float32)

@jax.custom_vjp
def low_back(v):
    return v

def low_keep(v):
    return (low(v), None)

def low_pass(kept, grad):
    return (grad,)

def back_keep(v):
    return (v, None)

def back_low(kept, grad):
    return (low(grad),)
low.defvjp(low_keep, low_pass)
low_back.defvjp(back_keep, back_low)

def dense(left, right):
    return jnp.dot(left, right, precision=lax.Precision.HIGHEST)

def dense_t(left, right):
    return lax.dot_general(left, right, (((1,), (1,)), ((), ())), precision=lax.Precision.HIGHEST)

def rms_norm(values, weight):
    return values * lax.rsqrt(lax.optimization_barrier(jnp.mean(values * values, axis=-1, keepdims=True)) + EPS) * weight

def segment_info(lengths, tokens):
    flat_lengths = lengths.reshape(-1)
    ends = jnp.cumsum(flat_lengths, dtype=jnp.int32)
    firsts = ends - flat_lengths
    places = jnp.arange(tokens, dtype=jnp.int32)
    segs = lax.optimization_barrier(jnp.sum((places[:, None] >= ends[None, :]).astype(jnp.int32), axis=1))
    starts = jnp.any(places[:, None] == firsts[None, :], axis=1)
    return (segs, starts)

def allowed_pairs(segs):
    places = jnp.arange(segs.shape[-1], dtype=jnp.int32)
    distance = places[:, None] - places[None, :]
    return (segs[:, None] == segs[None, :]) & (distance >= 0) & (distance < WINDOW)

def causal_conv(segs, stream, weight, offset):
    total = offset + stream * weight[:, 0]
    for lag_step in range(1, CONV):
        moved = jnp.concatenate([jnp.zeros_like(stream[..., :lag_step, :]), stream[..., :-lag_step, :]], axis=-2)
        moved_segs = jnp.concatenate([jnp.full_like(segs[..., :lag_step], -1), segs[..., :-lag_step]], axis=-1)
        linked = (segs == moved_segs).astype(stream.dtype)
        total = total + moved * weight[:, lag_step] * linked[..., None]
    return jax.nn.silu(total)

def combine_pairs(earlier, later):
    return (earlier[0] * later[0], later[0] * earlier[1] + later[1])

def blocked_scan(step_size, channel_in, input_map, output_map, keeping, rates, block_rows):
    groups, length, channels = step_size.shape
    block_count = length // block_rows

    def to_blocks(values):
        shaped = values.reshape((groups, block_count, block_rows) + values.shape[2:])
        return jnp.moveaxis(shaped, 1, 0)

    def advance(carry_state, pieces):
        step_block, channel_block, input_block, output_block, keep_block = pieces
        decay_rate = jnp.exp(step_block[..., None] * rates) * keep_block[..., None, None]
        driven = (step_block * channel_block)[..., None] * input_block[:, :, None, :]
        decay_run, driven_run = lax.associative_scan(combine_pairs, (decay_rate, driven), axis=1)
        states = decay_run * carry_state[:, None] + driven_run
        return (states[:, -1], lax.optimization_barrier(jnp.sum(states * output_block[:, :, None, :], axis=-1)))
    zero_state = jnp.zeros((groups, channels, rates.shape[1]), step_size.dtype)
    pieces = (to_blocks(step_size), to_blocks(channel_in), to_blocks(input_map), to_blocks(output_map), to_blocks(keeping))
    _, outputs = lax.scan(jax.checkpoint(advance), zero_state, pieces)
    return jnp.moveaxis(outputs, 0, 1).reshape(groups, length, channels)

def selective_scan(starts, channel_in, step_raw, mixed_rows, gate_half, step_bias, decay_log, skip_gain):
    step_size = jax.nn.softplus(step_raw + step_bias)
    input_map = mixed_rows[..., DT_RANK:DT_RANK + STATE]
    output_map = mixed_rows[..., DT_RANK + STATE:]
    keeping = 1.0 - starts.astype(channel_in.dtype)
    scanned = blocked_scan(step_size, channel_in, input_map, output_map, keeping, -jnp.exp(decay_log), SCAN_BLOCK)
    return (scanned + skip_gain * channel_in) * jax.nn.silu(gate_half)

def attend_group(pieces):
    query, keys, values, segs = pieces
    allowed = allowed_pairs(segs)
    scores = low_back(jnp.einsum('qhd,khd->hqk', query, keys, precision=lax.Precision.HIGHEST) * (1.0 / math.sqrt(HEAD_DIM)))
    masked = jnp.where(allowed[None], scores, NEG_FILL)
    row_max = lax.optimization_barrier(jnp.max(masked, axis=-1, keepdims=True))
    shifted = jnp.exp(masked - row_max)
    probs = shifted / lax.optimization_barrier(jnp.sum(shifted, axis=-1, keepdims=True))
    return jnp.einsum('hqk,khd->qhd', low(probs), values, precision=lax.Precision.HIGHEST)

def feed_forward(normed, gate_up, down_mat):
    gate = low_back(dense(normed, gate_up[0]))
    upward = low_back(dense(normed, gate_up[1]))
    hidden = low(jax.nn.silu(gate) * upward)
    return low_back(dense_t(hidden, down_mat))

def layer_forward(segs, starts, stream, norm_gains, mixer_in, mixer_rows, conv_weight, conv_bias, step_bias, decay_log, skip_gain, early_gate_up, early_down, attention_in, attention_out, late_gate_up, late_down):
    groups = segs.shape[0]
    width = stream.shape[1]
    count_rows = stream.shape[0]

    def grouped(values):
        return values.reshape((groups, -1) + values.shape[1:])

    def ungrouped(values):
        return values.reshape((count_rows,) + values.shape[2:])

    def to_heads(values):
        return grouped(values).reshape(groups, -1, HEADS, HEAD_DIM)
    first = low(rms_norm(stream, norm_gains[0]))
    conv_in = low_back(dense(first, mixer_in[0]))
    gate_half = low_back(dense(first, mixer_in[1]))
    channel = low(causal_conv(segs, grouped(conv_in), conv_weight, conv_bias))
    out_mat = mixer_rows[:width]
    select_mat = mixer_rows[width:width + PROJ_OUT]
    step_mat = mixer_rows[width + PROJ_OUT:]
    mix_rows = low_back(dense_t(ungrouped(channel), select_mat))
    step_raw = low_back(dense(low(mix_rows[:, :DT_RANK]), step_mat))
    scanned = selective_scan(starts, channel, grouped(step_raw), grouped(mix_rows), grouped(gate_half), step_bias, decay_log, skip_gain)
    mixer_out = low(ungrouped(scanned))
    stream = stream + low_back(dense_t(mixer_out, out_mat))
    stream = stream + feed_forward(low(rms_norm(stream, norm_gains[1])), early_gate_up, early_down)
    third = low(rms_norm(stream, norm_gains[2]))
    query = to_heads(low(low_back(dense(third, attention_in[0]))))
    keys = to_heads(low(low_back(dense(third, attention_in[1]))))
    values = to_heads(low(low_back(dense(third, attention_in[2]))))
    attended = lax.map(jax.checkpoint(attend_group), (query, keys, values, segs))
    attended = low(low_back(attended.reshape(count_rows, -1)))
    stream = stream + low_back(dense_t(attended, attention_out))
    return stream + feed_forward(low(rms_norm(stream, norm_gains[3])), late_gate_up, late_down)

def reference(hidden_in, seq_lengths, norm_gains, mixer_in, mixer_rows, conv_weight, conv_bias, step_bias, decay_log, skip_gain, early_gate_up, early_down, attention_in, attention_out, late_gate_up, late_down, output_grad):
    segs, starts = jax.vmap(partial(segment_info, tokens=TOK_DEV))(seq_lengths.reshape(N_DP, MICRO * SEQS))
    result, layer_back = jax.vjp(partial(layer_forward, segs, starts), hidden_in.astype(jnp.float32), norm_gains, mixer_in.astype(jnp.float32), mixer_rows.astype(jnp.float32), conv_weight, conv_bias, step_bias, decay_log, skip_gain, early_gate_up.astype(jnp.float32), early_down.astype(jnp.float32), attention_in.astype(jnp.float32), attention_out.astype(jnp.float32), late_gate_up.astype(jnp.float32), late_down.astype(jnp.float32))
    grads = layer_back(output_grad.astype(jnp.float32))
    return (result, grads[0], grads[1], grads[2], grads[3], grads[4], grads[5], grads[6], grads[7], grads[8], grads[9], grads[10], grads[11], grads[12], grads[13], grads[14])
```

```python
from functools import partial
import math

import jax
import jax.numpy as jnp
from jax import lax
from jax.experimental import pallas as pl
from jax.experimental.pallas import tpu as pltpu
from jax.sharding import PartitionSpec as P

STATE = 16
CONV = 4
DT_RANK = 128
HEAD_DIM = 128
WINDOW = 2048
PROJ_OUT = 160


EPS = 1e-05
NEG_FILL = -1e30


def project(left, right):
    return jnp.dot(left, right, preferred_element_type=jnp.float32)


def project_t(left, right):
    return lax.dot_general(
        left, right, (((1,), (1,)), ((), ())), preferred_element_type=jnp.float32
    )


def outer_rows(left, right):
    return lax.dot_general(
        left, right, (((0,), (0,)), ((), ())), preferred_element_type=jnp.float32
    )


def rms_norm(values, weight):
    return values * lax.rsqrt(jnp.mean(values * values, axis=-1, keepdims=True) + EPS) * weight


def segment_info(lengths, tokens):
    flat_lengths = lengths.reshape(-1)
    ends = jnp.cumsum(flat_lengths, dtype=jnp.int32)
    firsts = ends - flat_lengths
    places = jnp.arange(tokens, dtype=jnp.int32)
    segs = jnp.sum((places[:, None] >= ends[None, :]).astype(jnp.int32), axis=1)
    starts = jnp.any(places[:, None] == firsts[None, :], axis=1)
    return (segs, starts)


def allowed_pairs(segs):
    places = jnp.arange(segs.shape[-1], dtype=jnp.int32)
    distance = places[:, None] - places[None, :]
    return (segs[:, None] == segs[None, :]) & (distance >= 0) & (distance < WINDOW)


def causal_conv(segs, stream, weight, offset):
    total = offset + stream * weight[:, 0]
    for lag_step in range(1, CONV):
        moved = jnp.concatenate(
            [jnp.zeros_like(stream[..., :lag_step, :]), stream[..., :-lag_step, :]], axis=-2
        )
        moved_segs = jnp.concatenate(
            [jnp.full_like(segs[..., :lag_step], -1), segs[..., :-lag_step]], axis=-1
        )
        linked = (segs == moved_segs).astype(stream.dtype)
        total = total + moved * weight[:, lag_step] * linked[..., None]
    return jax.nn.silu(total)


LANES = 128


def softplus(v):
    return jnp.maximum(v, 0.0) + jnp.log1p(jnp.exp(-jnp.abs(v)))


def scan_forward_kernel(
    groups, length, keep_ref, chan_ref, raw_ref, gate_ref, bias_ref, rate_ref, skip_ref, in_ref, out_ref,
    mixed_ref, step_s, drive_s, y_s,
):
    width = chan_ref.shape[1]
    blocks = width // LANES
    step_s[...] = softplus(raw_ref[...] + bias_ref[...])
    drive_s[...] = step_s[...] * chan_ref[...].astype(jnp.float32)
    rates = [rate_ref[:, pl.ds(b * LANES, LANES)] for b in range(blocks)]

    def advance(t, states):
        fresh = []
        for g in range(groups):
            row = g * length + t
            keep = keep_ref[row]
            input_map = in_ref[row]
            output_map = out_ref[row]
            for b in range(blocks):
                lanes = pl.ds(b * LANES, LANES)
                decay = jnp.exp(step_s[pl.ds(row, 1), lanes] * rates[b]) * keep
                state = decay * states[g * blocks + b] + drive_s[pl.ds(row, 1), lanes] * input_map
                y_s[pl.ds(row, 1), lanes] = jnp.sum(state * output_map, axis=0, keepdims=True)
                fresh.append(state)
        return tuple(fresh)

    zero = jnp.zeros((STATE, LANES), jnp.float32)
    lax.fori_loop(0, length, advance, (zero,) * (groups * blocks))
    gate = gate_ref[...]
    silu = gate / (1.0 + jnp.exp(-gate))
    mixed_ref[...] = (
        (y_s[...] + skip_ref[...] * chan_ref[...].astype(jnp.float32)) * silu
    ).astype(mixed_ref.dtype)


def scan_forward(keep, channel, step_raw, gate_half, step_bias, rates_t, skip_gain, in_wide, out_wide, groups, width):
    tokens, channels = channel.shape
    column = pl.BlockSpec((tokens, width), lambda i: (0, i))
    row = pl.BlockSpec((1, width), lambda i: (0, i))
    maps = pl.BlockSpec((tokens, STATE, LANES), lambda i: (0, 0, 0))
    return pl.pallas_call(
        partial(scan_forward_kernel, groups, tokens // groups),
        grid=(channels // width,),
        in_specs=[
            pl.BlockSpec(memory_space=pltpu.SMEM), column, column, column, row,
            pl.BlockSpec((STATE, width), lambda i: (0, i)), row, maps, maps,
        ],
        out_specs=column,
        out_shape=jax.ShapeDtypeStruct((tokens, channels), jnp.bfloat16),
        scratch_shapes=[pltpu.VMEM((tokens, width), jnp.float32)] * 3,
        compiler_params=pltpu.CompilerParams(vmem_limit_bytes=48 << 20),
        cost_estimate=pl.CostEstimate(flops=1, bytes_accessed=28 << 20, transcendentals=0),
        name="scan_forward",
    )(keep, channel, step_raw, gate_half, step_bias[None], rates_t, skip_gain[None], in_wide, out_wide)


def scan_backward_kernel(
    groups, length, keep_ref, chan_ref, raw_ref, gate_ref, dmix_ref, bias_ref, rate_ref, skip_ref, in_ref, out_ref,
    dchan_ref, draw_ref, dgate_ref, din_ref, dout_ref, dbias_ref, drate_ref, dskip_ref,
    step_s, drive_s, y_s, dy_s, dd_s, ds_s, state_s, decay_s,
):
    width = chan_ref.shape[1]
    blocks = width // LANES
    chan = chan_ref[...].astype(jnp.float32)
    step_s[...] = softplus(raw_ref[...] + bias_ref[...])
    drive_s[...] = step_s[...] * chan
    gate = gate_ref[...]
    sig = 1.0 / (1.0 + jnp.exp(-gate))
    dy_s[...] = dmix_ref[...] * (gate * sig)
    rates = [rate_ref[:, pl.ds(b * LANES, LANES)] for b in range(blocks)]

    @pl.when(pl.program_id(0) == 0)
    def _():
        din_ref[...] = jnp.zeros_like(din_ref)
        dout_ref[...] = jnp.zeros_like(dout_ref)

    def advance(t, states):
        fresh = []
        for g in range(groups):
            row = g * length + t
            keep = keep_ref[row]
            input_map = in_ref[row]
            output_map = out_ref[row]
            total = None
            for b in range(blocks):
                lanes = pl.ds(b * LANES, LANES)
                decay = jnp.exp(step_s[pl.ds(row, 1), lanes] * rates[b]) * keep
                decay_s[row, :, lanes] = decay
                carried = decay * states[g * blocks + b]
                state_s[row, :, lanes] = carried
                state = carried + drive_s[pl.ds(row, 1), lanes] * input_map
                y_s[pl.ds(row, 1), lanes] = jnp.sum(state * output_map, axis=0, keepdims=True)
                term = state * dy_s[pl.ds(row, 1), lanes]
                total = term if total is None else total + term
                fresh.append(state)
            dout_ref[row] += total
        return tuple(fresh)

    zero = jnp.zeros((STATE, LANES), jnp.float32)
    count = groups * blocks
    lax.fori_loop(0, length, advance, (zero,) * count)

    def retreat(back, carry):
        t = length - 1 - back
        fresh, rate_sums = [], []
        for g in range(groups):
            row = g * length + t
            input_map = in_ref[row]
            output_map = out_ref[row]
            total = None
            for b in range(blocks):
                lanes = pl.ds(b * LANES, LANES)
                at = g * blocks + b
                dstate = carry[0][at] + dy_s[pl.ds(row, 1), lanes] * output_map
                dlog = dstate * state_s[row, :, lanes]
                dd_s[pl.ds(row, 1), lanes] = jnp.sum(dstate * input_map, axis=0, keepdims=True)
                ds_s[pl.ds(row, 1), lanes] = jnp.sum(dlog * rates[b], axis=0, keepdims=True)
                term = dstate * drive_s[pl.ds(row, 1), lanes]
                total = term if total is None else total + term
                rate_sums.append(carry[1][at] + dlog * step_s[pl.ds(row, 1), lanes])
                fresh.append(dstate * decay_s[row, :, lanes])
            din_ref[row] += total
        return (tuple(fresh), tuple(rate_sums))

    _, rate_sums = lax.fori_loop(0, length, retreat, ((zero,) * count, (zero,) * count))
    for b in range(blocks):
        lanes = pl.ds(b * LANES, LANES)
        drate_ref[:, lanes] = rates[b] * sum(rate_sums[g * blocks + b] for g in range(groups))
    direct = y_s[...] + skip_ref[...] * chan
    dgate_ref[...] = (dmix_ref[...] * direct * (sig * (1.0 + gate * (1.0 - sig)))).astype(dgate_ref.dtype)
    dskip_ref[...] = jnp.sum(dy_s[...] * chan, axis=0, keepdims=True)
    dchan_ref[...] = dd_s[...] * step_s[...] + skip_ref[...] * dy_s[...]
    shifted = raw_ref[...] + bias_ref[...]
    draw = (ds_s[...] + dd_s[...] * chan) / (1.0 + jnp.exp(-shifted))
    draw_ref[...] = draw.astype(draw_ref.dtype)
    dbias_ref[...] = jnp.sum(draw, axis=0, keepdims=True)


def scan_backward(
    keep, channel, step_raw, gate_half, dmixed, step_bias, rates_t, skip_gain, in_wide, out_wide, groups, width
):
    tokens, channels = channel.shape
    column = pl.BlockSpec((tokens, width), lambda i: (0, i))
    row = pl.BlockSpec((1, width), lambda i: (0, i))
    states = pl.BlockSpec((STATE, width), lambda i: (0, i))
    maps = pl.BlockSpec((tokens, STATE, LANES), lambda i: (0, 0, 0))
    sheet = jax.ShapeDtypeStruct((tokens, channels), jnp.float32)
    low = jax.ShapeDtypeStruct((tokens, channels), jnp.bfloat16)
    wide = jax.ShapeDtypeStruct((tokens, STATE, LANES), jnp.float32)
    line = jax.ShapeDtypeStruct((1, channels), jnp.float32)
    return pl.pallas_call(
        partial(scan_backward_kernel, groups, tokens // groups),
        grid=(channels // width,),
        in_specs=[
            pl.BlockSpec(memory_space=pltpu.SMEM), column, column, column, column, row, states, row, maps, maps,
        ],
        out_specs=[column, column, column, maps, maps, row, states, row],
        out_shape=[
            sheet, low, low, wide, wide, line, jax.ShapeDtypeStruct((STATE, channels), jnp.float32), line,
        ],
        scratch_shapes=[pltpu.VMEM((tokens, width), jnp.float32)] * 6
        + [pltpu.VMEM((tokens, STATE, width), jnp.float32)] * 2,
        compiler_params=pltpu.CompilerParams(vmem_limit_bytes=56 << 20),
        cost_estimate=pl.CostEstimate(flops=1, bytes_accessed=75 << 20, transcendentals=0),
        name="scan_backward",
    )(keep, channel, step_raw, gate_half, dmixed, step_bias[None], rates_t, skip_gain[None], in_wide, out_wide)


def attention_scores(query, keys, allowed):
    scores = jnp.einsum("qhd,khd->hqk", query, keys, preferred_element_type=jnp.float32) * (
        1.0 / math.sqrt(HEAD_DIM)
    )
    return jnp.where(allowed[None], scores, NEG_FILL)


def attention_forward(query, keys, values, allowed):
    scores = attention_scores(query, keys, allowed)
    row_max = jnp.max(scores, axis=-1, keepdims=True)
    shifted = jnp.exp(scores - row_max)
    totals = jnp.sum(shifted, axis=-1, keepdims=True)
    probs = shifted / totals
    mixed = jnp.einsum(
        "hqk,khd->qhd", probs.astype(jnp.bfloat16), values, preferred_element_type=jnp.float32
    )
    return (mixed, row_max + jnp.log(totals))


def attention_backward(query, keys, values, allowed, log_total, grad_mixed):
    scale = 1.0 / math.sqrt(HEAD_DIM)
    probs = jnp.exp(attention_scores(query, keys, allowed) - log_total)
    grad_values = jnp.einsum(
        "hqk,qhd->khd", probs.astype(jnp.bfloat16), grad_mixed, preferred_element_type=jnp.float32
    )
    grad_probs = jnp.einsum("qhd,khd->hqk", grad_mixed, values, preferred_element_type=jnp.float32)
    inner_sum = jnp.sum(probs * grad_probs, axis=-1, keepdims=True)
    grad_scores = (probs * (grad_probs - inner_sum)).astype(jnp.bfloat16)
    grad_query = (
        jnp.einsum("hqk,khd->qhd", grad_scores, keys, preferred_element_type=jnp.float32) * scale
    )
    grad_keys = (
        jnp.einsum("hqk,qhd->khd", grad_scores, query, preferred_element_type=jnp.float32) * scale
    )
    return (grad_query, grad_keys, grad_values)


def gated_unit(gate, upward):
    return jax.nn.silu(gate) * upward


def ffn_forward(normed_low, gate_up, down_mat):
    gate = project(normed_low, gate_up[0])
    upward = project(normed_low, gate_up[1])
    hidden = gated_unit(gate, upward).astype(jnp.bfloat16)
    return (project_t(hidden, down_mat), gate, upward, hidden)


def ffn_backward(grad_low, normed_low, gate, upward, hidden, gate_up, down_mat):
    grad_hidden = project(grad_low, down_mat)
    down_grad = outer_rows(grad_low, hidden)
    _, unit_back = jax.vjp(gated_unit, gate, upward)
    grad_gate, grad_up = unit_back(grad_hidden)
    gate_low = grad_gate.astype(jnp.bfloat16)
    up_low = grad_up.astype(jnp.bfloat16)
    joined_grad = outer_rows(normed_low, jnp.concatenate([gate_low, up_low], axis=1))
    grad_normed = project_t(gate_low, gate_up[0]) + project_t(up_low, gate_up[1])
    return (grad_normed, joined_grad, down_grad)


def flatten_low(grad_heads, tokens):
    return grad_heads.astype(jnp.bfloat16).reshape(tokens, -1)


def collect(stacked, row_block):
    return (
        lax.all_gather(stacked, "dp", axis=1, tiled=True),
        lax.all_gather(row_block, "dp", axis=0, tiled=True),
    )


def spread_grads(joined, row_block, count):
    summed = (
        lax.psum_scatter(joined.astype(jnp.bfloat16), "dp", scatter_dimension=0, tiled=True),
        lax.psum_scatter(row_block.astype(jnp.bfloat16), "dp", scatter_dimension=0, tiled=True),
    )
    rows_here = summed[0].shape[0]
    restacked = jnp.transpose(summed[0].reshape(rows_here, count, -1), (1, 0, 2))
    return (restacked.astype(jnp.float32), summed[1].astype(jnp.float32))


def branch_total(piece_sum):
    return lax.psum(piece_sum, "tensor")


def input_total(piece_sum):
    return lax.psum(piece_sum, "tensor")


def body(
    hidden_in,
    seq_lengths,
    norm_gains,
    mixer_in,
    mixer_rows,
    conv_weight,
    conv_bias,
    step_bias,
    decay_log,
    skip_gain,
    early_gate_up,
    early_down,
    attention_in,
    attention_out,
    late_gate_up,
    late_down,
    output_grad,
):
    tokens = hidden_in.shape[0]
    width = hidden_in.shape[1]
    segs, starts = segment_info(seq_lengths, tokens)
    allowed = allowed_pairs(segs)
    stream_zero = hidden_in.astype(jnp.float32)
    mixer_stack, mixer_mats = collect(mixer_in, mixer_rows)
    first_normed, first_back = jax.vjp(rms_norm, stream_zero, norm_gains[0])
    first_low = first_normed.astype(jnp.bfloat16)
    conv_in = project(first_low, mixer_stack[0])
    gate_half = project(first_low, mixer_stack[1])
    channel_full, conv_back = jax.vjp(partial(causal_conv, segs), conv_in, conv_weight, conv_bias)
    channel_low = channel_full.astype(jnp.bfloat16)
    mix_rows = lax.psum(project_t(channel_low, mixer_mats[width : width + PROJ_OUT]), "tensor")
    rank_low = mix_rows[:, :DT_RANK].astype(jnp.bfloat16)
    step_raw = project(rank_low, mixer_mats[width + PROJ_OUT :])
    groups = seq_lengths.shape[0]
    keeping = 1.0 - starts.astype(jnp.float32)
    rates_t = -jnp.exp(decay_log).T
    wide = (tokens, STATE, LANES)
    in_wide = jnp.broadcast_to(mix_rows[:, DT_RANK : DT_RANK + STATE, None], wide)
    out_wide = jnp.broadcast_to(mix_rows[:, DT_RANK + STATE :, None], wide)
    mixer_low = scan_forward(
        keeping, channel_low, step_raw, gate_half, step_bias, rates_t, skip_gain, in_wide, out_wide, groups, LANES
    )
    stream_one = stream_zero + branch_total(project_t(mixer_low, mixer_mats[:width]))
    early_stack, early_mat = collect(early_gate_up, early_down)
    second_normed, second_back = jax.vjp(rms_norm, stream_one, norm_gains[1])
    second_low = second_normed.astype(jnp.bfloat16)
    early_part, early_gate, early_up, early_hidden = ffn_forward(second_low, early_stack, early_mat)
    stream_two = stream_one + branch_total(early_part)
    focus_stack, focus_mat = collect(attention_in, attention_out)
    heads_here = focus_stack.shape[2] // HEAD_DIM
    third_normed, third_back = jax.vjp(rms_norm, stream_two, norm_gains[2])
    third_low = third_normed.astype(jnp.bfloat16)
    query = (
        project(third_low, focus_stack[0])
        .astype(jnp.bfloat16)
        .reshape(tokens, heads_here, HEAD_DIM)
    )
    keys = (
        project(third_low, focus_stack[1])
        .astype(jnp.bfloat16)
        .reshape(tokens, heads_here, HEAD_DIM)
    )
    values = (
        project(third_low, focus_stack[2])
        .astype(jnp.bfloat16)
        .reshape(tokens, heads_here, HEAD_DIM)
    )
    attended, log_total = attention_forward(query, keys, values, allowed)
    attended_low = attended.reshape(tokens, heads_here * HEAD_DIM).astype(jnp.bfloat16)
    stream_three = stream_two + branch_total(project_t(attended_low, focus_mat))
    late_stack, late_mat = collect(late_gate_up, late_down)
    fourth_normed, fourth_back = jax.vjp(rms_norm, stream_three, norm_gains[3])
    fourth_low = fourth_normed.astype(jnp.bfloat16)
    late_part, late_gate, late_up, late_hidden = ffn_forward(fourth_low, late_stack, late_mat)
    output = stream_three + branch_total(late_part)
    grad_three = output_grad.astype(jnp.float32)
    late_pair = (late_stack, late_mat)
    grad_fourth, late_joined, late_mat_grad = ffn_backward(
        output_grad, fourth_low, late_gate, late_up, late_hidden, late_pair[0], late_pair[1]
    )
    grad_stream, gain_four = fourth_back(input_total(grad_fourth))
    grad_three = grad_three + grad_stream
    late_grads = spread_grads(late_joined, late_mat_grad, 2)
    focus_pair = (focus_stack, focus_mat)
    grad_branch_low = grad_three.astype(jnp.bfloat16)
    focus_mat_grad = outer_rows(grad_branch_low, attended_low)
    grad_attended = (
        project(grad_branch_low, focus_pair[1])
        .astype(jnp.bfloat16)
        .reshape(tokens, heads_here, HEAD_DIM)
    )
    grad_query, grad_keys, grad_values = attention_backward(
        query, keys, values, allowed, log_total, grad_attended
    )
    query_low = flatten_low(grad_query, tokens)
    keys_low = flatten_low(grad_keys, tokens)
    values_low = flatten_low(grad_values, tokens)
    focus_joined = outer_rows(third_low, jnp.concatenate([query_low, keys_low, values_low], axis=1))
    grad_third = (
        project_t(query_low, focus_pair[0][0])
        + project_t(keys_low, focus_pair[0][1])
        + project_t(values_low, focus_pair[0][2])
    )
    grad_stream, gain_three = third_back(input_total(grad_third))
    grad_two = grad_three + grad_stream
    focus_grads = spread_grads(focus_joined, focus_mat_grad, 3)
    early_pair = (early_stack, early_mat)
    grad_second, early_joined, early_mat_grad = ffn_backward(
        grad_two.astype(jnp.bfloat16),
        second_low,
        early_gate,
        early_up,
        early_hidden,
        early_pair[0],
        early_pair[1],
    )
    grad_stream, gain_two = second_back(input_total(grad_second))
    grad_one = grad_two + grad_stream
    early_grads = spread_grads(early_joined, early_mat_grad, 2)
    mixer_pair = (mixer_stack, mixer_mats)
    grad_mixer_low = grad_one.astype(jnp.bfloat16)
    out_mat_grad = outer_rows(grad_mixer_low, mixer_low)
    grad_scanned = project(grad_mixer_low, mixer_pair[1][:width])
    (
        grad_channel,
        grad_step_low,
        gate_low,
        in_sums,
        out_sums,
        step_bias_grad,
        decay_log_grad,
        skip_gain_grad,
    ) = scan_backward(
        keeping, channel_low, step_raw, gate_half, grad_scanned, step_bias, rates_t, skip_gain, in_wide, out_wide,
        groups, LANES,
    )
    step_mat_grad = outer_rows(rank_low, grad_step_low)
    grad_rank = project_t(grad_step_low, mixer_pair[1][width + PROJ_OUT :])
    grad_rows = lax.psum(
        jnp.concatenate([grad_rank, jnp.sum(in_sums, axis=-1), jnp.sum(out_sums, axis=-1)], axis=1), "tensor"
    )
    grad_rows_low = grad_rows.astype(jnp.bfloat16)
    select_mat_grad = outer_rows(grad_rows_low, channel_low)
    grad_channel = grad_channel + project(grad_rows_low, mixer_pair[1][width : width + PROJ_OUT])
    grad_conv_in, conv_weight_grad, conv_bias_grad = conv_back(grad_channel)
    conv_low = grad_conv_in.astype(jnp.bfloat16)
    mixer_joined = outer_rows(first_low, jnp.concatenate([conv_low, gate_low], axis=1))
    grad_first = project_t(conv_low, mixer_pair[0][0]) + project_t(gate_low, mixer_pair[0][1])
    grad_stream, gain_one = first_back(input_total(grad_first))
    input_grad = grad_one + grad_stream
    mixer_grads = spread_grads(
        mixer_joined, jnp.concatenate([out_mat_grad, select_mat_grad, step_mat_grad], axis=0), 2
    )
    small_sums = lax.psum(
        (
            jnp.stack([gain_one, gain_two, gain_three, gain_four]),
            conv_weight_grad,
            conv_bias_grad,
            step_bias_grad[0],
            decay_log_grad.T,
            skip_gain_grad[0],
        ),
        "dp",
    )
    return (
        output,
        input_grad,
        small_sums[0],
        mixer_grads[0],
        mixer_grads[1],
        small_sums[1],
        small_sums[2],
        small_sums[3],
        small_sums[4],
        small_sums[5],
        early_grads[0],
        early_grads[1],
        focus_grads[0],
        focus_grads[1],
        late_grads[0],
        late_grads[1],
    )


MESH = pl.DeviceIdType.MESH


def turns(group):
    return [turned for turned in (6, 2, 4) if turned & group == turned]


class Place:
    def __init__(self, ways):
        self.spot = lax.axis_index("dp")
        self.depth = lax.axis_index("tensor")
        self.ways = ways
        self.core = lax.rem(self.spot, 2)
        self.partner = self.spot + 1 - 2 * self.core

    def bit(self, axis, turned):
        value = lax.rem(self.spot // axis, 2)
        return 1 - value if turned & axis else value

    def across(self, turned):
        move = 0
        for axis in (2, 4):
            if turned & axis:
                move = move + axis * (1 - 2 * self.bit(axis, 0))
        return self.spot + move

    def side(self, group, turned=0):
        if group == 6:
            return self.bit(2, turned) + 2 * self.bit(4, turned)
        return self.bit(group, turned) if group else 0

    def along(self, offset):
        return lax.rem(self.depth + offset, self.ways)


def send(source, target, sems, at, spot, depth):
    copy = pltpu.make_async_remote_copy(
        src_ref=source,
        dst_ref=target,
        send_sem=sems[0].at[at],
        recv_sem=sems[1].at[at],
        device_id=(spot, depth),
        device_id_type=MESH,
    )
    copy.start()
    return copy


def greet(place, ways):
    barrier = pltpu.get_barrier_semaphore()
    peers = [(place.partner, place.depth)]
    peers += [(place.across(turned), place.depth) for turned in ways]
    peers += [(place.spot, place.along(offset)) for offset in range(1, place.ways)]
    for peer in peers:
        pl.semaphore_signal(barrier, inc=1, device_id=peer, device_id_type=MESH)
    pl.semaphore_wait(barrier, len(peers))


def rows_at(start, size, unit):
    return pl.ds(pl.multiple_of(start * unit, unit), size)


def reduce_stage(place, group, rows, parts, part_ref, near_s, sum_s, far_s, deep_s, sems):
    share = rows // place.ways
    step = part_ref.shape[1] // parts
    ways = turns(group) + [0]
    sides = len(ways)
    near = {}
    for part in range(parts):
        lanes = pl.ds(part * step, step)
        for at, turned in enumerate(ways):
            side = place.side(group, turned)
            near[part, turned] = send(
                part_ref.at[rows_at(side * 2 + 1 - place.core, rows, rows), lanes],
                near_s.at[rows_at(side, rows, rows), lanes],
                sems["near"], part * sides + at, place.partner, place.depth,
            )

    def joined(side, lanes):
        own = part_ref[rows_at(side * 2 + place.core, rows, rows), lanes].astype(jnp.float32)
        return own + near_s[rows_at(side, rows, rows), lanes].astype(jnp.float32)

    far = {}
    for part in range(parts):
        lanes = pl.ds(part * step, step)
        for at, turned in enumerate(ways[:-1]):
            side = place.side(group, turned)
            near[part, turned].wait_recv()
            sum_s[rows_at(side, rows, rows), lanes] = joined(side, lanes).astype(sum_s.dtype)
            far[part, turned] = send(
                sum_s.at[rows_at(side, rows, rows), lanes], far_s.at[at, :, lanes],
                sems["far"], part * (sides - 1) + at, place.across(turned), place.depth,
            )
    deep = []
    mine = place.side(group)
    for part in range(parts):
        lanes = pl.ds(part * step, step)
        near[part, 0].wait_recv()
        total = joined(mine, lanes)
        for at, turned in enumerate(ways[:-1]):
            far[part, turned].wait_recv()
            total = total + far_s[at, :, lanes].astype(jnp.float32)
        sum_s[rows_at(mine, rows, rows), lanes] = total.astype(sum_s.dtype)
        for offset in range(1, place.ways):
            deep.append(
                send(
                    sum_s.at[pl.ds(pl.multiple_of(mine * rows + place.along(offset) * share, share), share), lanes],
                    deep_s.at[offset - 1, :, lanes],
                    sems["deep"], part * (place.ways - 1) + offset - 1, place.spot, place.along(offset),
                )
            )
    for copy in deep:
        copy.wait_recv()
    total = sum_s[pl.ds(pl.multiple_of(mine * rows + place.depth * share, share), share), :].astype(jnp.float32)
    for offset in range(1, place.ways):
        total = total + deep_s[offset - 1].astype(jnp.float32)
    return total, list(near.values()) + list(far.values()) + deep


def gather_stage(place, group, rows, all_ref, sems):
    share = rows // place.ways
    ways = turns(group)
    mine = place.side(group)

    def piece(side, depth):
        return all_ref.at[pl.ds(pl.multiple_of((side * 2 + place.core) * rows + depth * share, share), share), :]

    own = piece(mine, place.depth)
    deep = [
        send(own, own, sems["deep_back"], offset - 1, place.spot, place.along(offset)) for offset in range(1, place.ways)
    ]
    far, near = {}, []
    for offset in range(place.ways):
        if offset:
            deep[offset - 1].wait_recv()
        came = piece(mine, place.along(place.ways - offset) if offset else place.depth)
        for at, turned in enumerate(ways):
            far[offset, turned] = send(
                came, came, sems["far_back"], offset * len(ways) + at, place.across(turned), place.depth
            )
        near.append(send(came, came, sems["near_back"], offset, place.partner, place.depth))
    for offset in range(place.ways):
        for at, turned in enumerate(ways):
            far[offset, turned].wait_recv()
            came = piece(place.side(group, turned), place.along(place.ways - offset) if offset else place.depth)
            near.append(
                send(came, came, sems["near_back"], (1 + at) * place.ways + offset, place.partner, place.depth)
            )
    for copy in near:
        copy.wait_recv()
    return deep + list(far.values()) + near


def spread_stage(place, rows, all_ref, sems):
    share = rows // place.ways
    own = all_ref.at[pl.ds(pl.multiple_of(place.depth * share, share), share), :]
    deep = [
        send(own, own, sems["deep_back"], offset - 1, place.spot, place.along(offset)) for offset in range(1, place.ways)
    ]
    return deep


def small_stage(place, half, sum_ref, small_s, sems):
    near = [
        send(
            sum_ref.at[pl.ds(part * half, half), :], small_s.at[part], sems["small"], part, place.partner, place.depth
        )
        for part in range(2)
    ]
    for copy in near:
        copy.wait()
    mine = pl.ds(pl.multiple_of(place.core * half, half), half)
    small_s[2] = sum_ref[mine, :] + small_s[place.core]
    chips = [
        send(small_s.at[2], small_s.at[3 + at], sems["small"], 2 + at, spot, place.depth)
        for at, spot in enumerate((place.across(2), place.across(4), place.across(6)))
    ]
    for copy in chips:
        copy.wait_recv()
    total = small_s[2] + small_s[3] + small_s[4] + small_s[5]
    small_s[6] = total
    deep = [
        send(
            small_s.at[6, pl.ds(half - 8, 8), :], small_s.at[6 + offset, pl.ds(half - 8, 8), :],
            sems["small"], 4 + offset, place.spot, place.along(offset),
        )
        for offset in range(1, place.ways)
    ]
    for copy in deep:
        copy.wait_recv()
    gains = small_s[6, half - 8 : half, :]
    for offset in range(1, place.ways):
        gains = gains + small_s[6 + offset, half - 8 : half, :]
    last = jnp.where(place.core == 1, gains, total[half - 8 : half, :])
    ready, came = 6 + place.ways, 7 + place.ways
    small_s[ready] = jnp.concatenate([total[: half - 8, :], last], axis=0)
    back = send(small_s.at[ready], small_s.at[came], sems["small"], 4 + place.ways, place.partner, place.depth)
    sum_ref[mine, :] = small_s[ready]
    back.wait_recv()
    sum_ref[pl.ds(pl.multiple_of((1 - place.core) * half, half), half), :] = small_s[came]
    return chips + deep + [back]


def sem_shapes(names):
    shapes = []
    for count in names.values():
        shapes += [pltpu.SemaphoreType.DMA((count,))] * 2
    return shapes


def sem_dict(names, refs):
    return {name: (refs[2 * at], refs[2 * at + 1]) for at, name in enumerate(names)}


def edge_kernel(kind, ways, rows, parts, in_group, out_group, names, *refs):
    place = Place(ways)
    share = rows // ways
    refs = list(refs)
    part_ref = refs.pop(0)
    if kind == "forward":
        stream_ref, gain_ref = refs.pop(0), refs.pop(0)
        all_ref, fresh_ref = refs.pop(0), refs.pop(0)
    elif kind in ("backward", "last"):
        stream_ref, gain_ref, grad_ref = refs.pop(0), refs.pop(0), refs.pop(0)
        small_ref = refs.pop(0) if kind == "last" else None
        all_ref = refs.pop(0)
        fresh_ref = refs.pop(0) if kind == "backward" else None
        dgain_ref = refs.pop(0)
    else:
        all_ref = refs.pop(0)
    near_s, sum_s, far_s, deep_s = refs.pop(0), refs.pop(0), refs.pop(0), refs.pop(0)
    if kind == "last":
        low_s, small_s = refs.pop(0), refs.pop(0)
    sems = sem_dict(names, refs)
    greet(place, turns(6) if kind == "last" else sorted({*turns(in_group), *turns(out_group)}))
    total, waiting = reduce_stage(
        place, in_group, rows, parts, part_ref, near_s, sum_s, far_s, deep_s, sems
    )
    if kind == "forward":
        fresh = stream_ref[...] + total
        fresh_ref[...] = fresh
        scale = lax.rsqrt(jnp.mean(fresh * fresh, axis=-1, keepdims=True) + EPS)
        value = fresh * scale * gain_ref[...]
    elif kind in ("backward", "last"):
        stream = stream_ref[...]
        scale = lax.rsqrt(jnp.mean(stream * stream, axis=-1, keepdims=True) + EPS)
        leaned = total * gain_ref[...]
        inner = jnp.mean(leaned * stream, axis=-1, keepdims=True)
        value = grad_ref[...] + scale * leaned - stream * (scale * scale * scale * inner)
        dgain = jnp.sum(total * stream * scale, axis=0, keepdims=True)
        if kind == "backward":
            dgain_ref[...] = dgain
            fresh_ref[...] = value
    else:
        value = total
    if kind == "last":
        low_s[pl.ds(pl.multiple_of(place.depth * share, share), share), :] = value.astype(low_s.dtype)
        half, span = small_ref.shape[0] // 2, small_ref.shape[1]
        dgain_ref[...] = small_ref[...]
        for at in range(dgain.shape[1] // span):
            dgain_ref[pl.ds(2 * half - 8 + at, 1), :] = dgain[:, at * span : (at + 1) * span]
        spread = spread_stage(place, rows, low_s, sems)
        waiting += spread + small_stage(place, half, dgain_ref, small_s, sems)
        for copy in spread:
            copy.wait_recv()
        all_ref[...] = low_s[...].astype(jnp.float32)
    else:
        spot = pl.multiple_of((place.side(out_group) * 2 + place.core) * rows + place.depth * share, share)
        all_ref[pl.ds(spot, share), :] = value.astype(all_ref.dtype)
        waiting += gather_stage(place, out_group, rows, all_ref, sems)
    for copy in waiting:
        copy.wait_send()


def edge(kind, part, extras, ways, rows, parts, in_group, out_group, ident, name):
    width = part.shape[1]
    share = rows // ways
    in_far, out_far = len(turns(in_group)), len(turns(out_group or 0))
    in_sides, out_sides = in_far + 1, out_far + 1
    dtype = part.dtype
    line = jax.ShapeDtypeStruct((1, width), jnp.float32)
    strip = jax.ShapeDtypeStruct((share, width), jnp.float32)
    whole = jax.ShapeDtypeStruct((out_sides * 2 * rows, width), dtype)
    outs = {
        "forward": [whole, strip],
        "backward": [whole, strip, line],
        "last": [jax.ShapeDtypeStruct((rows, width), jnp.float32)]
        + [jax.ShapeDtypeStruct(extra.shape, extra.dtype) for extra in extras[3:]],
        "sum": [whole],
    }[kind]
    names = {"near": parts * in_sides, "far": parts * in_far, "deep": parts * (ways - 1), "deep_back": ways - 1}
    if kind == "last":
        names["small"] = 5 + ways
    else:
        names.update({"far_back": ways * out_far, "near_back": ways * out_sides})
    if not in_group:
        del names["far"]
    if kind != "last" and not out_group:
        del names["far_back"]
    scratch = [
        pltpu.VMEM((in_sides * rows, width), dtype),
        pltpu.VMEM((in_sides * rows, width), dtype),
        pltpu.VMEM((max(in_far, 1), rows if in_far else 16, width), dtype),
        pltpu.VMEM((ways - 1, share, width), dtype),
    ]
    if kind == "last":
        scratch.append(pltpu.VMEM((rows, width), dtype))
        scratch.append(pltpu.VMEM((8 + ways, extras[3].shape[0] // 2, extras[3].shape[1]), jnp.float32))
    vmem = pl.BlockSpec(memory_space=pltpu.VMEM)
    return pl.pallas_call(
        partial(edge_kernel, kind, ways, rows, parts, in_group, out_group, names),
        in_specs=[vmem] * (1 + len(extras)),
        out_specs=[vmem] * len(outs),
        out_shape=outs,
        scratch_shapes=scratch + sem_shapes(names),
        compiler_params=pltpu.CompilerParams(
            collective_id=ident, has_side_effects=True, vmem_limit_bytes=40 << 20
        ),
        cost_estimate=pl.CostEstimate(flops=1, bytes_accessed=1, transcendentals=0),
        name=name,
    )(part, *extras)


def opening_kernel(ways, rows, hidden_ref, gain_ref, first_ref, send_sem, recv_sem):
    place = Place(ways)
    barrier = pltpu.get_barrier_semaphore()
    pl.semaphore_signal(barrier, inc=1, device_id=(place.partner, place.depth), device_id_type=MESH)
    pl.semaphore_wait(barrier, 1)
    stream = hidden_ref[...].astype(jnp.float32)
    scale = lax.rsqrt(jnp.mean(stream * stream, axis=-1, keepdims=True) + EPS)
    first_ref[rows_at(place.core, rows, rows), :] = (stream * scale * gain_ref[...]).astype(jnp.bfloat16)
    mine = first_ref.at[rows_at(place.core, rows, rows), :]
    send(mine, mine, (send_sem, recv_sem), 0, place.partner, place.depth).wait()


def opening(hidden, gain, ways, ident):
    rows, width = hidden.shape
    vmem = pl.BlockSpec(memory_space=pltpu.VMEM)
    return pl.pallas_call(
        partial(opening_kernel, ways, rows),
        in_specs=[vmem] * 2,
        out_specs=vmem,
        out_shape=jax.ShapeDtypeStruct((2 * rows, width), jnp.bfloat16),
        scratch_shapes=[pltpu.SemaphoreType.DMA((1,))] * 2,
        compiler_params=pltpu.CompilerParams(
            collective_id=ident, has_side_effects=True, vmem_limit_bytes=40 << 20
        ),
        cost_estimate=pl.CostEstimate(flops=1, bytes_accessed=1, transcendentals=0),
        name="opening",
    )(hidden, gain)


def probs_of(query, keys, allowed):
    scores = project_t(query, keys) * (1.0 / math.sqrt(HEAD_DIM))
    scores = jnp.where(allowed, scores, NEG_FILL)
    shifted = jnp.exp(scores - jnp.max(scores, axis=-1, keepdims=True))
    return shifted / jnp.sum(shifted, axis=-1, keepdims=True)


def allowed_in(down_ref, side_ref, rows, group):
    shape = (rows, rows)
    distance = lax.broadcasted_iota(jnp.int32, shape, 0) - lax.broadcasted_iota(jnp.int32, shape, 1)
    same = down_ref[group * rows : (group + 1) * rows, :] == side_ref[group : group + 1, :]
    return same & (distance >= 0) & (distance < WINDOW)


def attend_kernel(heads, rows, joint_ref, down_ref, side_ref, low_ref, out_ref):
    low_ref[...] = joint_ref[...].astype(jnp.bfloat16)
    size = heads * HEAD_DIM
    for group in range(joint_ref.shape[0] // rows):
        allowed = allowed_in(down_ref, side_ref, rows, group)
        span = slice(group * rows, (group + 1) * rows)
        for head in range(heads):
            at = slice(head * HEAD_DIM, (head + 1) * HEAD_DIM)
            query, keys, values = [
                low_ref[span, part * size + head * HEAD_DIM : part * size + (head + 1) * HEAD_DIM] for part in range(3)
            ]
            probs = probs_of(query, keys, allowed)
            out_ref[span, at] = project(probs.astype(jnp.bfloat16), values).astype(jnp.bfloat16)


def attend(joint, down, side, rows):
    count, size = joint.shape
    return pl.pallas_call(
        partial(attend_kernel, size // (3 * HEAD_DIM), rows),
        out_shape=[
            jax.ShapeDtypeStruct((count, size), jnp.bfloat16),
            jax.ShapeDtypeStruct((count, size // 3), jnp.bfloat16),
        ],
        compiler_params=pltpu.CompilerParams(vmem_limit_bytes=32 << 20),
        name="attend",
    )(joint, down, side)


def attend_back_kernel(heads, rows, low_ref, grad_ref, down_ref, side_ref, out_ref):
    size = heads * HEAD_DIM
    scale = 1.0 / math.sqrt(HEAD_DIM)
    for group in range(low_ref.shape[0] // rows):
        allowed = allowed_in(down_ref, side_ref, rows, group)
        span = slice(group * rows, (group + 1) * rows)
        for head in range(heads):
            places = [slice(part * size + head * HEAD_DIM, part * size + (head + 1) * HEAD_DIM) for part in range(3)]
            query, keys, values = [low_ref[span, place] for place in places]
            grad = grad_ref[span, head * HEAD_DIM : (head + 1) * HEAD_DIM].astype(jnp.bfloat16)
            probs = probs_of(query, keys, allowed)
            grad_probs = project_t(grad, values)
            inner = jnp.sum(probs * grad_probs, axis=-1, keepdims=True)
            grad_scores = (probs * (grad_probs - inner)).astype(jnp.bfloat16)
            out_ref[span, places[0]] = (project(grad_scores, keys) * scale).astype(jnp.bfloat16)
            out_ref[span, places[1]] = (outer_rows(grad_scores, query) * scale).astype(jnp.bfloat16)
            out_ref[span, places[2]] = outer_rows(probs.astype(jnp.bfloat16), grad).astype(jnp.bfloat16)


def attend_back(low, grad, down, side, rows):
    count, size = low.shape
    return pl.pallas_call(
        partial(attend_back_kernel, size // (3 * HEAD_DIM), rows),
        out_shape=jax.ShapeDtypeStruct((count, size), jnp.bfloat16),
        compiler_params=pltpu.CompilerParams(vmem_limit_bytes=32 << 20),
        name="attend_back",
    )(low, grad, down, side)


def sub_of(spot, group):
    if group == 6:
        return spot
    return spot % 2 + (2 * ((spot // group) % 2) if group else 0)


def subs_of(group):
    return 2 * (len(turns(group)) + 1)


def pull(count, *sets):
    def cut(block, group, spot):
        size = block.shape[1] // subs_of(group)
        return block[:, sub_of(spot, group) * size : (sub_of(spot, group) + 1) * size]

    return jnp.stack(
        [
            jnp.concatenate([cut(block, group, spot) for blocks, group in sets for block in blocks], axis=1)
            for spot in range(count)
        ]
    )


def swap(stacked):
    return lax.all_to_all(stacked, "dp", 0, 0, tiled=True)


def settle(swapped, group, blocks):
    subs = subs_of(group)
    count = swapped.shape[0]
    size = swapped.shape[2] // blocks
    sums = []
    for sub in range(subs):
        sums.append(sum(swapped[spot].astype(jnp.float32) for spot in range(count) if sub_of(spot, group) == sub))
    return [
        jnp.concatenate([one[:, block * size : (block + 1) * size] for one in sums], axis=1) for block in range(blocks)
    ]


def by_half(place, first, second):
    return [jnp.where(place == 0, first, second), jnp.where(place == 0, second, first)]


def after(value, *others):
    return lax.optimization_barrier((value,) + others)[0]


def grouped_body(
    counts,
    early_group,
    focus_group,
    late_group,
    hidden_in,
    seq_lengths,
    norm_gains,
    mixer_in,
    mixer_rows,
    conv_weight,
    conv_bias,
    step_bias,
    decay_log,
    skip_gain,
    early_gate_up,
    early_down,
    attention_in,
    attention_out,
    late_gate_up,
    late_down,
    output_grad,
):
    spots, ways = counts
    rows, width = hidden_in.shape
    share = rows // ways
    spot = lax.axis_index("dp")
    depth = lax.axis_index("tensor")
    core = spot % 2
    low = jnp.bfloat16

    def swapped_core(value):
        return lax.ppermute(value, "dp", [(at, at ^ 1) for at in range(spots)])

    same_core = [[2 * chip + at for chip in range(spots // 2)] for at in range(2)]

    def whole_group(value, group):
        if group == 6:
            value = jnp.broadcast_to(value[None], (spots // 2,) + value.shape)
            value = lax.all_to_all(value, "dp", 0, 0, tiled=True, axis_index_groups=same_core)
        else:
            value = value[None]
        if group in (2, 4):
            moved = lax.ppermute(value, "dp", [(at, at ^ group) for at in range(spots)])
            value = jnp.concatenate(by_half((spot // group) % 2, value, moved))
        return jnp.stack(by_half(core, value, swapped_core(value)), axis=1).reshape(-1, value.shape[-1])

    def group_sum(part, group):
        part = part.reshape(-1, 2, rows, width)
        mine, other = by_half(core, part[:, 0], part[:, 1])
        part = mine + swapped_core(other)
        if group == 6:
            part = lax.all_to_all(part, "dp", 0, 0, tiled=True, axis_index_groups=same_core)
            return jnp.sum(part.astype(jnp.float32), axis=0).astype(low)
        if group:
            mine, other = by_half((spot // group) % 2, part[0], part[1])
            return mine + lax.ppermute(other, "dp", [(at, at ^ group) for at in range(spots)])
        return part[0]

    in_weights = swap(pull(spots, ([mixer_in[0], mixer_in[1]], 0)))

    other_lengths = swapped_core(seq_lengths)
    lengths = jnp.where(
        core == 0, jnp.stack([seq_lengths, other_lengths]), jnp.stack([other_lengths, seq_lengths])
    )
    segs, starts = jax.vmap(lambda own: segment_info(own, rows))(lengths)
    flat_segs = (segs + jnp.arange(2, dtype=jnp.int32)[:, None] * rows).reshape(-1)
    keeping = 1.0 - starts.reshape(-1).astype(jnp.float32)
    groups = 2 * seq_lengths.shape[0]

    first_low = opening(hidden_in, norm_gains[0:1], ways, 20)
    row_weights = swap(after(pull(spots, ([mixer_rows], 0)), in_weights, first_low))
    stream_zero = lax.dynamic_slice_in_dim(hidden_in, depth * share, share, 0).astype(jnp.float32)

    channels = conv_weight.shape[0] // 2

    def half(values):
        return lax.dynamic_slice_in_dim(values, core * channels, channels, 0)

    taps, offset, bias, decay, skip = [half(v) for v in (conv_weight, conv_bias, step_bias, decay_log, skip_gain)]
    in_mat = in_weights.reshape(width, 2 * channels)
    both = project(first_low, in_mat)
    conv_in, gate_half = both[:, :channels], both[:, channels:]
    channel_full, conv_back = jax.vjp(partial(causal_conv, flat_segs), conv_in, taps, offset)
    channel_low = channel_full.astype(low)
    row_mat = row_weights.reshape(-1, channels)
    early_blocks = [early_gate_up[0], early_gate_up[1], early_down]
    focus_blocks = [attention_in[0], attention_in[1], attention_in[2], attention_out]
    middle_weights = swap(
        after(pull(spots, (early_blocks, early_group), (focus_blocks, focus_group)), row_weights, both)
    ).reshape(width, -1)
    units = 3 * early_down.shape[1] // subs_of(early_group)
    early_mat, focus_mat = middle_weights[:, :units], middle_weights[:, units:]
    out_mat = row_mat[:width]
    select_mat = row_mat[width : width + PROJ_OUT]
    step_mat = row_mat[width + PROJ_OUT :]

    def mixed_sum(part, ident, name):
        padded = jnp.pad(part, ((0, 0), (0, 256 - PROJ_OUT)))
        return edge("sum", padded, [], ways, rows, 1, 0, 0, ident, name)[0][:, :PROJ_OUT]

    mix_rows = mixed_sum(project_t(channel_low, select_mat), 1, "mix_sum")
    rank_low = mix_rows[:, :DT_RANK].astype(low)
    step_raw = project(rank_low, step_mat)
    rates_t = -jnp.exp(decay).T
    wide = (2 * rows, STATE, LANES)
    in_wide = jnp.broadcast_to(mix_rows[:, DT_RANK : DT_RANK + STATE, None], wide)
    out_wide = jnp.broadcast_to(mix_rows[:, DT_RANK + STATE :, None], wide)
    mixer_low = scan_forward(
        keeping, channel_low, step_raw, gate_half, bias, rates_t, skip, in_wide, out_wide, groups, LANES
    )
    second_low, stream_one = edge(
        "forward", project_t(mixer_low, out_mat).astype(low), [stream_zero, norm_gains[1:2]],
        ways, rows, 4, 0, early_group, 2, "edge_one",
    )

    late_blocks = [late_gate_up[0], late_gate_up[1], late_down]
    late_weights = swap(after(pull(spots, (late_blocks, late_group)), middle_weights, second_low))

    def ffn(normed, mat):
        units = mat.shape[1] // 3
        both = project(normed, mat[:, : 2 * units])
        hidden = gated_unit(both[:, :units], both[:, units:]).astype(low)
        return project_t(hidden, mat[:, 2 * units :]).astype(low), both, hidden

    early_part, early_both, early_hidden = ffn(second_low, early_mat)
    third_low, stream_two = edge(
        "forward", early_part, [stream_one, norm_gains[2:3]], ways, rows, 4, early_group, 0, 3, "edge_two"
    )

    last_grad = whole_group(after(output_grad, late_weights, third_low), late_group)
    heads_width = focus_mat.shape[1] // 4
    down, side = flat_segs[:, None], flat_segs.reshape(2, rows)
    joint_low, attended_low = attend(project(third_low, focus_mat[:, : 3 * heads_width]), down, side, rows)
    fourth_low, stream_three = edge(
        "forward", project_t(attended_low, focus_mat[:, 3 * heads_width :]).astype(low),
        [stream_two, norm_gains[3:4]], ways, rows, 4, 0, late_group, 4, "edge_three",
    )

    late_mat = late_weights.reshape(width, -1)
    late_part, late_both, late_hidden = ffn(fourth_low, late_mat)

    def ffn_back(grad_low, normed, both, hidden, mat):
        units = mat.shape[1] // 3
        grad_hidden = project(grad_low, mat[:, 2 * units :])
        _, unit_back = jax.vjp(gated_unit, both[:, :units], both[:, units:])
        both_low = jnp.concatenate(unit_back(grad_hidden), axis=1).astype(low)
        grad_normed = project_t(both_low, mat[:, : 2 * units]).astype(low)
        joint = jnp.concatenate([outer_rows(normed, both_low), outer_rows(grad_low, hidden)], axis=1)
        return grad_normed, joint.astype(low).reshape(spots, -1, 3 * units)

    grad_fourth, late_joint = ffn_back(last_grad, fourth_low, late_both, late_hidden, late_mat)
    grad_zero = lax.dynamic_slice_in_dim(output_grad, depth * share, share, 0).astype(jnp.float32)
    output_part = group_sum(late_part, late_group)
    grad_low_three, grad_three, gain_four = edge(
        "backward", after(grad_fourth, output_part), [stream_three, norm_gains[3:4], grad_zero],
        ways, rows, 4, late_group, 0, 5, "edge_four",
    )
    late_swapped = swap(after(late_joint, grad_low_three))

    output_rows = lax.all_to_all(output_part.reshape(ways, share, width), "tensor", 0, 0, tiled=True)
    output_rows = stream_three + jnp.sum(output_rows.astype(jnp.float32), axis=0)
    output = lax.all_gather(output_rows, "tensor", axis=0, tiled=True)

    grad_attended = project(grad_low_three, focus_mat[:, 3 * heads_width :])
    joint_grad = attend_back(joint_low, grad_attended, down, side, rows)
    grad_low_two, grad_two, gain_three = edge(
        "backward", project_t(joint_grad, focus_mat[:, : 3 * heads_width]).astype(low),
        [stream_two, norm_gains[2:3], grad_three], ways, rows, 4, 0, early_group, 6, "edge_five",
    )
    focus_joint = jnp.concatenate(
        [outer_rows(third_low, joint_grad), outer_rows(grad_low_three, attended_low)], axis=1
    ).astype(low)
    focus_swapped = swap(after(focus_joint.reshape(spots, -1, 4 * heads_width), late_swapped, grad_low_two))

    grad_second, early_joint = ffn_back(grad_low_two, second_low, early_both, early_hidden, early_mat)
    grad_low_one, grad_one, gain_two = edge(
        "backward", after(grad_second, late_swapped), [stream_one, norm_gains[1:2], grad_two],
        ways, rows, 4, early_group, 0, 7, "edge_six",
    )

    early_swapped = swap(after(early_joint, focus_swapped, grad_low_one))

    grad_scanned = after(project(grad_low_one, out_mat), focus_swapped)
    (
        grad_channel,
        grad_step_low,
        gate_low,
        in_sums,
        out_sums,
        bias_grad,
        decay_grad,
        skip_grad,
    ) = scan_backward(
        keeping, channel_low, step_raw, gate_half, grad_scanned, bias, rates_t, skip, in_wide, out_wide,
        groups, LANES,
    )
    grad_rank = project_t(grad_step_low, step_mat)
    grad_rows = mixed_sum(
        jnp.concatenate([grad_rank, jnp.sum(in_sums, axis=-1), jnp.sum(out_sums, axis=-1)], axis=1), 8, "mix_grad_sum"
    )
    grad_rows_low = grad_rows.astype(low)
    rows_joint = jnp.concatenate(
        [
            outer_rows(grad_low_one, mixer_low),
            outer_rows(grad_rows_low, channel_low),
            outer_rows(rank_low, grad_step_low),
        ],
        axis=0,
    ).astype(low)
    grad_channel = grad_channel + project(grad_rows_low, select_mat)
    grad_conv_in, taps_grad, offset_grad = conv_back(grad_channel)
    conv_low = grad_conv_in.astype(low)
    in_grad = jnp.concatenate([conv_low, gate_low], axis=1)
    grad_first = project_t(in_grad, in_mat).astype(low)
    in_joints = [outer_rows(first_low, grad).astype(low) for grad in (conv_low, gate_low)]
    mixer_joint = jnp.concatenate(
        [joint.reshape(spots, -1, channels) for joint in (in_joints[0], in_joints[1], rows_joint)], axis=1
    )
    mixer_swapped = swap(after(mixer_joint, early_swapped))
    lines = jnp.concatenate([taps_grad.T, offset_grad[None], bias_grad, skip_grad, decay_grad], axis=0)
    lines = jnp.pad(lines, ((0, 1), (0, 0)))
    blank = jnp.zeros_like(lines)
    lines = jnp.where(core == 0, jnp.concatenate([lines, blank], axis=1), jnp.concatenate([blank, lines], axis=1))
    gains = jnp.concatenate([jnp.zeros_like(gain_two), gain_two, gain_three, gain_four], axis=0)
    small = jnp.concatenate([lines, gains.reshape(8, -1)], axis=0)
    input_grad, small = edge(
        "last", grad_first, [stream_zero, norm_gains[0:1], grad_one, small],
        ways, rows, 4, 0, None, 9, "edge_seven",
    )
    lines = small[: CONV + 3 + STATE]
    gains = small[-8:].reshape(norm_gains.shape)

    late_grads = settle(late_swapped, late_group, 3)
    focus_grads = settle(focus_swapped, focus_group, 4)
    early_grads = settle(early_swapped, early_group, 3)
    mixer_grads = settle(mixer_swapped, 0, 1)[0]
    in_rows = mixer_in.shape[1]
    return (
        output,
        input_grad,
        gains,
        mixer_grads[: 2 * in_rows].reshape(2, in_rows, -1),
        mixer_grads[2 * in_rows :],
        lines[:CONV].T,
        lines[CONV],
        lines[CONV + 1],
        lines[CONV + 3 :].T,
        lines[CONV + 2],
        jnp.stack(early_grads[:2]),
        early_grads[2],
        jnp.stack(focus_grads[:3]),
        focus_grads[3],
        jnp.stack(late_grads[:2]),
        late_grads[2],
    )


def solution(mesh):
    counts = (mesh.shape["dp"], mesh.shape["tensor"])
    chosen = partial(grouped_body, counts, 6, 0, 6) if counts == (8, 4) else body
    return jax.shard_map(
        chosen,
        mesh=mesh,
        in_specs=(
            P("dp", None),
            P("dp", None),
            P(),
            P(None, "dp", "tensor"),
            P("dp", "tensor"),
            P("tensor", None),
            P("tensor"),
            P("tensor"),
            P("tensor", None),
            P("tensor"),
            P(None, "dp", "tensor"),
            P("dp", "tensor"),
            P(None, "dp", "tensor"),
            P("dp", "tensor"),
            P(None, "dp", "tensor"),
            P("dp", "tensor"),
            P("dp", None),
        ),
        out_specs=(
            P("dp", None),
            P("dp", None),
            P(),
            P(None, "dp", "tensor"),
            P("dp", "tensor"),
            P("tensor", None),
            P("tensor"),
            P("tensor"),
            P("tensor", None),
            P("tensor"),
            P(None, "dp", "tensor"),
            P("dp", "tensor"),
            P(None, "dp", "tensor"),
            P("dp", "tensor"),
            P(None, "dp", "tensor"),
            P("dp", "tensor"),
        ),
        check_vma=False,
    )
```

```python
from functools import partial
import math

import jax
import jax.numpy as jnp
from jax import lax
from jax.experimental import pallas as pl
from jax.experimental.pallas import tpu as pltpu
from jax.sharding import PartitionSpec as P

STATE = 16
CONV = 4
DT_RANK = 128
HEAD_DIM = 128
WINDOW = 2048
PROJ_OUT = 160


EPS = 1e-05
NEG_FILL = -1e30


def project(left, right):
    return jnp.dot(left, right, preferred_element_type=jnp.float32)


def project_t(left, right):
    return lax.dot_general(
        left, right, (((1,), (1,)), ((), ())), preferred_element_type=jnp.float32
    )


def outer_rows(left, right):
    return lax.dot_general(
        left, right, (((0,), (0,)), ((), ())), preferred_element_type=jnp.float32
    )


def rms_norm(values, weight):
    return values * lax.rsqrt(jnp.mean(values * values, axis=-1, keepdims=True) + EPS) * weight


def segment_info(lengths, tokens):
    flat_lengths = lengths.reshape(-1)
    ends = jnp.cumsum(flat_lengths, dtype=jnp.int32)
    firsts = ends - flat_lengths
    places = jnp.arange(tokens, dtype=jnp.int32)
    segs = jnp.sum((places[:, None] >= ends[None, :]).astype(jnp.int32), axis=1)
    starts = jnp.any(places[:, None] == firsts[None, :], axis=1)
    return (segs, starts)


def allowed_pairs(segs):
    places = jnp.arange(segs.shape[-1], dtype=jnp.int32)
    distance = places[:, None] - places[None, :]
    return (segs[:, None] == segs[None, :]) & (distance >= 0) & (distance < WINDOW)


def causal_conv(segs, stream, weight, offset):
    total = offset + stream * weight[:, 0]
    for lag_step in range(1, CONV):
        moved = jnp.concatenate(
            [jnp.zeros_like(stream[..., :lag_step, :]), stream[..., :-lag_step, :]], axis=-2
        )
        moved_segs = jnp.concatenate(
            [jnp.full_like(segs[..., :lag_step], -1), segs[..., :-lag_step]], axis=-1
        )
        linked = (segs == moved_segs).astype(stream.dtype)
        total = total + moved * weight[:, lag_step] * linked[..., None]
    return jax.nn.silu(total)


LANES = 128


def softplus(v):
    return jnp.maximum(v, 0.0) + jnp.log1p(jnp.exp(-jnp.abs(v)))


def scan_forward_kernel(
    groups, length, keep_ref, chan_ref, raw_ref, gate_ref, bias_ref, rate_ref, skip_ref, in_ref, out_ref,
    mixed_ref, step_s, drive_s, y_s,
):
    width = chan_ref.shape[1]
    blocks = width // LANES
    step_s[...] = softplus(raw_ref[...] + bias_ref[...])
    drive_s[...] = step_s[...] * chan_ref[...].astype(jnp.float32)
    rates = [rate_ref[:, pl.ds(b * LANES, LANES)] for b in range(blocks)]

    def advance(t, states):
        fresh = []
        for g in range(groups):
            row = g * length + t
            keep = keep_ref[row]
            input_map = in_ref[row]
            output_map = out_ref[row]
            for b in range(blocks):
                lanes = pl.ds(b * LANES, LANES)
                decay = jnp.exp(step_s[pl.ds(row, 1), lanes] * rates[b]) * keep
                state = decay * states[g * blocks + b] + drive_s[pl.ds(row, 1), lanes] * input_map
                y_s[pl.ds(row, 1), lanes] = jnp.sum(state * output_map, axis=0, keepdims=True)
                fresh.append(state)
        return tuple(fresh)

    zero = jnp.zeros((STATE, LANES), jnp.float32)
    lax.fori_loop(0, length, advance, (zero,) * (groups * blocks))
    gate = gate_ref[...]
    silu = gate / (1.0 + jnp.exp(-gate))
    mixed_ref[...] = (
        (y_s[...] + skip_ref[...] * chan_ref[...].astype(jnp.float32)) * silu
    ).astype(mixed_ref.dtype)


def scan_forward(keep, channel, step_raw, gate_half, step_bias, rates_t, skip_gain, in_wide, out_wide, groups, width):
    tokens, channels = channel.shape
    column = pl.BlockSpec((tokens, width), lambda i: (0, i))
    row = pl.BlockSpec((1, width), lambda i: (0, i))
    maps = pl.BlockSpec((tokens, STATE, LANES), lambda i: (0, 0, 0))
    return pl.pallas_call(
        partial(scan_forward_kernel, groups, tokens // groups),
        grid=(channels // width,),
        in_specs=[
            pl.BlockSpec(memory_space=pltpu.SMEM), column, column, column, row,
            pl.BlockSpec((STATE, width), lambda i: (0, i)), row, maps, maps,
        ],
        out_specs=column,
        out_shape=jax.ShapeDtypeStruct((tokens, channels), jnp.bfloat16),
        scratch_shapes=[pltpu.VMEM((tokens, width), jnp.float32)] * 3,
        compiler_params=pltpu.CompilerParams(vmem_limit_bytes=48 << 20),
        cost_estimate=pl.CostEstimate(flops=1, bytes_accessed=1 << 34, transcendentals=0),
        name="scan_forward",
    )(keep, channel, step_raw, gate_half, step_bias[None], rates_t, skip_gain[None], in_wide, out_wide)


def scan_backward_kernel(
    groups, length, keep_ref, chan_ref, raw_ref, gate_ref, dmix_ref, bias_ref, rate_ref, skip_ref, in_ref, out_ref,
    dchan_ref, draw_ref, dgate_ref, din_ref, dout_ref, dbias_ref, drate_ref, dskip_ref,
    step_s, drive_s, y_s, dy_s, dd_s, ds_s, state_s, decay_s,
):
    width = chan_ref.shape[1]
    blocks = width // LANES
    chan = chan_ref[...].astype(jnp.float32)
    step_s[...] = softplus(raw_ref[...] + bias_ref[...])
    drive_s[...] = step_s[...] * chan
    gate = gate_ref[...]
    sig = 1.0 / (1.0 + jnp.exp(-gate))
    dy_s[...] = dmix_ref[...] * (gate * sig)
    rates = [rate_ref[:, pl.ds(b * LANES, LANES)] for b in range(blocks)]

    @pl.when(pl.program_id(0) == 0)
    def _():
        din_ref[...] = jnp.zeros_like(din_ref)
        dout_ref[...] = jnp.zeros_like(dout_ref)

    def advance(t, states):
        fresh = []
        for g in range(groups):
            row = g * length + t
            keep = keep_ref[row]
            input_map = in_ref[row]
            output_map = out_ref[row]
            total = None
            for b in range(blocks):
                lanes = pl.ds(b * LANES, LANES)
                decay = jnp.exp(step_s[pl.ds(row, 1), lanes] * rates[b]) * keep
                decay_s[row, :, lanes] = decay
                carried = decay * states[g * blocks + b]
                state_s[row, :, lanes] = carried
                state = carried + drive_s[pl.ds(row, 1), lanes] * input_map
                y_s[pl.ds(row, 1), lanes] = jnp.sum(state * output_map, axis=0, keepdims=True)
                term = state * dy_s[pl.ds(row, 1), lanes]
                total = term if total is None else total + term
                fresh.append(state)
            dout_ref[row] += total
        return tuple(fresh)

    zero = jnp.zeros((STATE, LANES), jnp.float32)
    count = groups * blocks
    lax.fori_loop(0, length, advance, (zero,) * count)

    def retreat(back, carry):
        t = length - 1 - back
        fresh, rate_sums = [], []
        for g in range(groups):
            row = g * length + t
            input_map = in_ref[row]
            output_map = out_ref[row]
            total = None
            for b in range(blocks):
                lanes = pl.ds(b * LANES, LANES)
                at = g * blocks + b
                dstate = carry[0][at] + dy_s[pl.ds(row, 1), lanes] * output_map
                dlog = dstate * state_s[row, :, lanes]
                dd_s[pl.ds(row, 1), lanes] = jnp.sum(dstate * input_map, axis=0, keepdims=True)
                ds_s[pl.ds(row, 1), lanes] = jnp.sum(dlog * rates[b], axis=0, keepdims=True)
                term = dstate * drive_s[pl.ds(row, 1), lanes]
                total = term if total is None else total + term
                rate_sums.append(carry[1][at] + dlog * step_s[pl.ds(row, 1), lanes])
                fresh.append(dstate * decay_s[row, :, lanes])
            din_ref[row] += total
        return (tuple(fresh), tuple(rate_sums))

    _, rate_sums = lax.fori_loop(0, length, retreat, ((zero,) * count, (zero,) * count))
    for b in range(blocks):
        lanes = pl.ds(b * LANES, LANES)
        drate_ref[:, lanes] = rates[b] * sum(rate_sums[g * blocks + b] for g in range(groups))
    direct = y_s[...] + skip_ref[...] * chan
    dgate_ref[...] = (dmix_ref[...] * direct * (sig * (1.0 + gate * (1.0 - sig)))).astype(dgate_ref.dtype)
    dskip_ref[...] = jnp.sum(dy_s[...] * chan, axis=0, keepdims=True)
    dchan_ref[...] = dd_s[...] * step_s[...] + skip_ref[...] * dy_s[...]
    shifted = raw_ref[...] + bias_ref[...]
    draw = (ds_s[...] + dd_s[...] * chan) / (1.0 + jnp.exp(-shifted))
    draw_ref[...] = draw.astype(draw_ref.dtype)
    dbias_ref[...] = jnp.sum(draw, axis=0, keepdims=True)


def scan_backward(
    keep, channel, step_raw, gate_half, dmixed, step_bias, rates_t, skip_gain, in_wide, out_wide, groups, width
):
    tokens, channels = channel.shape
    column = pl.BlockSpec((tokens, width), lambda i: (0, i))
    row = pl.BlockSpec((1, width), lambda i: (0, i))
    states = pl.BlockSpec((STATE, width), lambda i: (0, i))
    maps = pl.BlockSpec((tokens, STATE, LANES), lambda i: (0, 0, 0))
    sheet = jax.ShapeDtypeStruct((tokens, channels), jnp.float32)
    low = jax.ShapeDtypeStruct((tokens, channels), jnp.bfloat16)
    wide = jax.ShapeDtypeStruct((tokens, STATE, LANES), jnp.float32)
    line = jax.ShapeDtypeStruct((1, channels), jnp.float32)
    return pl.pallas_call(
        partial(scan_backward_kernel, groups, tokens // groups),
        grid=(channels // width,),
        in_specs=[
            pl.BlockSpec(memory_space=pltpu.SMEM), column, column, column, column, row, states, row, maps, maps,
        ],
        out_specs=[column, column, column, maps, maps, row, states, row],
        out_shape=[
            sheet, low, low, wide, wide, line, jax.ShapeDtypeStruct((STATE, channels), jnp.float32), line,
        ],
        scratch_shapes=[pltpu.VMEM((tokens, width), jnp.float32)] * 6
        + [pltpu.VMEM((tokens, STATE, width), jnp.float32)] * 2,
        compiler_params=pltpu.CompilerParams(vmem_limit_bytes=56 << 20),
        cost_estimate=pl.CostEstimate(flops=1, bytes_accessed=1 << 34, transcendentals=0),
        name="scan_backward",
    )(keep, channel, step_raw, gate_half, dmixed, step_bias[None], rates_t, skip_gain[None], in_wide, out_wide)


def attention_scores(query, keys, allowed):
    scores = jnp.einsum("qhd,khd->hqk", query, keys, preferred_element_type=jnp.float32) * (
        1.0 / math.sqrt(HEAD_DIM)
    )
    return jnp.where(allowed[None], scores, NEG_FILL)


def attention_forward(query, keys, values, allowed):
    scores = attention_scores(query, keys, allowed)
    row_max = jnp.max(scores, axis=-1, keepdims=True)
    shifted = jnp.exp(scores - row_max)
    totals = jnp.sum(shifted, axis=-1, keepdims=True)
    probs = shifted / totals
    mixed = jnp.einsum(
        "hqk,khd->qhd", probs.astype(jnp.bfloat16), values, preferred_element_type=jnp.float32
    )
    return (mixed, row_max + jnp.log(totals))


def attention_backward(query, keys, values, allowed, log_total, grad_mixed):
    scale = 1.0 / math.sqrt(HEAD_DIM)
    probs = jnp.exp(attention_scores(query, keys, allowed) - log_total)
    grad_values = jnp.einsum(
        "hqk,qhd->khd", probs.astype(jnp.bfloat16), grad_mixed, preferred_element_type=jnp.float32
    )
    grad_probs = jnp.einsum("qhd,khd->hqk", grad_mixed, values, preferred_element_type=jnp.float32)
    inner_sum = jnp.sum(probs * grad_probs, axis=-1, keepdims=True)
    grad_scores = (probs * (grad_probs - inner_sum)).astype(jnp.bfloat16)
    grad_query = (
        jnp.einsum("hqk,khd->qhd", grad_scores, keys, preferred_element_type=jnp.float32) * scale
    )
    grad_keys = (
        jnp.einsum("hqk,qhd->khd", grad_scores, query, preferred_element_type=jnp.float32) * scale
    )
    return (grad_query, grad_keys, grad_values)


def gated_unit(gate, upward):
    return jax.nn.silu(gate) * upward


def ffn_forward(normed_low, gate_up, down_mat):
    gate = project(normed_low, gate_up[0])
    upward = project(normed_low, gate_up[1])
    hidden = gated_unit(gate, upward).astype(jnp.bfloat16)
    return (project_t(hidden, down_mat), gate, upward, hidden)


def ffn_backward(grad_low, normed_low, gate, upward, hidden, gate_up, down_mat):
    grad_hidden = project(grad_low, down_mat)
    down_grad = outer_rows(grad_low, hidden)
    _, unit_back = jax.vjp(gated_unit, gate, upward)
    grad_gate, grad_up = unit_back(grad_hidden)
    gate_low = grad_gate.astype(jnp.bfloat16)
    up_low = grad_up.astype(jnp.bfloat16)
    joined_grad = outer_rows(normed_low, jnp.concatenate([gate_low, up_low], axis=1))
    grad_normed = project_t(gate_low, gate_up[0]) + project_t(up_low, gate_up[1])
    return (grad_normed, joined_grad, down_grad)


def flatten_low(grad_heads, tokens):
    return grad_heads.astype(jnp.bfloat16).reshape(tokens, -1)


def collect(stacked, row_block):
    return (
        lax.all_gather(stacked, "dp", axis=1, tiled=True),
        lax.all_gather(row_block, "dp", axis=0, tiled=True),
    )


def spread_grads(joined, row_block, count):
    summed = (
        lax.psum_scatter(joined.astype(jnp.bfloat16), "dp", scatter_dimension=0, tiled=True),
        lax.psum_scatter(row_block.astype(jnp.bfloat16), "dp", scatter_dimension=0, tiled=True),
    )
    rows_here = summed[0].shape[0]
    restacked = jnp.transpose(summed[0].reshape(rows_here, count, -1), (1, 0, 2))
    return (restacked.astype(jnp.float32), summed[1].astype(jnp.float32))


def branch_total(piece_sum):
    return lax.psum(piece_sum, "tensor")


def input_total(piece_sum):
    return lax.psum(piece_sum, "tensor")


def body(
    hidden_in,
    seq_lengths,
    norm_gains,
    mixer_in,
    mixer_rows,
    conv_weight,
    conv_bias,
    step_bias,
    decay_log,
    skip_gain,
    early_gate_up,
    early_down,
    attention_in,
    attention_out,
    late_gate_up,
    late_down,
    output_grad,
):
    tokens = hidden_in.shape[0]
    width = hidden_in.shape[1]
    segs, starts = segment_info(seq_lengths, tokens)
    allowed = allowed_pairs(segs)
    stream_zero = hidden_in.astype(jnp.float32)
    mixer_stack, mixer_mats = collect(mixer_in, mixer_rows)
    first_normed, first_back = jax.vjp(rms_norm, stream_zero, norm_gains[0])
    first_low = first_normed.astype(jnp.bfloat16)
    conv_in = project(first_low, mixer_stack[0])
    gate_half = project(first_low, mixer_stack[1])
    channel_full, conv_back = jax.vjp(partial(causal_conv, segs), conv_in, conv_weight, conv_bias)
    channel_low = channel_full.astype(jnp.bfloat16)
    mix_rows = lax.psum(project_t(channel_low, mixer_mats[width : width + PROJ_OUT]), "tensor")
    rank_low = mix_rows[:, :DT_RANK].astype(jnp.bfloat16)
    step_raw = project(rank_low, mixer_mats[width + PROJ_OUT :])
    groups = seq_lengths.shape[0]
    keeping = 1.0 - starts.astype(jnp.float32)
    rates_t = -jnp.exp(decay_log).T
    wide = (tokens, STATE, LANES)
    in_wide = jnp.broadcast_to(mix_rows[:, DT_RANK : DT_RANK + STATE, None], wide)
    out_wide = jnp.broadcast_to(mix_rows[:, DT_RANK + STATE :, None], wide)
    mixer_low = scan_forward(
        keeping, channel_low, step_raw, gate_half, step_bias, rates_t, skip_gain, in_wide, out_wide, groups, LANES
    )
    stream_one = stream_zero + branch_total(project_t(mixer_low, mixer_mats[:width]))
    early_stack, early_mat = collect(early_gate_up, early_down)
    second_normed, second_back = jax.vjp(rms_norm, stream_one, norm_gains[1])
    second_low = second_normed.astype(jnp.bfloat16)
    early_part, early_gate, early_up, early_hidden = ffn_forward(second_low, early_stack, early_mat)
    stream_two = stream_one + branch_total(early_part)
    focus_stack, focus_mat = collect(attention_in, attention_out)
    heads_here = focus_stack.shape[2] // HEAD_DIM
    third_normed, third_back = jax.vjp(rms_norm, stream_two, norm_gains[2])
    third_low = third_normed.astype(jnp.bfloat16)
    query = (
        project(third_low, focus_stack[0])
        .astype(jnp.bfloat16)
        .reshape(tokens, heads_here, HEAD_DIM)
    )
    keys = (
        project(third_low, focus_stack[1])
        .astype(jnp.bfloat16)
        .reshape(tokens, heads_here, HEAD_DIM)
    )
    values = (
        project(third_low, focus_stack[2])
        .astype(jnp.bfloat16)
        .reshape(tokens, heads_here, HEAD_DIM)
    )
    attended, log_total = attention_forward(query, keys, values, allowed)
    attended_low = attended.reshape(tokens, heads_here * HEAD_DIM).astype(jnp.bfloat16)
    stream_three = stream_two + branch_total(project_t(attended_low, focus_mat))
    late_stack, late_mat = collect(late_gate_up, late_down)
    fourth_normed, fourth_back = jax.vjp(rms_norm, stream_three, norm_gains[3])
    fourth_low = fourth_normed.astype(jnp.bfloat16)
    late_part, late_gate, late_up, late_hidden = ffn_forward(fourth_low, late_stack, late_mat)
    output = stream_three + branch_total(late_part)
    grad_three = output_grad.astype(jnp.float32)
    late_pair = (late_stack, late_mat)
    grad_fourth, late_joined, late_mat_grad = ffn_backward(
        output_grad, fourth_low, late_gate, late_up, late_hidden, late_pair[0], late_pair[1]
    )
    grad_stream, gain_four = fourth_back(input_total(grad_fourth))
    grad_three = grad_three + grad_stream
    late_grads = spread_grads(late_joined, late_mat_grad, 2)
    focus_pair = (focus_stack, focus_mat)
    grad_branch_low = grad_three.astype(jnp.bfloat16)
    focus_mat_grad = outer_rows(grad_branch_low, attended_low)
    grad_attended = (
        project(grad_branch_low, focus_pair[1])
        .astype(jnp.bfloat16)
        .reshape(tokens, heads_here, HEAD_DIM)
    )
    grad_query, grad_keys, grad_values = attention_backward(
        query, keys, values, allowed, log_total, grad_attended
    )
    query_low = flatten_low(grad_query, tokens)
    keys_low = flatten_low(grad_keys, tokens)
    values_low = flatten_low(grad_values, tokens)
    focus_joined = outer_rows(third_low, jnp.concatenate([query_low, keys_low, values_low], axis=1))
    grad_third = (
        project_t(query_low, focus_pair[0][0])
        + project_t(keys_low, focus_pair[0][1])
        + project_t(values_low, focus_pair[0][2])
    )
    grad_stream, gain_three = third_back(input_total(grad_third))
    grad_two = grad_three + grad_stream
    focus_grads = spread_grads(focus_joined, focus_mat_grad, 3)
    early_pair = (early_stack, early_mat)
    grad_second, early_joined, early_mat_grad = ffn_backward(
        grad_two.astype(jnp.bfloat16),
        second_low,
        early_gate,
        early_up,
        early_hidden,
        early_pair[0],
        early_pair[1],
    )
    grad_stream, gain_two = second_back(input_total(grad_second))
    grad_one = grad_two + grad_stream
    early_grads = spread_grads(early_joined, early_mat_grad, 2)
    mixer_pair = (mixer_stack, mixer_mats)
    grad_mixer_low = grad_one.astype(jnp.bfloat16)
    out_mat_grad = outer_rows(grad_mixer_low, mixer_low)
    grad_scanned = project(grad_mixer_low, mixer_pair[1][:width])
    (
        grad_channel,
        grad_step_low,
        gate_low,
        in_sums,
        out_sums,
        step_bias_grad,
        decay_log_grad,
        skip_gain_grad,
    ) = scan_backward(
        keeping, channel_low, step_raw, gate_half, grad_scanned, step_bias, rates_t, skip_gain, in_wide, out_wide,
        groups, LANES,
    )
    step_mat_grad = outer_rows(rank_low, grad_step_low)
    grad_rank = project_t(grad_step_low, mixer_pair[1][width + PROJ_OUT :])
    grad_rows = lax.psum(
        jnp.concatenate([grad_rank, jnp.sum(in_sums, axis=-1), jnp.sum(out_sums, axis=-1)], axis=1), "tensor"
    )
    grad_rows_low = grad_rows.astype(jnp.bfloat16)
    select_mat_grad = outer_rows(grad_rows_low, channel_low)
    grad_channel = grad_channel + project(grad_rows_low, mixer_pair[1][width : width + PROJ_OUT])
    grad_conv_in, conv_weight_grad, conv_bias_grad = conv_back(grad_channel)
    conv_low = grad_conv_in.astype(jnp.bfloat16)
    mixer_joined = outer_rows(first_low, jnp.concatenate([conv_low, gate_low], axis=1))
    grad_first = project_t(conv_low, mixer_pair[0][0]) + project_t(gate_low, mixer_pair[0][1])
    grad_stream, gain_one = first_back(input_total(grad_first))
    input_grad = grad_one + grad_stream
    mixer_grads = spread_grads(
        mixer_joined, jnp.concatenate([out_mat_grad, select_mat_grad, step_mat_grad], axis=0), 2
    )
    small_sums = lax.psum(
        (
            jnp.stack([gain_one, gain_two, gain_three, gain_four]),
            conv_weight_grad,
            conv_bias_grad,
            step_bias_grad[0],
            decay_log_grad.T,
            skip_gain_grad[0],
        ),
        "dp",
    )
    return (
        output,
        input_grad,
        small_sums[0],
        mixer_grads[0],
        mixer_grads[1],
        small_sums[1],
        small_sums[2],
        small_sums[3],
        small_sums[4],
        small_sums[5],
        early_grads[0],
        early_grads[1],
        focus_grads[0],
        focus_grads[1],
        late_grads[0],
        late_grads[1],
    )


MESH = pl.DeviceIdType.MESH


def turns(group):
    return [turned for turned in (6, 2, 4) if turned & group == turned]


class Place:
    def __init__(self, ways):
        self.spot = lax.axis_index("dp")
        self.depth = lax.axis_index("tensor")
        self.ways = ways
        self.core = lax.rem(self.spot, 2)
        self.partner = self.spot + 1 - 2 * self.core

    def bit(self, axis, turned):
        value = lax.rem(self.spot // axis, 2)
        return 1 - value if turned & axis else value

    def across(self, turned, swapped=False):
        move = 1 - 2 * self.core if swapped else 0
        for axis in (2, 4):
            if turned & axis:
                move = move + axis * (1 - 2 * self.bit(axis, 0))
        return self.spot + move

    def side(self, group, turned=0):
        if group == 6:
            return self.bit(2, turned) + 2 * self.bit(4, turned)
        return self.bit(group, turned) if group else 0

    def along(self, offset):
        return lax.rem(self.depth + offset, self.ways)


def send(source, target, sems, at, spot, depth):
    copy = pltpu.make_async_remote_copy(
        src_ref=source,
        dst_ref=target,
        send_sem=sems[0].at[at],
        recv_sem=sems[1].at[at],
        device_id=(spot, depth),
        device_id_type=MESH,
    )
    copy.start()
    return copy


def greet(place, ways, both=False):
    barrier = pltpu.get_barrier_semaphore()
    peers = [(place.partner, place.depth)]
    peers += [(place.across(turned), place.depth) for turned in ways]
    if both:
        peers += [(place.across(turned, True), place.depth) for turned in ways]
    peers += [(place.spot, place.along(offset)) for offset in range(1, place.ways)]
    for peer in peers:
        pl.semaphore_signal(barrier, inc=1, device_id=peer, device_id_type=MESH)
    pl.semaphore_wait(barrier, len(peers))


def rows_at(start, size, unit):
    return pl.ds(pl.multiple_of(start * unit, unit), size)


class Reduction:
    def __init__(self, place, group, rows, parts, part_ref, near_s, sum_s, far_s, sems, names):
        self.place, self.group, self.rows, self.parts = place, group, rows, parts
        self.part_ref, self.near_s, self.sum_s, self.far_s = part_ref, near_s, sum_s, far_s
        self.sems = [sems[name] for name in names]
        self.ways = turns(group) + [0]
        self.step = part_ref.shape[1] // parts
        self.near, self.far = {}, {}

    def lanes(self, part):
        return pl.ds(part * self.step, self.step)

    def block(self, side):
        return rows_at(side, self.rows, self.rows)

    def send_near(self):
        place = self.place
        for part in range(self.parts):
            for at, turned in enumerate(self.ways):
                side = place.side(self.group, turned)
                self.near[part, turned] = send(
                    self.part_ref.at[self.block(side * 2 + 1 - place.core), self.lanes(part)],
                    self.near_s.at[self.block(side), self.lanes(part)],
                    self.sems[0], part * len(self.ways) + at, place.partner, place.depth,
                )

    def joined(self, part, turned):
        self.near[part, turned].wait_recv()
        side, lanes = self.place.side(self.group, turned), self.lanes(part)
        own = self.part_ref[self.block(side * 2 + self.place.core), lanes].astype(jnp.float32)
        return own + self.near_s[self.block(side), lanes].astype(jnp.float32)

    def order(self):
        half = self.parts // 2
        return [at + first for at in range(half) for first in (0, half)]

    def leg(self, part):
        return (2, 4) if part < self.parts // 2 else (4, 2)

    def push(self, part, turned, slot, to, value):
        rows, lanes = self.block(self.place.side(self.group, turned)), self.lanes(part)
        self.sum_s[rows, lanes] = value.astype(self.sum_s.dtype)
        self.far[part, slot] = send(
            self.sum_s.at[rows, lanes], self.far_s.at[slot, :, lanes],
            self.sems[1], part * 3 + slot, self.place.across(to), self.place.depth,
        )

    def came(self, part, slot):
        self.far[part, slot].wait_recv()
        return self.far_s[slot, :, self.lanes(part)].astype(jnp.float32)

    def send_far(self):
        if self.group:
            for part in self.order():
                first, _ = self.leg(part)
                self.push(part, 6, 1, first, self.joined(part, 6))
                self.push(part, first, 0, first, self.joined(part, first))

    def relay(self):
        if self.group:
            for part in self.order():
                _, second = self.leg(part)
                value = self.joined(part, second) + self.came(part, 1)
                self.push(part, second, 2, second, value)

    def chip_sum(self, part):
        total = self.joined(part, 0)
        if self.group:
            total = total + self.came(part, 0) + self.came(part, 2)
        return total

    def sent(self):
        return list(self.near.values()) + list(self.far.values())


def deep_sends(place, share, source, start, deep_s, lanes, sems, at):
    return [
        send(
            source.at[pl.ds(pl.multiple_of(start + place.along(offset) * share, share), share), lanes],
            deep_s.at[offset - 1, :, lanes],
            sems, at + offset - 1, place.spot, place.along(offset),
        )
        for offset in range(1, place.ways)
    ]


def deep_total(place, share, source, start, deep_s, copies):
    for copy in copies:
        copy.wait_recv()
    total = source[pl.ds(pl.multiple_of(start + place.depth * share, share), share), :].astype(jnp.float32)
    for offset in range(1, place.ways):
        total = total + deep_s[offset - 1].astype(jnp.float32)
    return total


def reduce_stage(first, deep_s, sems, between):
    place, rows = first.place, first.rows
    share = rows // place.ways
    first.send_near()
    between(0)
    first.send_far()
    first.relay()
    between(1)
    deep = []
    mine = place.side(first.group)
    for part in first.order() if first.group else range(first.parts):
        first.sum_s[first.block(mine), first.lanes(part)] = first.chip_sum(part).astype(first.sum_s.dtype)
        deep += deep_sends(
            place, share, first.sum_s, mine * rows, deep_s, first.lanes(part), sems["deep"], part * (place.ways - 1)
        )
    return deep_total(place, share, first.sum_s, mine * rows, deep_s, deep), first.sent() + deep


def hand_on(place, group, rows_of, target, sems, base, far):
    half = target.shape[1] // 2
    for came, to, lanes in ((2, 4, pl.ds(0, half)), (4, 2, pl.ds(half, half))):
        far[came].wait_recv()
        block = target.at[rows_of(came), lanes]
        far[came, to] = send(block, block, sems, base + to // 2 + 1, place.across(to), place.depth)


def first_leg(place, block, sems, base):
    return {turned: send(block, block, sems, base + turned // 2 - 1, place.across(turned), place.depth) for turned in (2, 4)}


def gather_stage(place, group, rows, all_ref, sems, between):
    share = rows // place.ways

    def place_of(turned, offset):
        depth = place.along(place.ways - offset) if offset else place.depth
        return pl.ds(pl.multiple_of((place.side(group, turned) * 2 + place.core) * rows + depth * share, share), share)

    def to_partner(turned, offset, at):
        block = all_ref.at[place_of(turned, offset), :]
        return send(block, block, sems["near_back"], at * place.ways + offset, place.partner, place.depth)

    own = all_ref.at[place_of(0, 0), :]
    deep = [
        send(own, own, sems["deep_back"], offset - 1, place.spot, place.along(offset)) for offset in range(1, place.ways)
    ]
    far, near = [], []
    for offset in range(place.ways):
        if offset:
            deep[offset - 1].wait_recv()
        if group:
            far.append(first_leg(place, all_ref.at[place_of(0, offset), :], sems["far_back"], 4 * offset))
        near.append(to_partner(0, offset, 0))
        if offset == 0:
            between()
    if group:
        for offset in range(place.ways):
            hand_on(
                place, group, lambda turned: place_of(turned, offset), all_ref, sems["far_back"], 4 * offset, far[offset]
            )
            near.append(to_partner(2, offset, 1))
            near.append(to_partner(4, offset, 2))
        for offset in range(place.ways):
            far[offset][2, 4].wait_recv()
            far[offset][4, 2].wait_recv()
            near.append(to_partner(6, offset, 3))
    for copy in near:
        copy.wait_recv()
    return deep + [copy for one in far for copy in one.values()] + near


def exchange_start(place, source_ref, target_ref, sems):
    copies = [
        send(source_ref.at[spot], target_ref.at[place.spot], sems, at, spot, place.depth)
        for at, spot in enumerate(
            [place.across(turned, swapped) for turned in (6, 2, 4) for swapped in (False, True)] + [place.partner]
        )
    ]
    own = pltpu.make_async_copy(source_ref.at[place.spot], target_ref.at[place.spot], sems[1].at[7])
    own.start()
    return copies, own


def spread_stage(place, rows, all_ref, sems, name="deep_back"):
    share = rows // place.ways
    own = all_ref.at[pl.ds(pl.multiple_of(place.depth * share, share), share), :]
    deep = [
        send(own, own, sems[name], offset - 1, place.spot, place.along(offset)) for offset in range(1, place.ways)
    ]
    return deep


def small_stage(place, half, sum_ref, small_s, sems):
    near = [
        send(
            sum_ref.at[pl.ds(part * half, half), :], small_s.at[part], sems["small"], part, place.partner, place.depth
        )
        for part in range(2)
    ]
    for copy in near:
        copy.wait()
    mine = pl.ds(pl.multiple_of(place.core * half, half), half)
    small_s[2] = sum_ref[mine, :] + small_s[place.core]
    chips = [
        send(small_s.at[2], small_s.at[3 + at], sems["small"], 2 + at, spot, place.depth)
        for at, spot in enumerate((place.across(2), place.across(4), place.across(6)))
    ]
    for copy in chips:
        copy.wait_recv()
    total = small_s[2] + small_s[3] + small_s[4] + small_s[5]
    small_s[6] = total
    deep = [
        send(
            small_s.at[6, pl.ds(half - 8, 8), :], small_s.at[6 + offset, pl.ds(half - 8, 8), :],
            sems["small"], 4 + offset, place.spot, place.along(offset),
        )
        for offset in range(1, place.ways)
    ]
    for copy in deep:
        copy.wait_recv()
    gains = small_s[6, half - 8 : half, :]
    for offset in range(1, place.ways):
        gains = gains + small_s[6 + offset, half - 8 : half, :]
    last = jnp.where(place.core == 1, gains, total[half - 8 : half, :])
    ready, came = 6 + place.ways, 7 + place.ways
    small_s[ready] = jnp.concatenate([total[: half - 8, :], last], axis=0)
    back = send(small_s.at[ready], small_s.at[came], sems["small"], 4 + place.ways, place.partner, place.depth)
    sum_ref[mine, :] = small_s[ready]
    back.wait_recv()
    sum_ref[pl.ds(pl.multiple_of((1 - place.core) * half, half), half), :] = small_s[came]
    return chips + deep + [back]


def sem_shapes(names):
    shapes = []
    for count in names.values():
        shapes += [pltpu.SemaphoreType.DMA((count,))] * 2
    return shapes


def sem_dict(names, refs):
    return {name: (refs[2 * at], refs[2 * at + 1]) for at, name in enumerate(names)}


def edge_kernel(kind, extra, carrying, ways, rows, parts, in_group, out_group, names, counts, *refs):
    place = Place(ways)
    share = rows // ways
    ins, outs = list(refs[: counts[0]]), list(refs[counts[0] : counts[0] + counts[1]])
    scratch = list(refs[counts[0] + counts[1] : counts[0] + counts[1] + counts[2]])
    sems = sem_dict(names, refs[sum(counts) :])
    part_ref = ins.pop(0)
    near_s, sum_s, far_s, deep_s = [scratch.pop(0) for _ in range(4)]
    if kind == "forward":
        stream_ref, gain_ref = ins.pop(0), ins.pop(0)
    elif kind != "sum":
        stream_ref, gain_ref, grad_ref = ins.pop(0), ins.pop(0), ins.pop(0)
    all_ref = outs.pop(0)
    if kind != "sum" and kind != "last":
        fresh_ref = outs.pop(0)
    if kind == "backward":
        dgain_ref = outs.pop(0)
    if kind == "last":
        small_ref, late_ref, three_ref = ins.pop(0), ins.pop(0), ins.pop(0)
        dgain_ref, late_out_ref = outs.pop(0), outs.pop(0)
        low_s, small_s, late_s, late_low_s = [scratch.pop(0) for _ in range(4)]
    if carrying:
        source_ref, target_ref = ins.pop(), outs.pop()
    everyone = carrying or kind == "last"
    greet(place, turns(6) if everyone else sorted({*turns(in_group), *turns(out_group)}), carrying)
    first = Reduction(place, in_group, rows, parts, part_ref, near_s, sum_s, far_s, sems, ("near", "far"))
    waiting = []
    freight = {}
    if extra == "gather":
        load_ref, load_out_ref = ins.pop(0), outs.pop(0)

        def load_rows(turned):
            return rows_at(place.side(in_group, turned) * 2 + place.core, rows, rows)

        def between(stage):
            spot = rows_at(place.side(in_group) * 2 + place.core, rows, rows)
            if stage == 0:
                load_out_ref[spot, :] = load_ref[...]
                return
            own = load_out_ref.at[spot, :]
            if stage == 1:
                freight.update(first_leg(place, own, sems["load_far"], 0))
                freight[0] = send(own, own, sems["load_near"], 0, place.partner, place.depth)
            else:
                hand_on(place, in_group, load_rows, load_out_ref, sems["load_far"], 0, freight)

    elif extra == "reduce":
        second = Reduction(
            place, in_group, rows, parts, ins.pop(0), *[scratch.pop(0) for _ in range(3)], sems, ("load_near", "load_far")
        )
        load_out_ref = outs.pop(0)

        def between(stage):
            (second.send_near, second.send_far, second.relay)[stage]()

    else:

        def between(stage):
            pass

    carried = []

    def on_the_way(stage):
        between(stage)
        if carrying and stage == (1 if in_group else 0):
            carried.append(exchange_start(place, source_ref, target_ref, sems["exchange"]))

    if kind == "last":
        late = deep_sends(place, share, late_ref, 0, late_s, slice(None), sems["late"], 0)
        waiting += late
    total, copies = reduce_stage(first, deep_s, sems, on_the_way)
    waiting += copies
    if kind == "forward":
        fresh = stream_ref[...] + total
        fresh_ref[...] = fresh
        scale = lax.rsqrt(jnp.mean(fresh * fresh, axis=-1, keepdims=True) + EPS)
        value = fresh * scale * gain_ref[...]
    elif kind == "sum":
        value = total
    else:
        stream = stream_ref[...]
        scale = lax.rsqrt(jnp.mean(stream * stream, axis=-1, keepdims=True) + EPS)
        leaned = total * gain_ref[...]
        inner = jnp.mean(leaned * stream, axis=-1, keepdims=True)
        value = grad_ref[...] + scale * leaned - stream * (scale * scale * scale * inner)
        dgain = jnp.sum(total * stream * scale, axis=0, keepdims=True)
        if kind == "backward":
            dgain_ref[...] = dgain
            fresh_ref[...] = value
    if kind == "last":
        own = pl.ds(pl.multiple_of(place.depth * share, share), share)
        low_s[own, :] = value.astype(low_s.dtype)
        spread = spread_stage(place, rows, low_s, sems)
        late_total = three_ref[...] + deep_total(place, share, late_ref, 0, late_s, late)
        late_low_s[own, :] = late_total.astype(late_low_s.dtype)
        spread += spread_stage(place, rows, late_low_s, sems, "late_back")
        half, span = small_ref.shape[0] // 2, small_ref.shape[1]
        dgain_ref[...] = small_ref[...]
        for at in range(dgain.shape[1] // span):
            dgain_ref[pl.ds(2 * half - 8 + at, 1), :] = dgain[:, at * span : (at + 1) * span]
        waiting += spread + small_stage(place, half, dgain_ref, small_s, sems)
        for copy in spread:
            copy.wait_recv()
        all_ref[...] = low_s[...].astype(jnp.float32)
        late_out_ref[...] = late_low_s[...].astype(jnp.float32)
    else:
        spot = pl.multiple_of((place.side(out_group) * 2 + place.core) * rows + place.depth * share, share)
        all_ref[pl.ds(spot, share), :] = value.astype(all_ref.dtype)
        waiting += gather_stage(place, out_group, rows, all_ref, sems, partial(on_the_way, 2))
    if extra == "gather":
        last = []
        for at, turned in enumerate((2, 4, 6)):
            for key in ((2, 4), (4, 2)) if turned == 6 else ():
                freight[key].wait_recv()
            came = load_out_ref.at[load_rows(turned), :]
            last.append(send(came, came, sems["load_near"], 1 + at, place.partner, place.depth))
        for copy in last + [freight[0]]:
            copy.wait_recv()
        waiting += list(freight.values()) + last
    elif extra == "reduce":
        for part in range(parts):
            load_out_ref[:, second.lanes(part)] = second.chip_sum(part).astype(load_out_ref.dtype)
        waiting += second.sent()
    for copies, own in carried:
        for copy in copies:
            copy.wait_recv()
        own.wait()
        waiting += copies
    for copy in waiting:
        copy.wait_send()


def edge(kind, part, extras, ways, rows, parts, in_group, out_group, ident, name, extra=None, carried=None):
    width = part.shape[1]
    share = rows // ways
    in_far, out_far = len(turns(in_group)), len(turns(out_group or 0))
    in_sides, out_sides = in_far + 1, out_far + 1
    dtype = part.dtype
    line = jax.ShapeDtypeStruct((1, width), jnp.float32)
    strip = jax.ShapeDtypeStruct((share, width), jnp.float32)
    whole = jax.ShapeDtypeStruct((out_sides * 2 * rows, width), dtype)
    block = jax.ShapeDtypeStruct((rows, width), jnp.float32)
    outs = {
        "forward": [whole, strip],
        "backward": [whole, strip, line],
        "last": [block] + [jax.ShapeDtypeStruct(one.shape, one.dtype) for one in extras[3:4]] + [block],
        "sum": [whole],
    }[kind]
    names = {"near": parts * in_sides, "far": 3 * parts if in_far else 0, "deep": parts * (ways - 1), "deep_back": ways - 1}
    reducing = [
        pltpu.VMEM((in_sides * rows, width), dtype),
        pltpu.VMEM((in_sides * rows, width), dtype),
        pltpu.VMEM((max(in_far, 1), rows if in_far else 16, width), dtype),
    ]
    deep = pltpu.VMEM((ways - 1, share, width), dtype)
    scratch = reducing + [deep]
    if kind == "last":
        names.update({"small": 5 + ways, "late": ways - 1, "late_back": ways - 1})
        small = pltpu.VMEM((8 + ways, extras[3].shape[0] // 2, extras[3].shape[1]), jnp.float32)
        spread = pltpu.VMEM((rows, width), dtype)
        scratch += [spread, small, deep, spread]
    else:
        names.update({"far_back": 4 * ways if out_far else 0, "near_back": ways * out_sides})
    if extra == "gather":
        names.update({"load_far": 4, "load_near": in_sides})
        outs = outs + [jax.ShapeDtypeStruct((in_sides * 2 * rows, width), dtype)]
    elif extra == "reduce":
        names.update({"load_far": 3 * parts, "load_near": parts * in_sides})
        outs = outs + [jax.ShapeDtypeStruct((rows, width), dtype)]
        scratch = scratch + reducing
    vmem, whole_memory = pl.BlockSpec(memory_space=pltpu.VMEM), pl.BlockSpec(memory_space=pl.ANY)
    in_specs, out_specs = [vmem] * (1 + len(extras)), [vmem] * len(outs)
    if carried is not None:
        names["exchange"] = 8
        extras = list(extras) + [carried]
        outs = outs + [jax.ShapeDtypeStruct(carried.shape, carried.dtype)]
        in_specs, out_specs = in_specs + [whole_memory], out_specs + [whole_memory]
    names = {key: count for key, count in names.items() if count}
    if not in_far:
        names["far"] = 1
    return pl.pallas_call(
        partial(
            edge_kernel, kind, extra, carried is not None, ways, rows, parts, in_group, out_group, names,
            (1 + len(extras), len(outs), len(scratch)),
        ),
        in_specs=in_specs,
        out_specs=out_specs,
        out_shape=outs,
        scratch_shapes=scratch + sem_shapes(names),
        compiler_params=pltpu.CompilerParams(
            collective_id=ident, has_side_effects=True, vmem_limit_bytes=48 << 20
        ),
        cost_estimate=pl.CostEstimate(flops=1, bytes_accessed=1, transcendentals=0),
        name=name,
    )(part, *extras)


def opening_kernel(ways, rows, hidden_ref, gain_ref, first_ref, send_sem, recv_sem):
    place = Place(ways)
    barrier = pltpu.get_barrier_semaphore()
    pl.semaphore_signal(barrier, inc=1, device_id=(place.partner, place.depth), device_id_type=MESH)
    pl.semaphore_wait(barrier, 1)
    stream = hidden_ref[...].astype(jnp.float32)
    scale = lax.rsqrt(jnp.mean(stream * stream, axis=-1, keepdims=True) + EPS)
    first_ref[rows_at(place.core, rows, rows), :] = (stream * scale * gain_ref[...]).astype(jnp.bfloat16)
    mine = first_ref.at[rows_at(place.core, rows, rows), :]
    send(mine, mine, (send_sem, recv_sem), 0, place.partner, place.depth).wait()


def opening(hidden, gain, ways, ident):
    rows, width = hidden.shape
    vmem = pl.BlockSpec(memory_space=pltpu.VMEM)
    return pl.pallas_call(
        partial(opening_kernel, ways, rows),
        in_specs=[vmem] * 2,
        out_specs=vmem,
        out_shape=jax.ShapeDtypeStruct((2 * rows, width), jnp.bfloat16),
        scratch_shapes=[pltpu.SemaphoreType.DMA((1,))] * 2,
        compiler_params=pltpu.CompilerParams(
            collective_id=ident, has_side_effects=True, vmem_limit_bytes=40 << 20
        ),
        cost_estimate=pl.CostEstimate(flops=1, bytes_accessed=1, transcendentals=0),
        name="opening",
    )(hidden, gain)


def probs_of(query, keys, allowed):
    scores = project_t(query, keys) * (1.0 / math.sqrt(HEAD_DIM))
    scores = jnp.where(allowed, scores, NEG_FILL)
    shifted = jnp.exp(scores - jnp.max(scores, axis=-1, keepdims=True))
    return shifted / jnp.sum(shifted, axis=-1, keepdims=True)


def allowed_in(down_ref, side_ref, rows, group):
    shape = (rows, rows)
    distance = lax.broadcasted_iota(jnp.int32, shape, 0) - lax.broadcasted_iota(jnp.int32, shape, 1)
    same = down_ref[group * rows : (group + 1) * rows, :] == side_ref[group : group + 1, :]
    return same & (distance >= 0) & (distance < WINDOW)


def attend_kernel(heads, rows, joint_ref, down_ref, side_ref, low_ref, out_ref):
    low_ref[...] = joint_ref[...].astype(jnp.bfloat16)
    size = heads * HEAD_DIM
    for group in range(joint_ref.shape[0] // rows):
        allowed = allowed_in(down_ref, side_ref, rows, group)
        span = slice(group * rows, (group + 1) * rows)
        for head in range(heads):
            at = slice(head * HEAD_DIM, (head + 1) * HEAD_DIM)
            query, keys, values = [
                low_ref[span, part * size + head * HEAD_DIM : part * size + (head + 1) * HEAD_DIM] for part in range(3)
            ]
            probs = probs_of(query, keys, allowed)
            out_ref[span, at] = project(probs.astype(jnp.bfloat16), values).astype(jnp.bfloat16)


def attend(joint, down, side, rows):
    count, size = joint.shape
    return pl.pallas_call(
        partial(attend_kernel, size // (3 * HEAD_DIM), rows),
        out_shape=[
            jax.ShapeDtypeStruct((count, size), jnp.bfloat16),
            jax.ShapeDtypeStruct((count, size // 3), jnp.bfloat16),
        ],
        compiler_params=pltpu.CompilerParams(vmem_limit_bytes=32 << 20),
        name="attend",
    )(joint, down, side)


def attend_back_kernel(heads, rows, low_ref, grad_ref, down_ref, side_ref, out_ref):
    size = heads * HEAD_DIM
    scale = 1.0 / math.sqrt(HEAD_DIM)
    for group in range(low_ref.shape[0] // rows):
        allowed = allowed_in(down_ref, side_ref, rows, group)
        span = slice(group * rows, (group + 1) * rows)
        for head in range(heads):
            places = [slice(part * size + head * HEAD_DIM, part * size + (head + 1) * HEAD_DIM) for part in range(3)]
            query, keys, values = [low_ref[span, place] for place in places]
            grad = grad_ref[span, head * HEAD_DIM : (head + 1) * HEAD_DIM].astype(jnp.bfloat16)
            probs = probs_of(query, keys, allowed)
            grad_probs = project_t(grad, values)
            inner = jnp.sum(probs * grad_probs, axis=-1, keepdims=True)
            grad_scores = (probs * (grad_probs - inner)).astype(jnp.bfloat16)
            out_ref[span, places[0]] = (project(grad_scores, keys) * scale).astype(jnp.bfloat16)
            out_ref[span, places[1]] = (outer_rows(grad_scores, query) * scale).astype(jnp.bfloat16)
            out_ref[span, places[2]] = outer_rows(probs.astype(jnp.bfloat16), grad).astype(jnp.bfloat16)


def attend_back(low, grad, down, side, rows):
    count, size = low.shape
    return pl.pallas_call(
        partial(attend_back_kernel, size // (3 * HEAD_DIM), rows),
        out_shape=jax.ShapeDtypeStruct((count, size), jnp.bfloat16),
        compiler_params=pltpu.CompilerParams(vmem_limit_bytes=32 << 20),
        name="attend_back",
    )(low, grad, down, side)


def sub_of(spot, group):
    if group == 6:
        return spot
    return spot % 2 + (2 * ((spot // group) % 2) if group else 0)


def subs_of(group):
    return 2 * (len(turns(group)) + 1)


def pull(count, *sets):
    def cut(block, group, spot):
        size = block.shape[1] // subs_of(group)
        return block[:, sub_of(spot, group) * size : (sub_of(spot, group) + 1) * size]

    return jnp.stack(
        [
            jnp.concatenate([cut(block, group, spot) for blocks, group in sets for block in blocks], axis=1)
            for spot in range(count)
        ]
    )


def swap(stacked):
    return lax.all_to_all(stacked, "dp", 0, 0, tiled=True)


def settle(swapped, group, blocks):
    subs = subs_of(group)
    count = swapped.shape[0]
    size = swapped.shape[2] // blocks
    sums = []
    for sub in range(subs):
        sums.append(sum(swapped[spot].astype(jnp.float32) for spot in range(count) if sub_of(spot, group) == sub))
    return [
        jnp.concatenate([one[:, block * size : (block + 1) * size] for one in sums], axis=1) for block in range(blocks)
    ]


def after(value, *others):
    return lax.optimization_barrier((value,) + others)[0]


def grouped_body(
    counts,
    early_group,
    focus_group,
    late_group,
    hidden_in,
    seq_lengths,
    norm_gains,
    mixer_in,
    mixer_rows,
    conv_weight,
    conv_bias,
    step_bias,
    decay_log,
    skip_gain,
    early_gate_up,
    early_down,
    attention_in,
    attention_out,
    late_gate_up,
    late_down,
    output_grad,
):
    spots, ways = counts
    rows, width = hidden_in.shape
    share = rows // ways
    spot = lax.axis_index("dp")
    depth = lax.axis_index("tensor")
    core = spot % 2
    low = jnp.bfloat16

    def swapped_core(value):
        return lax.ppermute(value, "dp", [(at, at ^ 1) for at in range(spots)])

    in_weights = swap(pull(spots, ([mixer_in[0], mixer_in[1]], 0)))

    other_lengths = swapped_core(seq_lengths)
    lengths = jnp.where(
        core == 0, jnp.stack([seq_lengths, other_lengths]), jnp.stack([other_lengths, seq_lengths])
    )
    segs, starts = jax.vmap(lambda own: segment_info(own, rows))(lengths)
    flat_segs = (segs + jnp.arange(2, dtype=jnp.int32)[:, None] * rows).reshape(-1)
    keeping = 1.0 - starts.reshape(-1).astype(jnp.float32)
    groups = 2 * seq_lengths.shape[0]

    first_low = opening(hidden_in, norm_gains[0:1], ways, 20)
    row_weights = swap(after(pull(spots, ([mixer_rows], 0)), in_weights, first_low))
    stream_zero = lax.dynamic_slice_in_dim(hidden_in, depth * share, share, 0).astype(jnp.float32)

    channels = conv_weight.shape[0] // 2

    def half(values):
        return lax.dynamic_slice_in_dim(values, core * channels, channels, 0)

    taps, offset, bias, decay, skip = [half(v) for v in (conv_weight, conv_bias, step_bias, decay_log, skip_gain)]
    in_mat = in_weights.reshape(width, 2 * channels)
    both = project(first_low, in_mat)
    conv_in, gate_half = both[:, :channels], both[:, channels:]
    channel_full, conv_back = jax.vjp(partial(causal_conv, flat_segs), conv_in, taps, offset)
    channel_low = channel_full.astype(low)
    row_mat = row_weights.reshape(-1, channels)
    early_blocks = [early_gate_up[0], early_gate_up[1], early_down]
    focus_blocks = [attention_in[0], attention_in[1], attention_in[2], attention_out]
    early_weights = swap(after(pull(spots, (early_blocks, early_group)), row_weights, both))
    out_mat = row_mat[:width]
    select_mat = row_mat[width : width + PROJ_OUT]
    step_mat = row_mat[width + PROJ_OUT :]

    def mixed_sum(part, ident, name, carried=None):
        padded = jnp.pad(part, ((0, 0), (0, 256 - PROJ_OUT)))
        total, *came = edge("sum", padded, [], ways, rows, 1, 0, 0, ident, name, carried=carried)
        return total[:, :PROJ_OUT], *came

    mix_rows, = mixed_sum(project_t(channel_low, select_mat), 1, "mix_sum")
    rank_low = mix_rows[:, :DT_RANK].astype(low)
    step_raw = project(rank_low, step_mat)
    rates_t = -jnp.exp(decay).T
    wide = (2 * rows, STATE, LANES)
    in_wide = jnp.broadcast_to(mix_rows[:, DT_RANK : DT_RANK + STATE, None], wide)
    out_wide = jnp.broadcast_to(mix_rows[:, DT_RANK + STATE :, None], wide)
    mixer_low = scan_forward(
        keeping, channel_low, step_raw, gate_half, bias, rates_t, skip, in_wide, out_wide, groups, LANES
    )
    focus_weights = swap(after(pull(spots, (focus_blocks, focus_group)), early_weights, mixer_low))
    early_mat, focus_mat = [one.reshape(width, -1) for one in (early_weights, focus_weights)]
    second_low, stream_one = edge(
        "forward", project_t(mixer_low, out_mat).astype(low), [stream_zero, norm_gains[1:2]],
        ways, rows, 4, 0, early_group, 2, "edge_one",
    )

    def ffn(normed, mat):
        units = mat.shape[1] // 3
        both = project(normed, mat[:, : 2 * units])
        hidden = gated_unit(both[:, :units], both[:, units:]).astype(low)
        return project_t(hidden, mat[:, 2 * units :]).astype(low), both, hidden

    early_part, early_both, early_hidden = ffn(second_low, early_mat)
    third_low, stream_two, last_grad = edge(
        "forward", early_part, [stream_one, norm_gains[2:3], output_grad], ways, rows, 4, early_group, 0, 3, "edge_two",
        "gather",
    )

    late_blocks = [late_gate_up[0], late_gate_up[1], late_down]
    late_weights = swap(after(pull(spots, (late_blocks, late_group)), focus_weights, third_low))
    heads_width = focus_mat.shape[1] // 4
    down, side = flat_segs[:, None], flat_segs.reshape(2, rows)
    joint_low, attended_low = attend(project(third_low, focus_mat[:, : 3 * heads_width]), down, side, rows)
    fourth_low, stream_three = edge(
        "forward", project_t(attended_low, focus_mat[:, 3 * heads_width :]).astype(low),
        [stream_two, norm_gains[3:4]], ways, rows, 4, 0, late_group, 4, "edge_three",
    )

    late_mat = late_weights.reshape(width, -1)
    late_part, late_both, late_hidden = ffn(fourth_low, late_mat)

    def ffn_back(grad_low, normed, both, hidden, mat):
        units = mat.shape[1] // 3
        grad_hidden = project(grad_low, mat[:, 2 * units :])
        _, unit_back = jax.vjp(gated_unit, both[:, :units], both[:, units:])
        both_low = jnp.concatenate(unit_back(grad_hidden), axis=1).astype(low)
        grad_normed = project_t(both_low, mat[:, : 2 * units]).astype(low)
        joint = jnp.concatenate([outer_rows(normed, both_low), outer_rows(grad_low, hidden)], axis=1)
        return grad_normed, joint.astype(low).reshape(spots, -1, 3 * units)

    grad_fourth, late_joint = ffn_back(last_grad, fourth_low, late_both, late_hidden, late_mat)
    grad_zero = lax.dynamic_slice_in_dim(output_grad, depth * share, share, 0).astype(jnp.float32)
    grad_low_three, grad_three, gain_four, output_part = edge(
        "backward", grad_fourth, [stream_three, norm_gains[3:4], grad_zero, late_part],
        ways, rows, 4, late_group, 0, 5, "edge_four", "reduce",
    )

    grad_attended = project(grad_low_three, focus_mat[:, 3 * heads_width :])
    joint_grad = attend_back(joint_low, grad_attended, down, side, rows)
    grad_low_two, grad_two, gain_three, late_swapped = edge(
        "backward", project_t(joint_grad, focus_mat[:, : 3 * heads_width]).astype(low),
        [stream_two, norm_gains[2:3], grad_three], ways, rows, 4, 0, early_group, 6, "edge_five", carried=late_joint,
    )
    focus_joint = jnp.concatenate(
        [outer_rows(third_low, joint_grad), outer_rows(grad_low_three, attended_low)], axis=1
    ).astype(low)
    focus_joint = focus_joint.reshape(spots, -1, 4 * heads_width)

    grad_second, early_joint = ffn_back(grad_low_two, second_low, early_both, early_hidden, early_mat)
    grad_low_one, grad_one, gain_two, focus_swapped = edge(
        "backward", grad_second, [stream_one, norm_gains[1:2], grad_two],
        ways, rows, 4, early_group, 0, 7, "edge_six", carried=focus_joint,
    )
    early_swapped = swap(after(early_joint, grad_low_one))

    grad_scanned = project(grad_low_one, out_mat)
    (
        grad_channel,
        grad_step_low,
        gate_low,
        in_sums,
        out_sums,
        bias_grad,
        decay_grad,
        skip_grad,
    ) = scan_backward(
        keeping, channel_low, step_raw, gate_half, grad_scanned, bias, rates_t, skip, in_wide, out_wide,
        groups, LANES,
    )
    grad_channel, grad_step_low, in_sums, out_sums, early_swapped = lax.optimization_barrier(
        (grad_channel, grad_step_low, in_sums, out_sums, early_swapped)
    )
    grad_rank = project_t(grad_step_low, step_mat)
    gate_joint = outer_rows(first_low, gate_low).astype(low).reshape(spots, -1, channels)
    grad_rows, gate_swapped = mixed_sum(
        jnp.concatenate([grad_rank, jnp.sum(in_sums, axis=-1), jnp.sum(out_sums, axis=-1)], axis=1), 8, "mix_grad_sum",
        gate_joint,
    )
    grad_rows_low = grad_rows.astype(low)
    rows_joint = jnp.concatenate(
        [
            outer_rows(grad_low_one, mixer_low),
            outer_rows(grad_rows_low, channel_low),
            outer_rows(rank_low, grad_step_low),
        ],
        axis=0,
    ).astype(low)
    grad_channel = grad_channel + project(grad_rows_low, select_mat)
    grad_conv_in, taps_grad, offset_grad = conv_back(grad_channel)
    conv_low = grad_conv_in.astype(low)
    conv_joint = outer_rows(first_low, conv_low).astype(low).reshape(spots, -1, channels)
    in_grad = jnp.concatenate([conv_low, gate_low], axis=1)
    grad_first = project_t(in_grad, in_mat).astype(low)
    mixer_joint = jnp.concatenate([conv_joint, rows_joint.reshape(spots, -1, channels)], axis=1)
    mixer_joint = jnp.pad(mixer_joint, ((0, 0), (0, -mixer_joint.shape[1] % 16), (0, 0)))
    lines = jnp.concatenate([taps_grad.T, offset_grad[None], bias_grad, skip_grad, decay_grad], axis=0)
    lines = jnp.pad(lines, ((0, 1), (0, 0)))
    blank = jnp.zeros_like(lines)
    lines = jnp.where(core == 0, jnp.concatenate([lines, blank], axis=1), jnp.concatenate([blank, lines], axis=1))
    gains = jnp.concatenate([jnp.zeros_like(gain_two), gain_two, gain_three, gain_four], axis=0)
    small = jnp.concatenate([lines, gains.reshape(8, -1)], axis=0)
    input_grad, small, output, mixer_swapped = edge(
        "last", grad_first, [stream_zero, norm_gains[0:1], grad_one, small, output_part, stream_three],
        ways, rows, 4, 0, None, 9, "edge_seven", carried=mixer_joint,
    )
    lines = small[: CONV + 3 + STATE]
    gains = small[-8:].reshape(norm_gains.shape)
    late_grads = settle(late_swapped, late_group, 3)
    early_grads = settle(early_swapped, early_group, 3)
    focus_grads = settle(focus_swapped, focus_group, 4)
    gate_grad = settle(gate_swapped, 0, 1)[0]
    mixer_grads = settle(mixer_swapped, 0, 1)[0]
    in_rows = mixer_in.shape[1]
    return (
        output,
        input_grad,
        gains,
        jnp.stack([mixer_grads[:in_rows], gate_grad]),
        mixer_grads[in_rows : in_rows + mixer_rows.shape[0]],
        lines[:CONV].T,
        lines[CONV],
        lines[CONV + 1],
        lines[CONV + 3 :].T,
        lines[CONV + 2],
        jnp.stack(early_grads[:2]),
        early_grads[2],
        jnp.stack(focus_grads[:3]),
        focus_grads[3],
        jnp.stack(late_grads[:2]),
        late_grads[2],
    )


def solution(mesh):
    counts = (mesh.shape["dp"], mesh.shape["tensor"])
    chosen = partial(grouped_body, counts, 6, 0, 6) if counts == (8, 4) else body
    return jax.shard_map(
        chosen,
        mesh=mesh,
        in_specs=(
            P("dp", None),
            P("dp", None),
            P(),
            P(None, "dp", "tensor"),
            P("dp", "tensor"),
            P("tensor", None),
            P("tensor"),
            P("tensor"),
            P("tensor", None),
            P("tensor"),
            P(None, "dp", "tensor"),
            P("dp", "tensor"),
            P(None, "dp", "tensor"),
            P("dp", "tensor"),
            P(None, "dp", "tensor"),
            P("dp", "tensor"),
            P("dp", None),
        ),
        out_specs=(
            P("dp", None),
            P("dp", None),
            P(),
            P(None, "dp", "tensor"),
            P("dp", "tensor"),
            P("tensor", None),
            P("tensor"),
            P("tensor"),
            P("tensor", None),
            P("tensor"),
            P(None, "dp", "tensor"),
            P("dp", "tensor"),
            P(None, "dp", "tensor"),
            P("dp", "tensor"),
            P(None, "dp", "tensor"),
            P("dp", "tensor"),
        ),
        check_vma=False,
    )
```

```python
from functools import partial
import math

import jax
import jax.numpy as jnp
from jax import lax
from jax.experimental import pallas as pl
from jax.experimental.layout import Layout, with_layout_constraint
from jax.experimental.pallas import tpu as pltpu
from jax.sharding import PartitionSpec as P

STATE = 16
CONV = 4
DT_RANK = 128
HEAD_DIM = 128
WINDOW = 2048
PROJ_OUT = 160


EPS = 1e-05
NEG_FILL = -1e30


def project(left, right):
    return jnp.dot(left, right, preferred_element_type=jnp.float32)


def project_t(left, right):
    return lax.dot_general(
        left, right, (((1,), (1,)), ((), ())), preferred_element_type=jnp.float32
    )


def outer_rows(left, right):
    return lax.dot_general(
        left, right, (((0,), (0,)), ((), ())), preferred_element_type=jnp.float32
    )


def rms_norm(values, weight):
    return values * lax.rsqrt(jnp.mean(values * values, axis=-1, keepdims=True) + EPS) * weight


def segment_info(lengths, tokens):
    flat_lengths = lengths.reshape(-1)
    ends = jnp.cumsum(flat_lengths, dtype=jnp.int32)
    firsts = ends - flat_lengths
    places = jnp.arange(tokens, dtype=jnp.int32)
    segs = jnp.sum((places[:, None] >= ends[None, :]).astype(jnp.int32), axis=1)
    starts = jnp.any(places[:, None] == firsts[None, :], axis=1)
    return (segs, starts)


def allowed_pairs(segs):
    places = jnp.arange(segs.shape[-1], dtype=jnp.int32)
    distance = places[:, None] - places[None, :]
    return (segs[:, None] == segs[None, :]) & (distance >= 0) & (distance < WINDOW)


def causal_conv(segs, stream, weight, offset):
    total = offset + stream * weight[:, 0]
    for lag_step in range(1, CONV):
        moved = jnp.concatenate(
            [jnp.zeros_like(stream[..., :lag_step, :]), stream[..., :-lag_step, :]], axis=-2
        )
        moved_segs = jnp.concatenate(
            [jnp.full_like(segs[..., :lag_step], -1), segs[..., :-lag_step]], axis=-1
        )
        linked = (segs == moved_segs).astype(stream.dtype)
        total = total + moved * weight[:, lag_step] * linked[..., None]
    return jax.nn.silu(total)


LANES = 128


def softplus(v):
    return jnp.maximum(v, 0.0) + jnp.log1p(jnp.exp(-jnp.abs(v)))


def scan_forward_kernel(
    groups, length, keep_ref, chan_ref, raw_ref, gate_ref, bias_ref, rate_ref, skip_ref, in_ref, out_ref,
    mixed_ref, step_s, drive_s, y_s,
):
    width = chan_ref.shape[1]
    blocks = width // LANES
    step_s[...] = softplus(raw_ref[...] + bias_ref[...])
    drive_s[...] = step_s[...] * chan_ref[...].astype(jnp.float32)
    rates = [rate_ref[:, pl.ds(b * LANES, LANES)] for b in range(blocks)]

    def advance(t, states):
        fresh = []
        for g in range(groups):
            row = g * length + t
            keep = keep_ref[row]
            input_map = in_ref[row]
            output_map = out_ref[row]
            for b in range(blocks):
                lanes = pl.ds(b * LANES, LANES)
                decay = jnp.exp(step_s[pl.ds(row, 1), lanes] * rates[b]) * keep
                state = decay * states[g * blocks + b] + drive_s[pl.ds(row, 1), lanes] * input_map
                y_s[pl.ds(row, 1), lanes] = jnp.sum(state * output_map, axis=0, keepdims=True)
                fresh.append(state)
        return tuple(fresh)

    zero = jnp.zeros((STATE, LANES), jnp.float32)
    lax.fori_loop(0, length, advance, (zero,) * (groups * blocks))
    gate = gate_ref[...]
    silu = gate / (1.0 + jnp.exp(-gate))
    mixed_ref[...] = (
        (y_s[...] + skip_ref[...] * chan_ref[...].astype(jnp.float32)) * silu
    ).astype(mixed_ref.dtype)


def scan_forward(keep, channel, step_raw, gate_half, step_bias, rates_t, skip_gain, in_wide, out_wide, groups, width):
    tokens, channels = channel.shape
    column = pl.BlockSpec((tokens, width), lambda i: (0, i))
    row = pl.BlockSpec((1, width), lambda i: (0, i))
    maps = pl.BlockSpec((tokens, STATE, LANES), lambda i: (0, 0, 0))
    return pl.pallas_call(
        partial(scan_forward_kernel, groups, tokens // groups),
        grid=(channels // width,),
        in_specs=[
            pl.BlockSpec(memory_space=pltpu.SMEM), column, column, column, row,
            pl.BlockSpec((STATE, width), lambda i: (0, i)), row, maps, maps,
        ],
        out_specs=column,
        out_shape=jax.ShapeDtypeStruct((tokens, channels), jnp.bfloat16),
        scratch_shapes=[pltpu.VMEM((tokens, width), jnp.float32)] * 3,
        compiler_params=pltpu.CompilerParams(vmem_limit_bytes=48 << 20),
        cost_estimate=pl.CostEstimate(flops=1, bytes_accessed=1 << 34, transcendentals=0),
        name="scan_forward",
    )(keep, channel, step_raw, gate_half, step_bias[None], rates_t, skip_gain[None], in_wide, out_wide)


def scan_backward_kernel(
    groups, length, keep_ref, chan_ref, raw_ref, gate_ref, dmix_ref, bias_ref, rate_ref, skip_ref, in_ref, out_ref,
    dchan_ref, draw_ref, dgate_ref, din_ref, dout_ref, dbias_ref, drate_ref, dskip_ref,
    step_s, drive_s, y_s, dy_s, dd_s, ds_s, state_s, decay_s,
):
    width = chan_ref.shape[1]
    blocks = width // LANES
    chan = chan_ref[...].astype(jnp.float32)
    step_s[...] = softplus(raw_ref[...] + bias_ref[...])
    drive_s[...] = step_s[...] * chan
    gate = gate_ref[...]
    sig = 1.0 / (1.0 + jnp.exp(-gate))
    dy_s[...] = dmix_ref[...] * (gate * sig)
    rates = [rate_ref[:, pl.ds(b * LANES, LANES)] for b in range(blocks)]

    @pl.when(pl.program_id(0) == 0)
    def _():
        din_ref[...] = jnp.zeros_like(din_ref)
        dout_ref[...] = jnp.zeros_like(dout_ref)

    def advance(t, states):
        fresh = []
        for g in range(groups):
            row = g * length + t
            keep = keep_ref[row]
            input_map = in_ref[row]
            output_map = out_ref[row]
            total = None
            for b in range(blocks):
                lanes = pl.ds(b * LANES, LANES)
                decay = jnp.exp(step_s[pl.ds(row, 1), lanes] * rates[b]) * keep
                decay_s[row, :, lanes] = decay
                carried = decay * states[g * blocks + b]
                state_s[row, :, lanes] = carried
                state = carried + drive_s[pl.ds(row, 1), lanes] * input_map
                y_s[pl.ds(row, 1), lanes] = jnp.sum(state * output_map, axis=0, keepdims=True)
                term = state * dy_s[pl.ds(row, 1), lanes]
                total = term if total is None else total + term
                fresh.append(state)
            dout_ref[row] += total
        return tuple(fresh)

    zero = jnp.zeros((STATE, LANES), jnp.float32)
    count = groups * blocks
    lax.fori_loop(0, length, advance, (zero,) * count)

    def retreat(back, carry):
        t = length - 1 - back
        fresh, rate_sums = [], []
        for g in range(groups):
            row = g * length + t
            input_map = in_ref[row]
            output_map = out_ref[row]
            total = None
            for b in range(blocks):
                lanes = pl.ds(b * LANES, LANES)
                at = g * blocks + b
                dstate = carry[0][at] + dy_s[pl.ds(row, 1), lanes] * output_map
                dlog = dstate * state_s[row, :, lanes]
                dd_s[pl.ds(row, 1), lanes] = jnp.sum(dstate * input_map, axis=0, keepdims=True)
                ds_s[pl.ds(row, 1), lanes] = jnp.sum(dlog * rates[b], axis=0, keepdims=True)
                term = dstate * drive_s[pl.ds(row, 1), lanes]
                total = term if total is None else total + term
                rate_sums.append(carry[1][at] + dlog * step_s[pl.ds(row, 1), lanes])
                fresh.append(dstate * decay_s[row, :, lanes])
            din_ref[row] += total
        return (tuple(fresh), tuple(rate_sums))

    _, rate_sums = lax.fori_loop(0, length, retreat, ((zero,) * count, (zero,) * count))
    for b in range(blocks):
        lanes = pl.ds(b * LANES, LANES)
        drate_ref[:, lanes] = rates[b] * sum(rate_sums[g * blocks + b] for g in range(groups))
    direct = y_s[...] + skip_ref[...] * chan
    dgate_ref[...] = (dmix_ref[...] * direct * (sig * (1.0 + gate * (1.0 - sig)))).astype(dgate_ref.dtype)
    dskip_ref[...] = jnp.sum(dy_s[...] * chan, axis=0, keepdims=True)
    dchan_ref[...] = dd_s[...] * step_s[...] + skip_ref[...] * dy_s[...]
    shifted = raw_ref[...] + bias_ref[...]
    draw = (ds_s[...] + dd_s[...] * chan) / (1.0 + jnp.exp(-shifted))
    draw_ref[...] = draw.astype(draw_ref.dtype)
    dbias_ref[...] = jnp.sum(draw, axis=0, keepdims=True)


def scan_backward(
    keep, channel, step_raw, gate_half, dmixed, step_bias, rates_t, skip_gain, in_wide, out_wide, groups, width
):
    tokens, channels = channel.shape
    column = pl.BlockSpec((tokens, width), lambda i: (0, i))
    row = pl.BlockSpec((1, width), lambda i: (0, i))
    states = pl.BlockSpec((STATE, width), lambda i: (0, i))
    maps = pl.BlockSpec((tokens, STATE, LANES), lambda i: (0, 0, 0))
    sheet = jax.ShapeDtypeStruct((tokens, channels), jnp.float32)
    low = jax.ShapeDtypeStruct((tokens, channels), jnp.bfloat16)
    wide = jax.ShapeDtypeStruct((tokens, STATE, LANES), jnp.float32)
    line = jax.ShapeDtypeStruct((1, channels), jnp.float32)
    return pl.pallas_call(
        partial(scan_backward_kernel, groups, tokens // groups),
        grid=(channels // width,),
        in_specs=[
            pl.BlockSpec(memory_space=pltpu.SMEM), column, column, column, column, row, states, row, maps, maps,
        ],
        out_specs=[column, column, column, maps, maps, row, states, row],
        out_shape=[
            sheet, low, low, wide, wide, line, jax.ShapeDtypeStruct((STATE, channels), jnp.float32), line,
        ],
        scratch_shapes=[pltpu.VMEM((tokens, width), jnp.float32)] * 6
        + [pltpu.VMEM((tokens, STATE, width), jnp.float32)] * 2,
        compiler_params=pltpu.CompilerParams(vmem_limit_bytes=56 << 20),
        cost_estimate=pl.CostEstimate(flops=1, bytes_accessed=1 << 34, transcendentals=0),
        name="scan_backward",
    )(keep, channel, step_raw, gate_half, dmixed, step_bias[None], rates_t, skip_gain[None], in_wide, out_wide)


def attention_scores(query, keys, allowed):
    scores = jnp.einsum("qhd,khd->hqk", query, keys, preferred_element_type=jnp.float32) * (
        1.0 / math.sqrt(HEAD_DIM)
    )
    return jnp.where(allowed[None], scores, NEG_FILL)


def attention_forward(query, keys, values, allowed):
    scores = attention_scores(query, keys, allowed)
    row_max = jnp.max(scores, axis=-1, keepdims=True)
    shifted = jnp.exp(scores - row_max)
    totals = jnp.sum(shifted, axis=-1, keepdims=True)
    probs = shifted / totals
    mixed = jnp.einsum(
        "hqk,khd->qhd", probs.astype(jnp.bfloat16), values, preferred_element_type=jnp.float32
    )
    return (mixed, row_max + jnp.log(totals))


def attention_backward(query, keys, values, allowed, log_total, grad_mixed):
    scale = 1.0 / math.sqrt(HEAD_DIM)
    probs = jnp.exp(attention_scores(query, keys, allowed) - log_total)
    grad_values = jnp.einsum(
        "hqk,qhd->khd", probs.astype(jnp.bfloat16), grad_mixed, preferred_element_type=jnp.float32
    )
    grad_probs = jnp.einsum("qhd,khd->hqk", grad_mixed, values, preferred_element_type=jnp.float32)
    inner_sum = jnp.sum(probs * grad_probs, axis=-1, keepdims=True)
    grad_scores = (probs * (grad_probs - inner_sum)).astype(jnp.bfloat16)
    grad_query = (
        jnp.einsum("hqk,khd->qhd", grad_scores, keys, preferred_element_type=jnp.float32) * scale
    )
    grad_keys = (
        jnp.einsum("hqk,qhd->khd", grad_scores, query, preferred_element_type=jnp.float32) * scale
    )
    return (grad_query, grad_keys, grad_values)


def gated_unit(gate, upward):
    return jax.nn.silu(gate) * upward


def ffn_forward(normed_low, gate_up, down_mat):
    gate = project(normed_low, gate_up[0])
    upward = project(normed_low, gate_up[1])
    hidden = gated_unit(gate, upward).astype(jnp.bfloat16)
    return (project_t(hidden, down_mat), gate, upward, hidden)


def ffn_backward(grad_low, normed_low, gate, upward, hidden, gate_up, down_mat):
    grad_hidden = project(grad_low, down_mat)
    down_grad = outer_rows(grad_low, hidden)
    _, unit_back = jax.vjp(gated_unit, gate, upward)
    grad_gate, grad_up = unit_back(grad_hidden)
    gate_low = grad_gate.astype(jnp.bfloat16)
    up_low = grad_up.astype(jnp.bfloat16)
    joined_grad = outer_rows(normed_low, jnp.concatenate([gate_low, up_low], axis=1))
    grad_normed = project_t(gate_low, gate_up[0]) + project_t(up_low, gate_up[1])
    return (grad_normed, joined_grad, down_grad)


def flatten_low(grad_heads, tokens):
    return grad_heads.astype(jnp.bfloat16).reshape(tokens, -1)


def collect(stacked, row_block):
    return (
        lax.all_gather(stacked, "dp", axis=1, tiled=True),
        lax.all_gather(row_block, "dp", axis=0, tiled=True),
    )


def spread_grads(joined, row_block, count):
    summed = (
        lax.psum_scatter(joined.astype(jnp.bfloat16), "dp", scatter_dimension=0, tiled=True),
        lax.psum_scatter(row_block.astype(jnp.bfloat16), "dp", scatter_dimension=0, tiled=True),
    )
    rows_here = summed[0].shape[0]
    restacked = jnp.transpose(summed[0].reshape(rows_here, count, -1), (1, 0, 2))
    return (restacked.astype(jnp.float32), summed[1].astype(jnp.float32))


def branch_total(piece_sum):
    return lax.psum(piece_sum, "tensor")


def input_total(piece_sum):
    return lax.psum(piece_sum, "tensor")


def body(
    hidden_in,
    seq_lengths,
    norm_gains,
    mixer_in,
    mixer_rows,
    conv_weight,
    conv_bias,
    step_bias,
    decay_log,
    skip_gain,
    early_gate_up,
    early_down,
    attention_in,
    attention_out,
    late_gate_up,
    late_down,
    output_grad,
):
    tokens = hidden_in.shape[0]
    width = hidden_in.shape[1]
    segs, starts = segment_info(seq_lengths, tokens)
    allowed = allowed_pairs(segs)
    stream_zero = hidden_in.astype(jnp.float32)
    mixer_stack, mixer_mats = collect(mixer_in, mixer_rows)
    first_normed, first_back = jax.vjp(rms_norm, stream_zero, norm_gains[0])
    first_low = first_normed.astype(jnp.bfloat16)
    conv_in = project(first_low, mixer_stack[0])
    gate_half = project(first_low, mixer_stack[1])
    channel_full, conv_back = jax.vjp(partial(causal_conv, segs), conv_in, conv_weight, conv_bias)
    channel_low = channel_full.astype(jnp.bfloat16)
    mix_rows = lax.psum(project_t(channel_low, mixer_mats[width : width + PROJ_OUT]), "tensor")
    rank_low = mix_rows[:, :DT_RANK].astype(jnp.bfloat16)
    step_raw = project(rank_low, mixer_mats[width + PROJ_OUT :])
    groups = seq_lengths.shape[0]
    keeping = 1.0 - starts.astype(jnp.float32)
    rates_t = -jnp.exp(decay_log).T
    wide = (tokens, STATE, LANES)
    in_wide = jnp.broadcast_to(mix_rows[:, DT_RANK : DT_RANK + STATE, None], wide)
    out_wide = jnp.broadcast_to(mix_rows[:, DT_RANK + STATE :, None], wide)
    mixer_low = scan_forward(
        keeping, channel_low, step_raw, gate_half, step_bias, rates_t, skip_gain, in_wide, out_wide, groups, LANES
    )
    stream_one = stream_zero + branch_total(project_t(mixer_low, mixer_mats[:width]))
    early_stack, early_mat = collect(early_gate_up, early_down)
    second_normed, second_back = jax.vjp(rms_norm, stream_one, norm_gains[1])
    second_low = second_normed.astype(jnp.bfloat16)
    early_part, early_gate, early_up, early_hidden = ffn_forward(second_low, early_stack, early_mat)
    stream_two = stream_one + branch_total(early_part)
    focus_stack, focus_mat = collect(attention_in, attention_out)
    heads_here = focus_stack.shape[2] // HEAD_DIM
    third_normed, third_back = jax.vjp(rms_norm, stream_two, norm_gains[2])
    third_low = third_normed.astype(jnp.bfloat16)
    query = (
        project(third_low, focus_stack[0])
        .astype(jnp.bfloat16)
        .reshape(tokens, heads_here, HEAD_DIM)
    )
    keys = (
        project(third_low, focus_stack[1])
        .astype(jnp.bfloat16)
        .reshape(tokens, heads_here, HEAD_DIM)
    )
    values = (
        project(third_low, focus_stack[2])
        .astype(jnp.bfloat16)
        .reshape(tokens, heads_here, HEAD_DIM)
    )
    attended, log_total = attention_forward(query, keys, values, allowed)
    attended_low = attended.reshape(tokens, heads_here * HEAD_DIM).astype(jnp.bfloat16)
    stream_three = stream_two + branch_total(project_t(attended_low, focus_mat))
    late_stack, late_mat = collect(late_gate_up, late_down)
    fourth_normed, fourth_back = jax.vjp(rms_norm, stream_three, norm_gains[3])
    fourth_low = fourth_normed.astype(jnp.bfloat16)
    late_part, late_gate, late_up, late_hidden = ffn_forward(fourth_low, late_stack, late_mat)
    output = stream_three + branch_total(late_part)
    grad_three = output_grad.astype(jnp.float32)
    late_pair = (late_stack, late_mat)
    grad_fourth, late_joined, late_mat_grad = ffn_backward(
        output_grad, fourth_low, late_gate, late_up, late_hidden, late_pair[0], late_pair[1]
    )
    grad_stream, gain_four = fourth_back(input_total(grad_fourth))
    grad_three = grad_three + grad_stream
    late_grads = spread_grads(late_joined, late_mat_grad, 2)
    focus_pair = (focus_stack, focus_mat)
    grad_branch_low = grad_three.astype(jnp.bfloat16)
    focus_mat_grad = outer_rows(grad_branch_low, attended_low)
    grad_attended = (
        project(grad_branch_low, focus_pair[1])
        .astype(jnp.bfloat16)
        .reshape(tokens, heads_here, HEAD_DIM)
    )
    grad_query, grad_keys, grad_values = attention_backward(
        query, keys, values, allowed, log_total, grad_attended
    )
    query_low = flatten_low(grad_query, tokens)
    keys_low = flatten_low(grad_keys, tokens)
    values_low = flatten_low(grad_values, tokens)
    focus_joined = outer_rows(third_low, jnp.concatenate([query_low, keys_low, values_low], axis=1))
    grad_third = (
        project_t(query_low, focus_pair[0][0])
        + project_t(keys_low, focus_pair[0][1])
        + project_t(values_low, focus_pair[0][2])
    )
    grad_stream, gain_three = third_back(input_total(grad_third))
    grad_two = grad_three + grad_stream
    focus_grads = spread_grads(focus_joined, focus_mat_grad, 3)
    early_pair = (early_stack, early_mat)
    grad_second, early_joined, early_mat_grad = ffn_backward(
        grad_two.astype(jnp.bfloat16),
        second_low,
        early_gate,
        early_up,
        early_hidden,
        early_pair[0],
        early_pair[1],
    )
    grad_stream, gain_two = second_back(input_total(grad_second))
    grad_one = grad_two + grad_stream
    early_grads = spread_grads(early_joined, early_mat_grad, 2)
    mixer_pair = (mixer_stack, mixer_mats)
    grad_mixer_low = grad_one.astype(jnp.bfloat16)
    out_mat_grad = outer_rows(grad_mixer_low, mixer_low)
    grad_scanned = project(grad_mixer_low, mixer_pair[1][:width])
    (
        grad_channel,
        grad_step_low,
        gate_low,
        in_sums,
        out_sums,
        step_bias_grad,
        decay_log_grad,
        skip_gain_grad,
    ) = scan_backward(
        keeping, channel_low, step_raw, gate_half, grad_scanned, step_bias, rates_t, skip_gain, in_wide, out_wide,
        groups, LANES,
    )
    step_mat_grad = outer_rows(rank_low, grad_step_low)
    grad_rank = project_t(grad_step_low, mixer_pair[1][width + PROJ_OUT :])
    grad_rows = lax.psum(
        jnp.concatenate([grad_rank, jnp.sum(in_sums, axis=-1), jnp.sum(out_sums, axis=-1)], axis=1), "tensor"
    )
    grad_rows_low = grad_rows.astype(jnp.bfloat16)
    select_mat_grad = outer_rows(grad_rows_low, channel_low)
    grad_channel = grad_channel + project(grad_rows_low, mixer_pair[1][width : width + PROJ_OUT])
    grad_conv_in, conv_weight_grad, conv_bias_grad = conv_back(grad_channel)
    conv_low = grad_conv_in.astype(jnp.bfloat16)
    mixer_joined = outer_rows(first_low, jnp.concatenate([conv_low, gate_low], axis=1))
    grad_first = project_t(conv_low, mixer_pair[0][0]) + project_t(gate_low, mixer_pair[0][1])
    grad_stream, gain_one = first_back(input_total(grad_first))
    input_grad = grad_one + grad_stream
    mixer_grads = spread_grads(
        mixer_joined, jnp.concatenate([out_mat_grad, select_mat_grad, step_mat_grad], axis=0), 2
    )
    small_sums = lax.psum(
        (
            jnp.stack([gain_one, gain_two, gain_three, gain_four]),
            conv_weight_grad,
            conv_bias_grad,
            step_bias_grad[0],
            decay_log_grad.T,
            skip_gain_grad[0],
        ),
        "dp",
    )
    return (
        output,
        input_grad,
        small_sums[0],
        mixer_grads[0],
        mixer_grads[1],
        small_sums[1],
        small_sums[2],
        small_sums[3],
        small_sums[4],
        small_sums[5],
        early_grads[0],
        early_grads[1],
        focus_grads[0],
        focus_grads[1],
        late_grads[0],
        late_grads[1],
    )


MESH = pl.DeviceIdType.MESH


def turns(group):
    return [turned for turned in (6, 2, 4) if turned & group == turned]


class Place:
    def __init__(self, ways):
        self.spot = lax.axis_index("dp")
        self.depth = lax.axis_index("tensor")
        self.ways = ways
        self.core = lax.rem(self.spot, 2)
        self.partner = self.spot + 1 - 2 * self.core

    def bit(self, axis, turned):
        value = lax.rem(self.spot // axis, 2)
        return 1 - value if turned & axis else value

    def across(self, turned, swapped=False):
        move = 1 - 2 * self.core if swapped else 0
        for axis in (2, 4):
            if turned & axis:
                move = move + axis * (1 - 2 * self.bit(axis, 0))
        return self.spot + move

    def side(self, group, turned=0):
        if group == 6:
            return self.bit(2, turned) + 2 * self.bit(4, turned)
        return self.bit(group, turned) if group else 0

    def along(self, offset):
        return lax.rem(self.depth + offset, self.ways)


def send(source, target, sems, at, spot, depth):
    copy = pltpu.make_async_remote_copy(
        src_ref=source,
        dst_ref=target,
        send_sem=sems[0].at[at],
        recv_sem=sems[1].at[at],
        device_id=(spot, depth),
        device_id_type=MESH,
    )
    copy.start()
    return copy


def greet(place, ways, both=False):
    barrier = pltpu.get_barrier_semaphore()
    peers = [(place.partner, place.depth)]
    peers += [(place.across(turned), place.depth) for turned in ways]
    if both:
        peers += [(place.across(turned, True), place.depth) for turned in ways]
    peers += [(place.spot, place.along(offset)) for offset in range(1, place.ways)]
    for peer in peers:
        pl.semaphore_signal(barrier, inc=1, device_id=peer, device_id_type=MESH)
    pl.semaphore_wait(barrier, len(peers))


def rows_at(start, size, unit):
    return pl.ds(pl.multiple_of(start * unit, unit), size)


class Reduction:
    def __init__(self, place, group, rows, parts, part_ref, near_s, sum_s, far_s, sems, names):
        self.place, self.group, self.rows, self.parts = place, group, rows, parts
        self.part_ref, self.near_s, self.sum_s, self.far_s = part_ref, near_s, sum_s, far_s
        self.sems = [sems[name] for name in names]
        self.ways = turns(group) + [0]
        self.step = part_ref.shape[1] // parts
        self.near, self.far = {}, {}

    def lanes(self, part):
        return pl.ds(part * self.step, self.step)

    def block(self, side):
        return rows_at(side, self.rows, self.rows)

    def send_near(self):
        place = self.place
        for part in range(self.parts):
            for at, turned in enumerate(self.ways):
                side = place.side(self.group, turned)
                self.near[part, turned] = send(
                    self.part_ref.at[self.block(side * 2 + 1 - place.core), self.lanes(part)],
                    self.near_s.at[self.block(side), self.lanes(part)],
                    self.sems[0], part * len(self.ways) + at, place.partner, place.depth,
                )

    def joined(self, part, turned):
        self.near[part, turned].wait_recv()
        side, lanes = self.place.side(self.group, turned), self.lanes(part)
        own = self.part_ref[self.block(side * 2 + self.place.core), lanes].astype(jnp.float32)
        return own + self.near_s[self.block(side), lanes].astype(jnp.float32)

    def order(self):
        half = self.parts // 2
        return [at + first for at in range(half) for first in (0, half)]

    def leg(self, part):
        return (2, 4) if part < self.parts // 2 else (4, 2)

    def push(self, part, turned, slot, to, value):
        rows, lanes = self.block(self.place.side(self.group, turned)), self.lanes(part)
        self.sum_s[rows, lanes] = value.astype(self.sum_s.dtype)
        self.far[part, slot] = send(
            self.sum_s.at[rows, lanes], self.far_s.at[slot, :, lanes],
            self.sems[1], part * 3 + slot, self.place.across(to), self.place.depth,
        )

    def came(self, part, slot):
        self.far[part, slot].wait_recv()
        return self.far_s[slot, :, self.lanes(part)].astype(jnp.float32)

    def send_far(self):
        if self.group:
            for part in self.order():
                first, _ = self.leg(part)
                self.push(part, 6, 1, first, self.joined(part, 6))
                self.push(part, first, 0, first, self.joined(part, first))

    def relay(self):
        if self.group:
            for part in self.order():
                _, second = self.leg(part)
                value = self.joined(part, second) + self.came(part, 1)
                self.push(part, second, 2, second, value)

    def chip_sum(self, part):
        total = self.joined(part, 0)
        if self.group:
            total = total + self.came(part, 0) + self.came(part, 2)
        return total

    def sent(self):
        return list(self.near.values()) + list(self.far.values())


def deep_sends(place, share, source, start, deep_s, lanes, sems, at):
    return [
        send(
            source.at[pl.ds(pl.multiple_of(start + place.along(offset) * share, share), share), lanes],
            deep_s.at[offset - 1, :, lanes],
            sems, at + offset - 1, place.spot, place.along(offset),
        )
        for offset in range(1, place.ways)
    ]


def deep_total(place, share, source, start, deep_s, copies):
    for copy in copies:
        copy.wait_recv()
    total = source[pl.ds(pl.multiple_of(start + place.depth * share, share), share), :].astype(jnp.float32)
    for offset in range(1, place.ways):
        total = total + deep_s[offset - 1].astype(jnp.float32)
    return total


def reduce_stage(first, deep_s, sems, between):
    place, rows = first.place, first.rows
    share = rows // place.ways
    first.send_near()
    between(0)
    first.send_far()
    first.relay()
    between(1)
    deep = []
    mine = place.side(first.group)
    for part in first.order() if first.group else range(first.parts):
        first.sum_s[first.block(mine), first.lanes(part)] = first.chip_sum(part).astype(first.sum_s.dtype)
        deep += deep_sends(
            place, share, first.sum_s, mine * rows, deep_s, first.lanes(part), sems["deep"], part * (place.ways - 1)
        )
    return deep_total(place, share, first.sum_s, mine * rows, deep_s, deep), first.sent() + deep


def hand_on(place, group, rows_of, target, sems, base, far):
    half = target.shape[1] // 2
    for came, to, lanes in ((2, 4, pl.ds(0, half)), (4, 2, pl.ds(half, half))):
        far[came].wait_recv()
        block = target.at[rows_of(came), lanes]
        far[came, to] = send(block, block, sems, base + to // 2 + 1, place.across(to), place.depth)


def first_leg(place, block, sems, base):
    return {turned: send(block, block, sems, base + turned // 2 - 1, place.across(turned), place.depth) for turned in (2, 4)}


def gather_stage(place, group, rows, all_ref, sems, between):
    share = rows // place.ways

    def place_of(turned, offset):
        depth = place.along(place.ways - offset) if offset else place.depth
        return pl.ds(pl.multiple_of((place.side(group, turned) * 2 + place.core) * rows + depth * share, share), share)

    def to_partner(turned, offset, at):
        block = all_ref.at[place_of(turned, offset), :]
        return send(block, block, sems["near_back"], at * place.ways + offset, place.partner, place.depth)

    own = all_ref.at[place_of(0, 0), :]
    deep = [
        send(own, own, sems["deep_back"], offset - 1, place.spot, place.along(offset)) for offset in range(1, place.ways)
    ]
    far, near = [], []
    for offset in range(place.ways):
        if offset:
            deep[offset - 1].wait_recv()
        if group:
            far.append(first_leg(place, all_ref.at[place_of(0, offset), :], sems["far_back"], 4 * offset))
        near.append(to_partner(0, offset, 0))
        if offset == 0:
            between()
    if group:
        for offset in range(place.ways):
            hand_on(
                place, group, lambda turned: place_of(turned, offset), all_ref, sems["far_back"], 4 * offset, far[offset]
            )
            near.append(to_partner(2, offset, 1))
            near.append(to_partner(4, offset, 2))
        for offset in range(place.ways):
            far[offset][2, 4].wait_recv()
            far[offset][4, 2].wait_recv()
            near.append(to_partner(6, offset, 3))
    for copy in near:
        copy.wait_recv()
    return deep + [copy for one in far for copy in one.values()] + near


class Exchange:
    def __init__(self, place, items, sems):
        self.place, self.items, self.sems = place, items, sems
        self.copies, self.own = [], []

    def start(self):
        place = self.place
        spots = [place.across(turned, swapped) for turned in (6, 2, 4) for swapped in (False, True)] + [place.partner]
        for at, (source, target) in enumerate(self.items):
            for slot, spot in enumerate(spots):
                self.copies.append(
                    send(source(spot), target(place.spot), self.sems, at * 8 + slot, spot, place.depth)
                )
            own = pltpu.make_async_copy(source(place.spot), target(place.spot), self.sems[1].at[at * 8 + 7])
            own.start()
            self.own.append(own)

    def close(self):
        for copy in self.own + self.copies:
            copy.wait()


def columns_at(half, size):
    return pl.ds(pl.multiple_of(half * size, size), size)


def blocks_of(refs, size):
    return [(ref, at) for ref in refs for at in range(ref.shape[2] // size)]


def spread_items(size, refs, out):
    return [
        (
            lambda spot, ref=ref, at=at: ref.at[spot, :, pl.ds(at * size, size)],
            lambda spot, to=to: out.at[to, :, columns_at(spot, size)],
        )
        for to, (ref, at) in enumerate(blocks_of(refs, size))
    ]


def chip_items(size, refs, out):
    return [
        (
            lambda spot, ref=ref, at=at: ref.at[spot, :, pl.ds(at * size, size)],
            lambda spot, to=to: out.at[spot // 2, to, :, columns_at(spot % 2, size)],
        )
        for to, (ref, at) in enumerate(blocks_of(refs, size))
    ]


def layers(refs):
    return [ref.at[at] if len(ref.shape) == 3 else ref for ref in refs for at in range(ref.shape[0] if len(ref.shape) == 3 else 1)]


def plane_items(spots, refs, out):
    blocks = layers(refs)
    size = blocks[0].shape[1] // spots
    return [
        (
            lambda spot, block=block: block.at[:, columns_at(spot, size)],
            lambda spot, at=at: out.at[spot, :, pl.ds(at * size, size)],
        )
        for at, block in enumerate(blocks)
    ]


def core_items(refs, out):
    blocks = layers(refs)
    size = blocks[0].shape[1] // 2
    return [
        (
            lambda half, block=block: block.at[:, columns_at(half, size)],
            lambda spot, at=at: out.at[spot, :, pl.ds(at * size, size)],
        )
        for at, block in enumerate(blocks)
    ]


def handed_items(out):
    return [(None, lambda spot: out.at[spot])]


class Load:
    def __init__(self, mode, arrays, out, items, count, stage):
        self.mode, self.arrays, self.items, self.count, self.stage = mode, arrays, items, count, stage
        self.out = jax.ShapeDtypeStruct(out, arrays[0].dtype)

    def begin(self, place, refs, out, sems):
        if self.mode == "second":
            mover = Pull(place, self.items(out), sems)
            mover.second(False)
        elif self.mode == "first":
            mover = Pull(place, self.items(refs, out), sems)
            mover.first()
        else:
            mover = Exchange(place, self.items(refs, out), sems)
            mover.start()
        return mover


def spread_stage(place, rows, all_ref, sems, name="deep_back"):
    share = rows // place.ways
    own = all_ref.at[pl.ds(pl.multiple_of(place.depth * share, share), share), :]
    deep = [
        send(own, own, sems[name], offset - 1, place.spot, place.along(offset)) for offset in range(1, place.ways)
    ]
    return deep


def small_stage(place, half, sum_ref, small_s, sems):
    near = [
        send(
            sum_ref.at[pl.ds(part * half, half), :], small_s.at[part], sems["small"], part, place.partner, place.depth
        )
        for part in range(2)
    ]
    for copy in near:
        copy.wait()
    mine = pl.ds(pl.multiple_of(place.core * half, half), half)
    small_s[2] = sum_ref[mine, :] + small_s[place.core]
    chips = [
        send(small_s.at[2], small_s.at[3 + at], sems["small"], 2 + at, spot, place.depth)
        for at, spot in enumerate((place.across(2), place.across(4), place.across(6)))
    ]
    for copy in chips:
        copy.wait_recv()
    total = small_s[2] + small_s[3] + small_s[4] + small_s[5]
    small_s[6] = total
    deep = [
        send(
            small_s.at[6, pl.ds(half - 8, 8), :], small_s.at[6 + offset, pl.ds(half - 8, 8), :],
            sems["small"], 4 + offset, place.spot, place.along(offset),
        )
        for offset in range(1, place.ways)
    ]
    for copy in deep:
        copy.wait_recv()
    gains = small_s[6, half - 8 : half, :]
    for offset in range(1, place.ways):
        gains = gains + small_s[6 + offset, half - 8 : half, :]
    last = jnp.where(place.core == 1, gains, total[half - 8 : half, :])
    ready, came = 6 + place.ways, 7 + place.ways
    small_s[ready] = jnp.concatenate([total[: half - 8, :], last], axis=0)
    back = send(small_s.at[ready], small_s.at[came], sems["small"], 4 + place.ways, place.partner, place.depth)
    sum_ref[mine, :] = small_s[ready]
    back.wait_recv()
    sum_ref[pl.ds(pl.multiple_of((1 - place.core) * half, half), half), :] = small_s[came]
    return chips + deep + [back]


def sem_shapes(names):
    shapes = []
    for count in names.values():
        shapes += [pltpu.SemaphoreType.DMA((count,))] * 2
    return shapes


def sem_dict(names, refs):
    return {name: (refs[2 * at], refs[2 * at + 1]) for at, name in enumerate(names)}


def edge_kernel(kind, extra, loads, ways, rows, parts, in_group, out_group, names, counts, *refs):
    place = Place(ways)
    share = rows // ways
    ins, outs = list(refs[: counts[0]]), list(refs[counts[0] : counts[0] + counts[1]])
    scratch = list(refs[counts[0] + counts[1] : counts[0] + counts[1] + counts[2]])
    sems = sem_dict(names, refs[sum(counts) :])
    part_ref = ins.pop(0)
    near_s, sum_s, far_s, deep_s = [scratch.pop(0) for _ in range(4)]
    if kind == "forward":
        stream_ref, gain_ref = ins.pop(0), ins.pop(0)
    elif kind != "sum":
        stream_ref, gain_ref, grad_ref = ins.pop(0), ins.pop(0), ins.pop(0)
    all_ref = outs.pop(0)
    if kind != "sum" and kind != "last":
        fresh_ref = outs.pop(0)
    if kind == "backward":
        dgain_ref = outs.pop(0)
    if kind == "last":
        small_ref, late_ref, three_ref = ins.pop(0), ins.pop(0), ins.pop(0)
        dgain_ref, late_out_ref = outs.pop(0), outs.pop(0)
        low_s, small_s, late_s, late_low_s = [scratch.pop(0) for _ in range(4)]
    moving = []
    for load in reversed(loads):
        moving.append(([ins.pop() for _ in load.arrays][::-1], outs.pop()))
    moving = moving[::-1]
    everyone = loads or kind == "last"
    greet(place, turns(6) if everyone else sorted({*turns(in_group), *turns(out_group)}), bool(loads))
    first = Reduction(place, in_group, rows, parts, part_ref, near_s, sum_s, far_s, sems, ("near", "far"))
    waiting = []
    freight = {}
    if extra == "gather":
        load_ref, load_out_ref = ins.pop(0), outs.pop(0)

        def load_rows(turned):
            return rows_at(place.side(in_group, turned) * 2 + place.core, rows, rows)

        def between(stage):
            spot = rows_at(place.side(in_group) * 2 + place.core, rows, rows)
            if stage == 0:
                load_out_ref[spot, :] = load_ref[...]
                return
            own = load_out_ref.at[spot, :]
            if stage == 1:
                freight.update(first_leg(place, own, sems["load_far"], 0))
                freight[0] = send(own, own, sems["load_near"], 0, place.partner, place.depth)
            else:
                hand_on(place, in_group, load_rows, load_out_ref, sems["load_far"], 0, freight)

    elif extra == "reduce":
        second = Reduction(
            place, in_group, rows, parts, ins.pop(0), *[scratch.pop(0) for _ in range(3)], sems, ("load_near", "load_far")
        )
        load_out_ref = outs.pop(0)

        def between(stage):
            (second.send_near, second.send_far, second.relay)[stage]()

    else:

        def between(stage):
            pass

    carried = []

    def on_the_way(stage):
        between(stage)
        for at, load in enumerate(loads):
            if load.stage == stage:
                carried.append(load.begin(place, *moving[at], sems[f"load{at}"]))

    if kind == "last":
        late = deep_sends(place, share, late_ref, 0, late_s, slice(None), sems["late"], 0)
        waiting += late
    total, copies = reduce_stage(first, deep_s, sems, on_the_way)
    waiting += copies
    if kind == "forward":
        fresh = stream_ref[...] + total
        fresh_ref[...] = fresh
        scale = lax.rsqrt(jnp.mean(fresh * fresh, axis=-1, keepdims=True) + EPS)
        value = fresh * scale * gain_ref[...]
    elif kind == "sum":
        value = total
    else:
        stream = stream_ref[...]
        scale = lax.rsqrt(jnp.mean(stream * stream, axis=-1, keepdims=True) + EPS)
        leaned = total * gain_ref[...]
        inner = jnp.mean(leaned * stream, axis=-1, keepdims=True)
        value = grad_ref[...] + scale * leaned - stream * (scale * scale * scale * inner)
        dgain = jnp.sum(total * stream * scale, axis=0, keepdims=True)
        if kind == "backward":
            dgain_ref[...] = dgain
            fresh_ref[...] = value
    if kind == "last":
        own = pl.ds(pl.multiple_of(place.depth * share, share), share)
        low_s[own, :] = value.astype(low_s.dtype)
        spread = spread_stage(place, rows, low_s, sems)
        late_total = three_ref[...] + deep_total(place, share, late_ref, 0, late_s, late)
        late_low_s[own, :] = late_total.astype(late_low_s.dtype)
        spread += spread_stage(place, rows, late_low_s, sems, "late_back")
        half, span = small_ref.shape[0] // 2, small_ref.shape[1]
        dgain_ref[...] = small_ref[...]
        for at in range(dgain.shape[1] // span):
            dgain_ref[pl.ds(2 * half - 8 + at, 1), :] = dgain[:, at * span : (at + 1) * span]
        waiting += spread + small_stage(place, half, dgain_ref, small_s, sems)
        for copy in spread:
            copy.wait_recv()
        all_ref[...] = low_s[...].astype(jnp.float32)
        late_out_ref[...] = late_low_s[...].astype(jnp.float32)
    else:
        spot = pl.multiple_of((place.side(out_group) * 2 + place.core) * rows + place.depth * share, share)
        all_ref[pl.ds(spot, share), :] = value.astype(all_ref.dtype)
        waiting += gather_stage(place, out_group, rows, all_ref, sems, partial(on_the_way, 2))
    if extra == "gather":
        last = []
        for at, turned in enumerate((2, 4, 6)):
            for key in ((2, 4), (4, 2)) if turned == 6 else ():
                freight[key].wait_recv()
            came = load_out_ref.at[load_rows(turned), :]
            last.append(send(came, came, sems["load_near"], 1 + at, place.partner, place.depth))
        for copy in last + [freight[0]]:
            copy.wait_recv()
        waiting += list(freight.values()) + last
    elif extra == "reduce":
        for part in range(parts):
            load_out_ref[:, second.lanes(part)] = second.chip_sum(part).astype(load_out_ref.dtype)
        waiting += second.sent()
    for mover in carried:
        mover.close()
    for copy in waiting:
        copy.wait_send()


def edge(kind, part, extras, ways, rows, parts, in_group, out_group, ident, name, extra=None, loads=()):
    width = part.shape[1]
    share = rows // ways
    in_far, out_far = len(turns(in_group)), len(turns(out_group or 0))
    in_sides, out_sides = in_far + 1, out_far + 1
    dtype = part.dtype
    line = jax.ShapeDtypeStruct((1, width), jnp.float32)
    strip = jax.ShapeDtypeStruct((share, width), jnp.float32)
    whole = jax.ShapeDtypeStruct((out_sides * 2 * rows, width), dtype)
    block = jax.ShapeDtypeStruct((rows, width), jnp.float32)
    outs = {
        "forward": [whole, strip],
        "backward": [whole, strip, line],
        "last": [block] + [jax.ShapeDtypeStruct(one.shape, one.dtype) for one in extras[3:4]] + [block],
        "sum": [whole],
    }[kind]
    names = {"near": parts * in_sides, "far": 3 * parts if in_far else 0, "deep": parts * (ways - 1), "deep_back": ways - 1}
    reducing = [
        pltpu.VMEM((in_sides * rows, width), dtype),
        pltpu.VMEM((in_sides * rows, width), dtype),
        pltpu.VMEM((max(in_far, 1), rows if in_far else 16, width), dtype),
    ]
    deep = pltpu.VMEM((ways - 1, share, width), dtype)
    scratch = reducing + [deep]
    if kind == "last":
        names.update({"small": 5 + ways, "late": ways - 1, "late_back": ways - 1})
        small = pltpu.VMEM((8 + ways, extras[3].shape[0] // 2, extras[3].shape[1]), jnp.float32)
        spread = pltpu.VMEM((rows, width), dtype)
        scratch += [spread, small, deep, spread]
    else:
        names.update({"far_back": 4 * ways if out_far else 0, "near_back": ways * out_sides})
    if extra == "gather":
        names.update({"load_far": 4, "load_near": in_sides})
        outs = outs + [jax.ShapeDtypeStruct((in_sides * 2 * rows, width), dtype)]
    elif extra == "reduce":
        names.update({"load_far": 3 * parts, "load_near": parts * in_sides})
        outs = outs + [jax.ShapeDtypeStruct((rows, width), dtype)]
        scratch = scratch + reducing
    vmem, whole_memory = pl.BlockSpec(memory_space=pltpu.VMEM), pl.BlockSpec(memory_space=pl.ANY)
    in_specs, out_specs = [vmem] * (1 + len(extras)), [vmem] * len(outs)
    aliases, extras, outs = {}, list(extras), list(outs)
    for at, load in enumerate(loads):
        names[f"load{at}"] = 8 * load.count
        if load.mode == "second":
            aliases[1 + len(extras)] = len(outs)
        extras += load.arrays
        outs.append(load.out)
        in_specs += [whole_memory] * len(load.arrays)
        out_specs.append(whole_memory)
    names = {key: count for key, count in names.items() if count}
    if not in_far:
        names["far"] = 1
    return pl.pallas_call(
        partial(
            edge_kernel, kind, extra, loads, ways, rows, parts, in_group, out_group, names,
            (1 + len(extras), len(outs), len(scratch)),
        ),
        in_specs=in_specs,
        out_specs=out_specs,
        out_shape=outs,
        scratch_shapes=scratch + sem_shapes(names),
        input_output_aliases=aliases,
        compiler_params=pltpu.CompilerParams(
            collective_id=ident, has_side_effects=True, vmem_limit_bytes=48 << 20
        ),
        cost_estimate=pl.CostEstimate(flops=1, bytes_accessed=1, transcendentals=0),
        name=name,
    )(part, *extras)


class Pull:
    def __init__(self, place, items, sems):
        self.place, self.items, self.sems = place, items, sems
        self.copies, self.handed = {}, set()

    def go(self, at, key, slot, source, spot, target):
        self.copies[at, key] = send(source, target, self.sems, at * 8 + slot, spot, self.place.depth)

    def first(self):
        place = self.place
        for at, (source, target) in enumerate(self.items):
            mine = target(place.spot)
            for turned in (2, 4):
                self.go(at, (turned, False), turned - 2, source(place.core), place.across(turned), mine)
                self.go(at, (turned, True), turned - 1, source(1 - place.core), place.across(turned, True), mine)
            self.go(at, "near", 4, source(1 - place.core), place.partner, mine)
            own = pltpu.make_async_copy(source(place.core), mine, self.sems[1].at[at * 8 + 7])
            own.start()
            self.copies[at, "own"] = own

    def second(self, fresh=True):
        place = self.place
        for at, (_, target) in enumerate(self.items):
            for slot, turned, swapped, to in ((5, 2, False, 4), (6, 4, True, 2)):
                if fresh:
                    self.copies[at, (turned, swapped)].wait_recv()
                    self.handed.add((at, (turned, swapped)))
                block = target(place.across(turned, swapped))
                self.go(at, ("on", turned), slot, block, place.across(to), block)

    def close(self):
        for (at, key), copy in self.copies.items():
            if key == "own":
                copy.wait()
            else:
                if (at, key) not in self.handed:
                    copy.wait_recv()
                copy.wait_send()


def opening_kernel(ways, rows, hidden_ref, gain_ref, in_ref, rows_ref, first_ref, in_out, rows_out, *sems):
    place = Place(ways)
    greet_plane(place)
    size = rows_out.shape[2]
    items = [
        (
            lambda half, at=at: in_ref.at[at, :, columns_at(half, size)],
            lambda spot, at=at: in_out.at[spot, :, pl.ds(at * size, size)],
        )
        for at in range(in_ref.shape[0])
    ]
    items.append((lambda half: rows_ref.at[:, columns_at(half, size)], lambda spot: rows_out.at[spot]))
    pull = Pull(place, items, sems[2:])
    pull.first()
    stream = hidden_ref[...].astype(jnp.float32)
    scale = lax.rsqrt(jnp.mean(stream * stream, axis=-1, keepdims=True) + EPS)
    first_ref[rows_at(place.core, rows, rows), :] = (stream * scale * gain_ref[...]).astype(jnp.bfloat16)
    mine = first_ref.at[rows_at(place.core, rows, rows), :]
    copy = send(mine, mine, sems[:2], 0, place.partner, place.depth)
    pull.second()
    copy.wait()
    pull.close()


def greet_plane(place):
    barrier = pltpu.get_barrier_semaphore()
    peers = [place.partner] + [place.across(turned, swapped) for turned in (2, 4) for swapped in (False, True)]
    for peer in peers:
        pl.semaphore_signal(barrier, inc=1, device_id=(peer, place.depth), device_id_type=MESH)
    pl.semaphore_wait(barrier, len(peers))


def opening(hidden, gain, in_weights, row_weights, spots, ways, ident):
    rows, width = hidden.shape
    vmem, whole_memory = pl.BlockSpec(memory_space=pltpu.VMEM), pl.BlockSpec(memory_space=pl.ANY)
    kinds, depth, columns = in_weights.shape
    low = jnp.bfloat16
    return pl.pallas_call(
        partial(opening_kernel, ways, rows),
        in_specs=[vmem] * 2 + [whole_memory] * 2,
        out_specs=[vmem] + [whole_memory] * 2,
        out_shape=[
            jax.ShapeDtypeStruct((2 * rows, width), low),
            jax.ShapeDtypeStruct((spots, depth, kinds * columns // 2), low),
            jax.ShapeDtypeStruct((spots, row_weights.shape[0], columns // 2), low),
        ],
        scratch_shapes=[pltpu.SemaphoreType.DMA((1,))] * 2 + [pltpu.SemaphoreType.DMA((8 * (kinds + 1),))] * 2,
        compiler_params=pltpu.CompilerParams(
            collective_id=ident, has_side_effects=True, vmem_limit_bytes=40 << 20
        ),
        cost_estimate=pl.CostEstimate(flops=1, bytes_accessed=1, transcendentals=0),
        name="opening",
    )(hidden, gain, in_weights, row_weights)


def probs_of(query, keys, allowed):
    scores = project_t(query, keys) * (1.0 / math.sqrt(HEAD_DIM))
    scores = jnp.where(allowed, scores, NEG_FILL)
    shifted = jnp.exp(scores - jnp.max(scores, axis=-1, keepdims=True))
    return shifted / jnp.sum(shifted, axis=-1, keepdims=True)


def allowed_in(down_ref, side_ref, rows, group):
    shape = (rows, rows)
    distance = lax.broadcasted_iota(jnp.int32, shape, 0) - lax.broadcasted_iota(jnp.int32, shape, 1)
    same = down_ref[group * rows : (group + 1) * rows, :] == side_ref[group : group + 1, :]
    return same & (distance >= 0) & (distance < WINDOW)


def attend_kernel(heads, rows, joint_ref, down_ref, side_ref, low_ref, out_ref):
    low_ref[...] = joint_ref[...].astype(jnp.bfloat16)
    size = heads * HEAD_DIM
    for group in range(joint_ref.shape[0] // rows):
        allowed = allowed_in(down_ref, side_ref, rows, group)
        span = slice(group * rows, (group + 1) * rows)
        for head in range(heads):
            at = slice(head * HEAD_DIM, (head + 1) * HEAD_DIM)
            query, keys, values = [
                low_ref[span, part * size + head * HEAD_DIM : part * size + (head + 1) * HEAD_DIM] for part in range(3)
            ]
            probs = probs_of(query, keys, allowed)
            out_ref[span, at] = project(probs.astype(jnp.bfloat16), values).astype(jnp.bfloat16)


def attend(joint, down, side, rows):
    count, size = joint.shape
    return pl.pallas_call(
        partial(attend_kernel, size // (3 * HEAD_DIM), rows),
        out_shape=[
            jax.ShapeDtypeStruct((count, size), jnp.bfloat16),
            jax.ShapeDtypeStruct((count, size // 3), jnp.bfloat16),
        ],
        compiler_params=pltpu.CompilerParams(vmem_limit_bytes=32 << 20),
        name="attend",
    )(joint, down, side)


def attend_back_kernel(heads, rows, low_ref, grad_ref, down_ref, side_ref, out_ref):
    size = heads * HEAD_DIM
    scale = 1.0 / math.sqrt(HEAD_DIM)
    for group in range(low_ref.shape[0] // rows):
        allowed = allowed_in(down_ref, side_ref, rows, group)
        span = slice(group * rows, (group + 1) * rows)
        for head in range(heads):
            places = [slice(part * size + head * HEAD_DIM, part * size + (head + 1) * HEAD_DIM) for part in range(3)]
            query, keys, values = [low_ref[span, place] for place in places]
            grad = grad_ref[span, head * HEAD_DIM : (head + 1) * HEAD_DIM].astype(jnp.bfloat16)
            probs = probs_of(query, keys, allowed)
            grad_probs = project_t(grad, values)
            inner = jnp.sum(probs * grad_probs, axis=-1, keepdims=True)
            grad_scores = (probs * (grad_probs - inner)).astype(jnp.bfloat16)
            out_ref[span, places[0]] = (project(grad_scores, keys) * scale).astype(jnp.bfloat16)
            out_ref[span, places[1]] = (outer_rows(grad_scores, query) * scale).astype(jnp.bfloat16)
            out_ref[span, places[2]] = outer_rows(probs.astype(jnp.bfloat16), grad).astype(jnp.bfloat16)


def attend_back(low, grad, down, side, rows):
    count, size = low.shape
    return pl.pallas_call(
        partial(attend_back_kernel, size // (3 * HEAD_DIM), rows),
        out_shape=jax.ShapeDtypeStruct((count, size), jnp.bfloat16),
        compiler_params=pltpu.CompilerParams(vmem_limit_bytes=32 << 20),
        name="attend_back",
    )(low, grad, down, side)


def sub_of(spot, group):
    if group == 6:
        return spot
    return spot % 2 + (2 * ((spot // group) % 2) if group else 0)


def subs_of(group):
    return 2 * (len(turns(group)) + 1)


def pull(count, *sets):
    def cut(block, group, spot):
        size = block.shape[1] // subs_of(group)
        return block[:, sub_of(spot, group) * size : (sub_of(spot, group) + 1) * size]

    return jnp.stack(
        [
            jnp.concatenate([cut(block, group, spot) for blocks, group in sets for block in blocks], axis=1)
            for spot in range(count)
        ]
    )


def in_order(value):
    return with_layout_constraint(value, Layout(major_to_minor=tuple(range(value.ndim))))


def swap(stacked):
    return lax.all_to_all(stacked, "dp", 0, 0, tiled=True)


def spread_out_kernel(came_ref, pair_ref, last_ref):
    size = last_ref.shape[1]
    for at in range(2):
        pair_ref[at] = came_ref[0, :, at * size : (at + 1) * size].astype(jnp.float32)
    last_ref[...] = came_ref[0, :, 2 * size :].astype(jnp.float32)


def spread_out(came):
    spots, rows, columns = came.shape
    size = columns // 3
    return pl.pallas_call(
        spread_out_kernel,
        grid=(spots,),
        in_specs=[pl.BlockSpec((1, rows, columns), lambda i: (i, 0, 0))],
        out_specs=[
            pl.BlockSpec((2, rows, size), lambda i: (0, 0, i)),
            pl.BlockSpec((rows, size), lambda i: (0, i)),
        ],
        out_shape=[
            jax.ShapeDtypeStruct((2, rows, spots * size), jnp.float32),
            jax.ShapeDtypeStruct((rows, spots * size), jnp.float32),
        ],
        name="spread_out",
    )(came)


def chip_total(came):
    return jnp.sum(came.astype(jnp.float32), axis=0)


def after(value, *others):
    return lax.optimization_barrier((value,) + others)[0]


def grouped_body(
    counts,
    early_group,
    focus_group,
    late_group,
    hidden_in,
    seq_lengths,
    norm_gains,
    mixer_in,
    mixer_rows,
    conv_weight,
    conv_bias,
    step_bias,
    decay_log,
    skip_gain,
    early_gate_up,
    early_down,
    attention_in,
    attention_out,
    late_gate_up,
    late_down,
    output_grad,
):
    spots, ways = counts
    rows, width = hidden_in.shape
    share = rows // ways
    spot = lax.axis_index("dp")
    depth = lax.axis_index("tensor")
    core = spot % 2
    low = jnp.bfloat16

    def swapped_core(value):
        return lax.ppermute(value, "dp", [(at, at ^ 1) for at in range(spots)])

    own_rows = mixer_rows.shape[0]
    padded_rows = jnp.pad(mixer_rows, ((0, -own_rows % 16), (0, 0)))
    first_low, in_weights, row_weights = opening(
        hidden_in, norm_gains[0:1], mixer_in, padded_rows, spots, ways, 20
    )
    row_weights = row_weights[:, :own_rows]

    other_lengths = swapped_core(seq_lengths)
    lengths = jnp.where(
        core == 0, jnp.stack([seq_lengths, other_lengths]), jnp.stack([other_lengths, seq_lengths])
    )
    segs, starts = jax.vmap(lambda own: segment_info(own, rows))(lengths)
    flat_segs = (segs + jnp.arange(2, dtype=jnp.int32)[:, None] * rows).reshape(-1)
    keeping = 1.0 - starts.reshape(-1).astype(jnp.float32)
    groups = 2 * seq_lengths.shape[0]

    stream_zero = lax.dynamic_slice_in_dim(hidden_in, depth * share, share, 0).astype(jnp.float32)

    channels = conv_weight.shape[0] // 2

    def half(values):
        return lax.dynamic_slice_in_dim(values, core * channels, channels, 0)

    taps, offset, bias, decay, skip = [half(v) for v in (conv_weight, conv_bias, step_bias, decay_log, skip_gain)]
    in_mat = in_weights.reshape(width, 2 * channels)
    both = project(first_low, in_mat)
    conv_in, gate_half = both[:, :channels], both[:, channels:]
    channel_full, conv_back = jax.vjp(partial(causal_conv, flat_segs), conv_in, taps, offset)
    channel_low = channel_full.astype(low)
    row_mat = row_weights.reshape(-1, channels)
    early_blocks = [early_gate_up[0], early_gate_up[1], early_down]
    early_weights = swap(after(pull(spots, (early_blocks, early_group)), first_low))
    out_mat = row_mat[:width]
    select_mat = row_mat[width : width + PROJ_OUT]
    step_mat = row_mat[width + PROJ_OUT :]

    def spread_load(joints, size, stage):
        count = sum(one.shape[2] // size for one in joints)
        return Load(
            "exchange", joints, (count, joints[0].shape[1], spots * size), partial(spread_items, size), count, stage
        )

    def chip_load(joints, size, stage):
        count = sum(one.shape[2] // size for one in joints)
        out = (spots // 2, count, joints[0].shape[1], 2 * size)
        return Load("exchange", joints, out, partial(chip_items, size), count, stage)

    def by_spot(joint):
        return joint.astype(low).reshape(spots, -1, joint.shape[1])

    def mixed_sum(part, ident, name, loads=()):
        padded = jnp.pad(part, ((0, 0), (0, 256 - PROJ_OUT)))
        total, *came = edge("sum", padded, [], ways, rows, 1, 0, 0, ident, name, loads=loads)
        return total[:, :PROJ_OUT], *came

    mix_rows, = mixed_sum(project_t(channel_low, select_mat), 1, "mix_sum")
    rank_low = mix_rows[:, :DT_RANK].astype(low)
    step_raw = project(rank_low, step_mat)
    rates_t = -jnp.exp(decay).T
    wide = (2 * rows, STATE, LANES)
    in_wide = jnp.broadcast_to(mix_rows[:, DT_RANK : DT_RANK + STATE, None], wide)
    out_wide = jnp.broadcast_to(mix_rows[:, DT_RANK + STATE :, None], wide)
    mixer_low = scan_forward(
        keeping, channel_low, step_raw, gate_half, bias, rates_t, skip, in_wide, out_wide, groups, LANES
    )
    early_mat = early_weights.reshape(width, -1)
    focus_blocks = [attention_in, attention_out]
    heads_width = attention_out.shape[1] // 2
    focus_pull = Load("first", focus_blocks, (spots, width // spots, 4 * heads_width), core_items, 4, 0)
    second_low, stream_one, focus_half = edge(
        "forward", project_t(mixer_low, out_mat).astype(low), [stream_zero, norm_gains[1:2]],
        ways, rows, 4, 0, early_group, 2, "edge_one", loads=[focus_pull],
    )

    def ffn(normed, mat):
        units = mat.shape[1] // 3
        both = project(normed, mat[:, : 2 * units])
        hidden = gated_unit(both[:, :units], both[:, units:]).astype(low)
        return project_t(hidden, mat[:, 2 * units :]).astype(low), both, hidden

    early_part, early_both, early_hidden = ffn(second_low, early_mat)
    third_low, stream_two, last_grad, focus_weights = edge(
        "forward", early_part, [stream_one, norm_gains[2:3], output_grad], ways, rows, 4, early_group, 0, 3, "edge_two",
        "gather", [Load("second", [focus_half], focus_half.shape, handed_items, 1, 1)],
    )
    focus_mat = focus_weights.reshape(width, -1)

    late_pull = Load(
        "exchange", [late_gate_up, late_down], (spots, width // spots, 3 * late_down.shape[1] // spots),
        partial(plane_items, spots), 3, 0,
    )
    down, side = flat_segs[:, None], flat_segs.reshape(2, rows)
    joint_low, attended_low = attend(project(third_low, focus_mat[:, : 3 * heads_width]), down, side, rows)
    fourth_low, stream_three, late_weights = edge(
        "forward", project_t(attended_low, focus_mat[:, 3 * heads_width :]).astype(low),
        [stream_two, norm_gains[3:4]], ways, rows, 4, 0, late_group, 4, "edge_three", loads=[late_pull],
    )

    late_mat = late_weights.reshape(width, -1)
    late_part, late_both, late_hidden = ffn(fourth_low, late_mat)

    def ffn_back(grad_low, normed, both, hidden, mat):
        units = mat.shape[1] // 3
        grad_hidden = project(grad_low, mat[:, 2 * units :])
        _, unit_back = jax.vjp(gated_unit, both[:, :units], both[:, units:])
        both_low = jnp.concatenate(unit_back(grad_hidden), axis=1).astype(low)
        grad_normed = project_t(both_low, mat[:, : 2 * units]).astype(low)
        return grad_normed, [by_spot(outer_rows(normed, both_low)), by_spot(outer_rows(grad_low, hidden))]

    grad_fourth, late_joints = ffn_back(last_grad, fourth_low, late_both, late_hidden, late_mat)
    grad_zero = lax.dynamic_slice_in_dim(output_grad, depth * share, share, 0).astype(jnp.float32)
    grad_low_three, grad_three, gain_four, output_part = edge(
        "backward", grad_fourth, [stream_three, norm_gains[3:4], grad_zero, late_part],
        ways, rows, 4, late_group, 0, 5, "edge_four", "reduce",
    )

    grad_attended = project(grad_low_three, focus_mat[:, 3 * heads_width :])
    joint_grad = attend_back(joint_low, grad_attended, down, side, rows)
    grad_low_two, grad_two, gain_three, late_swapped = edge(
        "backward", project_t(joint_grad, focus_mat[:, : 3 * heads_width]).astype(low),
        [stream_two, norm_gains[2:3], grad_three], ways, rows, 4, 0, early_group, 6, "edge_five",
        loads=[spread_load(late_joints, late_joints[1].shape[2], 0)],
    )
    focus_joints = [by_spot(outer_rows(third_low, joint_grad)), by_spot(outer_rows(grad_low_three, attended_low))]

    grad_second, early_joints = ffn_back(grad_low_two, second_low, early_both, early_hidden, early_mat)
    grad_low_one, grad_one, gain_two, focus_swapped = edge(
        "backward", grad_second, [stream_one, norm_gains[1:2], grad_two],
        ways, rows, 4, early_group, 0, 7, "edge_six",
        loads=[chip_load(focus_joints, heads_width, 1)],
    )
    early_joints = [in_order(one) for one in early_joints]
    early_swapped = swap(after(in_order(jnp.concatenate(early_joints, axis=2)), grad_low_one))

    grad_scanned = project(grad_low_one, out_mat)
    (
        grad_channel,
        grad_step_low,
        gate_low,
        in_sums,
        out_sums,
        bias_grad,
        decay_grad,
        skip_grad,
    ) = scan_backward(
        keeping, channel_low, step_raw, gate_half, grad_scanned, bias, rates_t, skip, in_wide, out_wide,
        groups, LANES,
    )
    grad_channel, grad_step_low, in_sums, out_sums, early_swapped = lax.optimization_barrier(
        (grad_channel, grad_step_low, in_sums, out_sums, early_swapped)
    )
    grad_rank = project_t(grad_step_low, step_mat)
    gate_joint = outer_rows(first_low, gate_low).astype(low).reshape(spots, -1, channels)
    grad_rows, gate_swapped = mixed_sum(
        jnp.concatenate([grad_rank, jnp.sum(in_sums, axis=-1), jnp.sum(out_sums, axis=-1)], axis=1), 8, "mix_grad_sum",
        [chip_load([gate_joint], channels, 0)],
    )
    grad_rows_low = grad_rows.astype(low)
    rows_joint = jnp.concatenate(
        [
            outer_rows(grad_low_one, mixer_low),
            outer_rows(grad_rows_low, channel_low),
            outer_rows(rank_low, grad_step_low),
        ],
        axis=0,
    ).astype(low)
    grad_channel = grad_channel + project(grad_rows_low, select_mat)
    grad_conv_in, taps_grad, offset_grad = conv_back(grad_channel)
    conv_low = grad_conv_in.astype(low)
    conv_joint = outer_rows(first_low, conv_low).astype(low).reshape(spots, -1, channels)
    in_grad = jnp.concatenate([conv_low, gate_low], axis=1)
    grad_first = project_t(in_grad, in_mat).astype(low)
    rows_joint = rows_joint.reshape(spots, -1, channels)
    rows_joint = jnp.pad(rows_joint, ((0, 0), (0, -own_rows % 16), (0, 0)))
    lines = jnp.concatenate([taps_grad.T, offset_grad[None], bias_grad, skip_grad, decay_grad], axis=0)
    lines = jnp.pad(lines, ((0, 1), (0, 0)))
    blank = jnp.zeros_like(lines)
    lines = jnp.where(core == 0, jnp.concatenate([lines, blank], axis=1), jnp.concatenate([blank, lines], axis=1))
    gains = jnp.concatenate([jnp.zeros_like(gain_two), gain_two, gain_three, gain_four], axis=0)
    small = jnp.concatenate([lines, gains.reshape(8, -1)], axis=0)
    input_grad, small, output, conv_swapped, rows_swapped = edge(
        "last", grad_first, [stream_zero, norm_gains[0:1], grad_one, small, output_part, stream_three],
        ways, rows, 4, 0, None, 9, "edge_seven",
        loads=[chip_load([conv_joint], channels, 0), chip_load([rows_joint], channels, 0)],
    )
    lines = small[: CONV + 3 + STATE]
    gains = small[-8:].reshape(norm_gains.shape)
    early_gate_up_grad, early_down_grad = spread_out(early_swapped)
    return (
        output,
        input_grad,
        gains,
        jnp.stack([chip_total(conv_swapped[:, 0]), chip_total(gate_swapped[:, 0])]),
        chip_total(rows_swapped[:, 0, :own_rows]),
        lines[:CONV].T,
        lines[CONV],
        lines[CONV + 1],
        lines[CONV + 3 :].T,
        lines[CONV + 2],
        early_gate_up_grad,
        early_down_grad,
        chip_total(focus_swapped[:, :3]),
        chip_total(focus_swapped[:, 3]),
        late_swapped[:2].astype(jnp.float32),
        late_swapped[2].astype(jnp.float32),
    )


def solution(mesh):
    counts = (mesh.shape["dp"], mesh.shape["tensor"])
    chosen = partial(grouped_body, counts, 6, 0, 6) if counts == (8, 4) else body
    return jax.shard_map(
        chosen,
        mesh=mesh,
        in_specs=(
            P("dp", None),
            P("dp", None),
            P(),
            P(None, "dp", "tensor"),
            P("dp", "tensor"),
            P("tensor", None),
            P("tensor"),
            P("tensor"),
            P("tensor", None),
            P("tensor"),
            P(None, "dp", "tensor"),
            P("dp", "tensor"),
            P(None, "dp", "tensor"),
            P("dp", "tensor"),
            P(None, "dp", "tensor"),
            P("dp", "tensor"),
            P("dp", None),
        ),
        out_specs=(
            P("dp", None),
            P("dp", None),
            P(),
            P(None, "dp", "tensor"),
            P("dp", "tensor"),
            P("tensor", None),
            P("tensor"),
            P("tensor"),
            P("tensor", None),
            P("tensor"),
            P(None, "dp", "tensor"),
            P("dp", "tensor"),
            P(None, "dp", "tensor"),
            P("dp", "tensor"),
            P(None, "dp", "tensor"),
            P("dp", "tensor"),
        ),
        check_vma=False,
    )
```

```python
from functools import partial
import math

import jax
import jax.numpy as jnp
from jax import lax
from jax.experimental import pallas as pl
from jax.experimental.layout import Layout, with_layout_constraint
from jax.experimental.pallas import tpu as pltpu
from jax.sharding import PartitionSpec as P

STATE = 16
CONV = 4
DT_RANK = 128
HEAD_DIM = 128
WINDOW = 2048
PROJ_OUT = 160


EPS = 1e-05
NEG_FILL = -1e30


def project(left, right):
    return jnp.dot(left, right, preferred_element_type=jnp.float32)


def project_t(left, right):
    return lax.dot_general(
        left, right, (((1,), (1,)), ((), ())), preferred_element_type=jnp.float32
    )


def outer_rows(left, right):
    return lax.dot_general(
        left, right, (((0,), (0,)), ((), ())), preferred_element_type=jnp.float32
    )


def rms_norm(values, weight):
    return values * lax.rsqrt(jnp.mean(values * values, axis=-1, keepdims=True) + EPS) * weight


def segment_info(lengths, tokens):
    flat_lengths = lengths.reshape(-1)
    ends = jnp.cumsum(flat_lengths, dtype=jnp.int32)
    firsts = ends - flat_lengths
    places = jnp.arange(tokens, dtype=jnp.int32)
    segs = jnp.sum((places[:, None] >= ends[None, :]).astype(jnp.int32), axis=1)
    starts = jnp.any(places[:, None] == firsts[None, :], axis=1)
    return (segs, starts)


def allowed_pairs(segs):
    places = jnp.arange(segs.shape[-1], dtype=jnp.int32)
    distance = places[:, None] - places[None, :]
    return (segs[:, None] == segs[None, :]) & (distance >= 0) & (distance < WINDOW)


def causal_conv(segs, stream, weight, offset):
    total = offset + stream * weight[:, 0]
    for lag_step in range(1, CONV):
        moved = jnp.concatenate(
            [jnp.zeros_like(stream[..., :lag_step, :]), stream[..., :-lag_step, :]], axis=-2
        )
        moved_segs = jnp.concatenate(
            [jnp.full_like(segs[..., :lag_step], -1), segs[..., :-lag_step]], axis=-1
        )
        linked = (segs == moved_segs).astype(stream.dtype)
        total = total + moved * weight[:, lag_step] * linked[..., None]
    return jax.nn.silu(total)


LANES = 128


def softplus(v):
    return jnp.maximum(v, 0.0) + jnp.log1p(jnp.exp(-jnp.abs(v)))


def scan_forward_kernel(
    groups, length, keep_ref, chan_ref, raw_ref, gate_ref, bias_ref, rate_ref, skip_ref, in_ref, out_ref,
    mixed_ref, step_s, drive_s, y_s,
):
    width = chan_ref.shape[1]
    blocks = width // LANES
    step_s[...] = softplus(raw_ref[...] + bias_ref[...])
    drive_s[...] = step_s[...] * chan_ref[...].astype(jnp.float32)
    rates = [rate_ref[:, pl.ds(b * LANES, LANES)] for b in range(blocks)]

    def advance(t, states):
        fresh = []
        for g in range(groups):
            row = g * length + t
            keep = keep_ref[row]
            input_map = in_ref[row]
            output_map = out_ref[row]
            for b in range(blocks):
                lanes = pl.ds(b * LANES, LANES)
                decay = jnp.exp(step_s[pl.ds(row, 1), lanes] * rates[b]) * keep
                state = decay * states[g * blocks + b] + drive_s[pl.ds(row, 1), lanes] * input_map
                y_s[pl.ds(row, 1), lanes] = jnp.sum(state * output_map, axis=0, keepdims=True)
                fresh.append(state)
        return tuple(fresh)

    zero = jnp.zeros((STATE, LANES), jnp.float32)
    lax.fori_loop(0, length, advance, (zero,) * (groups * blocks))
    gate = gate_ref[...]
    silu = gate / (1.0 + jnp.exp(-gate))
    mixed_ref[...] = (
        (y_s[...] + skip_ref[...] * chan_ref[...].astype(jnp.float32)) * silu
    ).astype(mixed_ref.dtype)


def scan_forward(keep, channel, step_raw, gate_half, step_bias, rates_t, skip_gain, in_wide, out_wide, groups, width):
    tokens, channels = channel.shape
    column = pl.BlockSpec((tokens, width), lambda i: (0, i))
    row = pl.BlockSpec((1, width), lambda i: (0, i))
    maps = pl.BlockSpec((tokens, STATE, LANES), lambda i: (0, 0, 0))
    return pl.pallas_call(
        partial(scan_forward_kernel, groups, tokens // groups),
        grid=(channels // width,),
        in_specs=[
            pl.BlockSpec(memory_space=pltpu.SMEM), column, column, column, row,
            pl.BlockSpec((STATE, width), lambda i: (0, i)), row, maps, maps,
        ],
        out_specs=column,
        out_shape=jax.ShapeDtypeStruct((tokens, channels), jnp.bfloat16),
        scratch_shapes=[pltpu.VMEM((tokens, width), jnp.float32)] * 3,
        compiler_params=pltpu.CompilerParams(vmem_limit_bytes=48 << 20),
        cost_estimate=pl.CostEstimate(flops=1, bytes_accessed=1 << 34, transcendentals=0),
        name="scan_forward",
    )(keep, channel, step_raw, gate_half, step_bias[None], rates_t, skip_gain[None], in_wide, out_wide)


def scan_backward_kernel(
    groups, length, keep_ref, chan_ref, raw_ref, gate_ref, dmix_ref, bias_ref, rate_ref, skip_ref, in_ref, out_ref,
    dchan_ref, draw_ref, dgate_ref, din_ref, dout_ref, dbias_ref, drate_ref, dskip_ref,
    step_s, drive_s, y_s, dy_s, dd_s, ds_s, state_s, decay_s,
):
    width = chan_ref.shape[1]
    blocks = width // LANES
    chan = chan_ref[...].astype(jnp.float32)
    step_s[...] = softplus(raw_ref[...] + bias_ref[...])
    drive_s[...] = step_s[...] * chan
    gate = gate_ref[...]
    sig = 1.0 / (1.0 + jnp.exp(-gate))
    dy_s[...] = dmix_ref[...] * (gate * sig)
    rates = [rate_ref[:, pl.ds(b * LANES, LANES)] for b in range(blocks)]

    @pl.when(pl.program_id(0) == 0)
    def _():
        din_ref[...] = jnp.zeros_like(din_ref)
        dout_ref[...] = jnp.zeros_like(dout_ref)

    def advance(t, states):
        fresh = []
        for g in range(groups):
            row = g * length + t
            keep = keep_ref[row]
            input_map = in_ref[row]
            output_map = out_ref[row]
            total = None
            for b in range(blocks):
                lanes = pl.ds(b * LANES, LANES)
                decay = jnp.exp(step_s[pl.ds(row, 1), lanes] * rates[b]) * keep
                decay_s[row, :, lanes] = decay
                carried = decay * states[g * blocks + b]
                state_s[row, :, lanes] = carried
                state = carried + drive_s[pl.ds(row, 1), lanes] * input_map
                y_s[pl.ds(row, 1), lanes] = jnp.sum(state * output_map, axis=0, keepdims=True)
                term = state * dy_s[pl.ds(row, 1), lanes]
                total = term if total is None else total + term
                fresh.append(state)
            dout_ref[row] += total
        return tuple(fresh)

    zero = jnp.zeros((STATE, LANES), jnp.float32)
    count = groups * blocks
    lax.fori_loop(0, length, advance, (zero,) * count)

    def retreat(back, carry):
        t = length - 1 - back
        fresh, rate_sums = [], []
        for g in range(groups):
            row = g * length + t
            input_map = in_ref[row]
            output_map = out_ref[row]
            total = None
            for b in range(blocks):
                lanes = pl.ds(b * LANES, LANES)
                at = g * blocks + b
                dstate = carry[0][at] + dy_s[pl.ds(row, 1), lanes] * output_map
                dlog = dstate * state_s[row, :, lanes]
                dd_s[pl.ds(row, 1), lanes] = jnp.sum(dstate * input_map, axis=0, keepdims=True)
                ds_s[pl.ds(row, 1), lanes] = jnp.sum(dlog * rates[b], axis=0, keepdims=True)
                term = dstate * drive_s[pl.ds(row, 1), lanes]
                total = term if total is None else total + term
                rate_sums.append(carry[1][at] + dlog * step_s[pl.ds(row, 1), lanes])
                fresh.append(dstate * decay_s[row, :, lanes])
            din_ref[row] += total
        return (tuple(fresh), tuple(rate_sums))

    _, rate_sums = lax.fori_loop(0, length, retreat, ((zero,) * count, (zero,) * count))
    for b in range(blocks):
        lanes = pl.ds(b * LANES, LANES)
        drate_ref[:, lanes] = rates[b] * sum(rate_sums[g * blocks + b] for g in range(groups))
    direct = y_s[...] + skip_ref[...] * chan
    dgate_ref[...] = (dmix_ref[...] * direct * (sig * (1.0 + gate * (1.0 - sig)))).astype(dgate_ref.dtype)
    dskip_ref[...] = jnp.sum(dy_s[...] * chan, axis=0, keepdims=True)
    dchan_ref[...] = dd_s[...] * step_s[...] + skip_ref[...] * dy_s[...]
    shifted = raw_ref[...] + bias_ref[...]
    draw = (ds_s[...] + dd_s[...] * chan) / (1.0 + jnp.exp(-shifted))
    draw_ref[...] = draw.astype(draw_ref.dtype)
    dbias_ref[...] = jnp.sum(draw, axis=0, keepdims=True)


def scan_backward(
    keep, channel, step_raw, gate_half, dmixed, step_bias, rates_t, skip_gain, in_wide, out_wide, groups, width
):
    tokens, channels = channel.shape
    column = pl.BlockSpec((tokens, width), lambda i: (0, i))
    row = pl.BlockSpec((1, width), lambda i: (0, i))
    states = pl.BlockSpec((STATE, width), lambda i: (0, i))
    maps = pl.BlockSpec((tokens, STATE, LANES), lambda i: (0, 0, 0))
    sheet = jax.ShapeDtypeStruct((tokens, channels), jnp.float32)
    low = jax.ShapeDtypeStruct((tokens, channels), jnp.bfloat16)
    wide = jax.ShapeDtypeStruct((tokens, STATE, LANES), jnp.float32)
    line = jax.ShapeDtypeStruct((1, channels), jnp.float32)
    return pl.pallas_call(
        partial(scan_backward_kernel, groups, tokens // groups),
        grid=(channels // width,),
        in_specs=[
            pl.BlockSpec(memory_space=pltpu.SMEM), column, column, column, column, row, states, row, maps, maps,
        ],
        out_specs=[column, column, column, maps, maps, row, states, row],
        out_shape=[
            sheet, low, low, wide, wide, line, jax.ShapeDtypeStruct((STATE, channels), jnp.float32), line,
        ],
        scratch_shapes=[pltpu.VMEM((tokens, width), jnp.float32)] * 6
        + [pltpu.VMEM((tokens, STATE, width), jnp.float32)] * 2,
        compiler_params=pltpu.CompilerParams(vmem_limit_bytes=56 << 20),
        cost_estimate=pl.CostEstimate(flops=1, bytes_accessed=1 << 34, transcendentals=0),
        name="scan_backward",
    )(keep, channel, step_raw, gate_half, dmixed, step_bias[None], rates_t, skip_gain[None], in_wide, out_wide)


def attention_scores(query, keys, allowed):
    scores = jnp.einsum("qhd,khd->hqk", query, keys, preferred_element_type=jnp.float32) * (
        1.0 / math.sqrt(HEAD_DIM)
    )
    return jnp.where(allowed[None], scores, NEG_FILL)


def attention_forward(query, keys, values, allowed):
    scores = attention_scores(query, keys, allowed)
    row_max = jnp.max(scores, axis=-1, keepdims=True)
    shifted = jnp.exp(scores - row_max)
    totals = jnp.sum(shifted, axis=-1, keepdims=True)
    probs = shifted / totals
    mixed = jnp.einsum(
        "hqk,khd->qhd", probs.astype(jnp.bfloat16), values, preferred_element_type=jnp.float32
    )
    return (mixed, row_max + jnp.log(totals))


def attention_backward(query, keys, values, allowed, log_total, grad_mixed):
    scale = 1.0 / math.sqrt(HEAD_DIM)
    probs = jnp.exp(attention_scores(query, keys, allowed) - log_total)
    grad_values = jnp.einsum(
        "hqk,qhd->khd", probs.astype(jnp.bfloat16), grad_mixed, preferred_element_type=jnp.float32
    )
    grad_probs = jnp.einsum("qhd,khd->hqk", grad_mixed, values, preferred_element_type=jnp.float32)
    inner_sum = jnp.sum(probs * grad_probs, axis=-1, keepdims=True)
    grad_scores = (probs * (grad_probs - inner_sum)).astype(jnp.bfloat16)
    grad_query = (
        jnp.einsum("hqk,khd->qhd", grad_scores, keys, preferred_element_type=jnp.float32) * scale
    )
    grad_keys = (
        jnp.einsum("hqk,qhd->khd", grad_scores, query, preferred_element_type=jnp.float32) * scale
    )
    return (grad_query, grad_keys, grad_values)


def gated_unit(gate, upward):
    return jax.nn.silu(gate) * upward


def ffn_forward(normed_low, gate_up, down_mat):
    gate = project(normed_low, gate_up[0])
    upward = project(normed_low, gate_up[1])
    hidden = gated_unit(gate, upward).astype(jnp.bfloat16)
    return (project_t(hidden, down_mat), gate, upward, hidden)


def ffn_backward(grad_low, normed_low, gate, upward, hidden, gate_up, down_mat):
    grad_hidden = project(grad_low, down_mat)
    down_grad = outer_rows(grad_low, hidden)
    _, unit_back = jax.vjp(gated_unit, gate, upward)
    grad_gate, grad_up = unit_back(grad_hidden)
    gate_low = grad_gate.astype(jnp.bfloat16)
    up_low = grad_up.astype(jnp.bfloat16)
    joined_grad = outer_rows(normed_low, jnp.concatenate([gate_low, up_low], axis=1))
    grad_normed = project_t(gate_low, gate_up[0]) + project_t(up_low, gate_up[1])
    return (grad_normed, joined_grad, down_grad)


def flatten_low(grad_heads, tokens):
    return grad_heads.astype(jnp.bfloat16).reshape(tokens, -1)


def collect(stacked, row_block):
    return (
        lax.all_gather(stacked, "dp", axis=1, tiled=True),
        lax.all_gather(row_block, "dp", axis=0, tiled=True),
    )


def spread_grads(joined, row_block, count):
    summed = (
        lax.psum_scatter(joined.astype(jnp.bfloat16), "dp", scatter_dimension=0, tiled=True),
        lax.psum_scatter(row_block.astype(jnp.bfloat16), "dp", scatter_dimension=0, tiled=True),
    )
    rows_here = summed[0].shape[0]
    restacked = jnp.transpose(summed[0].reshape(rows_here, count, -1), (1, 0, 2))
    return (restacked.astype(jnp.float32), summed[1].astype(jnp.float32))


def branch_total(piece_sum):
    return lax.psum(piece_sum, "tensor")


def input_total(piece_sum):
    return lax.psum(piece_sum, "tensor")


def body(
    hidden_in,
    seq_lengths,
    norm_gains,
    mixer_in,
    mixer_rows,
    conv_weight,
    conv_bias,
    step_bias,
    decay_log,
    skip_gain,
    early_gate_up,
    early_down,
    attention_in,
    attention_out,
    late_gate_up,
    late_down,
    output_grad,
):
    tokens = hidden_in.shape[0]
    width = hidden_in.shape[1]
    segs, starts = segment_info(seq_lengths, tokens)
    allowed = allowed_pairs(segs)
    stream_zero = hidden_in.astype(jnp.float32)
    mixer_stack, mixer_mats = collect(mixer_in, mixer_rows)
    first_normed, first_back = jax.vjp(rms_norm, stream_zero, norm_gains[0])
    first_low = first_normed.astype(jnp.bfloat16)
    conv_in = project(first_low, mixer_stack[0])
    gate_half = project(first_low, mixer_stack[1])
    channel_full, conv_back = jax.vjp(partial(causal_conv, segs), conv_in, conv_weight, conv_bias)
    channel_low = channel_full.astype(jnp.bfloat16)
    mix_rows = lax.psum(project_t(channel_low, mixer_mats[width : width + PROJ_OUT]), "tensor")
    rank_low = mix_rows[:, :DT_RANK].astype(jnp.bfloat16)
    step_raw = project(rank_low, mixer_mats[width + PROJ_OUT :])
    groups = seq_lengths.shape[0]
    keeping = 1.0 - starts.astype(jnp.float32)
    rates_t = -jnp.exp(decay_log).T
    wide = (tokens, STATE, LANES)
    in_wide = jnp.broadcast_to(mix_rows[:, DT_RANK : DT_RANK + STATE, None], wide)
    out_wide = jnp.broadcast_to(mix_rows[:, DT_RANK + STATE :, None], wide)
    mixer_low = scan_forward(
        keeping, channel_low, step_raw, gate_half, step_bias, rates_t, skip_gain, in_wide, out_wide, groups, LANES
    )
    stream_one = stream_zero + branch_total(project_t(mixer_low, mixer_mats[:width]))
    early_stack, early_mat = collect(early_gate_up, early_down)
    second_normed, second_back = jax.vjp(rms_norm, stream_one, norm_gains[1])
    second_low = second_normed.astype(jnp.bfloat16)
    early_part, early_gate, early_up, early_hidden = ffn_forward(second_low, early_stack, early_mat)
    stream_two = stream_one + branch_total(early_part)
    focus_stack, focus_mat = collect(attention_in, attention_out)
    heads_here = focus_stack.shape[2] // HEAD_DIM
    third_normed, third_back = jax.vjp(rms_norm, stream_two, norm_gains[2])
    third_low = third_normed.astype(jnp.bfloat16)
    query = (
        project(third_low, focus_stack[0])
        .astype(jnp.bfloat16)
        .reshape(tokens, heads_here, HEAD_DIM)
    )
    keys = (
        project(third_low, focus_stack[1])
        .astype(jnp.bfloat16)
        .reshape(tokens, heads_here, HEAD_DIM)
    )
    values = (
        project(third_low, focus_stack[2])
        .astype(jnp.bfloat16)
        .reshape(tokens, heads_here, HEAD_DIM)
    )
    attended, log_total = attention_forward(query, keys, values, allowed)
    attended_low = attended.reshape(tokens, heads_here * HEAD_DIM).astype(jnp.bfloat16)
    stream_three = stream_two + branch_total(project_t(attended_low, focus_mat))
    late_stack, late_mat = collect(late_gate_up, late_down)
    fourth_normed, fourth_back = jax.vjp(rms_norm, stream_three, norm_gains[3])
    fourth_low = fourth_normed.astype(jnp.bfloat16)
    late_part, late_gate, late_up, late_hidden = ffn_forward(fourth_low, late_stack, late_mat)
    output = stream_three + branch_total(late_part)
    grad_three = output_grad.astype(jnp.float32)
    late_pair = (late_stack, late_mat)
    grad_fourth, late_joined, late_mat_grad = ffn_backward(
        output_grad, fourth_low, late_gate, late_up, late_hidden, late_pair[0], late_pair[1]
    )
    grad_stream, gain_four = fourth_back(input_total(grad_fourth))
    grad_three = grad_three + grad_stream
    late_grads = spread_grads(late_joined, late_mat_grad, 2)
    focus_pair = (focus_stack, focus_mat)
    grad_branch_low = grad_three.astype(jnp.bfloat16)
    focus_mat_grad = outer_rows(grad_branch_low, attended_low)
    grad_attended = (
        project(grad_branch_low, focus_pair[1])
        .astype(jnp.bfloat16)
        .reshape(tokens, heads_here, HEAD_DIM)
    )
    grad_query, grad_keys, grad_values = attention_backward(
        query, keys, values, allowed, log_total, grad_attended
    )
    query_low = flatten_low(grad_query, tokens)
    keys_low = flatten_low(grad_keys, tokens)
    values_low = flatten_low(grad_values, tokens)
    focus_joined = outer_rows(third_low, jnp.concatenate([query_low, keys_low, values_low], axis=1))
    grad_third = (
        project_t(query_low, focus_pair[0][0])
        + project_t(keys_low, focus_pair[0][1])
        + project_t(values_low, focus_pair[0][2])
    )
    grad_stream, gain_three = third_back(input_total(grad_third))
    grad_two = grad_three + grad_stream
    focus_grads = spread_grads(focus_joined, focus_mat_grad, 3)
    early_pair = (early_stack, early_mat)
    grad_second, early_joined, early_mat_grad = ffn_backward(
        grad_two.astype(jnp.bfloat16),
        second_low,
        early_gate,
        early_up,
        early_hidden,
        early_pair[0],
        early_pair[1],
    )
    grad_stream, gain_two = second_back(input_total(grad_second))
    grad_one = grad_two + grad_stream
    early_grads = spread_grads(early_joined, early_mat_grad, 2)
    mixer_pair = (mixer_stack, mixer_mats)
    grad_mixer_low = grad_one.astype(jnp.bfloat16)
    out_mat_grad = outer_rows(grad_mixer_low, mixer_low)
    grad_scanned = project(grad_mixer_low, mixer_pair[1][:width])
    (
        grad_channel,
        grad_step_low,
        gate_low,
        in_sums,
        out_sums,
        step_bias_grad,
        decay_log_grad,
        skip_gain_grad,
    ) = scan_backward(
        keeping, channel_low, step_raw, gate_half, grad_scanned, step_bias, rates_t, skip_gain, in_wide, out_wide,
        groups, LANES,
    )
    step_mat_grad = outer_rows(rank_low, grad_step_low)
    grad_rank = project_t(grad_step_low, mixer_pair[1][width + PROJ_OUT :])
    grad_rows = lax.psum(
        jnp.concatenate([grad_rank, jnp.sum(in_sums, axis=-1), jnp.sum(out_sums, axis=-1)], axis=1), "tensor"
    )
    grad_rows_low = grad_rows.astype(jnp.bfloat16)
    select_mat_grad = outer_rows(grad_rows_low, channel_low)
    grad_channel = grad_channel + project(grad_rows_low, mixer_pair[1][width : width + PROJ_OUT])
    grad_conv_in, conv_weight_grad, conv_bias_grad = conv_back(grad_channel)
    conv_low = grad_conv_in.astype(jnp.bfloat16)
    mixer_joined = outer_rows(first_low, jnp.concatenate([conv_low, gate_low], axis=1))
    grad_first = project_t(conv_low, mixer_pair[0][0]) + project_t(gate_low, mixer_pair[0][1])
    grad_stream, gain_one = first_back(input_total(grad_first))
    input_grad = grad_one + grad_stream
    mixer_grads = spread_grads(
        mixer_joined, jnp.concatenate([out_mat_grad, select_mat_grad, step_mat_grad], axis=0), 2
    )
    small_sums = lax.psum(
        (
            jnp.stack([gain_one, gain_two, gain_three, gain_four]),
            conv_weight_grad,
            conv_bias_grad,
            step_bias_grad[0],
            decay_log_grad.T,
            skip_gain_grad[0],
        ),
        "dp",
    )
    return (
        output,
        input_grad,
        small_sums[0],
        mixer_grads[0],
        mixer_grads[1],
        small_sums[1],
        small_sums[2],
        small_sums[3],
        small_sums[4],
        small_sums[5],
        early_grads[0],
        early_grads[1],
        focus_grads[0],
        focus_grads[1],
        late_grads[0],
        late_grads[1],
    )


MESH = pl.DeviceIdType.MESH


def turns(group):
    return [turned for turned in (6, 2, 4) if turned & group == turned]


class Place:
    def __init__(self, ways):
        self.spot = lax.axis_index("dp")
        self.depth = lax.axis_index("tensor")
        self.ways = ways
        self.core = lax.rem(self.spot, 2)
        self.partner = self.spot + 1 - 2 * self.core

    def bit(self, axis, turned):
        value = lax.rem(self.spot // axis, 2)
        return 1 - value if turned & axis else value

    def across(self, turned, swapped=False):
        move = 1 - 2 * self.core if swapped else 0
        for axis in (2, 4):
            if turned & axis:
                move = move + axis * (1 - 2 * self.bit(axis, 0))
        return self.spot + move

    def side(self, group, turned=0):
        if group == 6:
            return self.bit(2, turned) + 2 * self.bit(4, turned)
        return self.bit(group, turned) if group else 0

    def along(self, offset):
        return lax.rem(self.depth + offset, self.ways)


def send(source, target, sems, at, spot, depth):
    copy = pltpu.make_async_remote_copy(
        src_ref=source,
        dst_ref=target,
        send_sem=sems[0].at[at],
        recv_sem=sems[1].at[at],
        device_id=(spot, depth),
        device_id_type=MESH,
    )
    copy.start()
    return copy


def greet(place, ways, both=False):
    barrier = pltpu.get_barrier_semaphore()
    peers = [(place.partner, place.depth)]
    peers += [(place.across(turned), place.depth) for turned in ways]
    if both:
        peers += [(place.across(turned, True), place.depth) for turned in ways]
    peers += [(place.spot, place.along(offset)) for offset in range(1, place.ways)]
    for peer in peers:
        pl.semaphore_signal(barrier, inc=1, device_id=peer, device_id_type=MESH)
    pl.semaphore_wait(barrier, len(peers))


def rows_at(start, size, unit):
    return pl.ds(pl.multiple_of(start * unit, unit), size)


class Reduction:
    def __init__(self, place, group, rows, parts, part_ref, near_s, sum_s, far_s, sems, names):
        self.place, self.group, self.rows, self.parts = place, group, rows, parts
        self.part_ref, self.near_s, self.sum_s, self.far_s = part_ref, near_s, sum_s, far_s
        self.sems = [sems[name] for name in names]
        self.ways = turns(group) + [0]
        self.step = part_ref.shape[1] // parts
        self.near, self.far = {}, {}

    def lanes(self, part):
        return pl.ds(part * self.step, self.step)

    def block(self, side):
        return rows_at(side, self.rows, self.rows)

    def send_near(self):
        place = self.place
        for part in range(self.parts):
            for at, turned in enumerate(self.ways):
                side = place.side(self.group, turned)
                self.near[part, turned] = send(
                    self.part_ref.at[self.block(side * 2 + 1 - place.core), self.lanes(part)],
                    self.near_s.at[self.block(side), self.lanes(part)],
                    self.sems[0], part * len(self.ways) + at, place.partner, place.depth,
                )

    def joined(self, part, turned):
        self.near[part, turned].wait_recv()
        side, lanes = self.place.side(self.group, turned), self.lanes(part)
        own = self.part_ref[self.block(side * 2 + self.place.core), lanes].astype(jnp.float32)
        return own + self.near_s[self.block(side), lanes].astype(jnp.float32)

    def order(self):
        half = self.parts // 2
        return [at + first for at in range(half) for first in (0, half)]

    def leg(self, part):
        return (2, 4) if part < self.parts // 2 else (4, 2)

    def push(self, part, turned, slot, to, value):
        rows, lanes = self.block(self.place.side(self.group, turned)), self.lanes(part)
        self.sum_s[rows, lanes] = value.astype(self.sum_s.dtype)
        self.far[part, slot] = send(
            self.sum_s.at[rows, lanes], self.far_s.at[slot, :, lanes],
            self.sems[1], part * 3 + slot, self.place.across(to), self.place.depth,
        )

    def came(self, part, slot):
        self.far[part, slot].wait_recv()
        return self.far_s[slot, :, self.lanes(part)].astype(jnp.float32)

    def send_far(self):
        if self.group:
            for part in self.order():
                first, _ = self.leg(part)
                self.push(part, 6, 1, first, self.joined(part, 6))
                self.push(part, first, 0, first, self.joined(part, first))

    def relay(self):
        if self.group:
            for part in self.order():
                _, second = self.leg(part)
                value = self.joined(part, second) + self.came(part, 1)
                self.push(part, second, 2, second, value)

    def chip_sum(self, part):
        total = self.joined(part, 0)
        if self.group:
            total = total + self.came(part, 0) + self.came(part, 2)
        return total

    def sent(self):
        return list(self.near.values()) + list(self.far.values())


def deep_sends(place, share, source, start, deep_s, lanes, sems, at):
    return [
        send(
            source.at[pl.ds(pl.multiple_of(start + place.along(offset) * share, share), share), lanes],
            deep_s.at[offset - 1, :, lanes],
            sems, at + offset - 1, place.spot, place.along(offset),
        )
        for offset in range(1, place.ways)
    ]


def deep_total(place, share, source, start, deep_s, copies):
    for copy in copies:
        copy.wait_recv()
    total = source[pl.ds(pl.multiple_of(start + place.depth * share, share), share), :].astype(jnp.float32)
    for offset in range(1, place.ways):
        total = total + deep_s[offset - 1].astype(jnp.float32)
    return total


def reduce_stage(first, deep_s, sems, between):
    place, rows = first.place, first.rows
    share = rows // place.ways
    first.send_near()
    between(0)
    first.send_far()
    first.relay()
    between(1)
    deep = []
    mine = place.side(first.group)
    for part in first.order() if first.group else range(first.parts):
        first.sum_s[first.block(mine), first.lanes(part)] = first.chip_sum(part).astype(first.sum_s.dtype)
        deep += deep_sends(
            place, share, first.sum_s, mine * rows, deep_s, first.lanes(part), sems["deep"], part * (place.ways - 1)
        )
    return deep_total(place, share, first.sum_s, mine * rows, deep_s, deep), first.sent() + deep


def hand_on(place, group, rows_of, target, sems, base, far):
    half = target.shape[1] // 2
    for came, to, lanes in ((2, 4, pl.ds(0, half)), (4, 2, pl.ds(half, half))):
        far[came].wait_recv()
        block = target.at[rows_of(came), lanes]
        far[came, to] = send(block, block, sems, base + to // 2 + 1, place.across(to), place.depth)


def first_leg(place, block, sems, base):
    return {turned: send(block, block, sems, base + turned // 2 - 1, place.across(turned), place.depth) for turned in (2, 4)}


def gather_stage(place, group, rows, all_ref, sems, between):
    share = rows // place.ways

    def place_of(turned, offset):
        depth = place.along(place.ways - offset) if offset else place.depth
        return pl.ds(pl.multiple_of((place.side(group, turned) * 2 + place.core) * rows + depth * share, share), share)

    def to_partner(turned, offset, at):
        block = all_ref.at[place_of(turned, offset), :]
        return send(block, block, sems["near_back"], at * place.ways + offset, place.partner, place.depth)

    own = all_ref.at[place_of(0, 0), :]
    deep = [
        send(own, own, sems["deep_back"], offset - 1, place.spot, place.along(offset)) for offset in range(1, place.ways)
    ]
    far, near = [], []
    for offset in range(place.ways):
        if offset:
            deep[offset - 1].wait_recv()
        if group:
            far.append(first_leg(place, all_ref.at[place_of(0, offset), :], sems["far_back"], 4 * offset))
        near.append(to_partner(0, offset, 0))
        if offset == 0:
            between()
    if group:
        for offset in range(place.ways):
            hand_on(
                place, group, lambda turned: place_of(turned, offset), all_ref, sems["far_back"], 4 * offset, far[offset]
            )
            near.append(to_partner(2, offset, 1))
            near.append(to_partner(4, offset, 2))
        for offset in range(place.ways):
            far[offset][2, 4].wait_recv()
            far[offset][4, 2].wait_recv()
            near.append(to_partner(6, offset, 3))
    for copy in near:
        copy.wait_recv()
    return deep + [copy for one in far for copy in one.values()] + near


class Exchange:
    def __init__(self, place, items, sems):
        self.place, self.items, self.sems = place, items, sems
        self.copies, self.own = [], []

    def start(self):
        place = self.place
        spots = [place.across(turned, swapped) for turned in (6, 2, 4) for swapped in (False, True)] + [place.partner]
        for at, (source, target) in enumerate(self.items):
            for slot, spot in enumerate(spots):
                self.copies.append(
                    send(source(spot), target(place.spot), self.sems, at * 8 + slot, spot, place.depth)
                )
            own = pltpu.make_async_copy(source(place.spot), target(place.spot), self.sems[1].at[at * 8 + 7])
            own.start()
            self.own.append(own)

    def close(self):
        for copy in self.own + self.copies:
            copy.wait()


def columns_at(half, size):
    return pl.ds(pl.multiple_of(half * size, size), size)


def blocks_of(refs, size):
    return [(ref, at) for ref in refs for at in range(ref.shape[2] // size)]


def spread_items(size, refs, out):
    return [
        (
            lambda spot, ref=ref, at=at: ref.at[spot, :, pl.ds(at * size, size)],
            lambda spot, to=to: out.at[to, :, columns_at(spot, size)],
        )
        for to, (ref, at) in enumerate(blocks_of(refs, size))
    ]


def chip_items(size, refs, out):
    return [
        (
            lambda spot, ref=ref, at=at: ref.at[spot, :, pl.ds(at * size, size)],
            lambda spot, to=to: out.at[spot // 2, to, :, columns_at(spot % 2, size)],
        )
        for to, (ref, at) in enumerate(blocks_of(refs, size))
    ]


def layers(refs):
    return [ref.at[at] if len(ref.shape) == 3 else ref for ref in refs for at in range(ref.shape[0] if len(ref.shape) == 3 else 1)]


def plane_items(spots, refs, out):
    blocks = layers(refs)
    size = blocks[0].shape[1] // spots
    return [
        (
            lambda spot, block=block: block.at[:, columns_at(spot, size)],
            lambda spot, at=at: out.at[spot, :, pl.ds(at * size, size)],
        )
        for at, block in enumerate(blocks)
    ]


def core_items(refs, out):
    blocks = layers(refs)
    size = blocks[0].shape[1] // 2
    return [
        (
            lambda half, block=block: block.at[:, columns_at(half, size)],
            lambda spot, at=at: out.at[spot, :, pl.ds(at * size, size)],
        )
        for at, block in enumerate(blocks)
    ]


def handed_items(out):
    return [(None, lambda spot: out.at[spot])]


class Load:
    def __init__(self, mode, arrays, out, items, count, stage):
        self.mode, self.arrays, self.items, self.count, self.stage = mode, arrays, items, count, stage
        self.out = jax.ShapeDtypeStruct(out, arrays[0].dtype)

    def begin(self, place, refs, out, sems):
        if self.mode == "second":
            mover = Pull(place, self.items(out), sems)
            mover.second(False)
        elif self.mode == "first":
            mover = Pull(place, self.items(refs, out), sems)
            mover.first()
        else:
            mover = Exchange(place, self.items(refs, out), sems)
            mover.start()
        return mover


def spread_stage(place, rows, all_ref, sems, name="deep_back"):
    share = rows // place.ways
    own = all_ref.at[pl.ds(pl.multiple_of(place.depth * share, share), share), :]
    deep = [
        send(own, own, sems[name], offset - 1, place.spot, place.along(offset)) for offset in range(1, place.ways)
    ]
    return deep


def small_stage(place, half, sum_ref, small_s, sems):
    near = [
        send(
            sum_ref.at[pl.ds(part * half, half), :], small_s.at[part], sems["small"], part, place.partner, place.depth
        )
        for part in range(2)
    ]
    for copy in near:
        copy.wait()
    mine = pl.ds(pl.multiple_of(place.core * half, half), half)
    small_s[2] = sum_ref[mine, :] + small_s[place.core]
    chips = [
        send(small_s.at[2], small_s.at[3 + at], sems["small"], 2 + at, spot, place.depth)
        for at, spot in enumerate((place.across(2), place.across(4), place.across(6)))
    ]
    for copy in chips:
        copy.wait_recv()
    total = small_s[2] + small_s[3] + small_s[4] + small_s[5]
    small_s[6] = total
    deep = [
        send(
            small_s.at[6, pl.ds(half - 8, 8), :], small_s.at[6 + offset, pl.ds(half - 8, 8), :],
            sems["small"], 4 + offset, place.spot, place.along(offset),
        )
        for offset in range(1, place.ways)
    ]
    for copy in deep:
        copy.wait_recv()
    gains = small_s[6, half - 8 : half, :]
    for offset in range(1, place.ways):
        gains = gains + small_s[6 + offset, half - 8 : half, :]
    last = jnp.where(place.core == 1, gains, total[half - 8 : half, :])
    ready, came = 6 + place.ways, 7 + place.ways
    small_s[ready] = jnp.concatenate([total[: half - 8, :], last], axis=0)
    back = send(small_s.at[ready], small_s.at[came], sems["small"], 4 + place.ways, place.partner, place.depth)
    sum_ref[mine, :] = small_s[ready]
    back.wait_recv()
    sum_ref[pl.ds(pl.multiple_of((1 - place.core) * half, half), half), :] = small_s[came]
    return chips + deep + [back]


def sem_shapes(names):
    shapes = []
    for count in names.values():
        shapes += [pltpu.SemaphoreType.DMA((count,))] * 2
    return shapes


def sem_dict(names, refs):
    return {name: (refs[2 * at], refs[2 * at + 1]) for at, name in enumerate(names)}


def edge_kernel(kind, extra, loads, ways, rows, parts, in_group, out_group, names, counts, *refs):
    place = Place(ways)
    share = rows // ways
    ins, outs = list(refs[: counts[0]]), list(refs[counts[0] : counts[0] + counts[1]])
    scratch = list(refs[counts[0] + counts[1] : counts[0] + counts[1] + counts[2]])
    sems = sem_dict(names, refs[sum(counts) :])
    part_ref = ins.pop(0)
    near_s, sum_s, far_s, deep_s = [scratch.pop(0) for _ in range(4)]
    if kind == "forward":
        stream_ref, gain_ref = ins.pop(0), ins.pop(0)
    elif kind != "sum":
        stream_ref, gain_ref, grad_ref = ins.pop(0), ins.pop(0), ins.pop(0)
    all_ref = outs.pop(0)
    if kind != "sum" and kind != "last":
        fresh_ref = outs.pop(0)
    if kind == "backward":
        dgain_ref = outs.pop(0)
    if kind == "last":
        small_ref, late_ref, three_ref = ins.pop(0), ins.pop(0), ins.pop(0)
        dgain_ref, late_out_ref = outs.pop(0), outs.pop(0)
        low_s, small_s, late_s, late_low_s = [scratch.pop(0) for _ in range(4)]
    moving = []
    for load in reversed(loads):
        moving.append(([ins.pop() for _ in load.arrays][::-1], outs.pop()))
    moving = moving[::-1]
    everyone = loads or kind == "last"
    greet(place, turns(6) if everyone else sorted({*turns(in_group), *turns(out_group)}), bool(loads))
    first = Reduction(place, in_group, rows, parts, part_ref, near_s, sum_s, far_s, sems, ("near", "far"))
    waiting = []
    freight = {}
    if extra == "gather":
        load_ref, load_out_ref = ins.pop(0), outs.pop(0)

        def load_rows(turned):
            return rows_at(place.side(in_group, turned) * 2 + place.core, rows, rows)

        def between(stage):
            spot = rows_at(place.side(in_group) * 2 + place.core, rows, rows)
            if stage == 0:
                load_out_ref[spot, :] = load_ref[...]
                return
            own = load_out_ref.at[spot, :]
            if stage == 1:
                freight.update(first_leg(place, own, sems["load_far"], 0))
                freight[0] = send(own, own, sems["load_near"], 0, place.partner, place.depth)
            else:
                hand_on(place, in_group, load_rows, load_out_ref, sems["load_far"], 0, freight)

    elif extra == "reduce":
        second = Reduction(
            place, in_group, rows, parts, ins.pop(0), *[scratch.pop(0) for _ in range(3)], sems, ("load_near", "load_far")
        )
        load_out_ref = outs.pop(0)

        def between(stage):
            (second.send_near, second.send_far, second.relay)[stage]()

    else:

        def between(stage):
            pass

    carried = []

    def on_the_way(stage):
        between(stage)
        for at, load in enumerate(loads):
            if load.stage == stage:
                carried.append(load.begin(place, *moving[at], sems[f"load{at}"]))

    if kind == "last":
        late = deep_sends(place, share, late_ref, 0, late_s, slice(None), sems["late"], 0)
        waiting += late
    total, copies = reduce_stage(first, deep_s, sems, on_the_way)
    waiting += copies
    if kind == "forward":
        fresh = stream_ref[...] + total
        fresh_ref[...] = fresh
        scale = lax.rsqrt(jnp.mean(fresh * fresh, axis=-1, keepdims=True) + EPS)
        value = fresh * scale * gain_ref[...]
    elif kind == "sum":
        value = total
    else:
        stream = stream_ref[...]
        scale = lax.rsqrt(jnp.mean(stream * stream, axis=-1, keepdims=True) + EPS)
        leaned = total * gain_ref[...]
        inner = jnp.mean(leaned * stream, axis=-1, keepdims=True)
        value = grad_ref[...] + scale * leaned - stream * (scale * scale * scale * inner)
        dgain = jnp.sum(total * stream * scale, axis=0, keepdims=True)
        if kind == "backward":
            dgain_ref[...] = dgain
            fresh_ref[...] = value
    if kind == "last":
        own = pl.ds(pl.multiple_of(place.depth * share, share), share)
        low_s[own, :] = value.astype(low_s.dtype)
        spread = spread_stage(place, rows, low_s, sems)
        late_total = three_ref[...] + deep_total(place, share, late_ref, 0, late_s, late)
        late_low_s[own, :] = late_total.astype(late_low_s.dtype)
        spread += spread_stage(place, rows, late_low_s, sems, "late_back")
        half, span = small_ref.shape[0] // 2, small_ref.shape[1]
        dgain_ref[...] = small_ref[...]
        for at in range(dgain.shape[1] // span):
            dgain_ref[pl.ds(2 * half - 8 + at, 1), :] = dgain[:, at * span : (at + 1) * span]
        waiting += spread + small_stage(place, half, dgain_ref, small_s, sems)
        for copy in spread:
            copy.wait_recv()
        all_ref[...] = low_s[...].astype(jnp.float32)
        late_out_ref[...] = late_low_s[...].astype(jnp.float32)
    else:
        spot = pl.multiple_of((place.side(out_group) * 2 + place.core) * rows + place.depth * share, share)
        all_ref[pl.ds(spot, share), :] = value.astype(all_ref.dtype)
        waiting += gather_stage(place, out_group, rows, all_ref, sems, partial(on_the_way, 2))
    if extra == "gather":
        last = []
        for at, turned in enumerate((2, 4, 6)):
            for key in ((2, 4), (4, 2)) if turned == 6 else ():
                freight[key].wait_recv()
            came = load_out_ref.at[load_rows(turned), :]
            last.append(send(came, came, sems["load_near"], 1 + at, place.partner, place.depth))
        for copy in last + [freight[0]]:
            copy.wait_recv()
        waiting += list(freight.values()) + last
    elif extra == "reduce":
        for part in range(parts):
            load_out_ref[:, second.lanes(part)] = second.chip_sum(part).astype(load_out_ref.dtype)
        waiting += second.sent()
    for mover in carried:
        mover.close()
    for copy in waiting:
        copy.wait_send()


def edge(kind, part, extras, ways, rows, parts, in_group, out_group, ident, name, extra=None, loads=()):
    width = part.shape[1]
    share = rows // ways
    in_far, out_far = len(turns(in_group)), len(turns(out_group or 0))
    in_sides, out_sides = in_far + 1, out_far + 1
    dtype = part.dtype
    line = jax.ShapeDtypeStruct((1, width), jnp.float32)
    strip = jax.ShapeDtypeStruct((share, width), jnp.float32)
    whole = jax.ShapeDtypeStruct((out_sides * 2 * rows, width), dtype)
    block = jax.ShapeDtypeStruct((rows, width), jnp.float32)
    outs = {
        "forward": [whole, strip],
        "backward": [whole, strip, line],
        "last": [block] + [jax.ShapeDtypeStruct(one.shape, one.dtype) for one in extras[3:4]] + [block],
        "sum": [whole],
    }[kind]
    names = {"near": parts * in_sides, "far": 3 * parts if in_far else 0, "deep": parts * (ways - 1), "deep_back": ways - 1}
    reducing = [
        pltpu.VMEM((in_sides * rows, width), dtype),
        pltpu.VMEM((in_sides * rows, width), dtype),
        pltpu.VMEM((max(in_far, 1), rows if in_far else 16, width), dtype),
    ]
    deep = pltpu.VMEM((ways - 1, share, width), dtype)
    scratch = reducing + [deep]
    if kind == "last":
        names.update({"small": 5 + ways, "late": ways - 1, "late_back": ways - 1})
        small = pltpu.VMEM((8 + ways, extras[3].shape[0] // 2, extras[3].shape[1]), jnp.float32)
        spread = pltpu.VMEM((rows, width), dtype)
        scratch += [spread, small, deep, spread]
    else:
        names.update({"far_back": 4 * ways if out_far else 0, "near_back": ways * out_sides})
    if extra == "gather":
        names.update({"load_far": 4, "load_near": in_sides})
        outs = outs + [jax.ShapeDtypeStruct((in_sides * 2 * rows, width), dtype)]
    elif extra == "reduce":
        names.update({"load_far": 3 * parts, "load_near": parts * in_sides})
        outs = outs + [jax.ShapeDtypeStruct((rows, width), dtype)]
        scratch = scratch + reducing
    vmem, whole_memory = pl.BlockSpec(memory_space=pltpu.VMEM), pl.BlockSpec(memory_space=pl.ANY)
    in_specs, out_specs = [vmem] * (1 + len(extras)), [vmem] * len(outs)
    aliases, extras, outs = {}, list(extras), list(outs)
    for at, load in enumerate(loads):
        names[f"load{at}"] = 8 * load.count
        if load.mode == "second":
            aliases[1 + len(extras)] = len(outs)
        extras += load.arrays
        outs.append(load.out)
        in_specs += [whole_memory] * len(load.arrays)
        out_specs.append(whole_memory)
    names = {key: count for key, count in names.items() if count}
    if not in_far:
        names["far"] = 1
    return pl.pallas_call(
        partial(
            edge_kernel, kind, extra, loads, ways, rows, parts, in_group, out_group, names,
            (1 + len(extras), len(outs), len(scratch)),
        ),
        in_specs=in_specs,
        out_specs=out_specs,
        out_shape=outs,
        scratch_shapes=scratch + sem_shapes(names),
        input_output_aliases=aliases,
        compiler_params=pltpu.CompilerParams(
            collective_id=ident, has_side_effects=True, vmem_limit_bytes=48 << 20
        ),
        cost_estimate=pl.CostEstimate(flops=1, bytes_accessed=1, transcendentals=0),
        name=name,
    )(part, *extras)


class Pull:
    def __init__(self, place, items, sems):
        self.place, self.items, self.sems = place, items, sems
        self.copies, self.handed = {}, set()

    def go(self, at, key, slot, source, spot, target):
        self.copies[at, key] = send(source, target, self.sems, at * 8 + slot, spot, self.place.depth)

    def first(self):
        place = self.place
        for at, (source, target) in enumerate(self.items):
            mine = target(place.spot)
            for turned in (2, 4):
                self.go(at, (turned, False), turned - 2, source(place.core), place.across(turned), mine)
                self.go(at, (turned, True), turned - 1, source(1 - place.core), place.across(turned, True), mine)
            self.go(at, "near", 4, source(1 - place.core), place.partner, mine)
            own = pltpu.make_async_copy(source(place.core), mine, self.sems[1].at[at * 8 + 7])
            own.start()
            self.copies[at, "own"] = own

    def second(self, fresh=True):
        place = self.place
        for at, (_, target) in enumerate(self.items):
            for slot, turned, swapped, to in ((5, 2, False, 4), (6, 4, True, 2)):
                if fresh:
                    self.copies[at, (turned, swapped)].wait_recv()
                    self.handed.add((at, (turned, swapped)))
                block = target(place.across(turned, swapped))
                self.go(at, ("on", turned), slot, block, place.across(to), block)

    def close(self):
        for (at, key), copy in self.copies.items():
            if key == "own":
                copy.wait()
            else:
                if (at, key) not in self.handed:
                    copy.wait_recv()
                copy.wait_send()


def opening_kernel(ways, rows, hidden_ref, gain_ref, in_ref, rows_ref, first_ref, in_out, rows_out, *sems):
    place = Place(ways)
    greet_plane(place)
    size = rows_out.shape[2]
    items = [
        (
            lambda half, at=at: in_ref.at[at, :, columns_at(half, size)],
            lambda spot, at=at: in_out.at[spot, :, pl.ds(at * size, size)],
        )
        for at in range(in_ref.shape[0])
    ]
    items.append((lambda half: rows_ref.at[:, columns_at(half, size)], lambda spot: rows_out.at[spot]))
    pull = Pull(place, items, sems[2:])
    pull.first()
    stream = hidden_ref[...].astype(jnp.float32)
    scale = lax.rsqrt(jnp.mean(stream * stream, axis=-1, keepdims=True) + EPS)
    first_ref[rows_at(place.core, rows, rows), :] = (stream * scale * gain_ref[...]).astype(jnp.bfloat16)
    mine = first_ref.at[rows_at(place.core, rows, rows), :]
    copy = send(mine, mine, sems[:2], 0, place.partner, place.depth)
    pull.second()
    copy.wait()
    pull.close()


def greet_plane(place):
    barrier = pltpu.get_barrier_semaphore()
    peers = [place.partner] + [place.across(turned, swapped) for turned in (2, 4) for swapped in (False, True)]
    for peer in peers:
        pl.semaphore_signal(barrier, inc=1, device_id=(peer, place.depth), device_id_type=MESH)
    pl.semaphore_wait(barrier, len(peers))


def opening(hidden, gain, in_weights, row_weights, spots, ways, ident):
    rows, width = hidden.shape
    vmem, whole_memory = pl.BlockSpec(memory_space=pltpu.VMEM), pl.BlockSpec(memory_space=pl.ANY)
    kinds, depth, columns = in_weights.shape
    low = jnp.bfloat16
    return pl.pallas_call(
        partial(opening_kernel, ways, rows),
        in_specs=[vmem] * 2 + [whole_memory] * 2,
        out_specs=[vmem] + [whole_memory] * 2,
        out_shape=[
            jax.ShapeDtypeStruct((2 * rows, width), low),
            jax.ShapeDtypeStruct((spots, depth, kinds * columns // 2), low),
            jax.ShapeDtypeStruct((spots, row_weights.shape[0], columns // 2), low),
        ],
        scratch_shapes=[pltpu.SemaphoreType.DMA((1,))] * 2 + [pltpu.SemaphoreType.DMA((8 * (kinds + 1),))] * 2,
        compiler_params=pltpu.CompilerParams(
            collective_id=ident, has_side_effects=True, vmem_limit_bytes=40 << 20
        ),
        cost_estimate=pl.CostEstimate(flops=1, bytes_accessed=1, transcendentals=0),
        name="opening",
    )(hidden, gain, in_weights, row_weights)


def probs_of(query, keys, allowed):
    scores = project_t(query, keys) * (1.0 / math.sqrt(HEAD_DIM))
    scores = jnp.where(allowed, scores, NEG_FILL)
    shifted = jnp.exp(scores - jnp.max(scores, axis=-1, keepdims=True))
    return shifted / jnp.sum(shifted, axis=-1, keepdims=True)


def allowed_in(down_ref, side_ref, rows, group):
    shape = (rows, rows)
    distance = lax.broadcasted_iota(jnp.int32, shape, 0) - lax.broadcasted_iota(jnp.int32, shape, 1)
    same = down_ref[group * rows : (group + 1) * rows, :] == side_ref[group : group + 1, :]
    return same & (distance >= 0) & (distance < WINDOW)


def attend_kernel(heads, rows, joint_ref, down_ref, side_ref, low_ref, out_ref):
    low_ref[...] = joint_ref[...].astype(jnp.bfloat16)
    size = heads * HEAD_DIM
    for group in range(joint_ref.shape[0] // rows):
        allowed = allowed_in(down_ref, side_ref, rows, group)
        span = slice(group * rows, (group + 1) * rows)
        for head in range(heads):
            at = slice(head * HEAD_DIM, (head + 1) * HEAD_DIM)
            query, keys, values = [
                low_ref[span, part * size + head * HEAD_DIM : part * size + (head + 1) * HEAD_DIM] for part in range(3)
            ]
            probs = probs_of(query, keys, allowed)
            out_ref[span, at] = project(probs.astype(jnp.bfloat16), values).astype(jnp.bfloat16)


def attend(joint, down, side, rows):
    count, size = joint.shape
    return pl.pallas_call(
        partial(attend_kernel, size // (3 * HEAD_DIM), rows),
        out_shape=[
            jax.ShapeDtypeStruct((count, size), jnp.bfloat16),
            jax.ShapeDtypeStruct((count, size // 3), jnp.bfloat16),
        ],
        compiler_params=pltpu.CompilerParams(vmem_limit_bytes=32 << 20),
        name="attend",
    )(joint, down, side)


def attend_back_kernel(heads, rows, low_ref, grad_ref, down_ref, side_ref, out_ref):
    size = heads * HEAD_DIM
    scale = 1.0 / math.sqrt(HEAD_DIM)
    for group in range(low_ref.shape[0] // rows):
        allowed = allowed_in(down_ref, side_ref, rows, group)
        span = slice(group * rows, (group + 1) * rows)
        for head in range(heads):
            places = [slice(part * size + head * HEAD_DIM, part * size + (head + 1) * HEAD_DIM) for part in range(3)]
            query, keys, values = [low_ref[span, place] for place in places]
            grad = grad_ref[span, head * HEAD_DIM : (head + 1) * HEAD_DIM].astype(jnp.bfloat16)
            probs = probs_of(query, keys, allowed)
            grad_probs = project_t(grad, values)
            inner = jnp.sum(probs * grad_probs, axis=-1, keepdims=True)
            grad_scores = (probs * (grad_probs - inner)).astype(jnp.bfloat16)
            out_ref[span, places[0]] = (project(grad_scores, keys) * scale).astype(jnp.bfloat16)
            out_ref[span, places[1]] = (outer_rows(grad_scores, query) * scale).astype(jnp.bfloat16)
            out_ref[span, places[2]] = outer_rows(probs.astype(jnp.bfloat16), grad).astype(jnp.bfloat16)


def attend_back(low, grad, down, side, rows):
    count, size = low.shape
    return pl.pallas_call(
        partial(attend_back_kernel, size // (3 * HEAD_DIM), rows),
        out_shape=jax.ShapeDtypeStruct((count, size), jnp.bfloat16),
        compiler_params=pltpu.CompilerParams(vmem_limit_bytes=32 << 20),
        name="attend_back",
    )(low, grad, down, side)


def conv_total(stream, age_ref, taps_ref, offset_ref):
    moved = [stream] + [
        jnp.where(age_ref[...] >= lag, pltpu.roll(stream, lag, 0), 0.0) for lag in range(1, CONV)
    ]
    total = offset_ref[...]
    for lag in range(CONV):
        total = total + moved[lag] * taps_ref[lag : lag + 1, :]
    return total, moved


def front_kernel(first_ref, conv_mat_ref, gate_mat_ref, age_ref, taps_ref, offset_ref, select_ref, conv_ref, gate_ref,
                 channel_ref, mix_ref):
    stream = project(first_ref[...], conv_mat_ref[...])
    conv_ref[...] = stream
    gate_ref[...] = project(first_ref[...], gate_mat_ref[...])
    total, _ = conv_total(stream, age_ref, taps_ref, offset_ref)
    channel = (total / (1.0 + jnp.exp(-total))).astype(jnp.bfloat16)
    channel_ref[...] = channel

    @pl.when(pl.program_id(0) == 0)
    def _():
        mix_ref[...] = jnp.zeros_like(mix_ref)

    mix_ref[...] += project_t(channel, select_ref[...])


def front(first_low, in_mat, age, taps_t, offset, select):
    count, width = first_low.shape
    channels = in_mat.shape[1] // 2
    size = channels // 2
    column = pl.BlockSpec((count, size), lambda i: (0, i))
    sheet = jax.ShapeDtypeStruct((count, channels), jnp.float32)
    return pl.pallas_call(
        front_kernel,
        grid=(2,),
        in_specs=[
            pl.BlockSpec((count, width), lambda i: (0, 0)),
            pl.BlockSpec((width, size), lambda i: (0, i)),
            pl.BlockSpec((width, size), lambda i: (0, i + 2)),
            pl.BlockSpec((count, 1), lambda i: (0, 0)),
            pl.BlockSpec((CONV, size), lambda i: (0, i)),
            pl.BlockSpec((1, size), lambda i: (0, i)),
            pl.BlockSpec((select.shape[0], size), lambda i: (0, i)),
        ],
        out_specs=[column, column, column, pl.BlockSpec((count, select.shape[0]), lambda i: (0, 0))],
        out_shape=[
            sheet, sheet, jax.ShapeDtypeStruct((count, channels), jnp.bfloat16),
            jax.ShapeDtypeStruct((count, select.shape[0]), jnp.float32),
        ],
        compiler_params=pltpu.CompilerParams(vmem_limit_bytes=40 << 20),
        name="front",
    )(first_low, in_mat, in_mat, age, taps_t, offset, select)


def front_back_kernel(conv_ref, age_ref, left_ref, taps_ref, offset_ref, scan_ref, mix_ref, select_ref, low_ref, grads_ref):
    total, moved = conv_total(conv_ref[...], age_ref, taps_ref, offset_ref)
    sig = 1.0 / (1.0 + jnp.exp(-total))
    grad = (scan_ref[...] + project(mix_ref[...], select_ref[...])) * (sig * (1.0 + total * (1.0 - sig)))
    count = grad.shape[0]
    back = grad * taps_ref[0:1, :]
    for lag in range(1, CONV):
        back = back + jnp.where(left_ref[...] >= lag, pltpu.roll(grad, count - lag, 0), 0.0) * taps_ref[lag : lag + 1, :]
    low_ref[...] = back.astype(jnp.bfloat16)
    for lag in range(CONV):
        grads_ref[lag : lag + 1, :] = jnp.sum(grad * moved[lag], axis=0, keepdims=True)
    grads_ref[CONV : CONV + 1, :] = jnp.sum(grad, axis=0, keepdims=True)
    grads_ref[CONV + 1 :, :] = jnp.zeros((3, grad.shape[1]), jnp.float32)


def front_back(conv_in, age, left, taps_t, offset, grad_scan, grad_mix, select):
    count, channels = conv_in.shape
    size = channels // 2
    column = pl.BlockSpec((count, size), lambda i: (0, i))
    place = pl.BlockSpec((count, 1), lambda i: (0, 0))
    return pl.pallas_call(
        front_back_kernel,
        grid=(2,),
        in_specs=[
            column, place, place,
            pl.BlockSpec((CONV, size), lambda i: (0, i)),
            pl.BlockSpec((1, size), lambda i: (0, i)),
            column,
            pl.BlockSpec((count, select.shape[0]), lambda i: (0, 0)),
            pl.BlockSpec((select.shape[0], size), lambda i: (0, i)),
        ],
        out_specs=[column, pl.BlockSpec((8, size), lambda i: (0, i))],
        out_shape=[
            jax.ShapeDtypeStruct((count, channels), jnp.bfloat16),
            jax.ShapeDtypeStruct((8, channels), jnp.float32),
        ],
        compiler_params=pltpu.CompilerParams(vmem_limit_bytes=40 << 20),
        name="front_back",
    )(conv_in, age, left, taps_t, offset, grad_scan, grad_mix, select)


def sub_of(spot, group):
    if group == 6:
        return spot
    return spot % 2 + (2 * ((spot // group) % 2) if group else 0)


def subs_of(group):
    return 2 * (len(turns(group)) + 1)


def pull(count, *sets):
    def cut(block, group, spot):
        size = block.shape[1] // subs_of(group)
        return block[:, sub_of(spot, group) * size : (sub_of(spot, group) + 1) * size]

    return jnp.stack(
        [
            jnp.concatenate([cut(block, group, spot) for blocks, group in sets for block in blocks], axis=1)
            for spot in range(count)
        ]
    )


def in_order(value):
    return with_layout_constraint(value, Layout(major_to_minor=tuple(range(value.ndim))))


def swap(stacked):
    return lax.all_to_all(stacked, "dp", 0, 0, tiled=True)


def spread_out_kernel(came_ref, pair_ref, last_ref, sum_ref):
    size = last_ref.shape[1]
    half = came_ref.shape[2] - 3 * size
    spot = pl.program_id(0)
    for at in range(2):
        pair_ref[at] = came_ref[0, :, at * size : (at + 1) * size].astype(jnp.float32)
    last_ref[...] = came_ref[0, :, 2 * size : 3 * size].astype(jnp.float32)
    piece = came_ref[0, :, 3 * size :].astype(jnp.float32)
    for core in range(2):
        lanes = slice(core * half, (core + 1) * half)

        @pl.when(spot == core)
        def _():
            sum_ref[:, lanes] = piece

        @pl.when((spot > 1) & (lax.rem(spot, 2) == core))
        def _():
            sum_ref[:, lanes] += piece


def spread_out(came, columns):
    spots, rows, _ = came.shape
    size, half = columns // 3, came.shape[2] - columns
    return pl.pallas_call(
        spread_out_kernel,
        grid=(spots,),
        in_specs=[pl.BlockSpec((1, rows, came.shape[2]), lambda i: (i, 0, 0))],
        out_specs=[
            pl.BlockSpec((2, rows, size), lambda i: (0, 0, i)),
            pl.BlockSpec((rows, size), lambda i: (0, i)),
            pl.BlockSpec((rows, 2 * half), lambda i: (0, 0)),
        ],
        out_shape=[
            jax.ShapeDtypeStruct((2, rows, spots * size), jnp.float32),
            jax.ShapeDtypeStruct((rows, spots * size), jnp.float32),
            jax.ShapeDtypeStruct((rows, 2 * half), jnp.float32),
        ],
        name="spread_out",
    )(came)


def chip_total(came):
    return jnp.sum(came.astype(jnp.float32), axis=0)


def after(value, *others):
    return lax.optimization_barrier((value,) + others)[0]


def grouped_body(
    counts,
    early_group,
    focus_group,
    late_group,
    hidden_in,
    seq_lengths,
    norm_gains,
    mixer_in,
    mixer_rows,
    conv_weight,
    conv_bias,
    step_bias,
    decay_log,
    skip_gain,
    early_gate_up,
    early_down,
    attention_in,
    attention_out,
    late_gate_up,
    late_down,
    output_grad,
):
    spots, ways = counts
    rows, width = hidden_in.shape
    share = rows // ways
    spot = lax.axis_index("dp")
    depth = lax.axis_index("tensor")
    core = spot % 2
    low = jnp.bfloat16

    def swapped_core(value):
        return lax.ppermute(value, "dp", [(at, at ^ 1) for at in range(spots)])

    own_rows = mixer_rows.shape[0]
    padded_rows = jnp.pad(mixer_rows, ((0, -own_rows % 16), (0, 0)))
    first_low, in_weights, row_weights = opening(
        hidden_in, norm_gains[0:1], mixer_in, padded_rows, spots, ways, 20
    )
    row_weights = row_weights[:, :own_rows]

    other_lengths = swapped_core(seq_lengths)
    lengths = jnp.where(
        core == 0, jnp.stack([seq_lengths, other_lengths]), jnp.stack([other_lengths, seq_lengths])
    )
    segs, starts = jax.vmap(lambda own: segment_info(own, rows))(lengths)
    flat_segs = (segs + jnp.arange(2, dtype=jnp.int32)[:, None] * rows).reshape(-1)
    keeping = 1.0 - starts.reshape(-1).astype(jnp.float32)
    groups = 2 * seq_lengths.shape[0]
    flat_lengths = lengths.reshape(2, -1)
    ends = jnp.cumsum(flat_lengths, axis=1) + jnp.arange(2, dtype=jnp.int32)[:, None] * rows
    firsts = (ends - flat_lengths).reshape(1, -1)
    ends = ends.reshape(1, -1)
    places = jnp.arange(2 * rows, dtype=jnp.int32)[:, None]
    age = places - jnp.max(jnp.where(firsts <= places, firsts, 0), axis=1, keepdims=True)
    left = jnp.min(jnp.where(ends > places, ends, 2 * rows), axis=1, keepdims=True) - 1 - places

    stream_zero = lax.dynamic_slice_in_dim(hidden_in, depth * share, share, 0).astype(jnp.float32)

    channels = conv_weight.shape[0] // 2

    def half(values):
        return lax.dynamic_slice_in_dim(values, core * channels, channels, 0)

    taps, offset, bias, decay, skip = [half(v) for v in (conv_weight, conv_bias, step_bias, decay_log, skip_gain)]
    in_mat = in_weights.reshape(width, 2 * channels)
    taps_t = taps.T
    row_mat = row_weights.reshape(-1, channels)
    early_blocks = [early_gate_up[0], early_gate_up[1], early_down]
    early_weights = swap(after(pull(spots, (early_blocks, early_group)), first_low))
    out_mat = row_mat[:width]
    select_mat = row_mat[width : width + PROJ_OUT]
    step_mat = row_mat[width + PROJ_OUT :]

    def spread_load(joints, size, stage):
        count = sum(one.shape[2] // size for one in joints)
        return Load(
            "exchange", joints, (count, joints[0].shape[1], spots * size), partial(spread_items, size), count, stage
        )

    def chip_load(joints, size, stage):
        count = sum(one.shape[2] // size for one in joints)
        out = (spots // 2, count, joints[0].shape[1], 2 * size)
        return Load("exchange", joints, out, partial(chip_items, size), count, stage)

    def by_spot(joint):
        return joint.astype(low).reshape(spots, -1, joint.shape[1])

    def mixed_sum(part, ident, name, loads=()):
        total, *came = edge("sum", part, [], ways, rows, 1, 0, 0, ident, name, loads=loads)
        return total[:, :PROJ_OUT], *came

    wide_select = jnp.pad(select_mat, ((0, 256 - PROJ_OUT), (0, 0)))
    conv_in, gate_half, channel_low, mix_part = front(first_low, in_mat, age, taps_t, offset[None], wide_select)
    mix_rows, = mixed_sum(mix_part, 1, "mix_sum")
    rank_low = mix_rows[:, :DT_RANK].astype(low)
    step_raw = project(rank_low, step_mat)
    rates_t = -jnp.exp(decay).T
    wide = (2 * rows, STATE, LANES)
    in_wide = jnp.broadcast_to(mix_rows[:, DT_RANK : DT_RANK + STATE, None], wide)
    out_wide = jnp.broadcast_to(mix_rows[:, DT_RANK + STATE :, None], wide)
    mixer_low = scan_forward(
        keeping, channel_low, step_raw, gate_half, bias, rates_t, skip, in_wide, out_wide, groups, LANES
    )
    early_mat = early_weights.reshape(width, -1)
    focus_blocks = [attention_in, attention_out]
    heads_width = attention_out.shape[1] // 2
    focus_pull = Load("first", focus_blocks, (spots, width // spots, 4 * heads_width), core_items, 4, 0)
    second_low, stream_one, focus_half = edge(
        "forward", project_t(mixer_low, out_mat).astype(low), [stream_zero, norm_gains[1:2]],
        ways, rows, 4, 0, early_group, 2, "edge_one", loads=[focus_pull],
    )

    def ffn(normed, mat):
        units = mat.shape[1] // 3
        both = project(normed, mat[:, : 2 * units])
        hidden = gated_unit(both[:, :units], both[:, units:]).astype(low)
        return project_t(hidden, mat[:, 2 * units :]).astype(low), both, hidden

    early_part, early_both, early_hidden = ffn(second_low, early_mat)
    third_low, stream_two, last_grad, focus_weights = edge(
        "forward", early_part, [stream_one, norm_gains[2:3], output_grad], ways, rows, 4, early_group, 0, 3, "edge_two",
        "gather", [Load("second", [focus_half], focus_half.shape, handed_items, 1, 1)],
    )
    focus_mat = focus_weights.reshape(width, -1)

    late_pull = Load(
        "exchange", [late_gate_up, late_down], (spots, width // spots, 3 * late_down.shape[1] // spots),
        partial(plane_items, spots), 3, 0,
    )
    down, side = flat_segs[:, None], flat_segs.reshape(2, rows)
    joint_low, attended_low = attend(project(third_low, focus_mat[:, : 3 * heads_width]), down, side, rows)
    fourth_low, stream_three, late_weights = edge(
        "forward", project_t(attended_low, focus_mat[:, 3 * heads_width :]).astype(low),
        [stream_two, norm_gains[3:4]], ways, rows, 4, 0, late_group, 4, "edge_three", loads=[late_pull],
    )

    late_mat = late_weights.reshape(width, -1)
    late_part, late_both, late_hidden = ffn(fourth_low, late_mat)

    def ffn_back(grad_low, normed, both, hidden, mat):
        units = mat.shape[1] // 3
        grad_hidden = project(grad_low, mat[:, 2 * units :])
        _, unit_back = jax.vjp(gated_unit, both[:, :units], both[:, units:])
        both_low = jnp.concatenate(unit_back(grad_hidden), axis=1).astype(low)
        grad_normed = project_t(both_low, mat[:, : 2 * units]).astype(low)
        return grad_normed, [by_spot(outer_rows(normed, both_low)), by_spot(outer_rows(grad_low, hidden))]

    grad_fourth, late_joints = ffn_back(last_grad, fourth_low, late_both, late_hidden, late_mat)
    grad_zero = lax.dynamic_slice_in_dim(output_grad, depth * share, share, 0).astype(jnp.float32)
    grad_low_three, grad_three, gain_four, output_part, late_down_swapped = edge(
        "backward", grad_fourth, [stream_three, norm_gains[3:4], grad_zero, late_part],
        ways, rows, 4, late_group, 0, 5, "edge_four", "reduce",
        [spread_load(late_joints[1:], late_joints[1].shape[2], 1)],
    )

    grad_attended = project(grad_low_three, focus_mat[:, 3 * heads_width :])
    joint_grad = attend_back(joint_low, grad_attended, down, side, rows)
    grad_low_two, grad_two, gain_three, late_swapped = edge(
        "backward", project_t(joint_grad, focus_mat[:, : 3 * heads_width]).astype(low),
        [stream_two, norm_gains[2:3], grad_three], ways, rows, 4, 0, early_group, 6, "edge_five",
        loads=[spread_load(late_joints[:1], late_joints[1].shape[2], 0)],
    )
    focus_joints = [by_spot(outer_rows(third_low, joint_grad)), by_spot(outer_rows(grad_low_three, attended_low))]

    grad_second, early_joints = ffn_back(grad_low_two, second_low, early_both, early_hidden, early_mat)
    grad_low_one, grad_one, gain_two, focus_swapped = edge(
        "backward", grad_second, [stream_one, norm_gains[1:2], grad_two],
        ways, rows, 4, early_group, 0, 7, "edge_six",
        loads=[chip_load(focus_joints[:1], heads_width, 1)],
    )
    early_joints = [in_order(one) for one in early_joints + focus_joints[1:]]
    early_swapped = swap(after(in_order(jnp.concatenate(early_joints, axis=2)), grad_low_one))

    grad_scanned = project(grad_low_one, out_mat)
    (
        grad_channel,
        grad_step_low,
        gate_low,
        in_sums,
        out_sums,
        bias_grad,
        decay_grad,
        skip_grad,
    ) = scan_backward(
        keeping, channel_low, step_raw, gate_half, grad_scanned, bias, rates_t, skip, in_wide, out_wide,
        groups, LANES,
    )
    grad_rank = project_t(grad_step_low, step_mat)
    gate_joint = outer_rows(first_low, gate_low).astype(low).reshape(spots, -1, channels)
    rest = mix_part[:, PROJ_OUT:]
    grad_rows, gate_swapped = mixed_sum(
        after(
            jnp.concatenate(
                [grad_rank, jnp.sum(in_sums, axis=-1), jnp.sum(out_sums, axis=-1), jnp.zeros_like(rest)], axis=1
            ),
            early_swapped,
        ),
        8, "mix_grad_sum",
        [chip_load([gate_joint], channels, 0)],
    )
    grad_rows_low = grad_rows.astype(low)
    rows_joint = jnp.concatenate(
        [
            outer_rows(grad_low_one, mixer_low),
            outer_rows(grad_rows_low, channel_low),
            outer_rows(rank_low, grad_step_low),
        ],
        axis=0,
    ).astype(low)
    grad_wide_low = jnp.pad(grad_rows_low, ((0, 0), (0, 256 - PROJ_OUT)))
    conv_low, conv_grads = front_back(
        conv_in, age, left, taps_t, offset[None], grad_channel, grad_wide_low, wide_select
    )
    conv_joint = outer_rows(first_low, conv_low).astype(low).reshape(spots, -1, channels)
    in_grad = jnp.concatenate([conv_low, gate_low], axis=1)
    grad_first = project_t(in_grad, in_mat).astype(low)
    rows_joint = rows_joint.reshape(spots, -1, channels)
    rows_joint = jnp.pad(rows_joint, ((0, 0), (0, -own_rows % 16), (0, 0)))
    lines = jnp.concatenate([conv_grads[: CONV + 1], bias_grad, skip_grad, decay_grad], axis=0)
    lines = jnp.pad(lines, ((0, 1), (0, 0)))
    blank = jnp.zeros_like(lines)
    lines = jnp.where(core == 0, jnp.concatenate([lines, blank], axis=1), jnp.concatenate([blank, lines], axis=1))
    gains = jnp.concatenate([jnp.zeros_like(gain_two), gain_two, gain_three, gain_four], axis=0)
    small = jnp.concatenate([lines, gains.reshape(8, -1)], axis=0)
    input_grad, small, output, conv_swapped, rows_swapped = edge(
        "last", grad_first, [stream_zero, norm_gains[0:1], grad_one, small, output_part, stream_three],
        ways, rows, 4, 0, None, 9, "edge_seven",
        loads=[chip_load([conv_joint], channels, 0), chip_load([rows_joint], channels, 0)],
    )
    lines = small[: CONV + 3 + STATE]
    gains = small[-8:].reshape(norm_gains.shape)
    early_gate_up_grad, early_down_grad, focus_out_grad = spread_out(early_swapped, 3 * early_down.shape[1] // spots)
    return (
        output,
        input_grad,
        gains,
        jnp.stack([chip_total(conv_swapped[:, 0]), chip_total(gate_swapped[:, 0])]),
        chip_total(rows_swapped[:, 0, :own_rows]),
        lines[:CONV].T,
        lines[CONV],
        lines[CONV + 1],
        lines[CONV + 3 :].T,
        lines[CONV + 2],
        early_gate_up_grad,
        early_down_grad,
        chip_total(focus_swapped),
        focus_out_grad,
        late_swapped.astype(jnp.float32),
        late_down_swapped[0].astype(jnp.float32),
    )


def solution(mesh):
    counts = (mesh.shape["dp"], mesh.shape["tensor"])
    chosen = partial(grouped_body, counts, 6, 0, 6) if counts == (8, 4) else body
    return jax.shard_map(
        chosen,
        mesh=mesh,
        in_specs=(
            P("dp", None),
            P("dp", None),
            P(),
            P(None, "dp", "tensor"),
            P("dp", "tensor"),
            P("tensor", None),
            P("tensor"),
            P("tensor"),
            P("tensor", None),
            P("tensor"),
            P(None, "dp", "tensor"),
            P("dp", "tensor"),
            P(None, "dp", "tensor"),
            P("dp", "tensor"),
            P(None, "dp", "tensor"),
            P("dp", "tensor"),
            P("dp", None),
        ),
        out_specs=(
            P("dp", None),
            P("dp", None),
            P(),
            P(None, "dp", "tensor"),
            P("dp", "tensor"),
            P("tensor", None),
            P("tensor"),
            P("tensor"),
            P("tensor", None),
            P("tensor"),
            P(None, "dp", "tensor"),
            P("dp", "tensor"),
            P(None, "dp", "tensor"),
            P("dp", "tensor"),
            P(None, "dp", "tensor"),
            P("dp", "tensor"),
        ),
        check_vma=False,
    )
```

```python
from functools import partial
import math

import jax
import jax.numpy as jnp
from jax import lax
from jax.experimental import pallas as pl
from jax.experimental.layout import Layout, with_layout_constraint
from jax.experimental.pallas import tpu as pltpu
from jax.sharding import PartitionSpec as P

STATE = 16
CONV = 4
DT_RANK = 128
HEAD_DIM = 128
WINDOW = 2048
PROJ_OUT = 160


EPS = 1e-05
NEG_FILL = -1e30


def project(left, right):
    return jnp.dot(left, right, preferred_element_type=jnp.float32)


def project_t(left, right):
    return lax.dot_general(
        left, right, (((1,), (1,)), ((), ())), preferred_element_type=jnp.float32
    )


def outer_rows(left, right):
    return lax.dot_general(
        left, right, (((0,), (0,)), ((), ())), preferred_element_type=jnp.float32
    )


def rms_norm(values, weight):
    return values * lax.rsqrt(jnp.mean(values * values, axis=-1, keepdims=True) + EPS) * weight


def segment_info(lengths, tokens):
    flat_lengths = lengths.reshape(-1)
    ends = jnp.cumsum(flat_lengths, dtype=jnp.int32)
    firsts = ends - flat_lengths
    places = jnp.arange(tokens, dtype=jnp.int32)
    segs = jnp.sum((places[:, None] >= ends[None, :]).astype(jnp.int32), axis=1)
    starts = jnp.any(places[:, None] == firsts[None, :], axis=1)
    return (segs, starts)


def allowed_pairs(segs):
    places = jnp.arange(segs.shape[-1], dtype=jnp.int32)
    distance = places[:, None] - places[None, :]
    return (segs[:, None] == segs[None, :]) & (distance >= 0) & (distance < WINDOW)


def causal_conv(segs, stream, weight, offset):
    total = offset + stream * weight[:, 0]
    for lag_step in range(1, CONV):
        moved = jnp.concatenate(
            [jnp.zeros_like(stream[..., :lag_step, :]), stream[..., :-lag_step, :]], axis=-2
        )
        moved_segs = jnp.concatenate(
            [jnp.full_like(segs[..., :lag_step], -1), segs[..., :-lag_step]], axis=-1
        )
        linked = (segs == moved_segs).astype(stream.dtype)
        total = total + moved * weight[:, lag_step] * linked[..., None]
    return jax.nn.silu(total)


LANES = 128


def softplus(v):
    return jnp.maximum(v, 0.0) + jnp.log1p(jnp.exp(-jnp.abs(v)))


def scan_forward_kernel(
    groups, length, keep_ref, chan_ref, raw_ref, gate_ref, bias_ref, rate_ref, skip_ref, in_ref, out_ref,
    mixed_ref, step_s, drive_s, y_s,
):
    width = chan_ref.shape[1]
    blocks = width // LANES
    step_s[...] = softplus(raw_ref[...] + bias_ref[...])
    drive_s[...] = step_s[...] * chan_ref[...].astype(jnp.float32)
    rates = [rate_ref[:, pl.ds(b * LANES, LANES)] for b in range(blocks)]

    def advance(t, states):
        fresh = []
        for g in range(groups):
            row = g * length + t
            keep = keep_ref[row]
            input_map = in_ref[row]
            output_map = out_ref[row]
            for b in range(blocks):
                lanes = pl.ds(b * LANES, LANES)
                decay = jnp.exp(step_s[pl.ds(row, 1), lanes] * rates[b]) * keep
                state = decay * states[g * blocks + b] + drive_s[pl.ds(row, 1), lanes] * input_map
                y_s[pl.ds(row, 1), lanes] = jnp.sum(state * output_map, axis=0, keepdims=True)
                fresh.append(state)
        return tuple(fresh)

    zero = jnp.zeros((STATE, LANES), jnp.float32)
    lax.fori_loop(0, length, advance, (zero,) * (groups * blocks))
    gate = gate_ref[...]
    silu = gate / (1.0 + jnp.exp(-gate))
    mixed_ref[...] = (
        (y_s[...] + skip_ref[...] * chan_ref[...].astype(jnp.float32)) * silu
    ).astype(mixed_ref.dtype)


def scan_forward(keep, channel, step_raw, gate_half, step_bias, rates_t, skip_gain, in_wide, out_wide, groups, width):
    tokens, channels = channel.shape
    column = pl.BlockSpec((tokens, width), lambda i: (0, i))
    row = pl.BlockSpec((1, width), lambda i: (0, i))
    maps = pl.BlockSpec((tokens, STATE, LANES), lambda i: (0, 0, 0))
    return pl.pallas_call(
        partial(scan_forward_kernel, groups, tokens // groups),
        grid=(channels // width,),
        in_specs=[
            pl.BlockSpec(memory_space=pltpu.SMEM), column, column, column, row,
            pl.BlockSpec((STATE, width), lambda i: (0, i)), row, maps, maps,
        ],
        out_specs=column,
        out_shape=jax.ShapeDtypeStruct((tokens, channels), jnp.bfloat16),
        scratch_shapes=[pltpu.VMEM((tokens, width), jnp.float32)] * 3,
        compiler_params=pltpu.CompilerParams(vmem_limit_bytes=48 << 20),
        cost_estimate=pl.CostEstimate(flops=1, bytes_accessed=1 << 34, transcendentals=0),
        name="scan_forward",
    )(keep, channel, step_raw, gate_half, step_bias[None], rates_t, skip_gain[None], in_wide, out_wide)


def scan_backward_kernel(
    groups, length, keep_ref, chan_ref, raw_ref, gate_ref, dmix_ref, bias_ref, rate_ref, skip_ref, in_ref, out_ref,
    dchan_ref, draw_ref, dgate_ref, din_ref, dout_ref, dbias_ref, drate_ref, dskip_ref,
    step_s, drive_s, y_s, dy_s, dd_s, ds_s, state_s, decay_s,
):
    width = chan_ref.shape[1]
    blocks = width // LANES
    chan = chan_ref[...].astype(jnp.float32)
    step_s[...] = softplus(raw_ref[...] + bias_ref[...])
    drive_s[...] = step_s[...] * chan
    gate = gate_ref[...]
    sig = 1.0 / (1.0 + jnp.exp(-gate))
    dy_s[...] = dmix_ref[...] * (gate * sig)
    rates = [rate_ref[:, pl.ds(b * LANES, LANES)] for b in range(blocks)]

    @pl.when(pl.program_id(0) == 0)
    def _():
        din_ref[...] = jnp.zeros_like(din_ref)
        dout_ref[...] = jnp.zeros_like(dout_ref)

    def advance(t, states):
        fresh = []
        for g in range(groups):
            row = g * length + t
            keep = keep_ref[row]
            input_map = in_ref[row]
            output_map = out_ref[row]
            total = None
            for b in range(blocks):
                lanes = pl.ds(b * LANES, LANES)
                decay = jnp.exp(step_s[pl.ds(row, 1), lanes] * rates[b]) * keep
                decay_s[row, :, lanes] = decay
                carried = decay * states[g * blocks + b]
                state_s[row, :, lanes] = carried
                state = carried + drive_s[pl.ds(row, 1), lanes] * input_map
                y_s[pl.ds(row, 1), lanes] = jnp.sum(state * output_map, axis=0, keepdims=True)
                term = state * dy_s[pl.ds(row, 1), lanes]
                total = term if total is None else total + term
                fresh.append(state)
            dout_ref[row] += total
        return tuple(fresh)

    zero = jnp.zeros((STATE, LANES), jnp.float32)
    count = groups * blocks
    lax.fori_loop(0, length, advance, (zero,) * count)

    def retreat(back, carry):
        t = length - 1 - back
        fresh, rate_sums = [], []
        for g in range(groups):
            row = g * length + t
            input_map = in_ref[row]
            output_map = out_ref[row]
            total = None
            for b in range(blocks):
                lanes = pl.ds(b * LANES, LANES)
                at = g * blocks + b
                dstate = carry[0][at] + dy_s[pl.ds(row, 1), lanes] * output_map
                dlog = dstate * state_s[row, :, lanes]
                dd_s[pl.ds(row, 1), lanes] = jnp.sum(dstate * input_map, axis=0, keepdims=True)
                ds_s[pl.ds(row, 1), lanes] = jnp.sum(dlog * rates[b], axis=0, keepdims=True)
                term = dstate * drive_s[pl.ds(row, 1), lanes]
                total = term if total is None else total + term
                rate_sums.append(carry[1][at] + dlog * step_s[pl.ds(row, 1), lanes])
                fresh.append(dstate * decay_s[row, :, lanes])
            din_ref[row] += total
        return (tuple(fresh), tuple(rate_sums))

    _, rate_sums = lax.fori_loop(0, length, retreat, ((zero,) * count, (zero,) * count))
    for b in range(blocks):
        lanes = pl.ds(b * LANES, LANES)
        drate_ref[:, lanes] = rates[b] * sum(rate_sums[g * blocks + b] for g in range(groups))
    direct = y_s[...] + skip_ref[...] * chan
    dgate_ref[...] = (dmix_ref[...] * direct * (sig * (1.0 + gate * (1.0 - sig)))).astype(dgate_ref.dtype)
    dskip_ref[...] = jnp.sum(dy_s[...] * chan, axis=0, keepdims=True)
    dchan_ref[...] = dd_s[...] * step_s[...] + skip_ref[...] * dy_s[...]
    shifted = raw_ref[...] + bias_ref[...]
    draw = (ds_s[...] + dd_s[...] * chan) / (1.0 + jnp.exp(-shifted))
    draw_ref[...] = draw.astype(draw_ref.dtype)
    dbias_ref[...] = jnp.sum(draw, axis=0, keepdims=True)


def scan_backward(
    keep, channel, step_raw, gate_half, dmixed, step_bias, rates_t, skip_gain, in_wide, out_wide, groups, width
):
    tokens, channels = channel.shape
    column = pl.BlockSpec((tokens, width), lambda i: (0, i))
    row = pl.BlockSpec((1, width), lambda i: (0, i))
    states = pl.BlockSpec((STATE, width), lambda i: (0, i))
    maps = pl.BlockSpec((tokens, STATE, LANES), lambda i: (0, 0, 0))
    sheet = jax.ShapeDtypeStruct((tokens, channels), jnp.float32)
    low = jax.ShapeDtypeStruct((tokens, channels), jnp.bfloat16)
    wide = jax.ShapeDtypeStruct((tokens, STATE, LANES), jnp.float32)
    line = jax.ShapeDtypeStruct((1, channels), jnp.float32)
    return pl.pallas_call(
        partial(scan_backward_kernel, groups, tokens // groups),
        grid=(channels // width,),
        in_specs=[
            pl.BlockSpec(memory_space=pltpu.SMEM), column, column, column, column, row, states, row, maps, maps,
        ],
        out_specs=[column, column, column, maps, maps, row, states, row],
        out_shape=[
            sheet, low, low, wide, wide, line, jax.ShapeDtypeStruct((STATE, channels), jnp.float32), line,
        ],
        scratch_shapes=[pltpu.VMEM((tokens, width), jnp.float32)] * 6
        + [pltpu.VMEM((tokens, STATE, width), jnp.float32)] * 2,
        compiler_params=pltpu.CompilerParams(vmem_limit_bytes=56 << 20),
        cost_estimate=pl.CostEstimate(flops=1, bytes_accessed=1 << 34, transcendentals=0),
        name="scan_backward",
    )(keep, channel, step_raw, gate_half, dmixed, step_bias[None], rates_t, skip_gain[None], in_wide, out_wide)


def attention_scores(query, keys, allowed):
    scores = jnp.einsum("qhd,khd->hqk", query, keys, preferred_element_type=jnp.float32) * (
        1.0 / math.sqrt(HEAD_DIM)
    )
    return jnp.where(allowed[None], scores, NEG_FILL)


def attention_forward(query, keys, values, allowed):
    scores = attention_scores(query, keys, allowed)
    row_max = jnp.max(scores, axis=-1, keepdims=True)
    shifted = jnp.exp(scores - row_max)
    totals = jnp.sum(shifted, axis=-1, keepdims=True)
    probs = shifted / totals
    mixed = jnp.einsum(
        "hqk,khd->qhd", probs.astype(jnp.bfloat16), values, preferred_element_type=jnp.float32
    )
    return (mixed, row_max + jnp.log(totals))


def attention_backward(query, keys, values, allowed, log_total, grad_mixed):
    scale = 1.0 / math.sqrt(HEAD_DIM)
    probs = jnp.exp(attention_scores(query, keys, allowed) - log_total)
    grad_values = jnp.einsum(
        "hqk,qhd->khd", probs.astype(jnp.bfloat16), grad_mixed, preferred_element_type=jnp.float32
    )
    grad_probs = jnp.einsum("qhd,khd->hqk", grad_mixed, values, preferred_element_type=jnp.float32)
    inner_sum = jnp.sum(probs * grad_probs, axis=-1, keepdims=True)
    grad_scores = (probs * (grad_probs - inner_sum)).astype(jnp.bfloat16)
    grad_query = (
        jnp.einsum("hqk,khd->qhd", grad_scores, keys, preferred_element_type=jnp.float32) * scale
    )
    grad_keys = (
        jnp.einsum("hqk,qhd->khd", grad_scores, query, preferred_element_type=jnp.float32) * scale
    )
    return (grad_query, grad_keys, grad_values)


def gated_unit(gate, upward):
    return jax.nn.silu(gate) * upward


def ffn_forward(normed_low, gate_up, down_mat):
    gate = project(normed_low, gate_up[0])
    upward = project(normed_low, gate_up[1])
    hidden = gated_unit(gate, upward).astype(jnp.bfloat16)
    return (project_t(hidden, down_mat), gate, upward, hidden)


def ffn_backward(grad_low, normed_low, gate, upward, hidden, gate_up, down_mat):
    grad_hidden = project(grad_low, down_mat)
    down_grad = outer_rows(grad_low, hidden)
    _, unit_back = jax.vjp(gated_unit, gate, upward)
    grad_gate, grad_up = unit_back(grad_hidden)
    gate_low = grad_gate.astype(jnp.bfloat16)
    up_low = grad_up.astype(jnp.bfloat16)
    joined_grad = outer_rows(normed_low, jnp.concatenate([gate_low, up_low], axis=1))
    grad_normed = project_t(gate_low, gate_up[0]) + project_t(up_low, gate_up[1])
    return (grad_normed, joined_grad, down_grad)


def flatten_low(grad_heads, tokens):
    return grad_heads.astype(jnp.bfloat16).reshape(tokens, -1)


def collect(stacked, row_block):
    return (
        lax.all_gather(stacked, "dp", axis=1, tiled=True),
        lax.all_gather(row_block, "dp", axis=0, tiled=True),
    )


def spread_grads(joined, row_block, count):
    summed = (
        lax.psum_scatter(joined.astype(jnp.bfloat16), "dp", scatter_dimension=0, tiled=True),
        lax.psum_scatter(row_block.astype(jnp.bfloat16), "dp", scatter_dimension=0, tiled=True),
    )
    rows_here = summed[0].shape[0]
    restacked = jnp.transpose(summed[0].reshape(rows_here, count, -1), (1, 0, 2))
    return (restacked.astype(jnp.float32), summed[1].astype(jnp.float32))


def branch_total(piece_sum):
    return lax.psum(piece_sum, "tensor")


def input_total(piece_sum):
    return lax.psum(piece_sum, "tensor")


def body(
    hidden_in,
    seq_lengths,
    norm_gains,
    mixer_in,
    mixer_rows,
    conv_weight,
    conv_bias,
    step_bias,
    decay_log,
    skip_gain,
    early_gate_up,
    early_down,
    attention_in,
    attention_out,
    late_gate_up,
    late_down,
    output_grad,
):
    tokens = hidden_in.shape[0]
    width = hidden_in.shape[1]
    segs, starts = segment_info(seq_lengths, tokens)
    allowed = allowed_pairs(segs)
    stream_zero = hidden_in.astype(jnp.float32)
    mixer_stack, mixer_mats = collect(mixer_in, mixer_rows)
    first_normed, first_back = jax.vjp(rms_norm, stream_zero, norm_gains[0])
    first_low = first_normed.astype(jnp.bfloat16)
    conv_in = project(first_low, mixer_stack[0])
    gate_half = project(first_low, mixer_stack[1])
    channel_full, conv_back = jax.vjp(partial(causal_conv, segs), conv_in, conv_weight, conv_bias)
    channel_low = channel_full.astype(jnp.bfloat16)
    mix_rows = lax.psum(project_t(channel_low, mixer_mats[width : width + PROJ_OUT]), "tensor")
    rank_low = mix_rows[:, :DT_RANK].astype(jnp.bfloat16)
    step_raw = project(rank_low, mixer_mats[width + PROJ_OUT :])
    groups = seq_lengths.shape[0]
    keeping = 1.0 - starts.astype(jnp.float32)
    rates_t = -jnp.exp(decay_log).T
    wide = (tokens, STATE, LANES)
    in_wide = jnp.broadcast_to(mix_rows[:, DT_RANK : DT_RANK + STATE, None], wide)
    out_wide = jnp.broadcast_to(mix_rows[:, DT_RANK + STATE :, None], wide)
    mixer_low = scan_forward(
        keeping, channel_low, step_raw, gate_half, step_bias, rates_t, skip_gain, in_wide, out_wide, groups, LANES
    )
    stream_one = stream_zero + branch_total(project_t(mixer_low, mixer_mats[:width]))
    early_stack, early_mat = collect(early_gate_up, early_down)
    second_normed, second_back = jax.vjp(rms_norm, stream_one, norm_gains[1])
    second_low = second_normed.astype(jnp.bfloat16)
    early_part, early_gate, early_up, early_hidden = ffn_forward(second_low, early_stack, early_mat)
    stream_two = stream_one + branch_total(early_part)
    focus_stack, focus_mat = collect(attention_in, attention_out)
    heads_here = focus_stack.shape[2] // HEAD_DIM
    third_normed, third_back = jax.vjp(rms_norm, stream_two, norm_gains[2])
    third_low = third_normed.astype(jnp.bfloat16)
    query = (
        project(third_low, focus_stack[0])
        .astype(jnp.bfloat16)
        .reshape(tokens, heads_here, HEAD_DIM)
    )
    keys = (
        project(third_low, focus_stack[1])
        .astype(jnp.bfloat16)
        .reshape(tokens, heads_here, HEAD_DIM)
    )
    values = (
        project(third_low, focus_stack[2])
        .astype(jnp.bfloat16)
        .reshape(tokens, heads_here, HEAD_DIM)
    )
    attended, log_total = attention_forward(query, keys, values, allowed)
    attended_low = attended.reshape(tokens, heads_here * HEAD_DIM).astype(jnp.bfloat16)
    stream_three = stream_two + branch_total(project_t(attended_low, focus_mat))
    late_stack, late_mat = collect(late_gate_up, late_down)
    fourth_normed, fourth_back = jax.vjp(rms_norm, stream_three, norm_gains[3])
    fourth_low = fourth_normed.astype(jnp.bfloat16)
    late_part, late_gate, late_up, late_hidden = ffn_forward(fourth_low, late_stack, late_mat)
    output = stream_three + branch_total(late_part)
    grad_three = output_grad.astype(jnp.float32)
    late_pair = (late_stack, late_mat)
    grad_fourth, late_joined, late_mat_grad = ffn_backward(
        output_grad, fourth_low, late_gate, late_up, late_hidden, late_pair[0], late_pair[1]
    )
    grad_stream, gain_four = fourth_back(input_total(grad_fourth))
    grad_three = grad_three + grad_stream
    late_grads = spread_grads(late_joined, late_mat_grad, 2)
    focus_pair = (focus_stack, focus_mat)
    grad_branch_low = grad_three.astype(jnp.bfloat16)
    focus_mat_grad = outer_rows(grad_branch_low, attended_low)
    grad_attended = (
        project(grad_branch_low, focus_pair[1])
        .astype(jnp.bfloat16)
        .reshape(tokens, heads_here, HEAD_DIM)
    )
    grad_query, grad_keys, grad_values = attention_backward(
        query, keys, values, allowed, log_total, grad_attended
    )
    query_low = flatten_low(grad_query, tokens)
    keys_low = flatten_low(grad_keys, tokens)
    values_low = flatten_low(grad_values, tokens)
    focus_joined = outer_rows(third_low, jnp.concatenate([query_low, keys_low, values_low], axis=1))
    grad_third = (
        project_t(query_low, focus_pair[0][0])
        + project_t(keys_low, focus_pair[0][1])
        + project_t(values_low, focus_pair[0][2])
    )
    grad_stream, gain_three = third_back(input_total(grad_third))
    grad_two = grad_three + grad_stream
    focus_grads = spread_grads(focus_joined, focus_mat_grad, 3)
    early_pair = (early_stack, early_mat)
    grad_second, early_joined, early_mat_grad = ffn_backward(
        grad_two.astype(jnp.bfloat16),
        second_low,
        early_gate,
        early_up,
        early_hidden,
        early_pair[0],
        early_pair[1],
    )
    grad_stream, gain_two = second_back(input_total(grad_second))
    grad_one = grad_two + grad_stream
    early_grads = spread_grads(early_joined, early_mat_grad, 2)
    mixer_pair = (mixer_stack, mixer_mats)
    grad_mixer_low = grad_one.astype(jnp.bfloat16)
    out_mat_grad = outer_rows(grad_mixer_low, mixer_low)
    grad_scanned = project(grad_mixer_low, mixer_pair[1][:width])
    (
        grad_channel,
        grad_step_low,
        gate_low,
        in_sums,
        out_sums,
        step_bias_grad,
        decay_log_grad,
        skip_gain_grad,
    ) = scan_backward(
        keeping, channel_low, step_raw, gate_half, grad_scanned, step_bias, rates_t, skip_gain, in_wide, out_wide,
        groups, LANES,
    )
    step_mat_grad = outer_rows(rank_low, grad_step_low)
    grad_rank = project_t(grad_step_low, mixer_pair[1][width + PROJ_OUT :])
    grad_rows = lax.psum(
        jnp.concatenate([grad_rank, jnp.sum(in_sums, axis=-1), jnp.sum(out_sums, axis=-1)], axis=1), "tensor"
    )
    grad_rows_low = grad_rows.astype(jnp.bfloat16)
    select_mat_grad = outer_rows(grad_rows_low, channel_low)
    grad_channel = grad_channel + project(grad_rows_low, mixer_pair[1][width : width + PROJ_OUT])
    grad_conv_in, conv_weight_grad, conv_bias_grad = conv_back(grad_channel)
    conv_low = grad_conv_in.astype(jnp.bfloat16)
    mixer_joined = outer_rows(first_low, jnp.concatenate([conv_low, gate_low], axis=1))
    grad_first = project_t(conv_low, mixer_pair[0][0]) + project_t(gate_low, mixer_pair[0][1])
    grad_stream, gain_one = first_back(input_total(grad_first))
    input_grad = grad_one + grad_stream
    mixer_grads = spread_grads(
        mixer_joined, jnp.concatenate([out_mat_grad, select_mat_grad, step_mat_grad], axis=0), 2
    )
    small_sums = lax.psum(
        (
            jnp.stack([gain_one, gain_two, gain_three, gain_four]),
            conv_weight_grad,
            conv_bias_grad,
            step_bias_grad[0],
            decay_log_grad.T,
            skip_gain_grad[0],
        ),
        "dp",
    )
    return (
        output,
        input_grad,
        small_sums[0],
        mixer_grads[0],
        mixer_grads[1],
        small_sums[1],
        small_sums[2],
        small_sums[3],
        small_sums[4],
        small_sums[5],
        early_grads[0],
        early_grads[1],
        focus_grads[0],
        focus_grads[1],
        late_grads[0],
        late_grads[1],
    )


MESH = pl.DeviceIdType.MESH


def turns(group):
    return [turned for turned in (6, 2, 4) if turned & group == turned]


class Place:
    def __init__(self, ways):
        self.spot = lax.axis_index("dp")
        self.depth = lax.axis_index("tensor")
        self.ways = ways
        self.core = lax.rem(self.spot, 2)
        self.partner = self.spot + 1 - 2 * self.core

    def bit(self, axis, turned):
        value = lax.rem(self.spot // axis, 2)
        return 1 - value if turned & axis else value

    def across(self, turned, swapped=False):
        move = 1 - 2 * self.core if swapped else 0
        for axis in (2, 4):
            if turned & axis:
                move = move + axis * (1 - 2 * self.bit(axis, 0))
        return self.spot + move

    def side(self, group, turned=0):
        if group == 6:
            return self.bit(2, turned) + 2 * self.bit(4, turned)
        return self.bit(group, turned) if group else 0

    def along(self, offset):
        return lax.rem(self.depth + offset, self.ways)


def send(source, target, sems, at, spot, depth):
    copy = pltpu.make_async_remote_copy(
        src_ref=source,
        dst_ref=target,
        send_sem=sems[0].at[at],
        recv_sem=sems[1].at[at],
        device_id=(spot, depth),
        device_id_type=MESH,
    )
    copy.start()
    return copy


def greet(place, ways, both=False):
    barrier = pltpu.get_barrier_semaphore()
    peers = [(place.partner, place.depth)]
    peers += [(place.across(turned), place.depth) for turned in ways]
    if both:
        peers += [(place.across(turned, True), place.depth) for turned in ways]
    peers += [(place.spot, place.along(offset)) for offset in range(1, place.ways)]
    for peer in peers:
        pl.semaphore_signal(barrier, inc=1, device_id=peer, device_id_type=MESH)
    pl.semaphore_wait(barrier, len(peers))


def rows_at(start, size, unit):
    return pl.ds(pl.multiple_of(start * unit, unit), size)


class Reduction:
    def __init__(self, place, group, rows, parts, part_ref, near_s, sum_s, far_s, sems, names):
        self.place, self.group, self.rows, self.parts = place, group, rows, parts
        self.part_ref, self.near_s, self.sum_s, self.far_s = part_ref, near_s, sum_s, far_s
        self.sems = [sems[name] for name in names]
        self.ways = turns(group) + [0]
        self.step = part_ref.shape[1] // parts
        self.near, self.far = {}, {}

    def lanes(self, part):
        return pl.ds(part * self.step, self.step)

    def block(self, side):
        return rows_at(side, self.rows, self.rows)

    def send_near(self):
        place = self.place
        for part in range(self.parts):
            for at, turned in enumerate(self.ways):
                side = place.side(self.group, turned)
                self.near[part, turned] = send(
                    self.part_ref.at[self.block(side * 2 + 1 - place.core), self.lanes(part)],
                    self.near_s.at[self.block(side), self.lanes(part)],
                    self.sems[0], part * len(self.ways) + at, place.partner, place.depth,
                )

    def joined(self, part, turned):
        self.near[part, turned].wait_recv()
        side, lanes = self.place.side(self.group, turned), self.lanes(part)
        own = self.part_ref[self.block(side * 2 + self.place.core), lanes].astype(jnp.float32)
        return own + self.near_s[self.block(side), lanes].astype(jnp.float32)

    def order(self):
        half = self.parts // 2
        return [at + first for at in range(half) for first in (0, half)]

    def leg(self, part):
        return (2, 4) if part < self.parts // 2 else (4, 2)

    def push(self, part, turned, slot, to, value):
        rows, lanes = self.block(self.place.side(self.group, turned)), self.lanes(part)
        self.sum_s[rows, lanes] = value.astype(self.sum_s.dtype)
        self.far[part, slot] = send(
            self.sum_s.at[rows, lanes], self.far_s.at[slot, :, lanes],
            self.sems[1], part * 3 + slot, self.place.across(to), self.place.depth,
        )

    def came(self, part, slot):
        self.far[part, slot].wait_recv()
        return self.far_s[slot, :, self.lanes(part)].astype(jnp.float32)

    def send_far(self):
        if self.group:
            for part in self.order():
                first, _ = self.leg(part)
                self.push(part, 6, 1, first, self.joined(part, 6))
                self.push(part, first, 0, first, self.joined(part, first))

    def relay(self):
        if self.group:
            for part in self.order():
                _, second = self.leg(part)
                value = self.joined(part, second) + self.came(part, 1)
                self.push(part, second, 2, second, value)

    def chip_sum(self, part):
        total = self.joined(part, 0)
        if self.group:
            total = total + self.came(part, 0) + self.came(part, 2)
        return total

    def sent(self):
        return list(self.near.values()) + list(self.far.values())


def deep_sends(place, share, source, start, deep_s, lanes, sems, at):
    return [
        send(
            source.at[pl.ds(pl.multiple_of(start + place.along(offset) * share, share), share), lanes],
            deep_s.at[offset - 1, :, lanes],
            sems, at + offset - 1, place.spot, place.along(offset),
        )
        for offset in range(1, place.ways)
    ]


def deep_total(place, share, source, start, deep_s, copies):
    for copy in copies:
        copy.wait_recv()
    total = source[pl.ds(pl.multiple_of(start + place.depth * share, share), share), :].astype(jnp.float32)
    for offset in range(1, place.ways):
        total = total + deep_s[offset - 1].astype(jnp.float32)
    return total


def reduce_stage(first, deep_s, sems, between):
    place, rows = first.place, first.rows
    share = rows // place.ways
    first.send_near()
    between(0)
    first.send_far()
    first.relay()
    between(1)
    deep = []
    mine = place.side(first.group)
    for part in first.order() if first.group else range(first.parts):
        first.sum_s[first.block(mine), first.lanes(part)] = first.chip_sum(part).astype(first.sum_s.dtype)
        deep += deep_sends(
            place, share, first.sum_s, mine * rows, deep_s, first.lanes(part), sems["deep"], part * (place.ways - 1)
        )
    return deep_total(place, share, first.sum_s, mine * rows, deep_s, deep), first.sent() + deep


def hand_on(place, group, rows_of, target, sems, base, far):
    half = target.shape[1] // 2
    for came, to, lanes in ((2, 4, pl.ds(0, half)), (4, 2, pl.ds(half, half))):
        far[came].wait_recv()
        block = target.at[rows_of(came), lanes]
        far[came, to] = send(block, block, sems, base + to // 2 + 1, place.across(to), place.depth)


def first_leg(place, block, sems, base):
    return {turned: send(block, block, sems, base + turned // 2 - 1, place.across(turned), place.depth) for turned in (2, 4)}


def gather_stage(place, group, rows, all_ref, sems, between):
    share = rows // place.ways

    def place_of(turned, offset):
        depth = place.along(place.ways - offset) if offset else place.depth
        return pl.ds(pl.multiple_of((place.side(group, turned) * 2 + place.core) * rows + depth * share, share), share)

    def to_partner(turned, offset, at):
        block = all_ref.at[place_of(turned, offset), :]
        return send(block, block, sems["near_back"], at * place.ways + offset, place.partner, place.depth)

    own = all_ref.at[place_of(0, 0), :]
    deep = [
        send(own, own, sems["deep_back"], offset - 1, place.spot, place.along(offset)) for offset in range(1, place.ways)
    ]
    far, near = [], []
    for offset in range(place.ways):
        if offset:
            deep[offset - 1].wait_recv()
        if group:
            far.append(first_leg(place, all_ref.at[place_of(0, offset), :], sems["far_back"], 4 * offset))
        near.append(to_partner(0, offset, 0))
        if offset == 0:
            between()
    if group:
        for offset in range(place.ways):
            hand_on(
                place, group, lambda turned: place_of(turned, offset), all_ref, sems["far_back"], 4 * offset, far[offset]
            )
            near.append(to_partner(2, offset, 1))
            near.append(to_partner(4, offset, 2))
        for offset in range(place.ways):
            far[offset][2, 4].wait_recv()
            far[offset][4, 2].wait_recv()
            near.append(to_partner(6, offset, 3))
    for copy in near:
        copy.wait_recv()
    return deep + [copy for one in far for copy in one.values()] + near


class Exchange:
    def __init__(self, place, items, sems):
        self.place, self.items, self.sems = place, items, sems
        self.copies, self.own = [], []

    def start(self):
        place = self.place
        spots = [place.across(turned, swapped) for turned in (6, 2, 4) for swapped in (False, True)] + [place.partner]
        for at, (source, target) in enumerate(self.items):
            for slot, spot in enumerate(spots):
                self.copies.append(
                    send(source(spot), target(place.spot), self.sems, at * 8 + slot, spot, place.depth)
                )
            own = pltpu.make_async_copy(source(place.spot), target(place.spot), self.sems[1].at[at * 8 + 7])
            own.start()
            self.own.append(own)

    def close(self):
        for copy in self.own + self.copies:
            copy.wait()


def columns_at(half, size):
    return pl.ds(pl.multiple_of(half * size, size), size)


def blocks_of(refs, size):
    return [(ref, at) for ref in refs for at in range(ref.shape[2] // size)]


def spread_items(size, refs, out):
    return [
        (
            lambda spot, ref=ref, at=at: ref.at[spot, :, pl.ds(at * size, size)],
            lambda spot, to=to: out.at[to, :, columns_at(spot, size)],
        )
        for to, (ref, at) in enumerate(blocks_of(refs, size))
    ]


def chip_items(size, refs, out):
    return [
        (
            lambda spot, ref=ref, at=at: ref.at[spot, :, pl.ds(at * size, size)],
            lambda spot, to=to: out.at[spot // 2, to, :, columns_at(spot % 2, size)],
        )
        for to, (ref, at) in enumerate(blocks_of(refs, size))
    ]


def layers(refs):
    return [ref.at[at] if len(ref.shape) == 3 else ref for ref in refs for at in range(ref.shape[0] if len(ref.shape) == 3 else 1)]


def plane_items(spots, refs, out):
    blocks = layers(refs)
    size = blocks[0].shape[1] // spots
    return [
        (
            lambda spot, block=block: block.at[:, columns_at(spot, size)],
            lambda spot, at=at: out.at[spot, :, pl.ds(at * size, size)],
        )
        for at, block in enumerate(blocks)
    ]


def core_items(refs, out):
    blocks = layers(refs)
    size = blocks[0].shape[1] // 2
    return [
        (
            lambda half, block=block: block.at[:, columns_at(half, size)],
            lambda spot, at=at: out.at[spot, :, pl.ds(at * size, size)],
        )
        for at, block in enumerate(blocks)
    ]


def handed_items(out):
    return [(None, lambda spot: out.at[spot])]


class Load:
    def __init__(self, mode, arrays, out, items, count, stage):
        self.mode, self.arrays, self.items, self.count, self.stage = mode, arrays, items, count, stage
        self.out = jax.ShapeDtypeStruct(out, arrays[0].dtype)

    def begin(self, place, refs, out, sems):
        if self.mode == "second":
            mover = Pull(place, self.items(out), sems)
            mover.second(False)
        elif self.mode == "first":
            mover = Pull(place, self.items(refs, out), sems)
            mover.first()
        else:
            mover = Exchange(place, self.items(refs, out), sems)
            mover.start()
        return mover


def spread_stage(place, rows, all_ref, sems, name="deep_back"):
    share = rows // place.ways
    own = all_ref.at[pl.ds(pl.multiple_of(place.depth * share, share), share), :]
    deep = [
        send(own, own, sems[name], offset - 1, place.spot, place.along(offset)) for offset in range(1, place.ways)
    ]
    return deep


def small_stage(place, half, sum_ref, small_s, sems):
    near = [
        send(
            sum_ref.at[pl.ds(part * half, half), :], small_s.at[part], sems["small"], part, place.partner, place.depth
        )
        for part in range(2)
    ]
    for copy in near:
        copy.wait()
    mine = pl.ds(pl.multiple_of(place.core * half, half), half)
    small_s[2] = sum_ref[mine, :] + small_s[place.core]
    chips = [
        send(small_s.at[2], small_s.at[3 + at], sems["small"], 2 + at, spot, place.depth)
        for at, spot in enumerate((place.across(2), place.across(4), place.across(6)))
    ]
    for copy in chips:
        copy.wait_recv()
    total = small_s[2] + small_s[3] + small_s[4] + small_s[5]
    small_s[6] = total
    deep = [
        send(
            small_s.at[6, pl.ds(half - 8, 8), :], small_s.at[6 + offset, pl.ds(half - 8, 8), :],
            sems["small"], 4 + offset, place.spot, place.along(offset),
        )
        for offset in range(1, place.ways)
    ]
    for copy in deep:
        copy.wait_recv()
    gains = small_s[6, half - 8 : half, :]
    for offset in range(1, place.ways):
        gains = gains + small_s[6 + offset, half - 8 : half, :]
    last = jnp.where(place.core == 1, gains, total[half - 8 : half, :])
    ready, came = 6 + place.ways, 7 + place.ways
    small_s[ready] = jnp.concatenate([total[: half - 8, :], last], axis=0)
    back = send(small_s.at[ready], small_s.at[came], sems["small"], 4 + place.ways, place.partner, place.depth)
    sum_ref[mine, :] = small_s[ready]
    back.wait_recv()
    sum_ref[pl.ds(pl.multiple_of((1 - place.core) * half, half), half), :] = small_s[came]
    return chips + deep + [back]


def sem_shapes(names):
    shapes = []
    for count in names.values():
        shapes += [pltpu.SemaphoreType.DMA((count,))] * 2
    return shapes


def sem_dict(names, refs):
    return {name: (refs[2 * at], refs[2 * at + 1]) for at, name in enumerate(names)}


def edge_kernel(kind, extra, loads, ways, rows, parts, in_group, out_group, names, counts, *refs):
    place = Place(ways)
    share = rows // ways
    ins, outs = list(refs[: counts[0]]), list(refs[counts[0] : counts[0] + counts[1]])
    scratch = list(refs[counts[0] + counts[1] : counts[0] + counts[1] + counts[2]])
    sems = sem_dict(names, refs[sum(counts) :])
    part_ref = ins.pop(0)
    near_s, sum_s, far_s, deep_s = [scratch.pop(0) for _ in range(4)]
    if kind == "forward":
        stream_ref, gain_ref = ins.pop(0), ins.pop(0)
    elif kind != "sum":
        stream_ref, gain_ref, grad_ref = ins.pop(0), ins.pop(0), ins.pop(0)
    all_ref = outs.pop(0)
    if kind != "sum" and kind != "last":
        fresh_ref = outs.pop(0)
    if kind == "backward":
        dgain_ref = outs.pop(0)
    if kind == "last":
        small_ref, late_ref, three_ref = ins.pop(0), ins.pop(0), ins.pop(0)
        dgain_ref, late_out_ref = outs.pop(0), outs.pop(0)
        low_s, small_s, late_s, late_low_s = [scratch.pop(0) for _ in range(4)]
    moving = []
    for load in reversed(loads):
        moving.append(([ins.pop() for _ in load.arrays][::-1], outs.pop()))
    moving = moving[::-1]
    everyone = loads or kind == "last"
    greet(place, turns(6) if everyone else sorted({*turns(in_group), *turns(out_group)}), bool(loads))
    first = Reduction(place, in_group, rows, parts, part_ref, near_s, sum_s, far_s, sems, ("near", "far"))
    waiting = []
    freight = {}
    if extra == "gather":
        load_ref, load_out_ref = ins.pop(0), outs.pop(0)

        def load_rows(turned):
            return rows_at(place.side(in_group, turned) * 2 + place.core, rows, rows)

        def between(stage):
            spot = rows_at(place.side(in_group) * 2 + place.core, rows, rows)
            if stage == 0:
                load_out_ref[spot, :] = load_ref[...]
                return
            own = load_out_ref.at[spot, :]
            if stage == 1:
                freight.update(first_leg(place, own, sems["load_far"], 0))
                freight[0] = send(own, own, sems["load_near"], 0, place.partner, place.depth)
            else:
                hand_on(place, in_group, load_rows, load_out_ref, sems["load_far"], 0, freight)

    elif extra == "reduce":
        second = Reduction(
            place, in_group, rows, parts, ins.pop(0), *[scratch.pop(0) for _ in range(3)], sems, ("load_near", "load_far")
        )
        load_out_ref = outs.pop(0)

        def between(stage):
            (second.send_near, second.send_far, second.relay)[stage]()

    else:

        def between(stage):
            pass

    carried = []

    def on_the_way(stage):
        between(stage)
        for at, load in enumerate(loads):
            if load.stage == stage:
                carried.append(load.begin(place, *moving[at], sems[f"load{at}"]))

    if kind == "last":
        late = deep_sends(place, share, late_ref, 0, late_s, slice(None), sems["late"], 0)
        waiting += late
    total, copies = reduce_stage(first, deep_s, sems, on_the_way)
    waiting += copies
    if kind == "forward":
        fresh = stream_ref[...] + total
        fresh_ref[...] = fresh
        scale = lax.rsqrt(jnp.mean(fresh * fresh, axis=-1, keepdims=True) + EPS)
        value = fresh * scale * gain_ref[...]
    elif kind == "sum":
        value = total
    else:
        stream = stream_ref[...]
        scale = lax.rsqrt(jnp.mean(stream * stream, axis=-1, keepdims=True) + EPS)
        leaned = total * gain_ref[...]
        inner = jnp.mean(leaned * stream, axis=-1, keepdims=True)
        value = grad_ref[...] + scale * leaned - stream * (scale * scale * scale * inner)
        dgain = jnp.sum(total * stream * scale, axis=0, keepdims=True)
        if kind == "backward":
            dgain_ref[...] = dgain
            fresh_ref[...] = value
    if kind == "last":
        own = pl.ds(pl.multiple_of(place.depth * share, share), share)
        low_s[own, :] = value.astype(low_s.dtype)
        spread = spread_stage(place, rows, low_s, sems)
        late_total = three_ref[...] + deep_total(place, share, late_ref, 0, late_s, late)
        late_low_s[own, :] = late_total.astype(late_low_s.dtype)
        spread += spread_stage(place, rows, late_low_s, sems, "late_back")
        half, span = small_ref.shape[0] // 2, small_ref.shape[1]
        dgain_ref[...] = small_ref[...]
        for at in range(dgain.shape[1] // span):
            dgain_ref[pl.ds(2 * half - 8 + at, 1), :] = dgain[:, at * span : (at + 1) * span]
        waiting += spread + small_stage(place, half, dgain_ref, small_s, sems)
        for copy in spread:
            copy.wait_recv()
        all_ref[...] = low_s[...].astype(jnp.float32)
        late_out_ref[...] = late_low_s[...].astype(jnp.float32)
    else:
        spot = pl.multiple_of((place.side(out_group) * 2 + place.core) * rows + place.depth * share, share)
        all_ref[pl.ds(spot, share), :] = value.astype(all_ref.dtype)
        waiting += gather_stage(place, out_group, rows, all_ref, sems, partial(on_the_way, 2))
    if extra == "gather":
        last = []
        for at, turned in enumerate((2, 4, 6)):
            for key in ((2, 4), (4, 2)) if turned == 6 else ():
                freight[key].wait_recv()
            came = load_out_ref.at[load_rows(turned), :]
            last.append(send(came, came, sems["load_near"], 1 + at, place.partner, place.depth))
        for copy in last + [freight[0]]:
            copy.wait_recv()
        waiting += list(freight.values()) + last
    elif extra == "reduce":
        for part in range(parts):
            load_out_ref[:, second.lanes(part)] = second.chip_sum(part).astype(load_out_ref.dtype)
        waiting += second.sent()
    for mover in carried:
        mover.close()
    for copy in waiting:
        copy.wait_send()


def edge(kind, part, extras, ways, rows, parts, in_group, out_group, ident, name, extra=None, loads=()):
    width = part.shape[1]
    share = rows // ways
    in_far, out_far = len(turns(in_group)), len(turns(out_group or 0))
    in_sides, out_sides = in_far + 1, out_far + 1
    dtype = part.dtype
    line = jax.ShapeDtypeStruct((1, width), jnp.float32)
    strip = jax.ShapeDtypeStruct((share, width), jnp.float32)
    whole = jax.ShapeDtypeStruct((out_sides * 2 * rows, width), dtype)
    block = jax.ShapeDtypeStruct((rows, width), jnp.float32)
    outs = {
        "forward": [whole, strip],
        "backward": [whole, strip, line],
        "last": [block] + [jax.ShapeDtypeStruct(one.shape, one.dtype) for one in extras[3:4]] + [block],
        "sum": [whole],
    }[kind]
    names = {"near": parts * in_sides, "far": 3 * parts if in_far else 0, "deep": parts * (ways - 1), "deep_back": ways - 1}
    reducing = [
        pltpu.VMEM((in_sides * rows, width), dtype),
        pltpu.VMEM((in_sides * rows, width), dtype),
        pltpu.VMEM((max(in_far, 1), rows if in_far else 16, width), dtype),
    ]
    deep = pltpu.VMEM((ways - 1, share, width), dtype)
    scratch = reducing + [deep]
    if kind == "last":
        names.update({"small": 5 + ways, "late": ways - 1, "late_back": ways - 1})
        small = pltpu.VMEM((8 + ways, extras[3].shape[0] // 2, extras[3].shape[1]), jnp.float32)
        spread = pltpu.VMEM((rows, width), dtype)
        scratch += [spread, small, deep, spread]
    else:
        names.update({"far_back": 4 * ways if out_far else 0, "near_back": ways * out_sides})
    if extra == "gather":
        names.update({"load_far": 4, "load_near": in_sides})
        outs = outs + [jax.ShapeDtypeStruct((in_sides * 2 * rows, width), dtype)]
    elif extra == "reduce":
        names.update({"load_far": 3 * parts, "load_near": parts * in_sides})
        outs = outs + [jax.ShapeDtypeStruct((rows, width), dtype)]
        scratch = scratch + reducing
    vmem, whole_memory = pl.BlockSpec(memory_space=pltpu.VMEM), pl.BlockSpec(memory_space=pl.ANY)
    in_specs, out_specs = [vmem] * (1 + len(extras)), [vmem] * len(outs)
    aliases, extras, outs = {}, list(extras), list(outs)
    for at, load in enumerate(loads):
        names[f"load{at}"] = 8 * load.count
        if load.mode == "second":
            aliases[1 + len(extras)] = len(outs)
        extras += load.arrays
        outs.append(load.out)
        in_specs += [whole_memory] * len(load.arrays)
        out_specs.append(whole_memory)
    names = {key: count for key, count in names.items() if count}
    if not in_far:
        names["far"] = 1
    return pl.pallas_call(
        partial(
            edge_kernel, kind, extra, loads, ways, rows, parts, in_group, out_group, names,
            (1 + len(extras), len(outs), len(scratch)),
        ),
        in_specs=in_specs,
        out_specs=out_specs,
        out_shape=outs,
        scratch_shapes=scratch + sem_shapes(names),
        input_output_aliases=aliases,
        compiler_params=pltpu.CompilerParams(
            collective_id=ident, has_side_effects=True, vmem_limit_bytes=48 << 20
        ),
        cost_estimate=pl.CostEstimate(flops=1, bytes_accessed=1, transcendentals=0),
        name=name,
    )(part, *extras)


class Pull:
    def __init__(self, place, items, sems):
        self.place, self.items, self.sems = place, items, sems
        self.copies, self.handed = {}, set()

    def go(self, at, key, slot, source, spot, target):
        self.copies[at, key] = send(source, target, self.sems, at * 8 + slot, spot, self.place.depth)

    def first(self):
        place = self.place
        for at, (source, target) in enumerate(self.items):
            mine = target(place.spot)
            for turned in (2, 4):
                self.go(at, (turned, False), turned - 2, source(place.core), place.across(turned), mine)
                self.go(at, (turned, True), turned - 1, source(1 - place.core), place.across(turned, True), mine)
            self.go(at, "near", 4, source(1 - place.core), place.partner, mine)
            own = pltpu.make_async_copy(source(place.core), mine, self.sems[1].at[at * 8 + 7])
            own.start()
            self.copies[at, "own"] = own

    def second(self, fresh=True):
        place = self.place
        for at, (_, target) in enumerate(self.items):
            for slot, turned, swapped, to in ((5, 2, False, 4), (6, 4, True, 2)):
                if fresh:
                    self.copies[at, (turned, swapped)].wait_recv()
                    self.handed.add((at, (turned, swapped)))
                block = target(place.across(turned, swapped))
                self.go(at, ("on", turned), slot, block, place.across(to), block)

    def close(self):
        for (at, key), copy in self.copies.items():
            if key == "own":
                copy.wait()
            else:
                if (at, key) not in self.handed:
                    copy.wait_recv()
                copy.wait_send()


def opening_kernel(ways, rows, hidden_ref, gain_ref, in_ref, rows_ref, first_ref, in_out, rows_out, *sems):
    place = Place(ways)
    greet_plane(place)
    size = rows_out.shape[2]
    items = [
        (
            lambda half, at=at: in_ref.at[at, :, columns_at(half, size)],
            lambda spot, at=at: in_out.at[spot, :, pl.ds(at * size, size)],
        )
        for at in range(in_ref.shape[0])
    ]
    items.append((lambda half: rows_ref.at[:, columns_at(half, size)], lambda spot: rows_out.at[spot]))
    pull = Pull(place, items, sems[2:])
    pull.first()
    stream = hidden_ref[...].astype(jnp.float32)
    scale = lax.rsqrt(jnp.mean(stream * stream, axis=-1, keepdims=True) + EPS)
    first_ref[rows_at(place.core, rows, rows), :] = (stream * scale * gain_ref[...]).astype(jnp.bfloat16)
    mine = first_ref.at[rows_at(place.core, rows, rows), :]
    copy = send(mine, mine, sems[:2], 0, place.partner, place.depth)
    pull.second()
    copy.wait()
    pull.close()


def greet_plane(place):
    barrier = pltpu.get_barrier_semaphore()
    peers = [place.partner] + [place.across(turned, swapped) for turned in (2, 4) for swapped in (False, True)]
    for peer in peers:
        pl.semaphore_signal(barrier, inc=1, device_id=(peer, place.depth), device_id_type=MESH)
    pl.semaphore_wait(barrier, len(peers))


def opening(hidden, gain, in_weights, row_weights, spots, ways, ident):
    rows, width = hidden.shape
    vmem, whole_memory = pl.BlockSpec(memory_space=pltpu.VMEM), pl.BlockSpec(memory_space=pl.ANY)
    kinds, depth, columns = in_weights.shape
    low = jnp.bfloat16
    return pl.pallas_call(
        partial(opening_kernel, ways, rows),
        in_specs=[vmem] * 2 + [whole_memory] * 2,
        out_specs=[vmem] + [whole_memory] * 2,
        out_shape=[
            jax.ShapeDtypeStruct((2 * rows, width), low),
            jax.ShapeDtypeStruct((spots, depth, kinds * columns // 2), low),
            jax.ShapeDtypeStruct((spots, row_weights.shape[0], columns // 2), low),
        ],
        scratch_shapes=[pltpu.SemaphoreType.DMA((1,))] * 2 + [pltpu.SemaphoreType.DMA((8 * (kinds + 1),))] * 2,
        compiler_params=pltpu.CompilerParams(
            collective_id=ident, has_side_effects=True, vmem_limit_bytes=40 << 20
        ),
        cost_estimate=pl.CostEstimate(flops=1, bytes_accessed=1, transcendentals=0),
        name="opening",
    )(hidden, gain, in_weights, row_weights)


def probs_of(query, keys, allowed):
    scores = project_t(query, keys) * (1.0 / math.sqrt(HEAD_DIM))
    scores = jnp.where(allowed, scores, NEG_FILL)
    shifted = jnp.exp(scores - jnp.max(scores, axis=-1, keepdims=True))
    return shifted / jnp.sum(shifted, axis=-1, keepdims=True)


def allowed_in(down_ref, side_ref, rows, group):
    shape = (rows, rows)
    distance = lax.broadcasted_iota(jnp.int32, shape, 0) - lax.broadcasted_iota(jnp.int32, shape, 1)
    same = down_ref[group * rows : (group + 1) * rows, :] == side_ref[group : group + 1, :]
    return same & (distance >= 0) & (distance < WINDOW)


def attend_kernel(heads, rows, joint_ref, down_ref, side_ref, low_ref, out_ref):
    low_ref[...] = joint_ref[...].astype(jnp.bfloat16)
    size = heads * HEAD_DIM
    for group in range(joint_ref.shape[0] // rows):
        allowed = allowed_in(down_ref, side_ref, rows, group)
        span = slice(group * rows, (group + 1) * rows)
        for head in range(heads):
            at = slice(head * HEAD_DIM, (head + 1) * HEAD_DIM)
            query, keys, values = [
                low_ref[span, part * size + head * HEAD_DIM : part * size + (head + 1) * HEAD_DIM] for part in range(3)
            ]
            probs = probs_of(query, keys, allowed)
            out_ref[span, at] = project(probs.astype(jnp.bfloat16), values).astype(jnp.bfloat16)


def attend(joint, down, side, rows):
    count, size = joint.shape
    return pl.pallas_call(
        partial(attend_kernel, size // (3 * HEAD_DIM), rows),
        out_shape=[
            jax.ShapeDtypeStruct((count, size), jnp.bfloat16),
            jax.ShapeDtypeStruct((count, size // 3), jnp.bfloat16),
        ],
        compiler_params=pltpu.CompilerParams(vmem_limit_bytes=32 << 20),
        name="attend",
    )(joint, down, side)


def attend_back_kernel(heads, rows, low_ref, grad_ref, down_ref, side_ref, out_ref):
    size = heads * HEAD_DIM
    scale = 1.0 / math.sqrt(HEAD_DIM)
    for group in range(low_ref.shape[0] // rows):
        allowed = allowed_in(down_ref, side_ref, rows, group)
        span = slice(group * rows, (group + 1) * rows)
        for head in range(heads):
            places = [slice(part * size + head * HEAD_DIM, part * size + (head + 1) * HEAD_DIM) for part in range(3)]
            query, keys, values = [low_ref[span, place] for place in places]
            grad = grad_ref[span, head * HEAD_DIM : (head + 1) * HEAD_DIM].astype(jnp.bfloat16)
            probs = probs_of(query, keys, allowed)
            grad_probs = project_t(grad, values)
            inner = jnp.sum(probs * grad_probs, axis=-1, keepdims=True)
            grad_scores = (probs * (grad_probs - inner)).astype(jnp.bfloat16)
            out_ref[span, places[0]] = (project(grad_scores, keys) * scale).astype(jnp.bfloat16)
            out_ref[span, places[1]] = (outer_rows(grad_scores, query) * scale).astype(jnp.bfloat16)
            out_ref[span, places[2]] = outer_rows(probs.astype(jnp.bfloat16), grad).astype(jnp.bfloat16)


def attend_back(low, grad, down, side, rows):
    count, size = low.shape
    return pl.pallas_call(
        partial(attend_back_kernel, size // (3 * HEAD_DIM), rows),
        out_shape=jax.ShapeDtypeStruct((count, size), jnp.bfloat16),
        compiler_params=pltpu.CompilerParams(vmem_limit_bytes=32 << 20),
        name="attend_back",
    )(low, grad, down, side)


def conv_total(stream, age_ref, taps_ref, offset_ref):
    moved = [stream] + [
        jnp.where(age_ref[...] >= lag, pltpu.roll(stream, lag, 0), 0.0) for lag in range(1, CONV)
    ]
    total = offset_ref[...]
    for lag in range(CONV):
        total = total + moved[lag] * taps_ref[lag : lag + 1, :]
    return total, moved


def front_kernel(first_ref, conv_mat_ref, gate_mat_ref, age_ref, taps_ref, offset_ref, select_ref, conv_ref, gate_ref,
                 channel_ref, mix_ref):
    stream = project(first_ref[...], conv_mat_ref[...])
    conv_ref[...] = stream
    gate_ref[...] = project(first_ref[...], gate_mat_ref[...])
    total, _ = conv_total(stream, age_ref, taps_ref, offset_ref)
    channel = (total / (1.0 + jnp.exp(-total))).astype(jnp.bfloat16)
    channel_ref[...] = channel

    @pl.when(pl.program_id(0) == 0)
    def _():
        mix_ref[...] = jnp.zeros_like(mix_ref)

    mix_ref[...] += project_t(channel, select_ref[...])


def front(first_low, in_mat, age, taps_t, offset, select):
    count, width = first_low.shape
    channels = in_mat.shape[1] // 2
    size = channels // 2
    column = pl.BlockSpec((count, size), lambda i: (0, i))
    sheet = jax.ShapeDtypeStruct((count, channels), jnp.float32)
    return pl.pallas_call(
        front_kernel,
        grid=(2,),
        in_specs=[
            pl.BlockSpec((count, width), lambda i: (0, 0)),
            pl.BlockSpec((width, size), lambda i: (0, i)),
            pl.BlockSpec((width, size), lambda i: (0, i + 2)),
            pl.BlockSpec((count, 1), lambda i: (0, 0)),
            pl.BlockSpec((CONV, size), lambda i: (0, i)),
            pl.BlockSpec((1, size), lambda i: (0, i)),
            pl.BlockSpec((select.shape[0], size), lambda i: (0, i)),
        ],
        out_specs=[column, column, column, pl.BlockSpec((count, select.shape[0]), lambda i: (0, 0))],
        out_shape=[
            sheet, sheet, jax.ShapeDtypeStruct((count, channels), jnp.bfloat16),
            jax.ShapeDtypeStruct((count, select.shape[0]), jnp.float32),
        ],
        compiler_params=pltpu.CompilerParams(vmem_limit_bytes=40 << 20),
        name="front",
    )(first_low, in_mat, in_mat, age, taps_t, offset, select)


def front_back_kernel(conv_ref, age_ref, left_ref, taps_ref, offset_ref, scan_ref, mix_ref, select_ref, low_ref, grads_ref):
    total, moved = conv_total(conv_ref[...], age_ref, taps_ref, offset_ref)
    sig = 1.0 / (1.0 + jnp.exp(-total))
    grad = (scan_ref[...] + project(mix_ref[...], select_ref[...])) * (sig * (1.0 + total * (1.0 - sig)))
    count = grad.shape[0]
    back = grad * taps_ref[0:1, :]
    for lag in range(1, CONV):
        back = back + jnp.where(left_ref[...] >= lag, pltpu.roll(grad, count - lag, 0), 0.0) * taps_ref[lag : lag + 1, :]
    low_ref[...] = back.astype(jnp.bfloat16)
    for lag in range(CONV):
        grads_ref[lag : lag + 1, :] = jnp.sum(grad * moved[lag], axis=0, keepdims=True)
    grads_ref[CONV : CONV + 1, :] = jnp.sum(grad, axis=0, keepdims=True)
    grads_ref[CONV + 1 :, :] = jnp.zeros((3, grad.shape[1]), jnp.float32)


def front_back(conv_in, age, left, taps_t, offset, grad_scan, grad_mix, select):
    count, channels = conv_in.shape
    size = channels // 2
    column = pl.BlockSpec((count, size), lambda i: (0, i))
    place = pl.BlockSpec((count, 1), lambda i: (0, 0))
    return pl.pallas_call(
        front_back_kernel,
        grid=(2,),
        in_specs=[
            column, place, place,
            pl.BlockSpec((CONV, size), lambda i: (0, i)),
            pl.BlockSpec((1, size), lambda i: (0, i)),
            column,
            pl.BlockSpec((count, select.shape[0]), lambda i: (0, 0)),
            pl.BlockSpec((select.shape[0], size), lambda i: (0, i)),
        ],
        out_specs=[column, pl.BlockSpec((8, size), lambda i: (0, i))],
        out_shape=[
            jax.ShapeDtypeStruct((count, channels), jnp.bfloat16),
            jax.ShapeDtypeStruct((8, channels), jnp.float32),
        ],
        compiler_params=pltpu.CompilerParams(vmem_limit_bytes=40 << 20),
        name="front_back",
    )(conv_in, age, left, taps_t, offset, grad_scan, grad_mix, select)


def sub_of(spot, group):
    if group == 6:
        return spot
    return spot % 2 + (2 * ((spot // group) % 2) if group else 0)


def subs_of(group):
    return 2 * (len(turns(group)) + 1)


def pull(count, *sets):
    def cut(block, group, spot):
        size = block.shape[1] // subs_of(group)
        return block[:, sub_of(spot, group) * size : (sub_of(spot, group) + 1) * size]

    return jnp.stack(
        [
            jnp.concatenate([cut(block, group, spot) for blocks, group in sets for block in blocks], axis=1)
            for spot in range(count)
        ]
    )


def in_order(value):
    return with_layout_constraint(value, Layout(major_to_minor=tuple(range(value.ndim))))


def swap(stacked):
    return lax.all_to_all(stacked, "dp", 0, 0, tiled=True)


def spread_out_kernel(came_ref, pair_ref, last_ref, sum_ref):
    size = last_ref.shape[1]
    half = came_ref.shape[2] - 3 * size
    spot = pl.program_id(0)
    for at in range(2):
        pair_ref[at] = came_ref[0, :, at * size : (at + 1) * size].astype(jnp.float32)
    last_ref[...] = came_ref[0, :, 2 * size : 3 * size].astype(jnp.float32)
    piece = came_ref[0, :, 3 * size :].astype(jnp.float32)
    for core in range(2):
        lanes = slice(core * half, (core + 1) * half)

        @pl.when(spot == core)
        def _():
            sum_ref[:, lanes] = piece

        @pl.when((spot > 1) & (lax.rem(spot, 2) == core))
        def _():
            sum_ref[:, lanes] += piece


def spread_out(came, columns):
    spots, rows, _ = came.shape
    size, half = columns // 3, came.shape[2] - columns
    return pl.pallas_call(
        spread_out_kernel,
        grid=(spots,),
        in_specs=[pl.BlockSpec((1, rows, came.shape[2]), lambda i: (i, 0, 0))],
        out_specs=[
            pl.BlockSpec((2, rows, size), lambda i: (0, 0, i)),
            pl.BlockSpec((rows, size), lambda i: (0, i)),
            pl.BlockSpec((rows, 2 * half), lambda i: (0, 0)),
        ],
        out_shape=[
            jax.ShapeDtypeStruct((2, rows, spots * size), jnp.float32),
            jax.ShapeDtypeStruct((rows, spots * size), jnp.float32),
            jax.ShapeDtypeStruct((rows, 2 * half), jnp.float32),
        ],
        name="spread_out",
    )(came)


def chip_total(came):
    return jnp.sum(came.astype(jnp.float32), axis=0)


def after(value, *others):
    return lax.optimization_barrier((value,) + others)[0]


def grouped_body(
    counts,
    early_group,
    focus_group,
    late_group,
    hidden_in,
    seq_lengths,
    norm_gains,
    mixer_in,
    mixer_rows,
    conv_weight,
    conv_bias,
    step_bias,
    decay_log,
    skip_gain,
    early_gate_up,
    early_down,
    attention_in,
    attention_out,
    late_gate_up,
    late_down,
    output_grad,
):
    spots, ways = counts
    rows, width = hidden_in.shape
    share = rows // ways
    spot = lax.axis_index("dp")
    depth = lax.axis_index("tensor")
    core = spot % 2
    low = jnp.bfloat16

    def swapped_core(value):
        return lax.ppermute(value, "dp", [(at, at ^ 1) for at in range(spots)])

    own_rows = mixer_rows.shape[0]
    padded_rows = jnp.pad(mixer_rows, ((0, -own_rows % 16), (0, 0)))
    first_low, in_weights, row_weights = opening(
        hidden_in, norm_gains[0:1], mixer_in, padded_rows, spots, ways, 20
    )
    row_weights = row_weights[:, :own_rows]

    other_lengths = swapped_core(seq_lengths)
    lengths = jnp.where(
        core == 0, jnp.stack([seq_lengths, other_lengths]), jnp.stack([other_lengths, seq_lengths])
    )
    segs, starts = jax.vmap(lambda own: segment_info(own, rows))(lengths)
    flat_segs = (segs + jnp.arange(2, dtype=jnp.int32)[:, None] * rows).reshape(-1)
    keeping = 1.0 - starts.reshape(-1).astype(jnp.float32)
    groups = 2 * seq_lengths.shape[0]
    flat_lengths = lengths.reshape(2, -1)
    ends = jnp.cumsum(flat_lengths, axis=1) + jnp.arange(2, dtype=jnp.int32)[:, None] * rows
    firsts = (ends - flat_lengths).reshape(1, -1)
    ends = ends.reshape(1, -1)
    places = jnp.arange(2 * rows, dtype=jnp.int32)[:, None]
    age = places - jnp.max(jnp.where(firsts <= places, firsts, 0), axis=1, keepdims=True)
    left = jnp.min(jnp.where(ends > places, ends, 2 * rows), axis=1, keepdims=True) - 1 - places

    stream_zero = lax.dynamic_slice_in_dim(hidden_in, depth * share, share, 0).astype(jnp.float32)

    channels = conv_weight.shape[0] // 2

    def half(values):
        return lax.dynamic_slice_in_dim(values, core * channels, channels, 0)

    taps, offset, bias, decay, skip = [half(v) for v in (conv_weight, conv_bias, step_bias, decay_log, skip_gain)]
    in_mat = in_weights.reshape(width, 2 * channels)
    taps_t = taps.T
    row_mat = row_weights.reshape(-1, channels)
    early_blocks = [early_gate_up[0], early_gate_up[1], early_down]
    early_weights = swap(after(pull(spots, (early_blocks, early_group)), first_low))
    out_mat = row_mat[:width]
    select_mat = row_mat[width : width + PROJ_OUT]
    step_mat = row_mat[width + PROJ_OUT :]

    def spread_load(joints, size, stage):
        count = sum(one.shape[2] // size for one in joints)
        return Load(
            "exchange", joints, (count, joints[0].shape[1], spots * size), partial(spread_items, size), count, stage
        )

    def chip_load(joints, size, stage):
        count = sum(one.shape[2] // size for one in joints)
        out = (spots // 2, count, joints[0].shape[1], 2 * size)
        return Load("exchange", joints, out, partial(chip_items, size), count, stage)

    def by_spot(joint):
        return joint.astype(low).reshape(spots, -1, joint.shape[1])

    def mixed_sum(part, ident, name, loads=()):
        total, *came = edge("sum", part, [], ways, rows, 1, 0, 0, ident, name, loads=loads)
        return total[:, :PROJ_OUT], *came

    wide_select = jnp.pad(select_mat, ((0, 256 - PROJ_OUT), (0, 0)))
    conv_in, gate_half, channel_low, mix_part = front(first_low, in_mat, age, taps_t, offset[None], wide_select)
    mix_rows, = mixed_sum(mix_part, 1, "mix_sum")
    rank_low = mix_rows[:, :DT_RANK].astype(low)
    step_raw = project(rank_low, step_mat)
    rates_t = -jnp.exp(decay).T
    wide = (2 * rows, STATE, LANES)
    in_wide = jnp.broadcast_to(mix_rows[:, DT_RANK : DT_RANK + STATE, None], wide)
    out_wide = jnp.broadcast_to(mix_rows[:, DT_RANK + STATE :, None], wide)
    mixer_low = scan_forward(
        keeping, channel_low, step_raw, gate_half, bias, rates_t, skip, in_wide, out_wide, groups, LANES
    )
    early_mat = early_weights.reshape(width, -1)
    focus_blocks = [attention_in, attention_out]
    heads_width = attention_out.shape[1] // 2
    focus_pull = Load("first", focus_blocks, (spots, width // spots, 4 * heads_width), core_items, 4, 0)
    second_low, stream_one, focus_half = edge(
        "forward", project_t(mixer_low, out_mat).astype(low), [stream_zero, norm_gains[1:2]],
        ways, rows, 4, 0, early_group, 2, "edge_one", loads=[focus_pull],
    )

    def ffn(normed, pair_mat, down_mat):
        units = down_mat.shape[1]
        both = project(normed, pair_mat)
        hidden = gated_unit(both[:, :units], both[:, units:]).astype(low)
        return project_t(hidden, down_mat).astype(low), both, hidden

    units = early_mat.shape[1] // 3
    early_mats = (early_mat[:, : 2 * units], early_mat[:, 2 * units :])
    late_size = late_down.shape[1] // spots
    late_pulls = [
        Load("exchange", [one], (spots, width // spots, blocks * late_size), partial(plane_items, spots), blocks, stage)
        for one, blocks, stage in ((late_gate_up, 2, 0), (late_down, 1, 2))
    ]
    early_part, early_both, early_hidden = ffn(second_low, *early_mats)
    third_low, stream_two, last_grad, focus_weights, late_down_weights = edge(
        "forward", early_part, [stream_one, norm_gains[2:3], output_grad], ways, rows, 4, early_group, 0, 3, "edge_two",
        "gather", [Load("second", [focus_half], focus_half.shape, handed_items, 1, 1), late_pulls[1]],
    )
    focus_mat = focus_weights.reshape(width, -1)

    down, side = flat_segs[:, None], flat_segs.reshape(2, rows)
    joint_low, attended_low = attend(project(third_low, focus_mat[:, : 3 * heads_width]), down, side, rows)
    fourth_low, stream_three, late_pair_weights = edge(
        "forward", project_t(attended_low, focus_mat[:, 3 * heads_width :]).astype(low),
        [stream_two, norm_gains[3:4]], ways, rows, 4, 0, late_group, 4, "edge_three", loads=late_pulls[:1],
    )

    late_mats = (late_pair_weights.reshape(width, -1), late_down_weights.reshape(width, -1))
    late_part, late_both, late_hidden = ffn(fourth_low, *late_mats)

    def ffn_back(grad_low, normed, both, hidden, pair_mat, down_mat):
        units = down_mat.shape[1]
        grad_hidden = project(grad_low, down_mat)
        _, unit_back = jax.vjp(gated_unit, both[:, :units], both[:, units:])
        both_low = jnp.concatenate(unit_back(grad_hidden), axis=1).astype(low)
        grad_normed = project_t(both_low, pair_mat).astype(low)
        return grad_normed, [by_spot(outer_rows(normed, both_low)), by_spot(outer_rows(grad_low, hidden))]

    grad_fourth, late_joints = ffn_back(last_grad, fourth_low, late_both, late_hidden, *late_mats)
    grad_zero = lax.dynamic_slice_in_dim(output_grad, depth * share, share, 0).astype(jnp.float32)
    grad_low_three, grad_three, gain_four, output_part, late_down_swapped = edge(
        "backward", grad_fourth, [stream_three, norm_gains[3:4], grad_zero, late_part],
        ways, rows, 4, late_group, 0, 5, "edge_four", "reduce",
        [spread_load(late_joints[1:], late_joints[1].shape[2], 1)],
    )

    grad_attended = project(grad_low_three, focus_mat[:, 3 * heads_width :])
    joint_grad = attend_back(joint_low, grad_attended, down, side, rows)
    grad_low_two, grad_two, gain_three, late_swapped = edge(
        "backward", project_t(joint_grad, focus_mat[:, : 3 * heads_width]).astype(low),
        [stream_two, norm_gains[2:3], grad_three], ways, rows, 4, 0, early_group, 6, "edge_five",
        loads=[spread_load(late_joints[:1], late_joints[1].shape[2], 0)],
    )
    focus_joints = [by_spot(outer_rows(third_low, joint_grad)), by_spot(outer_rows(grad_low_three, attended_low))]

    grad_second, early_joints = ffn_back(grad_low_two, second_low, early_both, early_hidden, *early_mats)
    grad_low_one, grad_one, gain_two, focus_swapped = edge(
        "backward", grad_second, [stream_one, norm_gains[1:2], grad_two],
        ways, rows, 4, early_group, 0, 7, "edge_six",
        loads=[chip_load(focus_joints[:1], heads_width, 1)],
    )
    early_joints = [in_order(one) for one in early_joints + focus_joints[1:]]
    early_swapped = swap(after(in_order(jnp.concatenate(early_joints, axis=2)), grad_low_one))

    grad_scanned = project(grad_low_one, out_mat)
    (
        grad_channel,
        grad_step_low,
        gate_low,
        in_sums,
        out_sums,
        bias_grad,
        decay_grad,
        skip_grad,
    ) = scan_backward(
        keeping, channel_low, step_raw, gate_half, grad_scanned, bias, rates_t, skip, in_wide, out_wide,
        groups, LANES,
    )
    grad_rank = project_t(grad_step_low, step_mat)
    gate_joint = outer_rows(first_low, gate_low).astype(low).reshape(spots, -1, channels)
    rest = mix_part[:, PROJ_OUT:]
    grad_rows, gate_swapped = mixed_sum(
        after(
            jnp.concatenate(
                [grad_rank, jnp.sum(in_sums, axis=-1), jnp.sum(out_sums, axis=-1), jnp.zeros_like(rest)], axis=1
            ),
            early_swapped,
        ),
        8, "mix_grad_sum",
        [chip_load([gate_joint], channels, 0)],
    )
    grad_rows_low = grad_rows.astype(low)
    rows_joint = jnp.concatenate(
        [
            outer_rows(grad_low_one, mixer_low),
            outer_rows(grad_rows_low, channel_low),
            outer_rows(rank_low, grad_step_low),
        ],
        axis=0,
    ).astype(low)
    grad_wide_low = jnp.pad(grad_rows_low, ((0, 0), (0, 256 - PROJ_OUT)))
    conv_low, conv_grads = front_back(
        conv_in, age, left, taps_t, offset[None], grad_channel, grad_wide_low, wide_select
    )
    conv_joint = outer_rows(first_low, conv_low).astype(low).reshape(spots, -1, channels)
    in_grad = jnp.concatenate([conv_low, gate_low], axis=1)
    grad_first = project_t(in_grad, in_mat).astype(low)
    rows_joint = rows_joint.reshape(spots, -1, channels)
    rows_joint = jnp.pad(rows_joint, ((0, 0), (0, -own_rows % 16), (0, 0)))
    lines = jnp.concatenate([conv_grads[: CONV + 1], bias_grad, skip_grad, decay_grad], axis=0)
    lines = jnp.pad(lines, ((0, 1), (0, 0)))
    blank = jnp.zeros_like(lines)
    lines = jnp.where(core == 0, jnp.concatenate([lines, blank], axis=1), jnp.concatenate([blank, lines], axis=1))
    gains = jnp.concatenate([jnp.zeros_like(gain_two), gain_two, gain_three, gain_four], axis=0)
    small = jnp.concatenate([lines, gains.reshape(8, -1)], axis=0)
    input_grad, small, output, conv_swapped, rows_swapped = edge(
        "last", grad_first, [stream_zero, norm_gains[0:1], grad_one, small, output_part, stream_three],
        ways, rows, 4, 0, None, 9, "edge_seven",
        loads=[chip_load([conv_joint], channels, 0), chip_load([rows_joint], channels, 0)],
    )
    lines = small[: CONV + 3 + STATE]
    gains = small[-8:].reshape(norm_gains.shape)
    early_gate_up_grad, early_down_grad, focus_out_grad = spread_out(early_swapped, 3 * early_down.shape[1] // spots)
    return (
        output,
        input_grad,
        gains,
        jnp.stack([chip_total(conv_swapped[:, 0]), chip_total(gate_swapped[:, 0])]),
        chip_total(rows_swapped[:, 0, :own_rows]),
        lines[:CONV].T,
        lines[CONV],
        lines[CONV + 1],
        lines[CONV + 3 :].T,
        lines[CONV + 2],
        early_gate_up_grad,
        early_down_grad,
        chip_total(focus_swapped),
        focus_out_grad,
        late_swapped.astype(jnp.float32),
        late_down_swapped[0].astype(jnp.float32),
    )


def solution(mesh):
    counts = (mesh.shape["dp"], mesh.shape["tensor"])
    chosen = partial(grouped_body, counts, 6, 0, 6) if counts == (8, 4) else body
    return jax.shard_map(
        chosen,
        mesh=mesh,
        in_specs=(
            P("dp", None),
            P("dp", None),
            P(),
            P(None, "dp", "tensor"),
            P("dp", "tensor"),
            P("tensor", None),
            P("tensor"),
            P("tensor"),
            P("tensor", None),
            P("tensor"),
            P(None, "dp", "tensor"),
            P("dp", "tensor"),
            P(None, "dp", "tensor"),
            P("dp", "tensor"),
            P(None, "dp", "tensor"),
            P("dp", "tensor"),
            P("dp", None),
        ),
        out_specs=(
            P("dp", None),
            P("dp", None),
            P(),
            P(None, "dp", "tensor"),
            P("dp", "tensor"),
            P("tensor", None),
            P("tensor"),
            P("tensor"),
            P("tensor", None),
            P("tensor"),
            P(None, "dp", "tensor"),
            P("dp", "tensor"),
            P(None, "dp", "tensor"),
            P("dp", "tensor"),
            P(None, "dp", "tensor"),
            P("dp", "tensor"),
        ),
        check_vma=False,
    )
```

```python
from functools import partial
import math

import jax
import jax.numpy as jnp
from jax import lax
from jax.experimental import pallas as pl
from jax.experimental.layout import Layout, with_layout_constraint
from jax.experimental.pallas import tpu as pltpu
from jax.sharding import PartitionSpec as P

STATE = 16
CONV = 4
DT_RANK = 128
HEAD_DIM = 128
WINDOW = 2048
PROJ_OUT = 160


EPS = 1e-05
NEG_FILL = -1e30


def project(left, right):
    return jnp.dot(left, right, preferred_element_type=jnp.float32)


def project_t(left, right):
    return lax.dot_general(
        left, right, (((1,), (1,)), ((), ())), preferred_element_type=jnp.float32
    )


def outer_rows(left, right):
    return lax.dot_general(
        left, right, (((0,), (0,)), ((), ())), preferred_element_type=jnp.float32
    )


def rms_norm(values, weight):
    return values * lax.rsqrt(jnp.mean(values * values, axis=-1, keepdims=True) + EPS) * weight


def segment_info(lengths, tokens):
    flat_lengths = lengths.reshape(-1)
    ends = jnp.cumsum(flat_lengths, dtype=jnp.int32)
    firsts = ends - flat_lengths
    places = jnp.arange(tokens, dtype=jnp.int32)
    segs = jnp.sum((places[:, None] >= ends[None, :]).astype(jnp.int32), axis=1)
    starts = jnp.any(places[:, None] == firsts[None, :], axis=1)
    return (segs, starts)


def allowed_pairs(segs):
    places = jnp.arange(segs.shape[-1], dtype=jnp.int32)
    distance = places[:, None] - places[None, :]
    return (segs[:, None] == segs[None, :]) & (distance >= 0) & (distance < WINDOW)


def causal_conv(segs, stream, weight, offset):
    total = offset + stream * weight[:, 0]
    for lag_step in range(1, CONV):
        moved = jnp.concatenate(
            [jnp.zeros_like(stream[..., :lag_step, :]), stream[..., :-lag_step, :]], axis=-2
        )
        moved_segs = jnp.concatenate(
            [jnp.full_like(segs[..., :lag_step], -1), segs[..., :-lag_step]], axis=-1
        )
        linked = (segs == moved_segs).astype(stream.dtype)
        total = total + moved * weight[:, lag_step] * linked[..., None]
    return jax.nn.silu(total)


LANES = 128


def softplus(v):
    return jnp.maximum(v, 0.0) + jnp.log1p(jnp.exp(-jnp.abs(v)))


def scan_forward_kernel(
    groups, length, keep_ref, chan_ref, raw_ref, gate_ref, bias_ref, rate_ref, skip_ref, in_ref, out_ref,
    mixed_ref, step_s, drive_s, y_s,
):
    width = chan_ref.shape[1]
    blocks = width // LANES
    step_s[...] = softplus(raw_ref[...] + bias_ref[...])
    drive_s[...] = step_s[...] * chan_ref[...].astype(jnp.float32)
    rates = [rate_ref[:, pl.ds(b * LANES, LANES)] for b in range(blocks)]

    def advance(t, states):
        fresh = []
        for g in range(groups):
            row = g * length + t
            keep = keep_ref[row]
            input_map = in_ref[row]
            output_map = out_ref[row]
            for b in range(blocks):
                lanes = pl.ds(b * LANES, LANES)
                decay = jnp.exp(step_s[pl.ds(row, 1), lanes] * rates[b]) * keep
                state = decay * states[g * blocks + b] + drive_s[pl.ds(row, 1), lanes] * input_map
                y_s[pl.ds(row, 1), lanes] = jnp.sum(state * output_map, axis=0, keepdims=True)
                fresh.append(state)
        return tuple(fresh)

    zero = jnp.zeros((STATE, LANES), jnp.float32)
    lax.fori_loop(0, length, advance, (zero,) * (groups * blocks))
    gate = gate_ref[...]
    silu = gate / (1.0 + jnp.exp(-gate))
    mixed_ref[...] = (
        (y_s[...] + skip_ref[...] * chan_ref[...].astype(jnp.float32)) * silu
    ).astype(mixed_ref.dtype)


def scan_forward(keep, channel, step_raw, gate_half, step_bias, rates_t, skip_gain, in_wide, out_wide, groups, width):
    tokens, channels = channel.shape
    column = pl.BlockSpec((tokens, width), lambda i: (0, i))
    row = pl.BlockSpec((1, width), lambda i: (0, i))
    maps = pl.BlockSpec((tokens, STATE, LANES), lambda i: (0, 0, 0))
    return pl.pallas_call(
        partial(scan_forward_kernel, groups, tokens // groups),
        grid=(channels // width,),
        in_specs=[
            pl.BlockSpec(memory_space=pltpu.SMEM), column, column, column, row,
            pl.BlockSpec((STATE, width), lambda i: (0, i)), row, maps, maps,
        ],
        out_specs=column,
        out_shape=jax.ShapeDtypeStruct((tokens, channels), jnp.bfloat16),
        scratch_shapes=[pltpu.VMEM((tokens, width), jnp.float32)] * 3,
        compiler_params=pltpu.CompilerParams(vmem_limit_bytes=48 << 20),
        cost_estimate=pl.CostEstimate(flops=1, bytes_accessed=1 << 34, transcendentals=0),
        name="scan_forward",
    )(keep, channel, step_raw, gate_half, step_bias[None], rates_t, skip_gain[None], in_wide, out_wide)


def scan_backward_kernel(
    groups, length, keep_ref, chan_ref, raw_ref, gate_ref, dmix_ref, bias_ref, rate_ref, skip_ref, in_ref, out_ref,
    dchan_ref, draw_ref, dgate_ref, din_ref, dout_ref, dbias_ref, drate_ref, dskip_ref,
    step_s, drive_s, y_s, dy_s, dd_s, ds_s, state_s, decay_s,
):
    width = chan_ref.shape[1]
    blocks = width // LANES
    chan = chan_ref[...].astype(jnp.float32)
    step_s[...] = softplus(raw_ref[...] + bias_ref[...])
    drive_s[...] = step_s[...] * chan
    gate = gate_ref[...]
    sig = 1.0 / (1.0 + jnp.exp(-gate))
    dy_s[...] = dmix_ref[...] * (gate * sig)
    rates = [rate_ref[:, pl.ds(b * LANES, LANES)] for b in range(blocks)]

    @pl.when(pl.program_id(0) == 0)
    def _():
        din_ref[...] = jnp.zeros_like(din_ref)
        dout_ref[...] = jnp.zeros_like(dout_ref)

    def advance(t, states):
        fresh = []
        for g in range(groups):
            row = g * length + t
            keep = keep_ref[row]
            input_map = in_ref[row]
            output_map = out_ref[row]
            total = None
            for b in range(blocks):
                lanes = pl.ds(b * LANES, LANES)
                decay = jnp.exp(step_s[pl.ds(row, 1), lanes] * rates[b]) * keep
                decay_s[row, :, lanes] = decay
                carried = decay * states[g * blocks + b]
                state_s[row, :, lanes] = carried
                state = carried + drive_s[pl.ds(row, 1), lanes] * input_map
                y_s[pl.ds(row, 1), lanes] = jnp.sum(state * output_map, axis=0, keepdims=True)
                term = state * dy_s[pl.ds(row, 1), lanes]
                total = term if total is None else total + term
                fresh.append(state)
            dout_ref[row] += total
        return tuple(fresh)

    zero = jnp.zeros((STATE, LANES), jnp.float32)
    count = groups * blocks
    lax.fori_loop(0, length, advance, (zero,) * count)

    def retreat(back, carry):
        t = length - 1 - back
        fresh, rate_sums = [], []
        for g in range(groups):
            row = g * length + t
            input_map = in_ref[row]
            output_map = out_ref[row]
            total = None
            for b in range(blocks):
                lanes = pl.ds(b * LANES, LANES)
                at = g * blocks + b
                dstate = carry[0][at] + dy_s[pl.ds(row, 1), lanes] * output_map
                dlog = dstate * state_s[row, :, lanes]
                dd_s[pl.ds(row, 1), lanes] = jnp.sum(dstate * input_map, axis=0, keepdims=True)
                ds_s[pl.ds(row, 1), lanes] = jnp.sum(dlog * rates[b], axis=0, keepdims=True)
                term = dstate * drive_s[pl.ds(row, 1), lanes]
                total = term if total is None else total + term
                rate_sums.append(carry[1][at] + dlog * step_s[pl.ds(row, 1), lanes])
                fresh.append(dstate * decay_s[row, :, lanes])
            din_ref[row] += total
        return (tuple(fresh), tuple(rate_sums))

    _, rate_sums = lax.fori_loop(0, length, retreat, ((zero,) * count, (zero,) * count))
    for b in range(blocks):
        lanes = pl.ds(b * LANES, LANES)
        drate_ref[:, lanes] = rates[b] * sum(rate_sums[g * blocks + b] for g in range(groups))
    direct = y_s[...] + skip_ref[...] * chan
    dgate_ref[...] = (dmix_ref[...] * direct * (sig * (1.0 + gate * (1.0 - sig)))).astype(dgate_ref.dtype)
    dskip_ref[...] = jnp.sum(dy_s[...] * chan, axis=0, keepdims=True)
    dchan_ref[...] = dd_s[...] * step_s[...] + skip_ref[...] * dy_s[...]
    shifted = raw_ref[...] + bias_ref[...]
    draw = (ds_s[...] + dd_s[...] * chan) / (1.0 + jnp.exp(-shifted))
    draw_ref[...] = draw.astype(draw_ref.dtype)
    dbias_ref[...] = jnp.sum(draw, axis=0, keepdims=True)


def scan_backward(
    keep, channel, step_raw, gate_half, dmixed, step_bias, rates_t, skip_gain, in_wide, out_wide, groups, width
):
    tokens, channels = channel.shape
    column = pl.BlockSpec((tokens, width), lambda i: (0, i))
    row = pl.BlockSpec((1, width), lambda i: (0, i))
    states = pl.BlockSpec((STATE, width), lambda i: (0, i))
    maps = pl.BlockSpec((tokens, STATE, LANES), lambda i: (0, 0, 0))
    sheet = jax.ShapeDtypeStruct((tokens, channels), jnp.float32)
    low = jax.ShapeDtypeStruct((tokens, channels), jnp.bfloat16)
    wide = jax.ShapeDtypeStruct((tokens, STATE, LANES), jnp.float32)
    line = jax.ShapeDtypeStruct((1, channels), jnp.float32)
    return pl.pallas_call(
        partial(scan_backward_kernel, groups, tokens // groups),
        grid=(channels // width,),
        in_specs=[
            pl.BlockSpec(memory_space=pltpu.SMEM), column, column, column, column, row, states, row, maps, maps,
        ],
        out_specs=[column, column, column, maps, maps, row, states, row],
        out_shape=[
            sheet, low, low, wide, wide, line, jax.ShapeDtypeStruct((STATE, channels), jnp.float32), line,
        ],
        scratch_shapes=[pltpu.VMEM((tokens, width), jnp.float32)] * 6
        + [pltpu.VMEM((tokens, STATE, width), jnp.float32)] * 2,
        compiler_params=pltpu.CompilerParams(vmem_limit_bytes=56 << 20),
        cost_estimate=pl.CostEstimate(flops=1, bytes_accessed=1 << 34, transcendentals=0),
        name="scan_backward",
    )(keep, channel, step_raw, gate_half, dmixed, step_bias[None], rates_t, skip_gain[None], in_wide, out_wide)


def attention_scores(query, keys, allowed):
    scores = jnp.einsum("qhd,khd->hqk", query, keys, preferred_element_type=jnp.float32) * (
        1.0 / math.sqrt(HEAD_DIM)
    )
    return jnp.where(allowed[None], scores, NEG_FILL)


def attention_forward(query, keys, values, allowed):
    scores = attention_scores(query, keys, allowed)
    row_max = jnp.max(scores, axis=-1, keepdims=True)
    shifted = jnp.exp(scores - row_max)
    totals = jnp.sum(shifted, axis=-1, keepdims=True)
    probs = shifted / totals
    mixed = jnp.einsum(
        "hqk,khd->qhd", probs.astype(jnp.bfloat16), values, preferred_element_type=jnp.float32
    )
    return (mixed, row_max + jnp.log(totals))


def attention_backward(query, keys, values, allowed, log_total, grad_mixed):
    scale = 1.0 / math.sqrt(HEAD_DIM)
    probs = jnp.exp(attention_scores(query, keys, allowed) - log_total)
    grad_values = jnp.einsum(
        "hqk,qhd->khd", probs.astype(jnp.bfloat16), grad_mixed, preferred_element_type=jnp.float32
    )
    grad_probs = jnp.einsum("qhd,khd->hqk", grad_mixed, values, preferred_element_type=jnp.float32)
    inner_sum = jnp.sum(probs * grad_probs, axis=-1, keepdims=True)
    grad_scores = (probs * (grad_probs - inner_sum)).astype(jnp.bfloat16)
    grad_query = (
        jnp.einsum("hqk,khd->qhd", grad_scores, keys, preferred_element_type=jnp.float32) * scale
    )
    grad_keys = (
        jnp.einsum("hqk,qhd->khd", grad_scores, query, preferred_element_type=jnp.float32) * scale
    )
    return (grad_query, grad_keys, grad_values)


def gated_unit(gate, upward):
    return jax.nn.silu(gate) * upward


def ffn_forward(normed_low, gate_up, down_mat):
    gate = project(normed_low, gate_up[0])
    upward = project(normed_low, gate_up[1])
    hidden = gated_unit(gate, upward).astype(jnp.bfloat16)
    return (project_t(hidden, down_mat), gate, upward, hidden)


def ffn_backward(grad_low, normed_low, gate, upward, hidden, gate_up, down_mat):
    grad_hidden = project(grad_low, down_mat)
    down_grad = outer_rows(grad_low, hidden)
    _, unit_back = jax.vjp(gated_unit, gate, upward)
    grad_gate, grad_up = unit_back(grad_hidden)
    gate_low = grad_gate.astype(jnp.bfloat16)
    up_low = grad_up.astype(jnp.bfloat16)
    joined_grad = outer_rows(normed_low, jnp.concatenate([gate_low, up_low], axis=1))
    grad_normed = project_t(gate_low, gate_up[0]) + project_t(up_low, gate_up[1])
    return (grad_normed, joined_grad, down_grad)


def flatten_low(grad_heads, tokens):
    return grad_heads.astype(jnp.bfloat16).reshape(tokens, -1)


def collect(stacked, row_block):
    return (
        lax.all_gather(stacked, "dp", axis=1, tiled=True),
        lax.all_gather(row_block, "dp", axis=0, tiled=True),
    )


def spread_grads(joined, row_block, count):
    summed = (
        lax.psum_scatter(joined.astype(jnp.bfloat16), "dp", scatter_dimension=0, tiled=True),
        lax.psum_scatter(row_block.astype(jnp.bfloat16), "dp", scatter_dimension=0, tiled=True),
    )
    rows_here = summed[0].shape[0]
    restacked = jnp.transpose(summed[0].reshape(rows_here, count, -1), (1, 0, 2))
    return (restacked.astype(jnp.float32), summed[1].astype(jnp.float32))


def branch_total(piece_sum):
    return lax.psum(piece_sum, "tensor")


def input_total(piece_sum):
    return lax.psum(piece_sum, "tensor")


def body(
    hidden_in,
    seq_lengths,
    norm_gains,
    mixer_in,
    mixer_rows,
    conv_weight,
    conv_bias,
    step_bias,
    decay_log,
    skip_gain,
    early_gate_up,
    early_down,
    attention_in,
    attention_out,
    late_gate_up,
    late_down,
    output_grad,
):
    tokens = hidden_in.shape[0]
    width = hidden_in.shape[1]
    segs, starts = segment_info(seq_lengths, tokens)
    allowed = allowed_pairs(segs)
    stream_zero = hidden_in.astype(jnp.float32)
    mixer_stack, mixer_mats = collect(mixer_in, mixer_rows)
    first_normed, first_back = jax.vjp(rms_norm, stream_zero, norm_gains[0])
    first_low = first_normed.astype(jnp.bfloat16)
    conv_in = project(first_low, mixer_stack[0])
    gate_half = project(first_low, mixer_stack[1])
    channel_full, conv_back = jax.vjp(partial(causal_conv, segs), conv_in, conv_weight, conv_bias)
    channel_low = channel_full.astype(jnp.bfloat16)
    mix_rows = lax.psum(project_t(channel_low, mixer_mats[width : width + PROJ_OUT]), "tensor")
    rank_low = mix_rows[:, :DT_RANK].astype(jnp.bfloat16)
    step_raw = project(rank_low, mixer_mats[width + PROJ_OUT :])
    groups = seq_lengths.shape[0]
    keeping = 1.0 - starts.astype(jnp.float32)
    rates_t = -jnp.exp(decay_log).T
    wide = (tokens, STATE, LANES)
    in_wide = jnp.broadcast_to(mix_rows[:, DT_RANK : DT_RANK + STATE, None], wide)
    out_wide = jnp.broadcast_to(mix_rows[:, DT_RANK + STATE :, None], wide)
    mixer_low = scan_forward(
        keeping, channel_low, step_raw, gate_half, step_bias, rates_t, skip_gain, in_wide, out_wide, groups, LANES
    )
    stream_one = stream_zero + branch_total(project_t(mixer_low, mixer_mats[:width]))
    early_stack, early_mat = collect(early_gate_up, early_down)
    second_normed, second_back = jax.vjp(rms_norm, stream_one, norm_gains[1])
    second_low = second_normed.astype(jnp.bfloat16)
    early_part, early_gate, early_up, early_hidden = ffn_forward(second_low, early_stack, early_mat)
    stream_two = stream_one + branch_total(early_part)
    focus_stack, focus_mat = collect(attention_in, attention_out)
    heads_here = focus_stack.shape[2] // HEAD_DIM
    third_normed, third_back = jax.vjp(rms_norm, stream_two, norm_gains[2])
    third_low = third_normed.astype(jnp.bfloat16)
    query = (
        project(third_low, focus_stack[0])
        .astype(jnp.bfloat16)
        .reshape(tokens, heads_here, HEAD_DIM)
    )
    keys = (
        project(third_low, focus_stack[1])
        .astype(jnp.bfloat16)
        .reshape(tokens, heads_here, HEAD_DIM)
    )
    values = (
        project(third_low, focus_stack[2])
        .astype(jnp.bfloat16)
        .reshape(tokens, heads_here, HEAD_DIM)
    )
    attended, log_total = attention_forward(query, keys, values, allowed)
    attended_low = attended.reshape(tokens, heads_here * HEAD_DIM).astype(jnp.bfloat16)
    stream_three = stream_two + branch_total(project_t(attended_low, focus_mat))
    late_stack, late_mat = collect(late_gate_up, late_down)
    fourth_normed, fourth_back = jax.vjp(rms_norm, stream_three, norm_gains[3])
    fourth_low = fourth_normed.astype(jnp.bfloat16)
    late_part, late_gate, late_up, late_hidden = ffn_forward(fourth_low, late_stack, late_mat)
    output = stream_three + branch_total(late_part)
    grad_three = output_grad.astype(jnp.float32)
    late_pair = (late_stack, late_mat)
    grad_fourth, late_joined, late_mat_grad = ffn_backward(
        output_grad, fourth_low, late_gate, late_up, late_hidden, late_pair[0], late_pair[1]
    )
    grad_stream, gain_four = fourth_back(input_total(grad_fourth))
    grad_three = grad_three + grad_stream
    late_grads = spread_grads(late_joined, late_mat_grad, 2)
    focus_pair = (focus_stack, focus_mat)
    grad_branch_low = grad_three.astype(jnp.bfloat16)
    focus_mat_grad = outer_rows(grad_branch_low, attended_low)
    grad_attended = (
        project(grad_branch_low, focus_pair[1])
        .astype(jnp.bfloat16)
        .reshape(tokens, heads_here, HEAD_DIM)
    )
    grad_query, grad_keys, grad_values = attention_backward(
        query, keys, values, allowed, log_total, grad_attended
    )
    query_low = flatten_low(grad_query, tokens)
    keys_low = flatten_low(grad_keys, tokens)
    values_low = flatten_low(grad_values, tokens)
    focus_joined = outer_rows(third_low, jnp.concatenate([query_low, keys_low, values_low], axis=1))
    grad_third = (
        project_t(query_low, focus_pair[0][0])
        + project_t(keys_low, focus_pair[0][1])
        + project_t(values_low, focus_pair[0][2])
    )
    grad_stream, gain_three = third_back(input_total(grad_third))
    grad_two = grad_three + grad_stream
    focus_grads = spread_grads(focus_joined, focus_mat_grad, 3)
    early_pair = (early_stack, early_mat)
    grad_second, early_joined, early_mat_grad = ffn_backward(
        grad_two.astype(jnp.bfloat16),
        second_low,
        early_gate,
        early_up,
        early_hidden,
        early_pair[0],
        early_pair[1],
    )
    grad_stream, gain_two = second_back(input_total(grad_second))
    grad_one = grad_two + grad_stream
    early_grads = spread_grads(early_joined, early_mat_grad, 2)
    mixer_pair = (mixer_stack, mixer_mats)
    grad_mixer_low = grad_one.astype(jnp.bfloat16)
    out_mat_grad = outer_rows(grad_mixer_low, mixer_low)
    grad_scanned = project(grad_mixer_low, mixer_pair[1][:width])
    (
        grad_channel,
        grad_step_low,
        gate_low,
        in_sums,
        out_sums,
        step_bias_grad,
        decay_log_grad,
        skip_gain_grad,
    ) = scan_backward(
        keeping, channel_low, step_raw, gate_half, grad_scanned, step_bias, rates_t, skip_gain, in_wide, out_wide,
        groups, LANES,
    )
    step_mat_grad = outer_rows(rank_low, grad_step_low)
    grad_rank = project_t(grad_step_low, mixer_pair[1][width + PROJ_OUT :])
    grad_rows = lax.psum(
        jnp.concatenate([grad_rank, jnp.sum(in_sums, axis=-1), jnp.sum(out_sums, axis=-1)], axis=1), "tensor"
    )
    grad_rows_low = grad_rows.astype(jnp.bfloat16)
    select_mat_grad = outer_rows(grad_rows_low, channel_low)
    grad_channel = grad_channel + project(grad_rows_low, mixer_pair[1][width : width + PROJ_OUT])
    grad_conv_in, conv_weight_grad, conv_bias_grad = conv_back(grad_channel)
    conv_low = grad_conv_in.astype(jnp.bfloat16)
    mixer_joined = outer_rows(first_low, jnp.concatenate([conv_low, gate_low], axis=1))
    grad_first = project_t(conv_low, mixer_pair[0][0]) + project_t(gate_low, mixer_pair[0][1])
    grad_stream, gain_one = first_back(input_total(grad_first))
    input_grad = grad_one + grad_stream
    mixer_grads = spread_grads(
        mixer_joined, jnp.concatenate([out_mat_grad, select_mat_grad, step_mat_grad], axis=0), 2
    )
    small_sums = lax.psum(
        (
            jnp.stack([gain_one, gain_two, gain_three, gain_four]),
            conv_weight_grad,
            conv_bias_grad,
            step_bias_grad[0],
            decay_log_grad.T,
            skip_gain_grad[0],
        ),
        "dp",
    )
    return (
        output,
        input_grad,
        small_sums[0],
        mixer_grads[0],
        mixer_grads[1],
        small_sums[1],
        small_sums[2],
        small_sums[3],
        small_sums[4],
        small_sums[5],
        early_grads[0],
        early_grads[1],
        focus_grads[0],
        focus_grads[1],
        late_grads[0],
        late_grads[1],
    )


MESH = pl.DeviceIdType.MESH


def turns(group):
    return [turned for turned in (6, 2, 4) if turned & group == turned]


class Place:
    def __init__(self, ways):
        self.spot = lax.axis_index("dp")
        self.depth = lax.axis_index("tensor")
        self.ways = ways
        self.core = lax.rem(self.spot, 2)
        self.partner = self.spot + 1 - 2 * self.core

    def bit(self, axis, turned):
        value = lax.rem(self.spot // axis, 2)
        return 1 - value if turned & axis else value

    def across(self, turned, swapped=False):
        move = 1 - 2 * self.core if swapped else 0
        for axis in (2, 4):
            if turned & axis:
                move = move + axis * (1 - 2 * self.bit(axis, 0))
        return self.spot + move

    def side(self, group, turned=0):
        if group == 6:
            return self.bit(2, turned) + 2 * self.bit(4, turned)
        return self.bit(group, turned) if group else 0

    def along(self, offset):
        return lax.rem(self.depth + offset, self.ways)


def send(source, target, sems, at, spot, depth):
    copy = pltpu.make_async_remote_copy(
        src_ref=source,
        dst_ref=target,
        send_sem=sems[0].at[at],
        recv_sem=sems[1].at[at],
        device_id=(spot, depth),
        device_id_type=MESH,
    )
    copy.start()
    return copy


def greet(place, ways, both=False):
    barrier = pltpu.get_barrier_semaphore()
    peers = [(place.partner, place.depth)]
    peers += [(place.across(turned), place.depth) for turned in ways]
    if both:
        peers += [(place.across(turned, True), place.depth) for turned in ways]
    peers += [(place.spot, place.along(offset)) for offset in range(1, place.ways)]
    for peer in peers:
        pl.semaphore_signal(barrier, inc=1, device_id=peer, device_id_type=MESH)
    pl.semaphore_wait(barrier, len(peers))


def rows_at(start, size, unit):
    return pl.ds(pl.multiple_of(start * unit, unit), size)


class Reduction:
    def __init__(self, place, group, rows, parts, part_ref, near_s, sum_s, far_s, sems, names):
        self.place, self.group, self.rows, self.parts = place, group, rows, parts
        self.part_ref, self.near_s, self.sum_s, self.far_s = part_ref, near_s, sum_s, far_s
        self.sems = [sems[name] for name in names]
        self.ways = turns(group) + [0]
        self.step = part_ref.shape[1] // parts
        self.near, self.far = {}, {}

    def lanes(self, part):
        return pl.ds(part * self.step, self.step)

    def block(self, side):
        return rows_at(side, self.rows, self.rows)

    def send_near(self):
        place = self.place
        for part in range(self.parts):
            for at, turned in enumerate(self.ways):
                side = place.side(self.group, turned)
                self.near[part, turned] = send(
                    self.part_ref.at[self.block(side * 2 + 1 - place.core), self.lanes(part)],
                    self.near_s.at[self.block(side), self.lanes(part)],
                    self.sems[0], part * len(self.ways) + at, place.partner, place.depth,
                )

    def joined(self, part, turned):
        self.near[part, turned].wait_recv()
        side, lanes = self.place.side(self.group, turned), self.lanes(part)
        own = self.part_ref[self.block(side * 2 + self.place.core), lanes].astype(jnp.float32)
        return own + self.near_s[self.block(side), lanes].astype(jnp.float32)

    def order(self):
        half = self.parts // 2
        return [at + first for at in range(half) for first in (0, half)]

    def leg(self, part):
        return (2, 4) if part < self.parts // 2 else (4, 2)

    def push(self, part, turned, slot, to, value):
        rows, lanes = self.block(self.place.side(self.group, turned)), self.lanes(part)
        self.sum_s[rows, lanes] = value.astype(self.sum_s.dtype)
        self.far[part, slot] = send(
            self.sum_s.at[rows, lanes], self.far_s.at[slot, :, lanes],
            self.sems[1], part * 3 + slot, self.place.across(to), self.place.depth,
        )

    def came(self, part, slot):
        self.far[part, slot].wait_recv()
        return self.far_s[slot, :, self.lanes(part)].astype(jnp.float32)

    def send_far(self):
        if self.group:
            for part in self.order():
                first, _ = self.leg(part)
                self.push(part, 6, 1, first, self.joined(part, 6))
                self.push(part, first, 0, first, self.joined(part, first))

    def relay(self):
        if self.group:
            for part in self.order():
                _, second = self.leg(part)
                value = self.joined(part, second) + self.came(part, 1)
                self.push(part, second, 2, second, value)

    def chip_sum(self, part):
        total = self.joined(part, 0)
        if self.group:
            total = total + self.came(part, 0) + self.came(part, 2)
        return total

    def sent(self):
        return list(self.near.values()) + list(self.far.values())


def deep_sends(place, share, source, start, deep_s, lanes, sems, at):
    return [
        send(
            source.at[pl.ds(pl.multiple_of(start + place.along(offset) * share, share), share), lanes],
            deep_s.at[offset - 1, :, lanes],
            sems, at + offset - 1, place.spot, place.along(offset),
        )
        for offset in range(1, place.ways)
    ]


def deep_total(place, share, source, start, deep_s, copies):
    for copy in copies:
        copy.wait_recv()
    total = source[pl.ds(pl.multiple_of(start + place.depth * share, share), share), :].astype(jnp.float32)
    for offset in range(1, place.ways):
        total = total + deep_s[offset - 1].astype(jnp.float32)
    return total


def reduce_stage(first, deep_s, sems, between):
    place, rows = first.place, first.rows
    share = rows // place.ways
    first.send_near()
    between(0)
    first.send_far()
    first.relay()
    between(1)
    deep = []
    mine = place.side(first.group)
    for part in first.order() if first.group else range(first.parts):
        first.sum_s[first.block(mine), first.lanes(part)] = first.chip_sum(part).astype(first.sum_s.dtype)
        deep += deep_sends(
            place, share, first.sum_s, mine * rows, deep_s, first.lanes(part), sems["deep"], part * (place.ways - 1)
        )
    return deep_total(place, share, first.sum_s, mine * rows, deep_s, deep), first.sent() + deep


def hand_on(place, group, rows_of, target, sems, base, far):
    half = target.shape[1] // 2
    for came, to, lanes in ((2, 4, pl.ds(0, half)), (4, 2, pl.ds(half, half))):
        far[came].wait_recv()
        block = target.at[rows_of(came), lanes]
        far[came, to] = send(block, block, sems, base + to // 2 + 1, place.across(to), place.depth)


def first_leg(place, block, sems, base):
    return {turned: send(block, block, sems, base + turned // 2 - 1, place.across(turned), place.depth) for turned in (2, 4)}


def gather_stage(place, group, rows, all_ref, sems, between):
    share = rows // place.ways

    def place_of(turned, offset):
        depth = place.along(place.ways - offset) if offset else place.depth
        return pl.ds(pl.multiple_of((place.side(group, turned) * 2 + place.core) * rows + depth * share, share), share)

    def to_partner(turned, offset, at):
        block = all_ref.at[place_of(turned, offset), :]
        return send(block, block, sems["near_back"], at * place.ways + offset, place.partner, place.depth)

    own = all_ref.at[place_of(0, 0), :]
    deep = [
        send(own, own, sems["deep_back"], offset - 1, place.spot, place.along(offset)) for offset in range(1, place.ways)
    ]
    far, near = [], []
    for offset in range(place.ways):
        if offset:
            deep[offset - 1].wait_recv()
        if group:
            far.append(first_leg(place, all_ref.at[place_of(0, offset), :], sems["far_back"], 4 * offset))
        near.append(to_partner(0, offset, 0))
        if offset == 0:
            between()
    if group:
        for offset in range(place.ways):
            hand_on(
                place, group, lambda turned: place_of(turned, offset), all_ref, sems["far_back"], 4 * offset, far[offset]
            )
            near.append(to_partner(2, offset, 1))
            near.append(to_partner(4, offset, 2))
        for offset in range(place.ways):
            far[offset][2, 4].wait_recv()
            far[offset][4, 2].wait_recv()
            near.append(to_partner(6, offset, 3))
    for copy in near:
        copy.wait_recv()
    return deep + [copy for one in far for copy in one.values()] + near


class Exchange:
    def __init__(self, place, items, sems):
        self.place, self.items, self.sems = place, items, sems
        self.copies, self.own = [], []

    def start(self):
        place = self.place
        spots = [place.across(turned, swapped) for turned in (6, 2, 4) for swapped in (False, True)] + [place.partner]
        for at, (source, target) in enumerate(self.items):
            for slot, spot in enumerate(spots):
                self.copies.append(
                    send(source(spot), target(place.spot), self.sems, at * 8 + slot, spot, place.depth)
                )
            own = pltpu.make_async_copy(source(place.spot), target(place.spot), self.sems[1].at[at * 8 + 7])
            own.start()
            self.own.append(own)

    def close(self):
        for copy in self.own + self.copies:
            copy.wait()


def columns_at(half, size):
    return pl.ds(pl.multiple_of(half * size, size), size)


def blocks_of(refs, size):
    return [(ref, at) for ref in refs for at in range(ref.shape[2] // size)]


def spread_items(size, refs, out):
    return [
        (
            lambda spot, ref=ref, at=at: ref.at[spot, :, pl.ds(at * size, size)],
            lambda spot, to=to: out.at[to, :, columns_at(spot, size)],
        )
        for to, (ref, at) in enumerate(blocks_of(refs, size))
    ]


def chip_items(size, refs, out):
    return [
        (
            lambda spot, ref=ref, at=at: ref.at[spot, :, pl.ds(at * size, size)],
            lambda spot, to=to: out.at[spot // 2, to, :, columns_at(spot % 2, size)],
        )
        for to, (ref, at) in enumerate(blocks_of(refs, size))
    ]


def layers(refs):
    return [ref.at[at] if len(ref.shape) == 3 else ref for ref in refs for at in range(ref.shape[0] if len(ref.shape) == 3 else 1)]


def plane_items(spots, refs, out):
    blocks = layers(refs)
    size = blocks[0].shape[1] // spots
    return [
        (
            lambda spot, block=block: block.at[:, columns_at(spot, size)],
            lambda spot, at=at: out.at[spot, :, pl.ds(at * size, size)],
        )
        for at, block in enumerate(blocks)
    ]


def core_items(refs, out):
    blocks = layers(refs)
    size = blocks[0].shape[1] // 2
    return [
        (
            lambda half, block=block: block.at[:, columns_at(half, size)],
            lambda spot, at=at: out.at[spot, :, pl.ds(at * size, size)],
        )
        for at, block in enumerate(blocks)
    ]


def handed_items(out):
    return [(None, lambda spot: out.at[spot])]


class Load:
    def __init__(self, mode, arrays, out, items, count, stage):
        self.mode, self.arrays, self.items, self.count, self.stage = mode, arrays, items, count, stage
        self.out = jax.ShapeDtypeStruct(out, arrays[0].dtype)

    def begin(self, place, refs, out, sems):
        if self.mode == "second":
            mover = Pull(place, self.items(out), sems)
            mover.second(False)
        elif self.mode == "first":
            mover = Pull(place, self.items(refs, out), sems)
            mover.first()
        else:
            mover = Exchange(place, self.items(refs, out), sems)
            mover.start()
        return mover


def spread_stage(place, rows, all_ref, sems, name="deep_back"):
    share = rows // place.ways
    own = all_ref.at[pl.ds(pl.multiple_of(place.depth * share, share), share), :]
    deep = [
        send(own, own, sems[name], offset - 1, place.spot, place.along(offset)) for offset in range(1, place.ways)
    ]
    return deep


def small_stage(place, half, sum_ref, small_s, sems):
    near = [
        send(
            sum_ref.at[pl.ds(part * half, half), :], small_s.at[part], sems["small"], part, place.partner, place.depth
        )
        for part in range(2)
    ]
    for copy in near:
        copy.wait()
    mine = pl.ds(pl.multiple_of(place.core * half, half), half)
    small_s[2] = sum_ref[mine, :] + small_s[place.core]
    chips = [
        send(small_s.at[2], small_s.at[3 + at], sems["small"], 2 + at, spot, place.depth)
        for at, spot in enumerate((place.across(2), place.across(4), place.across(6)))
    ]
    for copy in chips:
        copy.wait_recv()
    total = small_s[2] + small_s[3] + small_s[4] + small_s[5]
    small_s[6] = total
    deep = [
        send(
            small_s.at[6, pl.ds(half - 8, 8), :], small_s.at[6 + offset, pl.ds(half - 8, 8), :],
            sems["small"], 4 + offset, place.spot, place.along(offset),
        )
        for offset in range(1, place.ways)
    ]
    for copy in deep:
        copy.wait_recv()
    gains = small_s[6, half - 8 : half, :]
    for offset in range(1, place.ways):
        gains = gains + small_s[6 + offset, half - 8 : half, :]
    last = jnp.where(place.core == 1, gains, total[half - 8 : half, :])
    ready, came = 6 + place.ways, 7 + place.ways
    small_s[ready] = jnp.concatenate([total[: half - 8, :], last], axis=0)
    back = send(small_s.at[ready], small_s.at[came], sems["small"], 4 + place.ways, place.partner, place.depth)
    sum_ref[mine, :] = small_s[ready]
    back.wait_recv()
    sum_ref[pl.ds(pl.multiple_of((1 - place.core) * half, half), half), :] = small_s[came]
    return chips + deep + [back]


def sem_shapes(names):
    shapes = []
    for count in names.values():
        shapes += [pltpu.SemaphoreType.DMA((count,))] * 2
    return shapes


def sem_dict(names, refs):
    return {name: (refs[2 * at], refs[2 * at + 1]) for at, name in enumerate(names)}


def edge_kernel(kind, extra, loads, ways, rows, parts, in_group, out_group, names, counts, *refs):
    place = Place(ways)
    share = rows // ways
    ins, outs = list(refs[: counts[0]]), list(refs[counts[0] : counts[0] + counts[1]])
    scratch = list(refs[counts[0] + counts[1] : counts[0] + counts[1] + counts[2]])
    sems = sem_dict(names, refs[sum(counts) :])
    part_ref = ins.pop(0)
    near_s, sum_s, far_s, deep_s = [scratch.pop(0) for _ in range(4)]
    if kind == "forward":
        stream_ref, gain_ref = ins.pop(0), ins.pop(0)
    elif kind != "sum":
        stream_ref, gain_ref, grad_ref = ins.pop(0), ins.pop(0), ins.pop(0)
    all_ref = outs.pop(0)
    if kind != "sum" and kind != "last":
        fresh_ref = outs.pop(0)
    if kind == "backward":
        dgain_ref = outs.pop(0)
    if kind == "last":
        small_ref, late_ref, three_ref = ins.pop(0), ins.pop(0), ins.pop(0)
        dgain_ref, late_out_ref = outs.pop(0), outs.pop(0)
        low_s, small_s, late_s, late_low_s = [scratch.pop(0) for _ in range(4)]
    moving = []
    for load in reversed(loads):
        moving.append(([ins.pop() for _ in load.arrays][::-1], outs.pop()))
    moving = moving[::-1]
    everyone = loads or kind == "last"
    greet(place, turns(6) if everyone else sorted({*turns(in_group), *turns(out_group)}), bool(loads))
    first = Reduction(place, in_group, rows, parts, part_ref, near_s, sum_s, far_s, sems, ("near", "far"))
    waiting = []
    freight = {}
    if extra == "gather":
        load_ref, load_out_ref = ins.pop(0), outs.pop(0)

        def load_rows(turned):
            return rows_at(place.side(in_group, turned) * 2 + place.core, rows, rows)

        def between(stage):
            spot = rows_at(place.side(in_group) * 2 + place.core, rows, rows)
            if stage == 0:
                load_out_ref[spot, :] = load_ref[...]
                return
            own = load_out_ref.at[spot, :]
            if stage == 1:
                freight.update(first_leg(place, own, sems["load_far"], 0))
                freight[0] = send(own, own, sems["load_near"], 0, place.partner, place.depth)
            else:
                hand_on(place, in_group, load_rows, load_out_ref, sems["load_far"], 0, freight)

    elif extra == "reduce":
        second = Reduction(
            place, in_group, rows, parts, ins.pop(0), *[scratch.pop(0) for _ in range(3)], sems, ("load_near", "load_far")
        )
        load_out_ref = outs.pop(0)

        def between(stage):
            (second.send_near, second.send_far, second.relay)[stage]()

    else:

        def between(stage):
            pass

    carried = []

    def on_the_way(stage):
        between(stage)
        for at, load in enumerate(loads):
            if load.stage == stage:
                carried.append(load.begin(place, *moving[at], sems[f"load{at}"]))

    if kind == "last":
        late = deep_sends(place, share, late_ref, 0, late_s, slice(None), sems["late"], 0)
        waiting += late
    total, copies = reduce_stage(first, deep_s, sems, on_the_way)
    waiting += copies
    if kind == "forward":
        fresh = stream_ref[...] + total
        fresh_ref[...] = fresh
        scale = lax.rsqrt(jnp.mean(fresh * fresh, axis=-1, keepdims=True) + EPS)
        value = fresh * scale * gain_ref[...]
    elif kind == "sum":
        value = total
    else:
        stream = stream_ref[...]
        scale = lax.rsqrt(jnp.mean(stream * stream, axis=-1, keepdims=True) + EPS)
        leaned = total * gain_ref[...]
        inner = jnp.mean(leaned * stream, axis=-1, keepdims=True)
        value = grad_ref[...] + scale * leaned - stream * (scale * scale * scale * inner)
        dgain = jnp.sum(total * stream * scale, axis=0, keepdims=True)
        if kind == "backward":
            dgain_ref[...] = dgain
            fresh_ref[...] = value
    if kind == "last":
        own = pl.ds(pl.multiple_of(place.depth * share, share), share)
        low_s[own, :] = value.astype(low_s.dtype)
        spread = spread_stage(place, rows, low_s, sems)
        late_total = three_ref[...] + deep_total(place, share, late_ref, 0, late_s, late)
        late_low_s[own, :] = late_total.astype(late_low_s.dtype)
        spread += spread_stage(place, rows, late_low_s, sems, "late_back")
        half, span = small_ref.shape[0] // 2, small_ref.shape[1]
        dgain_ref[...] = small_ref[...]
        for at in range(dgain.shape[1] // span):
            dgain_ref[pl.ds(2 * half - 8 + at, 1), :] = dgain[:, at * span : (at + 1) * span]
        waiting += spread + small_stage(place, half, dgain_ref, small_s, sems)
        for copy in spread:
            copy.wait_recv()
        all_ref[...] = low_s[...].astype(jnp.float32)
        late_out_ref[...] = late_low_s[...].astype(jnp.float32)
    else:
        spot = pl.multiple_of((place.side(out_group) * 2 + place.core) * rows + place.depth * share, share)
        all_ref[pl.ds(spot, share), :] = value.astype(all_ref.dtype)
        waiting += gather_stage(place, out_group, rows, all_ref, sems, partial(on_the_way, 2))
    if extra == "gather":
        last = []
        for at, turned in enumerate((2, 4, 6)):
            for key in ((2, 4), (4, 2)) if turned == 6 else ():
                freight[key].wait_recv()
            came = load_out_ref.at[load_rows(turned), :]
            last.append(send(came, came, sems["load_near"], 1 + at, place.partner, place.depth))
        for copy in last + [freight[0]]:
            copy.wait_recv()
        waiting += list(freight.values()) + last
    elif extra == "reduce":
        for part in range(parts):
            load_out_ref[:, second.lanes(part)] = second.chip_sum(part).astype(load_out_ref.dtype)
        waiting += second.sent()
    for mover in carried:
        mover.close()
    for copy in waiting:
        copy.wait_send()


def edge(kind, part, extras, ways, rows, parts, in_group, out_group, ident, name, extra=None, loads=()):
    width = part.shape[1]
    share = rows // ways
    in_far, out_far = len(turns(in_group)), len(turns(out_group or 0))
    in_sides, out_sides = in_far + 1, out_far + 1
    dtype = part.dtype
    line = jax.ShapeDtypeStruct((1, width), jnp.float32)
    strip = jax.ShapeDtypeStruct((share, width), jnp.float32)
    whole = jax.ShapeDtypeStruct((out_sides * 2 * rows, width), dtype)
    block = jax.ShapeDtypeStruct((rows, width), jnp.float32)
    outs = {
        "forward": [whole, strip],
        "backward": [whole, strip, line],
        "last": [block] + [jax.ShapeDtypeStruct(one.shape, one.dtype) for one in extras[3:4]] + [block],
        "sum": [whole],
    }[kind]
    names = {"near": parts * in_sides, "far": 3 * parts if in_far else 0, "deep": parts * (ways - 1), "deep_back": ways - 1}
    reducing = [
        pltpu.VMEM((in_sides * rows, width), dtype),
        pltpu.VMEM((in_sides * rows, width), dtype),
        pltpu.VMEM((max(in_far, 1), rows if in_far else 16, width), dtype),
    ]
    deep = pltpu.VMEM((ways - 1, share, width), dtype)
    scratch = reducing + [deep]
    if kind == "last":
        names.update({"small": 5 + ways, "late": ways - 1, "late_back": ways - 1})
        small = pltpu.VMEM((8 + ways, extras[3].shape[0] // 2, extras[3].shape[1]), jnp.float32)
        spread = pltpu.VMEM((rows, width), dtype)
        scratch += [spread, small, deep, spread]
    else:
        names.update({"far_back": 4 * ways if out_far else 0, "near_back": ways * out_sides})
    if extra == "gather":
        names.update({"load_far": 4, "load_near": in_sides})
        outs = outs + [jax.ShapeDtypeStruct((in_sides * 2 * rows, width), dtype)]
    elif extra == "reduce":
        names.update({"load_far": 3 * parts, "load_near": parts * in_sides})
        outs = outs + [jax.ShapeDtypeStruct((rows, width), dtype)]
        scratch = scratch + reducing
    vmem, whole_memory = pl.BlockSpec(memory_space=pltpu.VMEM), pl.BlockSpec(memory_space=pl.ANY)
    in_specs, out_specs = [vmem] * (1 + len(extras)), [vmem] * len(outs)
    aliases, extras, outs = {}, list(extras), list(outs)
    for at, load in enumerate(loads):
        names[f"load{at}"] = 8 * load.count
        if load.mode == "second":
            aliases[1 + len(extras)] = len(outs)
        extras += load.arrays
        outs.append(load.out)
        in_specs += [whole_memory] * len(load.arrays)
        out_specs.append(whole_memory)
    names = {key: count for key, count in names.items() if count}
    if not in_far:
        names["far"] = 1
    return pl.pallas_call(
        partial(
            edge_kernel, kind, extra, loads, ways, rows, parts, in_group, out_group, names,
            (1 + len(extras), len(outs), len(scratch)),
        ),
        in_specs=in_specs,
        out_specs=out_specs,
        out_shape=outs,
        scratch_shapes=scratch + sem_shapes(names),
        input_output_aliases=aliases,
        compiler_params=pltpu.CompilerParams(
            collective_id=ident, has_side_effects=True, vmem_limit_bytes=48 << 20
        ),
        cost_estimate=pl.CostEstimate(flops=1, bytes_accessed=1, transcendentals=0),
        name=name,
    )(part, *extras)


class Pull:
    def __init__(self, place, items, sems):
        self.place, self.items, self.sems = place, items, sems
        self.copies, self.handed = {}, set()

    def go(self, at, key, slot, source, spot, target):
        self.copies[at, key] = send(source, target, self.sems, at * 8 + slot, spot, self.place.depth)

    def first(self):
        place = self.place
        for at, (source, target) in enumerate(self.items):
            mine = target(place.spot)
            for turned in (2, 4):
                self.go(at, (turned, False), turned - 2, source(place.core), place.across(turned), mine)
                self.go(at, (turned, True), turned - 1, source(1 - place.core), place.across(turned, True), mine)
            self.go(at, "near", 4, source(1 - place.core), place.partner, mine)
            own = pltpu.make_async_copy(source(place.core), mine, self.sems[1].at[at * 8 + 7])
            own.start()
            self.copies[at, "own"] = own

    def second(self, fresh=True):
        place = self.place
        for at, (_, target) in enumerate(self.items):
            for slot, turned, swapped, to in ((5, 2, False, 4), (6, 4, True, 2)):
                if fresh:
                    self.copies[at, (turned, swapped)].wait_recv()
                    self.handed.add((at, (turned, swapped)))
                block = target(place.across(turned, swapped))
                self.go(at, ("on", turned), slot, block, place.across(to), block)

    def close(self):
        for (at, key), copy in self.copies.items():
            if key == "own":
                copy.wait()
            else:
                if (at, key) not in self.handed:
                    copy.wait_recv()
                copy.wait_send()


def opening_kernel(ways, rows, hidden_ref, gain_ref, in_ref, rows_ref, first_ref, in_out, rows_out, *sems):
    place = Place(ways)
    greet_plane(place)
    size = rows_out.shape[2]
    items = [
        (
            lambda half, at=at: in_ref.at[at, :, columns_at(half, size)],
            lambda spot, at=at: in_out.at[spot, :, pl.ds(at * size, size)],
        )
        for at in range(in_ref.shape[0])
    ]
    items.append((lambda half: rows_ref.at[:, columns_at(half, size)], lambda spot: rows_out.at[spot]))
    pull = Pull(place, items, sems[2:])
    pull.first()
    stream = hidden_ref[...].astype(jnp.float32)
    scale = lax.rsqrt(jnp.mean(stream * stream, axis=-1, keepdims=True) + EPS)
    first_ref[rows_at(place.core, rows, rows), :] = (stream * scale * gain_ref[...]).astype(jnp.bfloat16)
    mine = first_ref.at[rows_at(place.core, rows, rows), :]
    copy = send(mine, mine, sems[:2], 0, place.partner, place.depth)
    pull.second()
    copy.wait()
    pull.close()


def greet_plane(place):
    barrier = pltpu.get_barrier_semaphore()
    peers = [place.partner] + [place.across(turned, swapped) for turned in (2, 4) for swapped in (False, True)]
    for peer in peers:
        pl.semaphore_signal(barrier, inc=1, device_id=(peer, place.depth), device_id_type=MESH)
    pl.semaphore_wait(barrier, len(peers))


def opening(hidden, gain, in_weights, row_weights, spots, ways, ident):
    rows, width = hidden.shape
    vmem, whole_memory = pl.BlockSpec(memory_space=pltpu.VMEM), pl.BlockSpec(memory_space=pl.ANY)
    kinds, depth, columns = in_weights.shape
    low = jnp.bfloat16
    return pl.pallas_call(
        partial(opening_kernel, ways, rows),
        in_specs=[vmem] * 2 + [whole_memory] * 2,
        out_specs=[vmem] + [whole_memory] * 2,
        out_shape=[
            jax.ShapeDtypeStruct((2 * rows, width), low),
            jax.ShapeDtypeStruct((spots, depth, kinds * columns // 2), low),
            jax.ShapeDtypeStruct((spots, row_weights.shape[0], columns // 2), low),
        ],
        scratch_shapes=[pltpu.SemaphoreType.DMA((1,))] * 2 + [pltpu.SemaphoreType.DMA((8 * (kinds + 1),))] * 2,
        compiler_params=pltpu.CompilerParams(
            collective_id=ident, has_side_effects=True, vmem_limit_bytes=40 << 20
        ),
        cost_estimate=pl.CostEstimate(flops=1, bytes_accessed=1, transcendentals=0),
        name="opening",
    )(hidden, gain, in_weights, row_weights)


def probs_of(query, keys, allowed):
    scores = project_t(query, keys) * (1.0 / math.sqrt(HEAD_DIM))
    scores = jnp.where(allowed, scores, NEG_FILL)
    shifted = jnp.exp(scores - jnp.max(scores, axis=-1, keepdims=True))
    return shifted / jnp.sum(shifted, axis=-1, keepdims=True)


def allowed_in(down_ref, side_ref, rows, group):
    shape = (rows, rows)
    distance = lax.broadcasted_iota(jnp.int32, shape, 0) - lax.broadcasted_iota(jnp.int32, shape, 1)
    same = down_ref[group * rows : (group + 1) * rows, :] == side_ref[group : group + 1, :]
    return same & (distance >= 0) & (distance < WINDOW)


def attend_kernel(heads, rows, joint_ref, down_ref, side_ref, low_ref, out_ref):
    low_ref[...] = joint_ref[...].astype(jnp.bfloat16)
    size = heads * HEAD_DIM
    for group in range(joint_ref.shape[0] // rows):
        allowed = allowed_in(down_ref, side_ref, rows, group)
        span = slice(group * rows, (group + 1) * rows)
        for head in range(heads):
            at = slice(head * HEAD_DIM, (head + 1) * HEAD_DIM)
            query, keys, values = [
                low_ref[span, part * size + head * HEAD_DIM : part * size + (head + 1) * HEAD_DIM] for part in range(3)
            ]
            probs = probs_of(query, keys, allowed)
            out_ref[span, at] = project(probs.astype(jnp.bfloat16), values).astype(jnp.bfloat16)


def attend(joint, down, side, rows):
    count, size = joint.shape
    return pl.pallas_call(
        partial(attend_kernel, size // (3 * HEAD_DIM), rows),
        out_shape=[
            jax.ShapeDtypeStruct((count, size), jnp.bfloat16),
            jax.ShapeDtypeStruct((count, size // 3), jnp.bfloat16),
        ],
        compiler_params=pltpu.CompilerParams(vmem_limit_bytes=32 << 20),
        name="attend",
    )(joint, down, side)


def attend_back_kernel(heads, rows, low_ref, grad_ref, down_ref, side_ref, out_ref):
    size = heads * HEAD_DIM
    scale = 1.0 / math.sqrt(HEAD_DIM)
    for group in range(low_ref.shape[0] // rows):
        allowed = allowed_in(down_ref, side_ref, rows, group)
        span = slice(group * rows, (group + 1) * rows)
        for head in range(heads):
            places = [slice(part * size + head * HEAD_DIM, part * size + (head + 1) * HEAD_DIM) for part in range(3)]
            query, keys, values = [low_ref[span, place] for place in places]
            grad = grad_ref[span, head * HEAD_DIM : (head + 1) * HEAD_DIM].astype(jnp.bfloat16)
            probs = probs_of(query, keys, allowed)
            grad_probs = project_t(grad, values)
            inner = jnp.sum(probs * grad_probs, axis=-1, keepdims=True)
            grad_scores = (probs * (grad_probs - inner)).astype(jnp.bfloat16)
            out_ref[span, places[0]] = (project(grad_scores, keys) * scale).astype(jnp.bfloat16)
            out_ref[span, places[1]] = (outer_rows(grad_scores, query) * scale).astype(jnp.bfloat16)
            out_ref[span, places[2]] = outer_rows(probs.astype(jnp.bfloat16), grad).astype(jnp.bfloat16)


def attend_back(low, grad, down, side, rows):
    count, size = low.shape
    return pl.pallas_call(
        partial(attend_back_kernel, size // (3 * HEAD_DIM), rows),
        out_shape=jax.ShapeDtypeStruct((count, size), jnp.bfloat16),
        compiler_params=pltpu.CompilerParams(vmem_limit_bytes=32 << 20),
        name="attend_back",
    )(low, grad, down, side)


def conv_total(stream, age_ref, taps_ref, offset_ref):
    moved = [stream] + [
        jnp.where(age_ref[...] >= lag, pltpu.roll(stream, lag, 0), 0.0) for lag in range(1, CONV)
    ]
    total = offset_ref[...]
    for lag in range(CONV):
        total = total + moved[lag] * taps_ref[lag : lag + 1, :]
    return total, moved


def front_kernel(first_ref, conv_mat_ref, gate_mat_ref, age_ref, taps_ref, offset_ref, select_ref, conv_ref, gate_ref,
                 channel_ref, mix_ref):
    stream = project(first_ref[...], conv_mat_ref[...])
    conv_ref[...] = stream
    gate_ref[...] = project(first_ref[...], gate_mat_ref[...])
    total, _ = conv_total(stream, age_ref, taps_ref, offset_ref)
    channel = (total / (1.0 + jnp.exp(-total))).astype(jnp.bfloat16)
    channel_ref[...] = channel

    @pl.when(pl.program_id(0) == 0)
    def _():
        mix_ref[...] = jnp.zeros_like(mix_ref)

    mix_ref[...] += project_t(channel, select_ref[...])


def front(first_low, in_mat, age, taps_t, offset, select):
    count, width = first_low.shape
    channels = in_mat.shape[1] // 2
    size = channels // 2
    column = pl.BlockSpec((count, size), lambda i: (0, i))
    sheet = jax.ShapeDtypeStruct((count, channels), jnp.float32)
    return pl.pallas_call(
        front_kernel,
        grid=(2,),
        in_specs=[
            pl.BlockSpec((count, width), lambda i: (0, 0)),
            pl.BlockSpec((width, size), lambda i: (0, i)),
            pl.BlockSpec((width, size), lambda i: (0, i + 2)),
            pl.BlockSpec((count, 1), lambda i: (0, 0)),
            pl.BlockSpec((CONV, size), lambda i: (0, i)),
            pl.BlockSpec((1, size), lambda i: (0, i)),
            pl.BlockSpec((select.shape[0], size), lambda i: (0, i)),
        ],
        out_specs=[column, column, column, pl.BlockSpec((count, select.shape[0]), lambda i: (0, 0))],
        out_shape=[
            sheet, sheet, jax.ShapeDtypeStruct((count, channels), jnp.bfloat16),
            jax.ShapeDtypeStruct((count, select.shape[0]), jnp.float32),
        ],
        compiler_params=pltpu.CompilerParams(vmem_limit_bytes=40 << 20),
        name="front",
    )(first_low, in_mat, in_mat, age, taps_t, offset, select)


def front_back_kernel(conv_ref, age_ref, left_ref, taps_ref, offset_ref, scan_ref, mix_ref, select_ref, low_ref, grads_ref):
    total, moved = conv_total(conv_ref[...], age_ref, taps_ref, offset_ref)
    sig = 1.0 / (1.0 + jnp.exp(-total))
    grad = (scan_ref[...] + project(mix_ref[...], select_ref[...])) * (sig * (1.0 + total * (1.0 - sig)))
    count = grad.shape[0]
    back = grad * taps_ref[0:1, :]
    for lag in range(1, CONV):
        back = back + jnp.where(left_ref[...] >= lag, pltpu.roll(grad, count - lag, 0), 0.0) * taps_ref[lag : lag + 1, :]
    low_ref[...] = back.astype(jnp.bfloat16)
    for lag in range(CONV):
        grads_ref[lag : lag + 1, :] = jnp.sum(grad * moved[lag], axis=0, keepdims=True)
    grads_ref[CONV : CONV + 1, :] = jnp.sum(grad, axis=0, keepdims=True)
    grads_ref[CONV + 1 :, :] = jnp.zeros((3, grad.shape[1]), jnp.float32)


def front_back(conv_in, age, left, taps_t, offset, grad_scan, grad_mix, select):
    count, channels = conv_in.shape
    size = channels // 2
    column = pl.BlockSpec((count, size), lambda i: (0, i))
    place = pl.BlockSpec((count, 1), lambda i: (0, 0))
    return pl.pallas_call(
        front_back_kernel,
        grid=(2,),
        in_specs=[
            column, place, place,
            pl.BlockSpec((CONV, size), lambda i: (0, i)),
            pl.BlockSpec((1, size), lambda i: (0, i)),
            column,
            pl.BlockSpec((count, select.shape[0]), lambda i: (0, 0)),
            pl.BlockSpec((select.shape[0], size), lambda i: (0, i)),
        ],
        out_specs=[column, pl.BlockSpec((8, size), lambda i: (0, i))],
        out_shape=[
            jax.ShapeDtypeStruct((count, channels), jnp.bfloat16),
            jax.ShapeDtypeStruct((8, channels), jnp.float32),
        ],
        compiler_params=pltpu.CompilerParams(vmem_limit_bytes=40 << 20),
        name="front_back",
    )(conv_in, age, left, taps_t, offset, grad_scan, grad_mix, select)


def sub_of(spot, group):
    if group == 6:
        return spot
    return spot % 2 + (2 * ((spot // group) % 2) if group else 0)


def subs_of(group):
    return 2 * (len(turns(group)) + 1)


def pull(count, *sets):
    def cut(block, group, spot):
        size = block.shape[1] // subs_of(group)
        return block[:, sub_of(spot, group) * size : (sub_of(spot, group) + 1) * size]

    return jnp.stack(
        [
            jnp.concatenate([cut(block, group, spot) for blocks, group in sets for block in blocks], axis=1)
            for spot in range(count)
        ]
    )


def in_order(value):
    return with_layout_constraint(value, Layout(major_to_minor=tuple(range(value.ndim))))


def swap(stacked):
    return lax.all_to_all(stacked, "dp", 0, 0, tiled=True)


def spread_out_kernel(came_ref, pair_ref, last_ref, sum_ref):
    size = last_ref.shape[1] // 2
    half = came_ref.shape[2] - 3 * size

    @pl.when(pl.program_id(0) == 0)
    def _():
        sum_ref[...] = jnp.zeros_like(sum_ref)

    for core in range(2):
        to = slice(core * size, (core + 1) * size)
        for at in range(2):
            pair_ref[at, :, to] = came_ref[core, :, at * size : (at + 1) * size].astype(jnp.float32)
        last_ref[:, to] = came_ref[core, :, 2 * size : 3 * size].astype(jnp.float32)
        sum_ref[:, core * half : (core + 1) * half] += came_ref[core, :, 3 * size :].astype(jnp.float32)


def spread_out(came, columns):
    spots, rows, _ = came.shape
    size, half = columns // 3, came.shape[2] - columns
    return pl.pallas_call(
        spread_out_kernel,
        grid=(spots // 2,),
        in_specs=[pl.BlockSpec((2, rows, came.shape[2]), lambda i: (i, 0, 0))],
        out_specs=[
            pl.BlockSpec((2, rows, 2 * size), lambda i: (0, 0, i)),
            pl.BlockSpec((rows, 2 * size), lambda i: (0, i)),
            pl.BlockSpec((rows, 2 * half), lambda i: (0, 0)),
        ],
        out_shape=[
            jax.ShapeDtypeStruct((2, rows, spots * size), jnp.float32),
            jax.ShapeDtypeStruct((rows, spots * size), jnp.float32),
            jax.ShapeDtypeStruct((rows, 2 * half), jnp.float32),
        ],
        compiler_params=pltpu.CompilerParams(vmem_limit_bytes=32 << 20),
        name="spread_out",
    )(came)


def chip_total(came):
    return jnp.sum(came.astype(jnp.float32), axis=0)


def after(value, *others):
    return lax.optimization_barrier((value,) + others)[0]


def grouped_body(
    counts,
    early_group,
    focus_group,
    late_group,
    hidden_in,
    seq_lengths,
    norm_gains,
    mixer_in,
    mixer_rows,
    conv_weight,
    conv_bias,
    step_bias,
    decay_log,
    skip_gain,
    early_gate_up,
    early_down,
    attention_in,
    attention_out,
    late_gate_up,
    late_down,
    output_grad,
):
    spots, ways = counts
    rows, width = hidden_in.shape
    share = rows // ways
    spot = lax.axis_index("dp")
    depth = lax.axis_index("tensor")
    core = spot % 2
    low = jnp.bfloat16

    def swapped_core(value):
        return lax.ppermute(value, "dp", [(at, at ^ 1) for at in range(spots)])

    own_rows = mixer_rows.shape[0]
    padded_rows = jnp.pad(mixer_rows, ((0, -own_rows % 16), (0, 0)))
    first_low, in_weights, row_weights = opening(
        hidden_in, norm_gains[0:1], mixer_in, padded_rows, spots, ways, 20
    )
    row_weights = row_weights[:, :own_rows]

    other_lengths = swapped_core(seq_lengths)
    lengths = jnp.where(
        core == 0, jnp.stack([seq_lengths, other_lengths]), jnp.stack([other_lengths, seq_lengths])
    )
    segs, starts = jax.vmap(lambda own: segment_info(own, rows))(lengths)
    flat_segs = (segs + jnp.arange(2, dtype=jnp.int32)[:, None] * rows).reshape(-1)
    keeping = 1.0 - starts.reshape(-1).astype(jnp.float32)
    groups = 2 * seq_lengths.shape[0]
    flat_lengths = lengths.reshape(2, -1)
    ends = jnp.cumsum(flat_lengths, axis=1) + jnp.arange(2, dtype=jnp.int32)[:, None] * rows
    firsts = (ends - flat_lengths).reshape(1, -1)
    ends = ends.reshape(1, -1)
    places = jnp.arange(2 * rows, dtype=jnp.int32)[:, None]
    age = places - jnp.max(jnp.where(firsts <= places, firsts, 0), axis=1, keepdims=True)
    left = jnp.min(jnp.where(ends > places, ends, 2 * rows), axis=1, keepdims=True) - 1 - places

    stream_zero = lax.dynamic_slice_in_dim(hidden_in, depth * share, share, 0).astype(jnp.float32)

    channels = conv_weight.shape[0] // 2

    def half(values):
        return lax.dynamic_slice_in_dim(values, core * channels, channels, 0)

    taps, offset, bias, decay, skip = [half(v) for v in (conv_weight, conv_bias, step_bias, decay_log, skip_gain)]
    in_mat = in_weights.reshape(width, 2 * channels)
    taps_t = taps.T
    row_mat = row_weights.reshape(-1, channels)
    early_blocks = [early_gate_up[0], early_gate_up[1], early_down]
    early_weights = swap(after(pull(spots, (early_blocks, early_group)), first_low))
    out_mat = row_mat[:width]
    select_mat = row_mat[width : width + PROJ_OUT]
    step_mat = row_mat[width + PROJ_OUT :]

    def spread_load(joints, size, stage):
        count = sum(one.shape[2] // size for one in joints)
        return Load(
            "exchange", joints, (count, joints[0].shape[1], spots * size), partial(spread_items, size), count, stage
        )

    def chip_load(joints, size, stage):
        count = sum(one.shape[2] // size for one in joints)
        out = (spots // 2, count, joints[0].shape[1], 2 * size)
        return Load("exchange", joints, out, partial(chip_items, size), count, stage)

    def by_spot(joint):
        return joint.astype(low).reshape(spots, -1, joint.shape[1])

    def mixed_sum(part, ident, name, loads=()):
        total, *came = edge("sum", part, [], ways, rows, 1, 0, 0, ident, name, loads=loads)
        return total[:, :PROJ_OUT], *came

    wide_select = jnp.pad(select_mat, ((0, 256 - PROJ_OUT), (0, 0)))
    conv_in, gate_half, channel_low, mix_part = front(first_low, in_mat, age, taps_t, offset[None], wide_select)
    mix_rows, = mixed_sum(mix_part, 1, "mix_sum")
    rank_low = mix_rows[:, :DT_RANK].astype(low)
    step_raw = project(rank_low, step_mat)
    rates_t = -jnp.exp(decay).T
    wide = (2 * rows, STATE, LANES)
    in_wide = jnp.broadcast_to(mix_rows[:, DT_RANK : DT_RANK + STATE, None], wide)
    out_wide = jnp.broadcast_to(mix_rows[:, DT_RANK + STATE :, None], wide)
    mixer_low = scan_forward(
        keeping, channel_low, step_raw, gate_half, bias, rates_t, skip, in_wide, out_wide, groups, LANES
    )
    early_mat = early_weights.reshape(width, -1)
    focus_blocks = [attention_in, attention_out]
    heads_width = attention_out.shape[1] // 2
    focus_pull = Load("first", focus_blocks, (spots, width // spots, 4 * heads_width), core_items, 4, 0)
    second_low, stream_one, focus_half = edge(
        "forward", project_t(mixer_low, out_mat).astype(low), [stream_zero, norm_gains[1:2]],
        ways, rows, 4, 0, early_group, 2, "edge_one", loads=[focus_pull],
    )

    def ffn(normed, mat):
        units = mat.shape[1] // 3
        both = project(normed, mat[:, : 2 * units])
        hidden = gated_unit(both[:, :units], both[:, units:]).astype(low)
        return project_t(hidden, mat[:, 2 * units :]).astype(low), both, hidden

    early_part, early_both, early_hidden = ffn(second_low, early_mat)
    third_low, stream_two, last_grad, focus_weights = edge(
        "forward", early_part, [stream_one, norm_gains[2:3], output_grad], ways, rows, 4, early_group, 0, 3, "edge_two",
        "gather", [Load("second", [focus_half], focus_half.shape, handed_items, 1, 1)],
    )
    focus_mat = focus_weights.reshape(width, -1)

    late_pull = Load(
        "exchange", [late_gate_up, late_down], (spots, width // spots, 3 * late_down.shape[1] // spots),
        partial(plane_items, spots), 3, 0,
    )
    down, side = flat_segs[:, None], flat_segs.reshape(2, rows)
    joint_low, attended_low = attend(project(third_low, focus_mat[:, : 3 * heads_width]), down, side, rows)
    fourth_low, stream_three, late_weights = edge(
        "forward", project_t(attended_low, focus_mat[:, 3 * heads_width :]).astype(low),
        [stream_two, norm_gains[3:4]], ways, rows, 4, 0, late_group, 4, "edge_three", loads=[late_pull],
    )

    late_mat = late_weights.reshape(width, -1)
    late_part, late_both, late_hidden = ffn(fourth_low, late_mat)

    def ffn_back(grad_low, normed, both, hidden, mat):
        units = mat.shape[1] // 3
        grad_hidden = project(grad_low, mat[:, 2 * units :])
        _, unit_back = jax.vjp(gated_unit, both[:, :units], both[:, units:])
        both_low = jnp.concatenate(unit_back(grad_hidden), axis=1).astype(low)
        grad_normed = project_t(both_low, mat[:, : 2 * units]).astype(low)
        return grad_normed, [by_spot(outer_rows(normed, both_low)), by_spot(outer_rows(grad_low, hidden))]

    grad_fourth, late_joints = ffn_back(last_grad, fourth_low, late_both, late_hidden, late_mat)
    grad_zero = lax.dynamic_slice_in_dim(output_grad, depth * share, share, 0).astype(jnp.float32)
    grad_low_three, grad_three, gain_four, output_part, late_down_swapped = edge(
        "backward", grad_fourth, [stream_three, norm_gains[3:4], grad_zero, late_part],
        ways, rows, 4, late_group, 0, 5, "edge_four", "reduce",
        [spread_load(late_joints[1:], late_joints[1].shape[2], 1)],
    )

    grad_attended = project(grad_low_three, focus_mat[:, 3 * heads_width :])
    joint_grad = attend_back(joint_low, grad_attended, down, side, rows)
    grad_low_two, grad_two, gain_three, late_swapped = edge(
        "backward", project_t(joint_grad, focus_mat[:, : 3 * heads_width]).astype(low),
        [stream_two, norm_gains[2:3], grad_three], ways, rows, 4, 0, early_group, 6, "edge_five",
        loads=[spread_load(late_joints[:1], late_joints[1].shape[2], 0)],
    )
    focus_joints = [by_spot(outer_rows(third_low, joint_grad)), by_spot(outer_rows(grad_low_three, attended_low))]

    grad_second, early_joints = ffn_back(grad_low_two, second_low, early_both, early_hidden, early_mat)
    grad_low_one, grad_one, gain_two, focus_swapped = edge(
        "backward", grad_second, [stream_one, norm_gains[1:2], grad_two],
        ways, rows, 4, early_group, 0, 7, "edge_six",
        loads=[chip_load(focus_joints[:1], heads_width, 1)],
    )
    early_joints = [in_order(one) for one in early_joints + focus_joints[1:]]
    early_swapped = swap(after(in_order(jnp.concatenate(early_joints, axis=2)), grad_low_one))

    grad_scanned = project(grad_low_one, out_mat)
    (
        grad_channel,
        grad_step_low,
        gate_low,
        in_sums,
        out_sums,
        bias_grad,
        decay_grad,
        skip_grad,
    ) = scan_backward(
        keeping, channel_low, step_raw, gate_half, grad_scanned, bias, rates_t, skip, in_wide, out_wide,
        groups, LANES,
    )
    grad_rank = project_t(grad_step_low, step_mat)
    gate_joint = outer_rows(first_low, gate_low).astype(low).reshape(spots, -1, channels)
    rest = mix_part[:, PROJ_OUT:]
    grad_rows, gate_swapped = mixed_sum(
        after(
            jnp.concatenate(
                [grad_rank, jnp.sum(in_sums, axis=-1), jnp.sum(out_sums, axis=-1), jnp.zeros_like(rest)], axis=1
            ),
            early_swapped,
        ),
        8, "mix_grad_sum",
        [chip_load([gate_joint], channels, 0)],
    )
    grad_rows_low = grad_rows.astype(low)
    rows_joint = jnp.concatenate(
        [
            outer_rows(grad_low_one, mixer_low),
            outer_rows(grad_rows_low, channel_low),
            outer_rows(rank_low, grad_step_low),
        ],
        axis=0,
    ).astype(low)
    grad_wide_low = jnp.pad(grad_rows_low, ((0, 0), (0, 256 - PROJ_OUT)))
    conv_low, conv_grads = front_back(
        conv_in, age, left, taps_t, offset[None], grad_channel, grad_wide_low, wide_select
    )
    conv_joint = outer_rows(first_low, conv_low).astype(low).reshape(spots, -1, channels)
    in_grad = jnp.concatenate([conv_low, gate_low], axis=1)
    grad_first = project_t(in_grad, in_mat).astype(low)
    rows_joint = rows_joint.reshape(spots, -1, channels)
    rows_joint = jnp.pad(rows_joint, ((0, 0), (0, -own_rows % 16), (0, 0)))
    lines = jnp.concatenate([conv_grads[: CONV + 1], bias_grad, skip_grad, decay_grad], axis=0)
    lines = jnp.pad(lines, ((0, 1), (0, 0)))
    blank = jnp.zeros_like(lines)
    lines = jnp.where(core == 0, jnp.concatenate([lines, blank], axis=1), jnp.concatenate([blank, lines], axis=1))
    gains = jnp.concatenate([jnp.zeros_like(gain_two), gain_two, gain_three, gain_four], axis=0)
    small = jnp.concatenate([lines, gains.reshape(8, -1)], axis=0)
    input_grad, small, output, conv_swapped, rows_swapped = edge(
        "last", grad_first, [stream_zero, norm_gains[0:1], grad_one, small, output_part, stream_three],
        ways, rows, 4, 0, None, 9, "edge_seven",
        loads=[chip_load([conv_joint], channels, 0), chip_load([rows_joint], channels, 0)],
    )
    lines = small[: CONV + 3 + STATE]
    gains = small[-8:].reshape(norm_gains.shape)
    early_gate_up_grad, early_down_grad, focus_out_grad = spread_out(early_swapped, 3 * early_down.shape[1] // spots)
    return (
        output,
        input_grad,
        gains,
        jnp.stack([chip_total(conv_swapped[:, 0]), chip_total(gate_swapped[:, 0])]),
        chip_total(rows_swapped[:, 0, :own_rows]),
        lines[:CONV].T,
        lines[CONV],
        lines[CONV + 1],
        lines[CONV + 3 :].T,
        lines[CONV + 2],
        early_gate_up_grad,
        early_down_grad,
        chip_total(focus_swapped),
        focus_out_grad,
        late_swapped.astype(jnp.float32),
        late_down_swapped[0].astype(jnp.float32),
    )


def solution(mesh):
    counts = (mesh.shape["dp"], mesh.shape["tensor"])
    chosen = partial(grouped_body, counts, 6, 0, 6) if counts == (8, 4) else body
    return jax.shard_map(
        chosen,
        mesh=mesh,
        in_specs=(
            P("dp", None),
            P("dp", None),
            P(),
            P(None, "dp", "tensor"),
            P("dp", "tensor"),
            P("tensor", None),
            P("tensor"),
            P("tensor"),
            P("tensor", None),
            P("tensor"),
            P(None, "dp", "tensor"),
            P("dp", "tensor"),
            P(None, "dp", "tensor"),
            P("dp", "tensor"),
            P(None, "dp", "tensor"),
            P("dp", "tensor"),
            P("dp", None),
        ),
        out_specs=(
            P("dp", None),
            P("dp", None),
            P(),
            P(None, "dp", "tensor"),
            P("dp", "tensor"),
            P("tensor", None),
            P("tensor"),
            P("tensor"),
            P("tensor", None),
            P("tensor"),
            P(None, "dp", "tensor"),
            P("dp", "tensor"),
            P(None, "dp", "tensor"),
            P("dp", "tensor"),
            P(None, "dp", "tensor"),
            P("dp", "tensor"),
        ),
        check_vma=False,
    )
```
